32 devices in a mesh: rows: 8 (over z, y), cols: 2 (over x), dp: 2 (over core).
Axes of the slice: x: 2, y: 2, z: 4, core: 2. Of those that a mesh axis runs over, the one named last changes fastest.
Arguments:
- features: bfloat16 [2, 32, 256, 512], P('dp', None, 'rows', 'cols'), may hold values from -6 to 6
- shifts: int32 [2, 32, 2], P('dp'), may hold values from -16 to 16, as said below
- first_kernel: bfloat16 [9, 32, 32], replicated, may hold values from -0.375 to 0.375
- bottle_kernel: bfloat16 [9, 32, 32], replicated, may hold values from -0.375 to 0.375
- second_kernel: bfloat16 [9, 32, 32], replicated, may hold values from -0.375 to 0.375
- cotangent: bfloat16 [2, 32, 256, 512], P('dp', None, 'rows', 'cols'), may hold values from -6 to 6
Outputs:
- prediction: bfloat16 [2, 32, 256, 512], P('dp', None, 'rows', 'cols')
- first_grad: float32 [9, 32, 32], replicated
- second_grad: float32 [9, 32, 32], replicated
The draws below stay inside these ranges and needn't reach their ends.
Inputs may be any that keep to these rules, and one draw needn't show every extreme that they name: `shifts`: every image has one channel displaced by exactly 16 and another by exactly -16 along one direction.
All inputs are finite; a program needn't handle non-finite values.
Results may differ from the reference program's by a relative error of at most 0.0059.
Values may be sent and summed in bfloat16 or wider, within the bound.
No kernel may reach another device: no remote copies, remote signals or barrier semaphores. Data moves between devices by JAX's collectives and lax.ppermute only.
A program may use at most 64 MiB of HBM per device.

```python
import math
import jax
import jax.numpy as jnp
from jax import lax

C = 32
MAXSHIFT = 16
POOL = 4
IMGS = 2
H = 256
W = 512


def draw_shifts(key, part):
    base_key, high_key, low_key, comp_key = jax.random.split(key, 4)
    shift_table = jax.random.randint(base_key, (IMGS, C, 2), -MAXSHIFT, MAXSHIFT + 1)
    high_chan = jax.random.randint(high_key, (IMGS, 1, 1), 0, C)
    low_chan = (high_chan + jax.random.randint(low_key, (IMGS, 1, 1), 1, C)) % C
    component = jax.random.randint(comp_key, (IMGS, 1, 1), 0, 2)
    chan_pos = jnp.arange(C)[None, :, None]
    comp_pos = jnp.arange(2)[None, None, :]
    shift_table = jnp.where((chan_pos == high_chan) & (comp_pos == component), MAXSHIFT, shift_table)
    shift_table = jnp.where((chan_pos == low_chan) & (comp_pos == component), -MAXSHIFT, shift_table)
    return shift_table.astype(jnp.int32)


def levels(own_key, shape, cuts, smallest, largest):
    def one(dim, parts):
        steps = jax.random.uniform(jax.random.fold_in(jax.random.fold_in(own_key, 6), dim), (parts,), jnp.float32, smallest / len(cuts), largest / len(cuts))
        return jnp.repeat(jnp.exp(steps), shape[dim] // parts).reshape((-1,) + (1,) * (len(shape) - dim - 1))

    level = one(*cuts[0])
    for cut in cuts[1:]:
        level = level * one(*cut)
    return level


def centred(own_key, shape, scale, bound, cuts=(), dtype=jnp.bfloat16):
    drawn = jax.random.normal(own_key, shape, jnp.float32) * scale
    if len(cuts) > 0:
        drawn = levels(own_key, shape, cuts, -0.22, 0.18) * drawn
    return jnp.clip(drawn, min=-bound, max=bound).astype(dtype)


def setup_inputs(seed: int = 0) -> dict:
    key_of = jax.random.split(jax.random.key(seed), 7)
    return {
        "features": centred(key_of[0], (IMGS, C, H, W), 1.0, 6.0, ((0, 2), (2, 8), (3, 2))),
        "shifts": draw_shifts(jax.random.fold_in(key_of[6], 71), 0),
        "first_kernel": centred(key_of[2], (9, C, C), (9 * C) ** -0.5, 0.375),
        "bottle_kernel": centred(key_of[3], (9, C, C), (9 * C) ** -0.5, 0.375),
        "second_kernel": centred(key_of[4], (9, C, C), (9 * C) ** -0.5, 0.375),
        "cotangent": centred(key_of[5], (IMGS, C, H, W), 1.0, 6.0, ((0, 2), (2, 8), (3, 2))),
    }


def stored(values):
    return lax.optimization_barrier(values.astype(jnp.bfloat16))

def pad_spatial(values, margin):
    return jnp.pad(values, ((0, 0), (margin, margin), (margin, margin)))

def convolve_one(values, kernel, transpose):
    height = values.shape[1]
    span = values.shape[2]
    padded = pad_spatial(values.astype(jnp.float32), 1)
    weights = kernel.astype(jnp.float32)
    result = jnp.zeros((weights.shape[1], height, span), jnp.float32)
    for tap_index in range(9):
        row_off = tap_index // 3 - 1
        col_off = tap_index % 3 - 1
        if transpose:
            window = padded[:, 1 - row_off:1 - row_off + height, 1 - col_off:1 - col_off + span]
            result = result + jnp.einsum('oi,ohw->ihw', weights[tap_index], window)
        else:
            window = padded[:, 1 + row_off:1 + row_off + height, 1 + col_off:1 + col_off + span]
            result = result + jnp.einsum('oi,ihw->ohw', weights[tap_index], window)
    return result

def convolve_all(values, kernel, transpose):
    return lax.map(lambda single: convolve_one(single, kernel, transpose), values)

def correlate_one(grad_out, values):
    height = values.shape[1]
    span = values.shape[2]
    padded = pad_spatial(values.astype(jnp.float32), 1)
    upper = grad_out.astype(jnp.float32)
    pieces = []
    for tap_index in range(9):
        row_off = tap_index // 3 - 1
        col_off = tap_index % 3 - 1
        window = padded[:, 1 + row_off:1 + row_off + height, 1 + col_off:1 + col_off + span]
        pieces.append(jnp.einsum('ohw,ihw->oi', upper, window))
    return jnp.stack(pieces)

def correlate(grad_out, values):
    return lax.optimization_barrier(jnp.sum(lax.map(lambda pair: correlate_one(pair[0], pair[1]), (grad_out, values)), axis=0))

def pool_sum(values):
    shape = values.shape
    return values.reshape(shape[0], shape[1], shape[2] // POOL, POOL, shape[3] // POOL, POOL).sum(axis=(3, 5))

def upsample(values):
    return jnp.repeat(jnp.repeat(values, POOL, axis=2), POOL, axis=3)

def warp_image(features, shifts):
    padded = jnp.pad(features, ((0, 0), (0, 0), (MAXSHIFT, MAXSHIFT), (MAXSHIFT, MAXSHIFT)))

    def single_plane(channel_plane, row_shift, col_shift):
        return lax.dynamic_slice(channel_plane, ((MAXSHIFT + row_shift).astype(jnp.int32), (MAXSHIFT + col_shift).astype(jnp.int32)), (H, W))
    return jax.vmap(jax.vmap(single_plane))(padded, shifts[..., 0], shifts[..., 1])

def reference(features, shifts, first_kernel, bottle_kernel, second_kernel, cotangent):
    warped = warp_image(features, shifts)
    first_pre = convolve_all(warped, first_kernel, False)
    first_act = stored(jax.nn.silu(first_pre))
    pooled = stored(pool_sum(first_act.astype(jnp.float32)) / (POOL * POOL))
    bottle = convolve_all(pooled, bottle_kernel, False)
    blended = stored(first_act.astype(jnp.float32) + upsample(bottle))
    prediction = convolve_all(blended, second_kernel, False).astype(jnp.bfloat16)
    blend_grad = stored(convolve_all(cotangent, second_kernel, True))
    coarse_grad = stored(pool_sum(blend_grad.astype(jnp.float32)))
    pooled_grad = convolve_all(coarse_grad, bottle_kernel, True)
    act_grad = blend_grad.astype(jnp.float32) + upsample(pooled_grad) / (POOL * POOL)
    sigma = jax.nn.sigmoid(first_pre)
    pre_grad = (act_grad * sigma * (1.0 + first_pre * (1.0 - sigma))).astype(jnp.bfloat16)
    factor = 1.0 / math.sqrt(IMGS * H * W)
    first_grad = correlate(pre_grad, warped) * factor
    second_grad = correlate(cotangent, blended) * factor
    return (prediction, first_grad, second_grad)
```

```python
import functools
import math

import jax
import jax.numpy as jnp
from jax import lax
from jax.experimental import pallas as pl
from jax.experimental.pallas import tpu as pltpu
from jax.sharding import PartitionSpec as P


MAXSHIFT = 16
POOL = 4
TILE = 128
SLOT = 32
EXT = 9
FHALO = MAXSHIFT + EXT
CHALO = 5
F32 = jnp.float32
BF16 = jnp.bfloat16
VMEM = pl.BlockSpec(memory_space=pltpu.VMEM)
SMEM = pl.BlockSpec(memory_space=pltpu.SMEM)
LIMIT = 56 * 1024 * 1024


def lanes_of(shape):
    return lax.broadcasted_iota(jnp.int32, shape, len(shape) - 1)


def turn(values, shift):
    width = values.shape[-1]
    return pltpu.roll(values, shift % width, values.ndim - 1)


def sides():
    row, col = lax.axis_index("rows"), lax.axis_index("cols")
    return (
        row > 0,
        row < lax.axis_size("rows") - 1,
        col > 0,
        col < lax.axis_size("cols") - 1,
    )


def pack_kernel(edges, feat, cot, feat_rows, cot_rows, up_msg, down_msg, col_msg, *rest):
    corner_msgs, (fs, cs) = rest[:-2], rest[-2:]
    chans, height, span = feat.shape
    tiles = span // TILE
    for src, dst, out in ((feat, fs, feat_rows), (cot, cs, cot_rows)):
        for c in range(chans):
            for t in range(tiles):
                dst[t, pl.ds(c, height, stride=chans), :] = src[
                    c, :, t * TILE : (t + 1) * TILE
                ].astype(F32)
        for t in range(tiles):
            out[:, t * TILE : (t + 1) * TILE] = dst[t].astype(BF16)
    cut = FHALO * chans
    up_msg[0:cut] = feat_rows[0:cut]
    up_msg[cut:] = cot_rows[0 : CHALO * chans]
    down_msg[0:cut] = feat_rows[(height - FHALO) * chans :]
    down_msg[cut:] = cot_rows[(height - CHALO) * chans :]
    lane = lanes_of((chans, TILE))
    for r in range(height):
        at = slice(r * chans, (r + 1) * chans)
        cots = jnp.where(lane < 2 * SLOT, turn(cs[0, at], SLOT), turn(cs[tiles - 1, at], -SLOT))
        feats = jnp.where(lane < 2 * SLOT, fs[0, at], fs[tiles - 1, at])
        outer = (lane < SLOT) | (lane >= TILE - SLOT)
        col_msg[at] = jnp.where(outer, feats, cots).astype(BF16)
    is_left = lax.axis_index("cols") == 0
    for (vertical, edge), msg in zip(edges, corner_msgs):
        f0 = 0 if vertical == "up" else height - FHALO
        c0 = 0 if vertical == "up" else height - CHALO
        pieces = [(fs, f0 + j) for j in range(FHALO)] + [(cs, c0 + j) for j in range(CHALO)]
        for q in range(0, len(pieces), POOL):
            total = jnp.zeros((chans, TILE), F32)
            for k, (ref, r) in enumerate(pieces[q : q + POOL]):
                at = slice(r * chans, (r + 1) * chans)
                if edge == "left":
                    piece = ref[0, at]
                elif edge == "right":
                    piece = turn(ref[tiles - 1, at], SLOT)
                else:
                    piece = jnp.where(is_left, turn(ref[tiles - 1, at], SLOT), ref[0, at])
                inside = (lane >= k * SLOT) & (lane < (k + 1) * SLOT)
                total = jnp.where(inside, turn(piece, k * SLOT), total)
            msg[(q // POOL) * chans : (q // POOL + 1) * chans] = total.astype(BF16)


def conv_sum(parts, chans, step):
    width = parts.shape[1]
    return (
        pltpu.roll(parts[0:chans], step, 1)
        + parts[chans : 2 * chans]
        + pltpu.roll(parts[2 * chans : 3 * chans], width - step, 1)
    )


def block_sum(values):
    width = values.shape[1]
    lane = lanes_of(values.shape)
    even = (lane & 1) == 0
    pair = values + jnp.where(even, pltpu.roll(values, width - 1, 1), pltpu.roll(values, 1, 1))
    low = (lane & 2) == 0
    return pair + jnp.where(low, pltpu.roll(pair, width - 2, 1), pltpu.roll(pair, 2, 1))


def correlate(u, views, acc, height, chans, span):
    for b in range(3):
        acc[b] = jnp.zeros(acc.shape[1:], F32)

    def group(g, _):
        at = pl.multiple_of(g * POOL * chans, POOL * chans)
        left = u[pl.ds(at, POOL * chans), 0:span]
        for b in range(3):
            right = views[b][pl.ds(at, (POOL + 2) * chans), 0:span]
            acc[b, :, 0 : (POOL + 2) * chans] += lax.dot_general(
                left, right, (((1,), (1,)), ((), ())), preferred_element_type=F32
            )
        return 0

    lax.fori_loop(0, height // POOL, group, 0)


def folded(acc, b, chans):
    total = None
    for k in range(POOL):
        block = acc[b, k * chans : (k + 1) * chans, :]
        block = block if k == 0 else turn(block, -k * chans)
        total = block if total is None else total + block
    return total[:, 0:TILE]


def main_kernel(
    shifts, feat, cot, up, down, col_r, col_l, up_r, up_l, down_r, down_l,
    w_first, w_back, w_bottle, w_bottle_back,
    grads, blended,
    fs, ws, warped, warped_m, warped_p, cots, back, coarse, act_grad, act, pooled, pre_grad, bl_m, bl_p, acc,
):
    chans = shifts.shape[0]
    span = feat.shape[1]
    height = feat.shape[0] // chans
    tiles = span // TILE
    width = span + TILE
    has_up, has_down, has_left, has_right = sides()
    lane = lanes_of((chans, TILE))
    right_lanes = (lane < SLOT) & has_right
    left_lanes = (lane >= TILE - SLOT) & has_left
    wide = lanes_of((chans, width))
    in_cols = (wide < span) | ((wide < span + TILE // 2) & has_right) | (
        (wide >= span + TILE // 2) & has_left
    )

    def rows_at(r, count=1):
        return slice(r * chans, (r + count) * chans)

    def halo_tile(right, left):
        return jnp.where(right_lanes, right, jnp.where(left_lanes, left, 0.0))

    def corner(right_ref, left_ref, slot):
        at, k = rows_at(slot // POOL), slot % POOL
        return halo_tile(
            turn(right_ref[at].astype(F32), -k * SLOT),
            turn(left_ref[at].astype(F32), TILE - SLOT - k * SLOT),
        )

    cots[rows_at(0, CHALO), 0:span] = up[rows_at(FHALO, CHALO)]
    cots[rows_at(CHALO, height), 0:span] = cot[...]
    cots[rows_at(CHALO + height, CHALO), 0:span] = down[rows_at(FHALO, CHALO)]
    for j in range(CHALO):
        cots[rows_at(j), span:width] = corner(up_r, up_l, FHALO + j).astype(BF16)
        cots[rows_at(CHALO + height + j), span:width] = corner(
            down_r, down_l, FHALO + j
        ).astype(BF16)
    for r in range(height):
        cots[rows_at(CHALO + r), span:width] = halo_tile(
            turn(col_r[rows_at(r)].astype(F32), -SLOT), turn(col_l[rows_at(r)].astype(F32), SLOT)
        ).astype(BF16)

    def back_group(g, seen):
        at = pl.multiple_of(g * POOL * chans, POOL * chans)
        parts = jnp.dot(
            w_back[...], cots[pl.ds(at, (POOL + 2) * chans), :], preferred_element_type=F32
        )
        total = None
        for k in range(POOL):
            row = conv_sum(parts[3 * k * chans : 3 * (k + 1) * chans], chans, 1).astype(BF16)
            back[pl.ds(pl.multiple_of(at + k * chans, chans), chans), :] = row[:, 0:span]
            row = row.astype(F32)
            total = row if total is None else total + row
        block = jnp.where(in_cols & seen, block_sum(total), 0.0)
        coarse[pl.ds(pl.multiple_of(g * chans, chans), chans), :] = block.astype(BF16)
        return 0

    groups = height // POOL
    back_group(0, has_up)
    back_group(groups + 1, has_down)
    lax.fori_loop(1, groups + 1, lambda g, _: back_group(g, True), 0)

    def grad_group(g, _):
        parts = jnp.dot(
            w_bottle_back[...],
            coarse[pl.ds(pl.multiple_of(g * chans, chans), 3 * chans), :],
            preferred_element_type=F32,
        )
        mean = conv_sum(parts, chans, POOL)[:, 0:span] * (1.0 / POOL**2)
        for k in range(POOL):
            at = pl.multiple_of((g * POOL + k) * chans, chans)
            act_grad[pl.ds(at, chans), :] = (
                back[pl.ds(pl.multiple_of(at + POOL * chans, chans), chans), :].astype(F32) + mean
            )
        return 0

    lax.fori_loop(0, groups, grad_group, 0)

    for t in range(tiles):
        part = slice(t * TILE, (t + 1) * TILE)
        fs[t, rows_at(0, FHALO)] = up[rows_at(0, FHALO), part].astype(F32)
        fs[t, rows_at(FHALO, height)] = feat[:, part].astype(F32)
        fs[t, rows_at(FHALO + height, FHALO)] = down[rows_at(0, FHALO), part].astype(F32)
    for j in range(FHALO):
        fs[tiles, rows_at(j)] = corner(up_r, up_l, j)
        fs[tiles, rows_at(FHALO + height + j)] = corner(down_r, down_l, j)
    for r in range(height):
        fs[tiles, rows_at(FHALO + r)] = halo_tile(
            col_r[rows_at(r)].astype(F32), col_l[rows_at(r)].astype(F32)
        )

    tall = height + 2 * EXT

    def warp(c, _):
        start = (MAXSHIFT + shifts[c, 0]) * chans + c
        plane = jnp.concatenate(
            [fs[t, pl.ds(start, tall, stride=chans), :] for t in range(tiles + 1)], axis=1
        )
        moved = pltpu.roll(plane, lax.rem(width - shifts[c, 1], width), 1)
        for t in range(tiles + 1):
            ws[t, pl.ds(c, tall, stride=chans), :] = moved[:, t * TILE : (t + 1) * TILE]
        return 0

    lax.fori_loop(0, chans, warp, 0)
    for j in range(tall):
        row = jnp.concatenate([ws[t, rows_at(j)] for t in range(tiles + 1)], axis=1)
        if j < EXT:
            row = jnp.where(in_cols & has_up, row, 0.0)
        elif j >= EXT + height:
            row = jnp.where(in_cols & has_down, row, 0.0)
        else:
            row = jnp.where(in_cols, row, 0.0)
        warped[rows_at(j)] = row.astype(BF16)
        if EXT - 1 <= j <= EXT + height:
            at = rows_at(j - EXT + 1)
            warped_m[at] = turn(row, 1)[:, 0:span].astype(BF16)
            warped_p[at] = turn(row, -1)[:, 0:span].astype(BF16)

    def first_group(g, seen, own):
        at = pl.multiple_of(g * POOL * chans, POOL * chans)
        parts = jnp.dot(
            w_first[...], warped[pl.ds(at, (POOL + 2) * chans), :], preferred_element_type=F32
        )
        total = None
        for k in range(POOL):
            pre = conv_sum(parts[3 * k * chans : 3 * (k + 1) * chans], chans, 1)
            sigma = 0.5 * jnp.tanh(0.5 * pre) + 0.5
            row = (pre * sigma).astype(BF16)
            here = pl.multiple_of(at + k * chans, chans)
            act[pl.ds(here, chans), :] = row
            row = row.astype(F32)
            total = row if total is None else total + row
            if own:
                there = pl.ds(pl.multiple_of(here - 2 * POOL * chans, chans), chans)
                pre, sigma = pre[:, 0:span], sigma[:, 0:span]
                pre_grad[there, :] = (
                    act_grad[there, :] * (sigma * (1.0 + pre * (1.0 - sigma)))
                ).astype(BF16)
        block = jnp.where(in_cols & seen, block_sum(total) * (1.0 / POOL**2), 0.0)
        pooled[pl.ds(pl.multiple_of(g * chans, chans), chans), :] = block.astype(BF16)
        return 0

    for g in (0, 1):
        first_group(g, has_up, False)
    for g in (groups + 2, groups + 3):
        first_group(g, has_down, False)
    lax.fori_loop(2, groups + 2, lambda g, _: first_group(g, True, True), 0)

    def blend_group(g, rows, seen):
        parts = jnp.dot(
            w_bottle[...],
            pooled[pl.ds(pl.multiple_of(g * chans, chans), 3 * chans), :],
            preferred_element_type=F32,
        )
        bottle = conv_sum(parts, chans, POOL)
        for k in rows:
            here = pl.multiple_of(((g + 1) * POOL + k) * chans, chans)
            there = pl.ds(pl.multiple_of((g * POOL + k - POOL + 1) * chans, chans), chans)
            row = act[pl.ds(here, chans), :].astype(F32) + bottle
            row = jnp.where(in_cols & seen, row, 0.0).astype(BF16)
            blended[there, :] = row
            row = row.astype(F32)
            bl_m[there, :] = turn(row, 1)[:, 0:span].astype(BF16)
            bl_p[there, :] = turn(row, -1)[:, 0:span].astype(BF16)
        return 0

    blend_group(0, (POOL - 1,), has_up)
    blend_group(groups + 1, (0,), has_down)
    lax.fori_loop(1, groups + 1, lambda g, _: blend_group(g, range(POOL), True), 0)

    own_rows = warped.at[pl.ds((EXT - 1) * chans, (height + 2) * chans)]
    correlate(pre_grad, (warped_m, own_rows, warped_p), acc, height, chans, span)
    for b in range(3):
        grads[rows_at(b)] = folded(acc, b, chans)
    correlate(cot, (bl_m, blended, bl_p), acc, height, chans, span)
    for b in range(3):
        grads[rows_at(3 + b)] = folded(acc, b, chans)


def predict_kernel(blended, w_second, out, scratch):
    chans, height, span = out.shape
    tiles = span // TILE

    def group(g, _):
        at = pl.multiple_of(g * POOL * chans, POOL * chans)
        parts = jnp.dot(
            w_second[...], blended[pl.ds(at, (POOL + 2) * chans), :], preferred_element_type=F32
        )
        for k in range(POOL):
            row = conv_sum(parts[3 * k * chans : 3 * (k + 1) * chans], chans, 1)
            for t in range(tiles):
                scratch[t, pl.ds(g * POOL + k, chans, stride=height), :] = row[
                    :, t * TILE : (t + 1) * TILE
                ]
        return 0

    lax.fori_loop(0, height // POOL, group, 0)
    for c in range(chans):
        for t in range(tiles):
            out[c, :, t * TILE : (t + 1) * TILE] = scratch[
                t, c * height : (c + 1) * height
            ].astype(BF16)


def final_kernel(factor, mine, other, first, second):
    chans = first.shape[1]
    for index, out in enumerate((first, second)):
        for b in range(3):
            at = slice((3 * index + b) * chans, (3 * index + b + 1) * chans)
            total = (mine[at] + other[at]) * factor
            for a in range(3):
                block = total if a == 0 else turn(total, -a * chans)
                out[3 * a + b] = block[:, 0:chans]


def banded(kernel, count):
    chans = kernel.shape[1]
    taps = kernel.reshape(3, 3, chans, chans).transpose(1, 2, 0, 3).reshape(3 * chans, 3 * chans)
    bands = [
        jnp.pad(taps, ((0, 0), (k * chans, (count - 1 - k) * chans))) for k in range(count)
    ]
    return jnp.concatenate(bands, axis=0)


def turned(kernel):
    return kernel[::-1].transpose(0, 2, 1)


def call(kernel, outs, scratch, n_in, flops=0, smem_first=False):
    specs = [VMEM] * n_in
    if smem_first:
        specs[0] = SMEM
    return pl.pallas_call(
        kernel,
        out_shape=outs,
        in_specs=specs,
        out_specs=jax.tree.map(lambda _: VMEM, outs),
        scratch_shapes=scratch,
        compiler_params=pltpu.CompilerParams(vmem_limit_bytes=LIMIT),
        cost_estimate=pl.CostEstimate(flops=flops, bytes_accessed=4 << 20, transcendentals=0),
    )


def shards(features, shifts, first_kernel, bottle_kernel, second_kernel, cotangent):
    imgs, chans, height, span = features.shape
    rows, cols, dp = (lax.axis_size(a) for a in ("rows", "cols", "dp"))
    tiles = span // TILE
    width = span + TILE
    full = height * chans

    def bf(*shape):
        return jax.ShapeDtypeStruct(shape, BF16)

    if cols == 2:
        edges = (("up", "single"), ("down", "single"))
    else:
        edges = tuple((v, e) for v in ("up", "down") for e in ("left", "right"))
    halo = (FHALO + CHALO) * chans
    packed = pl.cdiv(FHALO + CHALO, POOL) * chans
    feat_rows, cot_rows, up_msg, down_msg, col_msg, *corner_msgs = call(
        functools.partial(pack_kernel, edges),
        (bf(full, span), bf(full, span), bf(halo, span), bf(halo, span), bf(full, TILE))
        + tuple(bf(packed, TILE) for _ in edges),
        [pltpu.VMEM((tiles, full, TILE), F32)] * 2,
        2,
    )(features[0], cotangent[0])

    ahead = [(i, i + 1) for i in range(rows - 1)]
    astern = [(i + 1, i) for i in range(rows - 1)]
    up = lax.ppermute(down_msg, "rows", ahead)
    down = lax.ppermute(up_msg, "rows", astern)

    def diagonal(message, step, turns):
        pairs = []
        for i in range(rows):
            for j in range(cols):
                for move in turns:
                    if 0 <= i + step < rows and 0 <= j + move < cols:
                        pairs.append((i * cols + j, (i + step) * cols + j + move))
        return lax.ppermute(message, ("rows", "cols"), pairs)

    if cols == 2:
        col_r = col_l = lax.ppermute(col_msg, "cols", [(0, 1), (1, 0)])
        up_r = up_l = diagonal(corner_msgs[1], 1, (-1, 1))
        down_r = down_l = diagonal(corner_msgs[0], -1, (-1, 1))
    else:
        col_r = lax.ppermute(col_msg, "cols", [(i + 1, i) for i in range(cols - 1)])
        col_l = lax.ppermute(col_msg, "cols", [(i, i + 1) for i in range(cols - 1)])
        up_r = diagonal(corner_msgs[2], 1, (-1,))
        up_l = diagonal(corner_msgs[3], 1, (1,))
        down_r = diagonal(corner_msgs[0], -1, (-1,))
        down_l = diagonal(corner_msgs[1], -1, (1,))

    tall = height + 2 * EXT
    groups = height // POOL
    grads, blended = call(
        main_kernel,
        (jax.ShapeDtypeStruct((6 * chans, TILE), F32), bf((height + 2) * chans, width)),
        [
            pltpu.VMEM((tiles + 1, (height + 2 * FHALO) * chans, TILE), F32),
            pltpu.VMEM((tiles + 1, tall * chans, TILE), F32),
            pltpu.VMEM((tall * chans, width), BF16),
            pltpu.VMEM(((height + 2) * chans, span), BF16),
            pltpu.VMEM(((height + 2) * chans, span), BF16),
            pltpu.VMEM(((height + 2 * CHALO) * chans, width), BF16),
            pltpu.VMEM(((height + 2 * POOL) * chans, span), BF16),
            pltpu.VMEM(((groups + 2) * chans, width), BF16),
            pltpu.VMEM((full, span), F32),
            pltpu.VMEM(((height + 4 * POOL) * chans, width), BF16),
            pltpu.VMEM(((groups + 4) * chans, width), BF16),
            pltpu.VMEM((full, span), BF16),
            pltpu.VMEM(((height + 2) * chans, span), BF16),
            pltpu.VMEM(((height + 2) * chans, span), BF16),
            pltpu.VMEM((3, POOL * chans, 2 * TILE), F32),
        ],
        15,
        flops=10**9,
        smem_first=True,
    )(
        shifts[0], feat_rows, cot_rows, up, down, col_r, col_l, up_r, up_l, down_r, down_l,
        banded(first_kernel, POOL), banded(turned(second_kernel), POOL),
        banded(bottle_kernel, 1), banded(turned(bottle_kernel), 1),
    )
    prediction = call(
        predict_kernel,
        bf(chans, height, span),
        [pltpu.VMEM((tiles, full, TILE), F32)],
        2,
        flops=2 * 10**8,
    )(blended, banded(second_kernel, POOL))

    steps = []
    for axis, size in (("dp", dp), ("cols", cols), ("rows", rows)):
        bit = 1
        while bit < size:
            steps.append((axis, [(i, i ^ bit) for i in range(size)]))
            bit *= 2
    for axis, pairs in steps[:-1]:
        grads = grads + lax.ppermute(grads, axis, pairs)
    other = lax.ppermute(grads, *steps[-1])
    factor = 1.0 / math.sqrt(imgs * dp * height * rows * span * cols)
    shape = jax.ShapeDtypeStruct((9, chans, chans), F32)
    first_grad, second_grad = call(
        functools.partial(final_kernel, factor), (shape, shape), [], 2
    )(grads, other)
    return (prediction[None], first_grad, second_grad)


def solution(mesh):
    placed = (
        P("dp", None, "rows", "cols"),
        P("dp", None, None),
        P(),
        P(),
        P(),
        P("dp", None, "rows", "cols"),
    )
    return jax.shard_map(
        shards,
        mesh=mesh,
        in_specs=placed,
        out_specs=(P("dp", None, "rows", "cols"), P(), P()),
        check_vma=False,
    )
```

```python
import functools
import math

import jax
import jax.numpy as jnp
from jax import lax
from jax.experimental import pallas as pl
from jax.experimental.pallas import tpu as pltpu
from jax.sharding import PartitionSpec as P


MAXSHIFT = 16
POOL = 4
TILE = 128
SLOT = 32
EXT = 9
FHALO = MAXSHIFT + EXT
CHALO = 5
F32 = jnp.float32
BF16 = jnp.bfloat16
VMEM = pl.BlockSpec(memory_space=pltpu.VMEM)
SMEM = pl.BlockSpec(memory_space=pltpu.SMEM)
MIB = 1024 * 1024


def lanes_of(shape):
    return lax.broadcasted_iota(jnp.int32, shape, len(shape) - 1)


def turn(values, shift):
    width = values.shape[-1]
    if isinstance(shift, int):
        shift = shift % width
        if shift == 0:
            return values
    return pltpu.roll(values, shift, values.ndim - 1)


def has_sides():
    row, col = lax.axis_index("rows"), lax.axis_index("cols")
    return (
        row > 0,
        row < lax.axis_size("rows") - 1,
        col > 0,
        col < lax.axis_size("cols") - 1,
    )


def rows_at(r, chans, count=1):
    if isinstance(r, int):
        return slice(r * chans, (r + count) * chans)
    return pl.ds(pl.multiple_of(r * chans, chans), count * chans)


def by_rows(source, out):
    chans, height, span = source.shape
    for t in range(0, span, TILE):
        part = jnp.transpose(source[:, :, t : t + TILE], (1, 0, 2))
        out[:, t : t + TILE] = part.reshape(height * chans, TILE)


def feature_kernel(feat, feat_rows, up_msg, down_msg):
    chans, height = feat.shape[0], feat.shape[1]
    by_rows(feat, feat_rows)
    up_msg[...] = feat_rows[0 : FHALO * chans]
    down_msg[...] = feat_rows[(height - FHALO) * chans :]


def pack_kernel(edges, feat_rows, cot, cot_rows, up_msg, down_msg, col_msg, *corner_msgs):
    chans, height, span = cot.shape
    last = slice(span - TILE, span)
    by_rows(cot, cot_rows)
    up_msg[...] = cot_rows[0 : CHALO * chans]
    down_msg[...] = cot_rows[(height - CHALO) * chans :]
    lane = lanes_of((chans, TILE))
    is_left = lax.axis_index("cols") == 0
    for (vertical, edge), msg in zip(edges, corner_msgs):
        f0 = 0 if vertical == "up" else height - FHALO
        c0 = 0 if vertical == "up" else height - CHALO
        pieces = [(feat_rows, f0 + j) for j in range(FHALO)]
        pieces += [(cot_rows, c0 + j) for j in range(CHALO)]
        for q in range(0, len(pieces), POOL):
            total = jnp.zeros((chans, TILE), F32)
            for k, (ref, r) in enumerate(pieces[q : q + POOL]):
                at = rows_at(r, chans)
                if edge == "left":
                    piece = turn(ref[at, 0:TILE].astype(F32), k * SLOT)
                elif edge == "right":
                    piece = turn(ref[at, last].astype(F32), (k + 1) * SLOT)
                else:
                    piece = jnp.where(is_left, ref[at, last].astype(F32), ref[at, 0:TILE].astype(F32))
                    piece = turn(piece, jnp.where(is_left, (k + 1) * SLOT % TILE, k * SLOT))
                inside = (lane >= k * SLOT) & (lane < (k + 1) * SLOT)
                total = jnp.where(inside, piece, total)
            msg[rows_at(q // POOL, chans)] = total.astype(BF16)
    for r in range(height):
        at = rows_at(r, chans)
        cots = jnp.where(
            lane < 2 * SLOT,
            turn(cot_rows[at, 0:TILE].astype(F32), SLOT),
            turn(cot_rows[at, last].astype(F32), -SLOT),
        )
        feats = jnp.where(
            lane < 2 * SLOT, feat_rows[at, 0:TILE].astype(F32), feat_rows[at, last].astype(F32)
        )
        outer = (lane < SLOT) | (lane >= TILE - SLOT)
        col_msg[at] = jnp.where(outer, feats, cots).astype(BF16)


class Halo:

    def __init__(self, chans, single):
        _, _, has_left, has_right = has_sides()
        lane = lanes_of((chans, TILE))
        self.chans, self.single, self.has_right = chans, single, has_right
        self.right_lanes = (lane < SLOT) & has_right
        self.left_lanes = (lane >= TILE - SLOT) & has_left

    def tile(self, right, left):
        return jnp.where(self.right_lanes, right, jnp.where(self.left_lanes, left, 0.0))

    def turned(self, right_ref, left_ref, at, right_shift, left_shift):
        if self.single:
            both = right_ref[at].astype(F32)
            shift = jnp.where(self.has_right, right_shift % TILE, left_shift % TILE)
            both = turn(both, shift)
            return self.tile(both, both)
        return self.tile(
            turn(right_ref[at].astype(F32), right_shift), turn(left_ref[at].astype(F32), left_shift)
        )

    def corner(self, right_ref, left_ref, slot):
        at, k = rows_at(slot // POOL, self.chans), slot % POOL
        return self.turned(right_ref, left_ref, at, -k * SLOT, TILE - SLOT - k * SLOT)


def columns_seen(shape, span):
    _, _, has_left, has_right = has_sides()
    lane = lanes_of(shape)
    middle = span + TILE // 2
    return (lane < span) | ((lane < middle) & has_right) | ((lane >= middle) & has_left)


def block_ones(width):
    row = lax.broadcasted_iota(jnp.int32, (width, width), 0) // POOL
    col = lax.broadcasted_iota(jnp.int32, (width, width), 1) // POOL
    return jnp.where(row == col, 1.0, 0.0).astype(BF16)


def store_split(high, low, at, total):
    top = total.astype(BF16)
    high[at, :] = top
    low[at, :] = (total - top.astype(F32)).astype(BF16)


def block_sums(high, low, ones):
    return jnp.dot(high[...], ones, preferred_element_type=F32) + jnp.dot(
        low[...], ones, preferred_element_type=F32
    )


def fill_bands(out, kernel, count):
    chans = kernel.shape[1]
    out[...] = jnp.zeros(out.shape, out.dtype)
    for k in range(count):
        for b in range(3):
            for a in range(3):
                at = (b * (count + 2) + k + a) * chans
                out[k * chans : (k + 1) * chans, at : at + chans] = kernel[3 * a + b].astype(
                    out.dtype
                )


def fill_turned_bands(out, kernel, count):
    chans = kernel.shape[1]
    out[...] = jnp.zeros(out.shape, out.dtype)
    for k in range(count):
        for b in range(3):
            for a in range(3):
                at = (b * (count + 2) + k + a) * chans
                out[at : at + chans, k * chans : (k + 1) * chans] = kernel[8 - 3 * a - b].astype(
                    out.dtype
                )


def stacked(views, at):
    return jnp.concatenate([view[at, :] for view in views], axis=0)


def conv_sum(parts, chans, step):
    return (
        turn(parts[0:chans], step)
        + parts[chans : 2 * chans]
        + turn(parts[2 * chans : 3 * chans], -step)
    )


def back_kernel(
    single, cot, up, down, col_r, col_l, up_r, up_l, down_r, down_l, second, bottle,
    act_grad, view_m, view_0, view_p,
    cot_m, cot_0, cot_p, back, high, low, coarse, bands_f, bands, small_f, small,
):
    chans = second.shape[1]
    full, span = cot.shape
    height = full // chans
    width = span + TILE
    groups = height // POOL
    has_up, has_down, _, _ = has_sides()
    halo = Halo(chans, single)
    seen_cols = columns_seen((chans, width), span)

    fill_turned_bands(bands_f, second, POOL)
    bands[...] = bands_f[...].T.astype(BF16)
    fill_turned_bands(small_f, bottle, 1)
    small_t = small_f[...].T
    for b in range(3):
        small[rows_at(b, chans)] = small_t[0:chans, 3 * b * chans : 3 * (b + 1) * chans].astype(BF16)

    cot_0[rows_at(0, chans, CHALO), 0:span] = up[...]
    cot_0[rows_at(CHALO, chans, height), 0:span] = cot[...]
    cot_0[rows_at(CHALO + height, chans, CHALO), 0:span] = down[...]
    for j in range(CHALO):
        cot_0[rows_at(j, chans), span:width] = halo.corner(up_r, up_l, FHALO + j).astype(BF16)
        cot_0[rows_at(CHALO + height + j, chans), span:width] = halo.corner(
            down_r, down_l, FHALO + j
        ).astype(BF16)
    for r in range(height):
        cot_0[rows_at(CHALO + r, chans), span:width] = halo.turned(
            col_r, col_l, rows_at(r, chans), -SLOT, SLOT
        ).astype(BF16)
    for j in range(height + 2 * CHALO):
        at = rows_at(j, chans)
        cot_m[at] = turn(cot_0[at], 1)
        cot_p[at] = turn(cot_0[at], -1)
    inner = rows_at(CHALO - 1, chans, height + 2)
    view_m[...] = cot_m[inner, 0:span]
    view_0[...] = cot_0[inner, 0:span]
    view_p[...] = cot_p[inner, 0:span]

    def group(g, _):
        at = rows_at(g * POOL, chans, POOL + 2)
        rows = jnp.dot(
            bands[...], stacked((cot_m, cot_0, cot_p), at), preferred_element_type=F32
        ).astype(BF16)
        back[rows_at(g * POOL, chans, POOL), :] = rows[:, 0:span]
        rows = rows.astype(F32)
        total = rows[0:chans]
        for k in range(1, POOL):
            total = total + rows[k * chans : (k + 1) * chans]
        store_split(high, low, rows_at(g, chans), total)
        return 0

    lax.fori_loop(0, groups + 2, group, 0, unroll=2)
    sums = block_sums(high, low, block_ones(width))
    for g in range(groups + 2):
        at = rows_at(g, chans)
        seen = seen_cols
        if g == 0:
            seen = seen & has_up
        elif g == groups + 1:
            seen = seen & has_down
        coarse[at] = jnp.where(seen, sums[at], 0.0).astype(BF16)
    for g in range(groups):
        parts = jnp.dot(small[...], coarse[rows_at(g, chans, 3), :], preferred_element_type=F32)
        mean = conv_sum(parts, chans, POOL)[:, 0:span] * (1.0 / POOL**2)
        for k in range(POOL):
            r = g * POOL + k
            act_grad[rows_at(r, chans), :] = back[rows_at(r + POOL, chans), :].astype(F32) + mean


def correlate(u, u0, views, v0, acc, height, chans, span):
    acc[...] = jnp.zeros(acc.shape, F32)

    def group(g, _):
        left = jnp.concatenate(
            [view[rows_at(v0 + g * POOL, chans, POOL + 2), 0:span] for view in views], axis=0
        )
        right = u[rows_at(u0 + g * POOL, chans, POOL), 0:span]
        acc[...] += lax.dot_general(
            left, right, (((1,), (1,)), ((), ())), preferred_element_type=F32
        )
        return 0

    lax.fori_loop(0, height // POOL, group, 0, unroll=2)


def folded(acc, chans):
    lane = lanes_of((3 * chans, TILE))
    result = jnp.zeros((3 * chans, TILE), F32)
    for b in range(3):
        total = None
        for k in range(POOL):
            block = turn(
                acc[rows_at(b * (POOL + 2) + k, chans, 3), 0:TILE], (b - k) * chans
            )
            total = block if total is None else total + block
        result = jnp.where((lane >= b * chans) & (lane < (b + 1) * chans), total, result)
    return result


def main_kernel(
    single, shifts, feat, up, down, col_r, col_l, up_r, up_l, down_r, down_l,
    act_grad, view_m, view_0, view_p, first, bottle,
    grads, blended,
    fs, ws, warp_m, warp_0, warp_p, act, high, low, pooled, pre_grad, acc, bands_f, bands, small_f, small,
):
    chans = first.shape[1]
    full, span = feat.shape
    height = full // chans
    tiles = span // TILE
    width = span + TILE
    groups = height // POOL
    has_up, has_down, _, _ = has_sides()
    halo = Halo(chans, single)
    seen_cols = columns_seen((chans, width), span)

    fill_bands(bands_f, first, POOL)
    bands[...] = bands_f[...].astype(BF16)
    fill_bands(small_f, bottle, 1)
    for b in range(3):
        small[rows_at(b, chans)] = small_f[:, 3 * b * chans : 3 * (b + 1) * chans].astype(BF16)

    for t in range(tiles):
        part = slice(t * TILE, (t + 1) * TILE)
        fs[t, rows_at(0, chans, FHALO)] = up[:, part].astype(F32)
        fs[t, rows_at(FHALO, chans, height)] = feat[:, part].astype(F32)
        fs[t, rows_at(FHALO + height, chans, FHALO)] = down[:, part].astype(F32)
    for j in range(FHALO):
        fs[tiles, rows_at(j, chans)] = halo.corner(up_r, up_l, j)
        fs[tiles, rows_at(FHALO + height + j, chans)] = halo.corner(down_r, down_l, j)
    for r in range(height):
        at = rows_at(r, chans)
        fs[tiles, rows_at(FHALO + r, chans)] = halo.tile(
            col_r[at].astype(F32), col_l[at].astype(F32)
        )

    tall = height + 2 * EXT
    lane = lanes_of((tall, TILE))

    def warp(c, _):
        start = (MAXSHIFT + shifts[c, 0]) * chans + c
        move = shifts[c, 1]
        planes = [
            turn(fs[t, pl.ds(start, tall, stride=chans), :], jnp.where(move > 0, TILE - move, -move))
            for t in range(tiles + 1)
        ]
        inside = jnp.where(move > 0, lane, TILE - 1 - lane) < TILE - jnp.abs(move)
        for t in range(tiles + 1):
            after, before = planes[(t + 1) % (tiles + 1)], planes[t - 1]
            ws[t, pl.ds(c, tall, stride=chans), :] = jnp.where(
                inside, planes[t], jnp.where(move > 0, after, before)
            )
        return 0

    lax.fori_loop(0, chans, warp, 0, unroll=4)
    for j in range(tall):
        row = jnp.concatenate([ws[t, rows_at(j, chans)] for t in range(tiles + 1)], axis=1)
        seen = seen_cols
        if j < EXT:
            seen = seen & has_up
        elif j >= EXT + height:
            seen = seen & has_down
        row = jnp.where(seen, row, 0.0).astype(BF16)
        at = rows_at(j, chans)
        warp_0[at] = row
        warp_m[at] = turn(row, 1)
        warp_p[at] = turn(row, -1)

    def first_group(g, own):
        at = rows_at(g * POOL, chans, POOL + 2)
        pre = jnp.dot(
            bands[...], stacked((warp_m, warp_0, warp_p), at), preferred_element_type=F32
        )
        sigma = 0.5 * jnp.tanh(0.5 * pre) + 0.5
        rows = (pre * sigma).astype(BF16)
        act[rows_at(g * POOL, chans, POOL), :] = rows
        rows = rows.astype(F32)
        total = rows[0:chans]
        for k in range(1, POOL):
            total = total + rows[k * chans : (k + 1) * chans]
        store_split(high, low, rows_at(g, chans), total)
        if own:
            there = rows_at(g * POOL - 2 * POOL, chans, POOL)
            pre, sigma = pre[:, 0:span], sigma[:, 0:span]
            pre_grad[there, :] = (
                act_grad[there, :] * (sigma * (1.0 + pre * (1.0 - sigma)))
            ).astype(BF16)
        return 0

    for g in (0, 1, groups + 2, groups + 3):
        first_group(g, False)
    lax.fori_loop(2, groups + 2, lambda g, _: first_group(g, True), 0, unroll=2)
    sums = block_sums(high, low, block_ones(width))
    for g in range(groups + 4):
        at = rows_at(g, chans)
        seen = seen_cols
        if g < 2:
            seen = seen & has_up
        elif g >= groups + 2:
            seen = seen & has_down
        pooled[at] = jnp.where(seen, sums[at] * (1.0 / POOL**2), 0.0).astype(BF16)

    for g in range(groups + 2):
        parts = jnp.dot(small[...], pooled[rows_at(g, chans, 3), :], preferred_element_type=F32)
        bottle_row = conv_sum(parts, chans, POOL)
        rows, seen = range(POOL), seen_cols
        if g == 0:
            rows, seen = (POOL - 1,), seen & has_up
        elif g == groups + 1:
            rows, seen = (0,), seen & has_down
        for k in rows:
            row = act[rows_at((g + 1) * POOL + k, chans), :].astype(F32) + bottle_row
            blended[rows_at(g * POOL + k - POOL + 1, chans), :] = jnp.where(seen, row, 0.0).astype(
                BF16
            )

    correlate(pre_grad, 0, (warp_m, warp_0, warp_p), EXT - 1, acc, height, chans, span)
    first_part = folded(acc, chans)
    correlate(blended, 1, (view_m, view_0, view_p), 0, acc, height, chans, span)
    second_part = folded(acc, chans)
    lane = lanes_of((3 * chans, TILE))
    grads[0 : 3 * chans] = jnp.where(lane < 3 * chans, first_part, turn(second_part, 3 * chans))
    half = 3 * chans // 2
    grads[3 * chans :] = jnp.where(
        lane[0:half] < TILE // 2,
        turn(second_part[0:half], -chans),
        turn(second_part[half:], TILE // 2 - chans),
    )


def predict_kernel(part, blended, second, *rest):
    out, scratch, bands_f, bands = rest[-4:]
    chans, height, span = out.shape
    tiles = span // TILE
    bands_f[...] = jnp.zeros(bands_f.shape, F32)
    for k in range(POOL):
        for b in range(3):
            for a in range(3):
                bands_f[rows_at(3 * k + b, chans), (k + a) * chans : (k + a + 1) * chans] = second[
                    3 * a + b
                ].astype(F32)
    bands[...] = bands_f[...].astype(BF16)

    def group(g, _):
        at = rows_at(part * height + g * POOL, chans, POOL + 2)
        parts = jnp.dot(bands[...], blended[at, :], preferred_element_type=F32)
        for k in range(POOL):
            row = conv_sum(parts[3 * k * chans : 3 * (k + 1) * chans], chans, 1)
            for t in range(tiles):
                scratch[t, pl.ds(g * POOL + k, chans, stride=height), :] = row[
                    :, t * TILE : (t + 1) * TILE
                ]
        return 0

    lax.fori_loop(0, height // POOL, group, 0)
    for c in range(chans):
        for t in range(tiles):
            out[c, :, t * TILE : (t + 1) * TILE] = scratch[
                t, c * height : (c + 1) * height
            ].astype(BF16)


def final_kernel(factor, mine, other, first, second):
    chans = first.shape[1]
    total = (mine[...] + other[...]) * factor
    turned = total[0 : 3 * chans].T
    for b in range(3):
        for a in range(3):
            first[3 * a + b] = turned[b * chans : (b + 1) * chans, a * chans : (a + 1) * chans]
    half = 3 * chans // 2
    low = total[3 * chans :]
    both = jnp.concatenate([low, turn(low, -(TILE // 2))], axis=0)
    for a in range(3):
        at = slice((2 - a) * chans, (3 - a) * chans)
        second[3 * a + 2] = turn(total[at], -3 * chans)[:, 0:chans]
        second[3 * a + 1] = both[at, 0:chans]
        second[3 * a + 0] = turn(both[at], -chans)[:, 0:chans]


def call(kernel, outs, scratch, n_in, limit, flops=0, smem_first=False, **more):
    specs = [VMEM] * n_in
    if smem_first:
        specs[0] = SMEM
    more.setdefault("in_specs", specs)
    more.setdefault("out_specs", jax.tree.map(lambda _: VMEM, outs))
    return pl.pallas_call(
        kernel,
        out_shape=outs,
        scratch_shapes=scratch,
        compiler_params=pltpu.CompilerParams(vmem_limit_bytes=limit * MIB),
        cost_estimate=pl.CostEstimate(flops=flops, bytes_accessed=4 * MIB, transcendentals=0),
        **more,
    )


def predict(blended, second, shape, parts, part, before):
    chans, height, span = shape
    rows = height // parts
    tiles = span // TILE
    block = pl.BlockSpec((chans, rows, span), lambda i: (0, part, 0))
    whole = lambda a: pl.BlockSpec(a.shape, lambda i: (0,) * a.ndim)
    args = (blended, second)
    specs = [whole(a) for a in args]
    more = {}
    if before is not None:
        args += (before,)
        specs.append(pl.BlockSpec(memory_space=pl.ANY))
        more["input_output_aliases"] = {2: 0}
    return call(
        functools.partial(predict_kernel, part),
        jax.ShapeDtypeStruct(shape, BF16),
        [
            pltpu.VMEM((tiles, chans * rows, TILE), F32),
            pltpu.VMEM((3 * POOL * chans, (POOL + 2) * chans), F32),
            pltpu.VMEM((3 * POOL * chans, (POOL + 2) * chans), BF16),
        ],
        len(args),
        12,
        flops=10**9,
        grid=(1,),
        in_specs=specs,
        out_specs=block,
        **more,
    )(*args)


def shards(features, shifts, first_kernel, bottle_kernel, second_kernel, cotangent):
    imgs, chans, height, span = features.shape
    rows, cols, dp = (lax.axis_size(a) for a in ("rows", "cols", "dp"))
    tiles = span // TILE
    width = span + TILE
    full = height * chans
    groups = height // POOL
    single = cols == 2

    def bf(*shape):
        return jax.ShapeDtypeStruct(shape, BF16)

    ahead = [(i, i + 1) for i in range(rows - 1)]
    astern = [(i + 1, i) for i in range(rows - 1)]

    def diagonal(message, step, turns):
        pairs = []
        for i in range(rows):
            for j in range(cols):
                for move in turns:
                    if 0 <= i + step < rows and 0 <= j + move < cols:
                        pairs.append((i * cols + j, (i + step) * cols + j + move))
        return lax.ppermute(message, ("rows", "cols"), pairs)

    feat_rows, up_feat, down_feat = call(
        feature_kernel,
        (bf(full, span), bf(FHALO * chans, span), bf(FHALO * chans, span)),
        [],
        1,
        8,
    )(features[0])
    up_f = lax.ppermute(down_feat, "rows", ahead)
    down_f = lax.ppermute(up_feat, "rows", astern)

    if single:
        edges = (("up", "single"), ("down", "single"))
    else:
        edges = tuple((v, e) for v in ("up", "down") for e in ("left", "right"))
    packed = pl.cdiv(FHALO + CHALO, POOL) * chans
    cot_rows, up_cot, down_cot, col_msg, *corner_msgs = call(
        functools.partial(pack_kernel, edges),
        (bf(full, span), bf(CHALO * chans, span), bf(CHALO * chans, span), bf(full, TILE))
        + tuple(bf(packed, TILE) for _ in edges),
        [],
        2,
        8,
    )(feat_rows, cotangent[0])
    up_c = lax.ppermute(down_cot, "rows", ahead)
    down_c = lax.ppermute(up_cot, "rows", astern)
    if single:
        up_r = up_l = diagonal(corner_msgs[1], 1, (-1, 1))
        down_r = down_l = diagonal(corner_msgs[0], -1, (-1, 1))
        col_r = col_l = lax.ppermute(col_msg, "cols", [(0, 1), (1, 0)])
    else:
        up_r = diagonal(corner_msgs[2], 1, (-1,))
        up_l = diagonal(corner_msgs[3], 1, (1,))
        down_r = diagonal(corner_msgs[0], -1, (-1,))
        down_l = diagonal(corner_msgs[1], -1, (1,))
        col_r = lax.ppermute(col_msg, "cols", [(i + 1, i) for i in range(cols - 1)])
        col_l = lax.ppermute(col_msg, "cols", [(i, i + 1) for i in range(cols - 1)])

    tall_c = (height + 2 * CHALO) * chans
    view = bf((height + 2) * chans, span)
    band = 3 * (POOL + 2) * chans
    act_grad, *views = call(
        functools.partial(back_kernel, single),
        (jax.ShapeDtypeStruct((full, span), F32), view, view, view),
        [pltpu.VMEM((tall_c, width), BF16)] * 3
        + [pltpu.VMEM(((height + 2 * POOL) * chans, span), BF16)]
        + [pltpu.VMEM(((groups + 2) * chans, width), BF16)] * 3
        + [
            pltpu.VMEM((band, POOL * chans), F32),
            pltpu.VMEM((POOL * chans, band), BF16),
            pltpu.VMEM((9 * chans, TILE), F32),
            pltpu.VMEM((3 * chans, 3 * chans), BF16),
        ],
        11,
        16,
        flops=8 * 10**9,
    )(
        cot_rows, up_c, down_c, col_r, col_l, up_r, up_l, down_r, down_l,
        second_kernel, bottle_kernel,
    )

    tall = (height + 2 * EXT) * chans
    grads, blended = call(
        functools.partial(main_kernel, single),
        (jax.ShapeDtypeStruct((9 * chans // 2, TILE), F32), bf((height + 2) * chans, width)),
        [
            pltpu.VMEM((tiles + 1, (height + 2 * FHALO) * chans, TILE), F32),
            pltpu.VMEM((tiles + 1, tall, TILE), F32),
        ]
        + [pltpu.VMEM((tall, width), BF16)] * 3
        + [pltpu.VMEM(((height + 4 * POOL) * chans, width), BF16)]
        + [pltpu.VMEM(((groups + 4) * chans, width), BF16)] * 3
        + [
            pltpu.VMEM((full, span), BF16),
            pltpu.VMEM((band, POOL * chans), F32),
            pltpu.VMEM((POOL * chans, band), F32),
            pltpu.VMEM((POOL * chans, band), BF16),
            pltpu.VMEM((chans, 9 * chans), F32),
            pltpu.VMEM((3 * chans, 3 * chans), BF16),
        ],
        16,
        32,
        flops=10**10,
        smem_first=True,
    )(
        shifts[0], feat_rows, up_f, down_f, col_r, col_l, up_r, up_l, down_r, down_l,
        act_grad, *views, first_kernel, bottle_kernel,
    )

    steps = []
    for axis, size in (("dp", dp), ("cols", cols), ("rows", rows)):
        bit = 1
        while bit < size:
            steps.append((axis, [(i, i ^ bit) for i in range(size)]))
            bit *= 2
    parts, prediction = 2, None
    for step, (axis, pairs) in enumerate(steps):
        other = lax.ppermute(grads, axis, pairs)
        if 1 <= step <= parts:
            prediction = predict(
                blended, second_kernel, (chans, height, span), parts, step - 1, prediction
            )
            other, prediction = lax.optimization_barrier((other, prediction))
        if step < len(steps) - 1:
            grads = grads + other
            if step < parts:
                grads, blended = lax.optimization_barrier((grads, blended))
    factor = 1.0 / math.sqrt(imgs * dp * height * rows * span * cols)
    shape = jax.ShapeDtypeStruct((9, chans, chans), F32)
    first_grad, second_grad = call(
        functools.partial(final_kernel, factor), (shape, shape), [], 2, 2
    )(grads, other)
    return (prediction[None], first_grad, second_grad)


def solution(mesh):
    placed = (
        P("dp", None, "rows", "cols"),
        P("dp", None, None),
        P(),
        P(),
        P(),
        P("dp", None, "rows", "cols"),
    )
    return jax.shard_map(
        shards,
        mesh=mesh,
        in_specs=placed,
        out_specs=(P("dp", None, "rows", "cols"), P(), P()),
        check_vma=False,
    )
```

```python
import functools
import math

import jax
import jax.numpy as jnp
from jax import lax
from jax.experimental import pallas as pl
from jax.experimental.pallas import tpu as pltpu
from jax.sharding import PartitionSpec as P


MAXSHIFT = 16
POOL = 4
TILE = 128
SLOT = 32
EXT = 9
FHALO = MAXSHIFT + EXT
CHALO = 5
F32 = jnp.float32
BF16 = jnp.bfloat16
VMEM = pl.BlockSpec(memory_space=pltpu.VMEM)
SMEM = pl.BlockSpec(memory_space=pltpu.SMEM)
MIB = 1024 * 1024


def lanes_of(shape):
    return lax.broadcasted_iota(jnp.int32, shape, len(shape) - 1)


def turn(values, shift):
    width = values.shape[-1]
    if isinstance(shift, int):
        shift = shift % width
        if shift == 0:
            return values
    return pltpu.roll(values, shift, values.ndim - 1)


def has_sides():
    row, col = lax.axis_index("rows"), lax.axis_index("cols")
    return (
        row > 0,
        row < lax.axis_size("rows") - 1,
        col > 0,
        col < lax.axis_size("cols") - 1,
    )


def rows_at(r, chans, count=1):
    if isinstance(r, int):
        return slice(r * chans, (r + count) * chans)
    return pl.ds(pl.multiple_of(r * chans, chans), count * chans)


def by_rows(source, out):
    chans, height, span = source.shape
    for t in range(0, span, TILE):
        part = jnp.transpose(source[:, :, t : t + TILE], (1, 0, 2))
        out[:, t : t + TILE] = part.reshape(height * chans, TILE)


def feature_kernel(feat, feat_rows, up_msg, down_msg):
    chans, height = feat.shape[0], feat.shape[1]
    by_rows(feat, feat_rows)
    up_msg[...] = feat_rows[0 : FHALO * chans]
    down_msg[...] = feat_rows[(height - FHALO) * chans :]


def pack_kernel(edges, feat_rows, cot, cot_rows, up_msg, down_msg, col_msg, *corner_msgs):
    chans, height, span = cot.shape
    last = slice(span - TILE, span)
    by_rows(cot, cot_rows)
    up_msg[...] = cot_rows[0 : CHALO * chans]
    down_msg[...] = cot_rows[(height - CHALO) * chans :]
    lane = lanes_of((chans, TILE))
    is_left = lax.axis_index("cols") == 0
    for (vertical, edge), msg in zip(edges, corner_msgs):
        f0 = 0 if vertical == "up" else height - FHALO
        c0 = 0 if vertical == "up" else height - CHALO
        pieces = [(feat_rows, f0 + j) for j in range(FHALO)]
        pieces += [(cot_rows, c0 + j) for j in range(CHALO)]
        for q in range(0, len(pieces), POOL):
            total = jnp.zeros((chans, TILE), F32)
            for k, (ref, r) in enumerate(pieces[q : q + POOL]):
                at = rows_at(r, chans)
                if edge == "left":
                    piece = turn(ref[at, 0:TILE].astype(F32), k * SLOT)
                elif edge == "right":
                    piece = turn(ref[at, last].astype(F32), (k + 1) * SLOT)
                else:
                    piece = jnp.where(is_left, ref[at, last].astype(F32), ref[at, 0:TILE].astype(F32))
                    piece = turn(piece, jnp.where(is_left, (k + 1) * SLOT % TILE, k * SLOT))
                inside = (lane >= k * SLOT) & (lane < (k + 1) * SLOT)
                total = jnp.where(inside, piece, total)
            msg[rows_at(q // POOL, chans)] = total.astype(BF16)
    for r in range(height):
        at = rows_at(r, chans)
        cots = jnp.where(
            lane < 2 * SLOT,
            turn(cot_rows[at, 0:TILE].astype(F32), SLOT),
            turn(cot_rows[at, last].astype(F32), -SLOT),
        )
        feats = jnp.where(
            lane < 2 * SLOT, feat_rows[at, 0:TILE].astype(F32), feat_rows[at, last].astype(F32)
        )
        outer = (lane < SLOT) | (lane >= TILE - SLOT)
        col_msg[at] = jnp.where(outer, feats, cots).astype(BF16)


class Halo:

    def __init__(self, chans, single):
        _, _, has_left, has_right = has_sides()
        lane = lanes_of((chans, TILE))
        self.chans, self.single, self.has_right = chans, single, has_right
        self.right_lanes = (lane < SLOT) & has_right
        self.left_lanes = (lane >= TILE - SLOT) & has_left

    def tile(self, right, left):
        return jnp.where(self.right_lanes, right, jnp.where(self.left_lanes, left, 0.0))

    def turned(self, right_ref, left_ref, at, right_shift, left_shift):
        if self.single:
            both = right_ref[at].astype(F32)
            shift = jnp.where(self.has_right, right_shift % TILE, left_shift % TILE)
            both = turn(both, shift)
            return self.tile(both, both)
        return self.tile(
            turn(right_ref[at].astype(F32), right_shift), turn(left_ref[at].astype(F32), left_shift)
        )

    def corner(self, right_ref, left_ref, slot):
        at, k = rows_at(slot // POOL, self.chans), slot % POOL
        return self.turned(right_ref, left_ref, at, -k * SLOT, TILE - SLOT - k * SLOT)


def columns_seen(shape, span):
    _, _, has_left, has_right = has_sides()
    lane = lanes_of(shape)
    middle = span + TILE // 2
    return (lane < span) | ((lane < middle) & has_right) | ((lane >= middle) & has_left)


def block_ones(width):
    row = lax.broadcasted_iota(jnp.int32, (width, width), 0) // POOL
    col = lax.broadcasted_iota(jnp.int32, (width, width), 1) // POOL
    return jnp.where(row == col, 1.0, 0.0).astype(BF16)


def store_split(high, low, at, total):
    top = total.astype(BF16)
    high[at, :] = top
    low[at, :] = (total - top.astype(F32)).astype(BF16)


def block_sums(high, low, ones):
    return jnp.dot(high[...], ones, preferred_element_type=F32) + jnp.dot(
        low[...], ones, preferred_element_type=F32
    )


def fill_bands(out, kernel, count):
    chans = kernel.shape[1]
    out[...] = jnp.zeros(out.shape, out.dtype)
    for k in range(count):
        for b in range(3):
            for a in range(3):
                at = (b * (count + 2) + k + a) * chans
                out[k * chans : (k + 1) * chans, at : at + chans] = kernel[3 * a + b].astype(
                    out.dtype
                )


def fill_turned_bands(out, kernel, count):
    chans = kernel.shape[1]
    out[...] = jnp.zeros(out.shape, out.dtype)
    for k in range(count):
        for b in range(3):
            for a in range(3):
                at = (b * (count + 2) + k + a) * chans
                out[at : at + chans, k * chans : (k + 1) * chans] = kernel[8 - 3 * a - b].astype(
                    out.dtype
                )


def stacked(views, at):
    return jnp.concatenate([view[at, :] for view in views], axis=0)


def conv_sum(parts, chans, step):
    return (
        turn(parts[0:chans], step)
        + parts[chans : 2 * chans]
        + turn(parts[2 * chans : 3 * chans], -step)
    )


def back_kernel(
    single, cot, up, down, col_r, col_l, up_r, up_l, down_r, down_l, second, bottle,
    act_grad, view_m, view_0, view_p,
    cot_m, cot_0, cot_p, back, high, low, coarse, bands_f, bands, small_f, small,
):
    chans = second.shape[1]
    full, span = cot.shape
    height = full // chans
    width = span + TILE
    groups = height // POOL
    has_up, has_down, _, _ = has_sides()
    halo = Halo(chans, single)
    seen_cols = columns_seen((chans, width), span)

    fill_turned_bands(bands_f, second, POOL)
    bands[...] = bands_f[...].T.astype(BF16)
    fill_turned_bands(small_f, bottle, 1)
    small_t = small_f[...].T
    for b in range(3):
        small[rows_at(b, chans)] = small_t[0:chans, 3 * b * chans : 3 * (b + 1) * chans].astype(BF16)

    cot_0[rows_at(0, chans, CHALO), 0:span] = up[...]
    cot_0[rows_at(CHALO, chans, height), 0:span] = cot[...]
    cot_0[rows_at(CHALO + height, chans, CHALO), 0:span] = down[...]
    for j in range(CHALO):
        cot_0[rows_at(j, chans), span:width] = halo.corner(up_r, up_l, FHALO + j).astype(BF16)
        cot_0[rows_at(CHALO + height + j, chans), span:width] = halo.corner(
            down_r, down_l, FHALO + j
        ).astype(BF16)
    for r in range(height):
        cot_0[rows_at(CHALO + r, chans), span:width] = halo.turned(
            col_r, col_l, rows_at(r, chans), -SLOT, SLOT
        ).astype(BF16)
    for j in range(height + 2 * CHALO):
        at = rows_at(j, chans)
        cot_m[at] = turn(cot_0[at], 1)
        cot_p[at] = turn(cot_0[at], -1)
    inner = rows_at(CHALO - 1, chans, height + 2)
    view_m[...] = cot_m[inner, 0:span]
    view_0[...] = cot_0[inner, 0:span]
    view_p[...] = cot_p[inner, 0:span]

    def group(g, _):
        at = rows_at(g * POOL, chans, POOL + 2)
        rows = jnp.dot(
            bands[...], stacked((cot_m, cot_0, cot_p), at), preferred_element_type=F32
        ).astype(BF16)
        back[rows_at(g * POOL, chans, POOL), :] = rows[:, 0:span]
        rows = rows.astype(F32)
        total = rows[0:chans]
        for k in range(1, POOL):
            total = total + rows[k * chans : (k + 1) * chans]
        store_split(high, low, rows_at(g, chans), total)
        return 0

    lax.fori_loop(0, groups + 2, group, 0, unroll=2)
    sums = block_sums(high, low, block_ones(width))
    for g in range(groups + 2):
        at = rows_at(g, chans)
        seen = seen_cols
        if g == 0:
            seen = seen & has_up
        elif g == groups + 1:
            seen = seen & has_down
        coarse[at] = jnp.where(seen, sums[at], 0.0).astype(BF16)
    for g in range(groups):
        parts = jnp.dot(small[...], coarse[rows_at(g, chans, 3), :], preferred_element_type=F32)
        mean = conv_sum(parts, chans, POOL)[:, 0:span] * (1.0 / POOL**2)
        for k in range(POOL):
            r = g * POOL + k
            act_grad[rows_at(r, chans), :] = back[rows_at(r + POOL, chans), :].astype(F32) + mean


def correlate(u, u0, views, v0, acc, height, chans, span):
    acc[...] = jnp.zeros(acc.shape, F32)

    def group(g, _):
        left = jnp.concatenate(
            [view[rows_at(v0 + g * POOL, chans, POOL + 2), 0:span] for view in views], axis=0
        )
        right = u[rows_at(u0 + g * POOL, chans, POOL), 0:span]
        acc[...] += lax.dot_general(
            left, right, (((1,), (1,)), ((), ())), preferred_element_type=F32
        )
        return 0

    lax.fori_loop(0, height // POOL, group, 0, unroll=2)


def folded(acc, chans):
    lane = lanes_of((3 * chans, TILE))
    result = jnp.zeros((3 * chans, TILE), F32)
    for b in range(3):
        total = None
        for k in range(POOL):
            block = turn(
                acc[rows_at(b * (POOL + 2) + k, chans, 3), 0:TILE], (b - k) * chans
            )
            total = block if total is None else total + block
        result = jnp.where((lane >= b * chans) & (lane < (b + 1) * chans), total, result)
    return result


def main_kernel(
    single, shifts, feat, up, down, col_r, col_l, up_r, up_l, down_r, down_l,
    act_grad, view_m, view_0, view_p, first, bottle,
    grads, blended,
    fs, ws, warp_m, warp_0, warp_p, act, high, low, pooled, pre_grad, acc, bands_f, bands, small_f, small,
):
    chans = first.shape[1]
    full, span = feat.shape
    height = full // chans
    tiles = span // TILE
    width = span + TILE
    groups = height // POOL
    has_up, has_down, _, _ = has_sides()
    halo = Halo(chans, single)
    seen_cols = columns_seen((chans, width), span)

    fill_bands(bands_f, first, POOL)
    bands[...] = bands_f[...].astype(BF16)
    fill_bands(small_f, bottle, 1)
    for b in range(3):
        small[rows_at(b, chans)] = small_f[:, 3 * b * chans : 3 * (b + 1) * chans].astype(BF16)

    for t in range(tiles):
        part = slice(t * TILE, (t + 1) * TILE)
        fs[t, rows_at(0, chans, FHALO)] = up[:, part].astype(F32)
        fs[t, rows_at(FHALO, chans, height)] = feat[:, part].astype(F32)
        fs[t, rows_at(FHALO + height, chans, FHALO)] = down[:, part].astype(F32)
    for j in range(FHALO):
        fs[tiles, rows_at(j, chans)] = halo.corner(up_r, up_l, j)
        fs[tiles, rows_at(FHALO + height + j, chans)] = halo.corner(down_r, down_l, j)
    for r in range(height):
        at = rows_at(r, chans)
        fs[tiles, rows_at(FHALO + r, chans)] = halo.tile(
            col_r[at].astype(F32), col_l[at].astype(F32)
        )

    tall = height + 2 * EXT
    lane = lanes_of((tall, TILE))

    def warp(c, _):
        start = (MAXSHIFT + shifts[c, 0]) * chans + c
        move = shifts[c, 1]
        planes = [
            turn(fs[t, pl.ds(start, tall, stride=chans), :], jnp.where(move > 0, TILE - move, -move))
            for t in range(tiles + 1)
        ]
        inside = jnp.where(move > 0, lane, TILE - 1 - lane) < TILE - jnp.abs(move)
        for t in range(tiles + 1):
            after, before = planes[(t + 1) % (tiles + 1)], planes[t - 1]
            ws[t, pl.ds(c, tall, stride=chans), :] = jnp.where(
                inside, planes[t], jnp.where(move > 0, after, before)
            )
        return 0

    lax.fori_loop(0, chans, warp, 0, unroll=4)
    for j in range(tall):
        row = jnp.concatenate([ws[t, rows_at(j, chans)] for t in range(tiles + 1)], axis=1)
        seen = seen_cols
        if j < EXT:
            seen = seen & has_up
        elif j >= EXT + height:
            seen = seen & has_down
        row = jnp.where(seen, row, 0.0).astype(BF16)
        at = rows_at(j, chans)
        warp_0[at] = row
        warp_m[at] = turn(row, 1)
        warp_p[at] = turn(row, -1)

    def first_group(g, own):
        at = rows_at(g * POOL, chans, POOL + 2)
        pre = jnp.dot(
            bands[...], stacked((warp_m, warp_0, warp_p), at), preferred_element_type=F32
        )
        sigma = 0.5 * jnp.tanh(0.5 * pre) + 0.5
        rows = (pre * sigma).astype(BF16)
        act[rows_at(g * POOL, chans, POOL), :] = rows
        rows = rows.astype(F32)
        total = rows[0:chans]
        for k in range(1, POOL):
            total = total + rows[k * chans : (k + 1) * chans]
        store_split(high, low, rows_at(g, chans), total)
        if own:
            there = rows_at(g * POOL - 2 * POOL, chans, POOL)
            pre, sigma = pre[:, 0:span], sigma[:, 0:span]
            pre_grad[there, :] = (
                act_grad[there, :] * (sigma * (1.0 + pre * (1.0 - sigma)))
            ).astype(BF16)
        return 0

    for g in (0, 1, groups + 2, groups + 3):
        first_group(g, False)
    lax.fori_loop(2, groups + 2, lambda g, _: first_group(g, True), 0, unroll=2)
    sums = block_sums(high, low, block_ones(width))
    for g in range(groups + 4):
        at = rows_at(g, chans)
        seen = seen_cols
        if g < 2:
            seen = seen & has_up
        elif g >= groups + 2:
            seen = seen & has_down
        pooled[at] = jnp.where(seen, sums[at] * (1.0 / POOL**2), 0.0).astype(BF16)

    for g in range(groups + 2):
        parts = jnp.dot(small[...], pooled[rows_at(g, chans, 3), :], preferred_element_type=F32)
        bottle_row = conv_sum(parts, chans, POOL)
        rows, seen = range(POOL), seen_cols
        if g == 0:
            rows, seen = (POOL - 1,), seen & has_up
        elif g == groups + 1:
            rows, seen = (0,), seen & has_down
        for k in rows:
            row = act[rows_at((g + 1) * POOL + k, chans), :].astype(F32) + bottle_row
            blended[rows_at(g * POOL + k - POOL + 1, chans), :] = jnp.where(seen, row, 0.0).astype(
                BF16
            )

    correlate(pre_grad, 0, (warp_m, warp_0, warp_p), EXT - 1, acc, height, chans, span)
    first_part = folded(acc, chans)
    correlate(blended, 1, (view_m, view_0, view_p), 0, acc, height, chans, span)
    second_part = folded(acc, chans)
    lane = lanes_of((3 * chans, TILE))
    grads[0 : 3 * chans] = jnp.where(lane < 3 * chans, first_part, turn(second_part, 3 * chans))
    half = 3 * chans // 2
    grads[3 * chans :] = jnp.where(
        lane[0:half] < TILE // 2,
        turn(second_part[0:half], -chans),
        turn(second_part[half:], TILE // 2 - chans),
    )


def predict_kernel(part, blended, second, *rest):
    out, scratch, bands_f, bands = rest[-4:]
    chans, height, span = out.shape
    tiles = span // TILE
    bands_f[...] = jnp.zeros(bands_f.shape, F32)
    for k in range(POOL):
        for b in range(3):
            for a in range(3):
                bands_f[rows_at(3 * k + b, chans), (k + a) * chans : (k + a + 1) * chans] = second[
                    3 * a + b
                ].astype(F32)
    bands[...] = bands_f[...].astype(BF16)

    def group(g, _):
        at = rows_at(part * height + g * POOL, chans, POOL + 2)
        parts = jnp.dot(bands[...], blended[at, :], preferred_element_type=F32)
        for k in range(POOL):
            row = conv_sum(parts[3 * k * chans : 3 * (k + 1) * chans], chans, 1)
            for t in range(tiles):
                scratch[t, pl.ds(g * POOL + k, chans, stride=height), :] = row[
                    :, t * TILE : (t + 1) * TILE
                ]
        return 0

    lax.fori_loop(0, height // POOL, group, 0)
    for c in range(chans):
        for t in range(tiles):
            out[c, :, t * TILE : (t + 1) * TILE] = scratch[
                t, c * height : (c + 1) * height
            ].astype(BF16)


def final_kernel(factor, mine, other, first, second):
    chans = first.shape[1]
    total = (mine[...] + other[...]) * factor
    turned = total[0 : 3 * chans].T
    for b in range(3):
        for a in range(3):
            first[3 * a + b] = turned[b * chans : (b + 1) * chans, a * chans : (a + 1) * chans]
    half = 3 * chans // 2
    low = total[3 * chans :]
    both = jnp.concatenate([low, turn(low, -(TILE // 2))], axis=0)
    for a in range(3):
        at = slice((2 - a) * chans, (3 - a) * chans)
        second[3 * a + 2] = turn(total[at], -3 * chans)[:, 0:chans]
        second[3 * a + 1] = both[at, 0:chans]
        second[3 * a + 0] = turn(both[at], -chans)[:, 0:chans]


def call(kernel, outs, scratch, n_in, limit, flops=0, smem_first=False, **more):
    specs = [VMEM] * n_in
    if smem_first:
        specs[0] = SMEM
    more.setdefault("in_specs", specs)
    more.setdefault("out_specs", jax.tree.map(lambda _: VMEM, outs))
    return pl.pallas_call(
        kernel,
        out_shape=outs,
        scratch_shapes=scratch,
        compiler_params=pltpu.CompilerParams(vmem_limit_bytes=limit * MIB),
        cost_estimate=pl.CostEstimate(flops=flops, bytes_accessed=4 * MIB, transcendentals=0),
        **more,
    )


def predict(blended, second, shape, parts, part, before):
    chans, height, span = shape
    rows = height // parts
    tiles = span // TILE
    block = pl.BlockSpec((chans, rows, span), lambda i: (0, part, 0))
    whole = lambda a: pl.BlockSpec(a.shape, lambda i: (0,) * a.ndim)
    args = (blended, second)
    specs = [whole(a) for a in args]
    more = {}
    if before is not None:
        args += (before,)
        specs.append(pl.BlockSpec(memory_space=pl.ANY))
        more["input_output_aliases"] = {2: 0}
    return call(
        functools.partial(predict_kernel, part),
        jax.ShapeDtypeStruct(shape, BF16),
        [
            pltpu.VMEM((tiles, chans * rows, TILE), F32),
            pltpu.VMEM((3 * POOL * chans, (POOL + 2) * chans), F32),
            pltpu.VMEM((3 * POOL * chans, (POOL + 2) * chans), BF16),
        ],
        len(args),
        12,
        flops=10**9,
        grid=(1,),
        in_specs=specs,
        out_specs=block,
        **more,
    )(*args)


def shards(features, shifts, first_kernel, bottle_kernel, second_kernel, cotangent):
    imgs, chans, height, span = features.shape
    rows, cols, dp = (lax.axis_size(a) for a in ("rows", "cols", "dp"))
    tiles = span // TILE
    width = span + TILE
    full = height * chans
    groups = height // POOL
    single = cols == 2

    def bf(*shape):
        return jax.ShapeDtypeStruct(shape, BF16)

    ahead = [(i, i + 1) for i in range(rows - 1)]
    astern = [(i + 1, i) for i in range(rows - 1)]

    def diagonal(message, step, turns):
        pairs = []
        for i in range(rows):
            for j in range(cols):
                for move in turns:
                    if 0 <= i + step < rows and 0 <= j + move < cols:
                        pairs.append((i * cols + j, (i + step) * cols + j + move))
        return lax.ppermute(message, ("rows", "cols"), pairs)

    feat_rows, up_feat, down_feat = call(
        feature_kernel,
        (bf(full, span), bf(FHALO * chans, span), bf(FHALO * chans, span)),
        [],
        1,
        8,
    )(features[0])
    up_f = lax.ppermute(down_feat, "rows", ahead)
    down_f = lax.ppermute(up_feat, "rows", astern)

    if single:
        edges = (("up", "single"), ("down", "single"))
    else:
        edges = tuple((v, e) for v in ("up", "down") for e in ("left", "right"))
    packed = pl.cdiv(FHALO + CHALO, POOL) * chans
    cot_rows, up_cot, down_cot, col_msg, *corner_msgs = call(
        functools.partial(pack_kernel, edges),
        (bf(full, span), bf(CHALO * chans, span), bf(CHALO * chans, span), bf(full, TILE))
        + tuple(bf(packed, TILE) for _ in edges),
        [],
        2,
        8,
        flops=2 * 10**10,
    )(feat_rows, cotangent[0])
    up_c = lax.ppermute(down_cot, "rows", ahead)
    down_c = lax.ppermute(up_cot, "rows", astern)
    if single:
        up_r = up_l = diagonal(corner_msgs[1], 1, (-1, 1))
        down_r = down_l = diagonal(corner_msgs[0], -1, (-1, 1))
        col_r = col_l = lax.ppermute(col_msg, "cols", [(0, 1), (1, 0)])
    else:
        up_r = diagonal(corner_msgs[2], 1, (-1,))
        up_l = diagonal(corner_msgs[3], 1, (1,))
        down_r = diagonal(corner_msgs[0], -1, (-1,))
        down_l = diagonal(corner_msgs[1], -1, (1,))
        col_r = lax.ppermute(col_msg, "cols", [(i + 1, i) for i in range(cols - 1)])
        col_l = lax.ppermute(col_msg, "cols", [(i, i + 1) for i in range(cols - 1)])

    tall_c = (height + 2 * CHALO) * chans
    view = bf((height + 2) * chans, span)
    band = 3 * (POOL + 2) * chans
    act_grad, *views = call(
        functools.partial(back_kernel, single),
        (jax.ShapeDtypeStruct((full, span), F32), view, view, view),
        [pltpu.VMEM((tall_c, width), BF16)] * 3
        + [pltpu.VMEM(((height + 2 * POOL) * chans, span), BF16)]
        + [pltpu.VMEM(((groups + 2) * chans, width), BF16)] * 3
        + [
            pltpu.VMEM((band, POOL * chans), F32),
            pltpu.VMEM((POOL * chans, band), BF16),
            pltpu.VMEM((9 * chans, TILE), F32),
            pltpu.VMEM((3 * chans, 3 * chans), BF16),
        ],
        11,
        16,
    )(
        cot_rows, up_c, down_c, col_r, col_l, up_r, up_l, down_r, down_l,
        second_kernel, bottle_kernel,
    )

    tall = (height + 2 * EXT) * chans
    grads, blended = call(
        functools.partial(main_kernel, single),
        (jax.ShapeDtypeStruct((9 * chans // 2, TILE), F32), bf((height + 2) * chans, width)),
        [
            pltpu.VMEM((tiles + 1, (height + 2 * FHALO) * chans, TILE), F32),
            pltpu.VMEM((tiles + 1, tall, TILE), F32),
        ]
        + [pltpu.VMEM((tall, width), BF16)] * 3
        + [pltpu.VMEM(((height + 4 * POOL) * chans, width), BF16)]
        + [pltpu.VMEM(((groups + 4) * chans, width), BF16)] * 3
        + [
            pltpu.VMEM((full, span), BF16),
            pltpu.VMEM((band, POOL * chans), F32),
            pltpu.VMEM((POOL * chans, band), F32),
            pltpu.VMEM((POOL * chans, band), BF16),
            pltpu.VMEM((chans, 9 * chans), F32),
            pltpu.VMEM((3 * chans, 3 * chans), BF16),
        ],
        16,
        32,
        flops=10**10,
        smem_first=True,
    )(
        shifts[0], feat_rows, up_f, down_f, col_r, col_l, up_r, up_l, down_r, down_l,
        act_grad, *views, first_kernel, bottle_kernel,
    )

    steps = []
    for axis, size in (("dp", dp), ("cols", cols), ("rows", rows)):
        bit = 1
        while bit < size:
            steps.append((axis, [(i, i ^ bit) for i in range(size)]))
            bit *= 2
    parts, prediction = 2, None
    for step, (axis, pairs) in enumerate(steps):
        other = lax.ppermute(grads, axis, pairs)
        if 1 <= step <= parts:
            prediction = predict(
                blended, second_kernel, (chans, height, span), parts, step - 1, prediction
            )
            other, prediction = lax.optimization_barrier((other, prediction))
        if step < len(steps) - 1:
            grads = grads + other
            if step < parts:
                grads, blended = lax.optimization_barrier((grads, blended))
    factor = 1.0 / math.sqrt(imgs * dp * height * rows * span * cols)
    shape = jax.ShapeDtypeStruct((9, chans, chans), F32)
    first_grad, second_grad = call(
        functools.partial(final_kernel, factor), (shape, shape), [], 2, 2
    )(grads, other)
    return (prediction[None], first_grad, second_grad)


def solution(mesh):
    placed = (
        P("dp", None, "rows", "cols"),
        P("dp", None, None),
        P(),
        P(),
        P(),
        P("dp", None, "rows", "cols"),
    )
    return jax.shard_map(
        shards,
        mesh=mesh,
        in_specs=placed,
        out_specs=(P("dp", None, "rows", "cols"), P(), P()),
        check_vma=False,
    )
```

```python
import functools
import math

import jax
import jax.numpy as jnp
from jax import lax
from jax.experimental import pallas as pl
from jax.experimental.pallas import tpu as pltpu
from jax.sharding import PartitionSpec as P


MAXSHIFT = 16
POOL = 4
TILE = 128
SLOT = 32
EXT = 9
FHALO = MAXSHIFT + EXT
CHALO = 5
F32 = jnp.float32
BF16 = jnp.bfloat16
VMEM = pl.BlockSpec(memory_space=pltpu.VMEM)
SMEM = pl.BlockSpec(memory_space=pltpu.SMEM)
MIB = 1024 * 1024


def lanes_of(shape):
    return lax.broadcasted_iota(jnp.int32, shape, len(shape) - 1)


def turn(values, shift):
    width = values.shape[-1]
    if isinstance(shift, int):
        shift = shift % width
        if shift == 0:
            return values
    return pltpu.roll(values, shift, values.ndim - 1)


def has_sides():
    row, col = lax.axis_index("rows"), lax.axis_index("cols")
    return (
        row > 0,
        row < lax.axis_size("rows") - 1,
        col > 0,
        col < lax.axis_size("cols") - 1,
    )


def rows_at(r, chans, count=1):
    if isinstance(r, int):
        return slice(r * chans, (r + count) * chans)
    return pl.ds(pl.multiple_of(r * chans, chans), count * chans)


def to_rows(block):
    chans, height, span = block.shape
    return jnp.transpose(block, (1, 0, 2)).reshape(height * chans, span)


def to_planes(block, chans):
    height = block.shape[0] // chans
    return jnp.transpose(block.reshape(height, chans, block.shape[1]), (1, 0, 2))


def tiles_of(span):
    return [slice(t, t + TILE) for t in range(0, span, TILE)]


def is_even(axis):
    return lax.rem(lax.axis_index(axis), 2) == 0


def swaps(size):
    first = [(i, i ^ 1) for i in range(size)]
    second = [(i, i + 1) for i in range(1, size - 1, 2)]
    return [first, second + [(j, i) for i, j in second]]


def feature_kernel(feat, msg_a, msg_b, rows):
    chans, height, span = feat.shape
    for part in tiles_of(span):
        rows[:, part] = to_rows(feat[:, :, part])
    edge = (height - FHALO) * chans
    low = jnp.where(is_even("rows"), edge, 0)
    msg_a[...] = rows[pl.ds(pl.multiple_of(low, chans), FHALO * chans), :]
    msg_b[...] = rows[pl.ds(pl.multiple_of(edge - low, chans), FHALO * chans), :]


def column_kernel(feat, cot, cot_rows, *col_msgs):
    chans, height, span = feat.shape
    first, last = tiles_of(span)[0], tiles_of(span)[-1]
    for part in tiles_of(span):
        cot_rows[:, part] = to_rows(cot[:, :, part])
    count = TILE // SLOT
    block = height // count
    lane = lanes_of((chans, block, TILE))
    for index, msg in enumerate(col_msgs):
        sends_right = is_even("cols") if index == 0 else jnp.logical_not(is_even("cols"))
        total = jnp.zeros((chans, block, TILE), F32)
        inner = jnp.where(sends_right, TILE - 1 - lane, lane) < FHALO
        for k in range(count):
            at = slice(k * block, (k + 1) * block)
            feats = jnp.where(sends_right, feat[:, at, last].astype(F32), feat[:, at, first].astype(F32))
            cots = jnp.where(sends_right, cot[:, at, last].astype(F32), cot[:, at, first].astype(F32))
            cots = turn(cots, jnp.where(sends_right, TILE - FHALO, FHALO))
            piece = jnp.where(inner, feats, cots)
            piece = turn(piece, jnp.where(sends_right, (k + 1) * SLOT % TILE, k * SLOT))
            inside = (lane >= k * SLOT) & (lane < (k + 1) * SLOT)
            total = jnp.where(inside, piece, total)
        msg[...] = total.reshape(chans * block, TILE).astype(BF16)


def edge_kernel(cot_rows, *rest):
    cols, (msg_a, msg_b) = rest[:-2], rest[-2:]
    span = cot_rows.shape[1]
    size = msg_a.shape[0] - sum(c.shape[0] * TILE // span for c in cols)
    edge = cot_rows.shape[0] - size
    chans = size // CHALO
    low = jnp.where(is_even("rows"), edge, 0)
    msg_a[0:size] = cot_rows[pl.ds(pl.multiple_of(low, chans), size), :]
    msg_b[0:size] = cot_rows[pl.ds(pl.multiple_of(edge - low, chans), size), :]
    at = size
    for col in cols:
        count = col.shape[0] * TILE // span
        for t, part in enumerate(tiles_of(span)):
            block = col[t * count : (t + 1) * count]
            msg_a[at : at + count, part] = block
            msg_b[at : at + count, part] = block
        at += count


def corner_views(msg, size, cols):
    span = msg.shape[1]
    views, at = [], size
    for col in cols:
        count = col.shape[0] * TILE // span
        views.append(
            jnp.concatenate([msg[at : at + count, part] for part in tiles_of(span)], axis=0)
        )
        at += count
    return views


def halo_block(sources, k, chans, kind):
    rows = sources[0].shape[0] // chans
    lane = lanes_of((chans * rows, TILE))
    total = jnp.zeros((chans * rows, TILE), F32)
    if kind == "features":
        count, shift_r, shift_l = FHALO, -k * SLOT, TILE - (k + 1) * SLOT
    else:
        count, shift_r, shift_l = CHALO, -k * SLOT - FHALO, TILE - (k + 1) * SLOT + FHALO
    for index, source in enumerate(sources):
        from_right = is_even("cols") if index == 0 else jnp.logical_not(is_even("cols"))
        moved = turn(
            source.astype(F32), jnp.where(from_right, shift_r % TILE, shift_l % TILE)
        )
        total = jnp.where(
            jnp.where(from_right, lane, TILE - 1 - lane) < count, moved, total
        )
    return total.astype(BF16).reshape(chans, rows, TILE)


def columns_seen(shape, span):
    _, _, has_left, has_right = has_sides()
    lane = lanes_of(shape)
    middle = span + TILE // 2
    return (lane < span) | ((lane < middle) & has_right) | ((lane >= middle) & has_left)


def block_ones(width):
    row = lax.broadcasted_iota(jnp.int32, (width, width), 0) // POOL
    col = lax.broadcasted_iota(jnp.int32, (width, width), 1) // POOL
    return jnp.where(row == col, 1.0, 0.0).astype(BF16)


def store_split(high, low, at, total):
    top = total.astype(BF16)
    high[at, :] = top
    low[at, :] = (total - top.astype(F32)).astype(BF16)


def block_sums(high, low, ones):
    return jnp.dot(high[...], ones, preferred_element_type=F32) + jnp.dot(
        low[...], ones, preferred_element_type=F32
    )


def fill_bands(out, kernel, count):
    chans = kernel.shape[1]
    out[...] = jnp.zeros(out.shape, out.dtype)
    for k in range(count):
        for b in range(3):
            for a in range(3):
                at = (b * (count + 2) + k + a) * chans
                out[k * chans : (k + 1) * chans, at : at + chans] = kernel[3 * a + b].astype(
                    out.dtype
                )


def fill_turned_bands(out, kernel, count):
    chans = kernel.shape[1]
    out[...] = jnp.zeros(out.shape, out.dtype)
    for k in range(count):
        for b in range(3):
            for a in range(3):
                at = (b * (count + 2) + k + a) * chans
                out[at : at + chans, k * chans : (k + 1) * chans] = kernel[8 - 3 * a - b].astype(
                    out.dtype
                )


def stacked(views, at):
    return jnp.concatenate([view[at, :] for view in views], axis=0)


def conv_sum(parts, chans, step):
    return (
        turn(parts[0:chans], step)
        + parts[chans : 2 * chans]
        + turn(parts[2 * chans : 3 * chans], -step)
    )


def back_kernel(
    ncols, cot, msg_a, msg_b, *rest,
):
    cols, (
        second, bottle, act_grad, view_m, view_0, view_p,
        cot_m, cot_0, cot_p, back, high, low, coarse, bands_f, bands, small_f, small,
    ) = rest[:ncols], rest[ncols:]
    chans = second.shape[1]
    full, span = cot.shape
    height = full // chans
    width = span + TILE
    groups = height // POOL
    has_up, has_down, _, _ = has_sides()
    seen_cols = columns_seen((chans, width), span)

    fill_turned_bands(bands_f, second, POOL)
    bands[...] = bands_f[...].T.astype(BF16)
    fill_turned_bands(small_f, bottle, 1)
    small_t = small_f[...].T
    for b in range(3):
        small[rows_at(b, chans)] = small_t[0:chans, 3 * b * chans : 3 * (b + 1) * chans].astype(BF16)

    size = CHALO * chans
    count = TILE // SLOT
    block = height // count
    cot_0[rows_at(CHALO, chans, height), 0:span] = cot[...]
    for k in range(count):
        cot_0[rows_at(CHALO + k * block, chans, block), span:width] = to_rows(
            halo_block([c[...] for c in cols], k, chans, "cotangent")
        )

    def vertical(up, down):
        cot_0[rows_at(0, chans, CHALO), 0:span] = up[0:size]
        cot_0[rows_at(CHALO + height, chans, CHALO), 0:span] = down[0:size]
        corner = to_rows(
            halo_block(corner_views(up, size, cols), count - 1, chans, "cotangent")
        )
        cot_0[rows_at(0, chans, CHALO), span:width] = corner[(block - CHALO) * chans :]
        corner = to_rows(halo_block(corner_views(down, size, cols), 0, chans, "cotangent"))
        cot_0[rows_at(CHALO + height, chans, CHALO), span:width] = corner[0:size]

    pl.when(is_even("rows"))(lambda: vertical(msg_b, msg_a))
    pl.when(jnp.logical_not(is_even("rows")))(lambda: vertical(msg_a, msg_b))
    for j in range(height + 2 * CHALO):
        at = rows_at(j, chans)
        cot_m[at] = turn(cot_0[at], 1)
        cot_p[at] = turn(cot_0[at], -1)
    inner = rows_at(CHALO - 1, chans, height + 2)
    view_m[...] = cot_m[inner, 0:span]
    view_0[...] = cot_0[inner, 0:span]
    view_p[...] = cot_p[inner, 0:span]

    def group(g, _):
        at = rows_at(g * POOL, chans, POOL + 2)
        rows = jnp.dot(
            bands[...], stacked((cot_m, cot_0, cot_p), at), preferred_element_type=F32
        ).astype(BF16)
        back[rows_at(g * POOL, chans, POOL), :] = rows[:, 0:span]
        rows = rows.astype(F32)
        total = rows[0:chans]
        for k in range(1, POOL):
            total = total + rows[k * chans : (k + 1) * chans]
        store_split(high, low, rows_at(g, chans), total)
        return 0

    lax.fori_loop(0, groups + 2, group, 0, unroll=2)
    sums = block_sums(high, low, block_ones(width))
    for g in range(groups + 2):
        at = rows_at(g, chans)
        seen = seen_cols
        if g == 0:
            seen = seen & has_up
        elif g == groups + 1:
            seen = seen & has_down
        coarse[at] = jnp.where(seen, sums[at], 0.0).astype(BF16)
    for g in range(groups):
        parts = jnp.dot(small[...], coarse[rows_at(g, chans, 3), :], preferred_element_type=F32)
        mean = conv_sum(parts, chans, POOL)[:, 0:span] * (1.0 / POOL**2)
        for k in range(POOL):
            r = g * POOL + k
            act_grad[rows_at(r, chans), :] = back[rows_at(r + POOL, chans), :].astype(F32) + mean


def correlate(u, u0, views, v0, acc, height, chans, span):
    acc[...] = jnp.zeros(acc.shape, F32)

    def group(g, _):
        left = jnp.concatenate(
            [view[rows_at(v0 + g * POOL, chans, POOL + 2), 0:span] for view in views], axis=0
        )
        right = u[rows_at(u0 + g * POOL, chans, POOL), 0:span]
        acc[...] += lax.dot_general(
            left, right, (((1,), (1,)), ((), ())), preferred_element_type=F32
        )
        return 0

    lax.fori_loop(0, height // POOL, group, 0, unroll=2)


def folded(acc, chans):
    lane = lanes_of((3 * chans, TILE))
    result = jnp.zeros((3 * chans, TILE), F32)
    for b in range(3):
        total = None
        for k in range(POOL):
            block = turn(
                acc[rows_at(b * (POOL + 2) + k, chans, 3), 0:TILE], (b - k) * chans
            )
            total = block if total is None else total + block
        result = jnp.where((lane >= b * chans) & (lane < (b + 1) * chans), total, result)
    return result


def main_kernel(
    ncols, shifts, feat, feat_a, feat_b, msg_a, msg_b, *rest,
):
    cols, (
        act_grad, view_m, view_0, view_p, first, bottle, grads, blended,
        planes, moved, warp_m, warp_0, warp_p, act, high, low, pooled, pre_grad, acc,
        bands_f, bands, small_f, small,
    ) = rest[:ncols], rest[ncols:]
    chans, height, span = feat.shape
    tiles = span // TILE
    width = span + TILE
    groups = height // POOL
    has_up, has_down, has_left, has_right = has_sides()
    seen_cols = columns_seen((chans, width), span)

    fill_bands(bands_f, first, POOL)
    bands[...] = bands_f[...].astype(BF16)
    fill_bands(small_f, bottle, 1)
    for b in range(3):
        small[rows_at(b, chans)] = small_f[:, 3 * b * chans : 3 * (b + 1) * chans].astype(BF16)

    size = CHALO * chans
    count = TILE // SLOT
    block = height // count
    halo = slice(span, width)

    def halo_columns(sources, at):
        for k in range(count):
            planes[:, at + k * block : at + (k + 1) * block, halo] = halo_block(
                sources, k, chans, "features"
            )

    planes[:, height : 2 * height, 0:span] = feat[...]
    halo_columns([c[...] for c in cols], height)
    fill = (height - FHALO) * chans

    def vertical(up, up_msg, down, down_msg):
        for part in tiles_of(span):
            none = jnp.zeros((fill, TILE), BF16)
            planes[:, 0:height, part] = to_planes(
                jnp.concatenate([none, up[:, part]], axis=0), chans
            )
            planes[:, 2 * height : 3 * height, part] = to_planes(
                jnp.concatenate([down[:, part], none], axis=0), chans
            )
        halo_columns(corner_views(up_msg, size, cols), 0)
        halo_columns(corner_views(down_msg, size, cols), 2 * height)

    pl.when(is_even("rows"))(lambda: vertical(feat_b, msg_b, feat_a, msg_a))
    pl.when(jnp.logical_not(is_even("rows")))(lambda: vertical(feat_a, msg_a, feat_b, msg_b))

    tall = moved.shape[1]
    lane = lanes_of((tall, TILE))
    seen_halo = ((lane < TILE // 2) & has_right) | ((lane >= TILE // 2) & has_left)
    step = lanes_of((tall, 3 * height)) - lax.broadcasted_iota(jnp.int32, (tall, 3 * height), 0)

    def warp(c, _):
        pick = jnp.where(step == height - EXT + shifts[c, 0], 1.0, 0.0).astype(BF16)
        plane = jnp.dot(pick, planes[c], preferred_element_type=F32)
        move = shifts[c, 1]
        amount = jnp.where(move > 0, TILE - move, -move)
        parts = [turn(plane[:, part], amount) for part in tiles_of(width)]
        inside = jnp.where(move > 0, lane, TILE - 1 - lane) < TILE - jnp.abs(move)
        for t, part in enumerate(tiles_of(width)):
            after, before = parts[(t + 1) % (tiles + 1)], parts[t - 1]
            result = jnp.where(inside, parts[t], jnp.where(move > 0, after, before))
            if t == tiles:
                result = jnp.where(seen_halo, result, 0.0)
            moved[c, :, part] = result.astype(BF16)
        return 0

    lax.fori_loop(0, chans, warp, 0, unroll=4)
    chunk = 16
    for r in range(0, tall, chunk):
        for part in tiles_of(width):
            warp_0[rows_at(r, chans, chunk), part] = to_rows(moved[:, r : r + chunk, part])

    def clear(r, count):
        warp_0[rows_at(r, chans, count)] = jnp.zeros((count * chans, width), BF16)

    pl.when(jnp.logical_not(has_up))(lambda: clear(0, EXT))
    pl.when(jnp.logical_not(has_down))(lambda: clear(EXT + height, EXT))
    for j in range(height + 2 * EXT):
        at = rows_at(j, chans)
        warp_m[at] = turn(warp_0[at], 1)
        warp_p[at] = turn(warp_0[at], -1)

    def first_group(g, own):
        at = rows_at(g * POOL, chans, POOL + 2)
        pre = jnp.dot(
            bands[...], stacked((warp_m, warp_0, warp_p), at), preferred_element_type=F32
        )
        sigma = 0.5 * jnp.tanh(0.5 * pre) + 0.5
        rows = (pre * sigma).astype(BF16)
        act[rows_at(g * POOL, chans, POOL), :] = rows
        rows = rows.astype(F32)
        total = rows[0:chans]
        for k in range(1, POOL):
            total = total + rows[k * chans : (k + 1) * chans]
        store_split(high, low, rows_at(g, chans), total)
        if own:
            there = rows_at(g * POOL - 2 * POOL, chans, POOL)
            pre, sigma = pre[:, 0:span], sigma[:, 0:span]
            pre_grad[there, :] = (
                act_grad[there, :] * (sigma * (1.0 + pre * (1.0 - sigma)))
            ).astype(BF16)
        return 0

    for g in (0, 1, groups + 2, groups + 3):
        first_group(g, False)
    lax.fori_loop(2, groups + 2, lambda g, _: first_group(g, True), 0, unroll=2)
    sums = block_sums(high, low, block_ones(width))
    for g in range(groups + 4):
        at = rows_at(g, chans)
        seen = seen_cols
        if g < 2:
            seen = seen & has_up
        elif g >= groups + 2:
            seen = seen & has_down
        pooled[at] = jnp.where(seen, sums[at] * (1.0 / POOL**2), 0.0).astype(BF16)

    for g in range(groups + 2):
        parts = jnp.dot(small[...], pooled[rows_at(g, chans, 3), :], preferred_element_type=F32)
        bottle_row = conv_sum(parts, chans, POOL)
        rows, seen = range(POOL), seen_cols
        if g == 0:
            rows, seen = (POOL - 1,), seen & has_up
        elif g == groups + 1:
            rows, seen = (0,), seen & has_down
        for k in rows:
            row = act[rows_at((g + 1) * POOL + k, chans), :].astype(F32) + bottle_row
            blended[rows_at(g * POOL + k - POOL + 1, chans), :] = jnp.where(seen, row, 0.0).astype(
                BF16
            )

    correlate(pre_grad, 0, (warp_m, warp_0, warp_p), EXT - 1, acc, height, chans, span)
    first_part = folded(acc, chans)
    correlate(blended, 1, (view_m, view_0, view_p), 0, acc, height, chans, span)
    second_part = folded(acc, chans)
    lane = lanes_of((3 * chans, TILE))
    grads[0 : 3 * chans] = jnp.where(lane < 3 * chans, first_part, turn(second_part, 3 * chans))
    half = 3 * chans // 2
    grads[3 * chans :] = jnp.where(
        lane[0:half] < TILE // 2,
        turn(second_part[0:half], -chans),
        turn(second_part[half:], TILE // 2 - chans),
    )


def predict_kernel(part, blended, second, *rest):
    out, rows, bands_f, bands = rest[-4:]
    chans, height, span = out.shape
    bands_f[...] = jnp.zeros(bands_f.shape, F32)
    for k in range(POOL):
        for b in range(3):
            for a in range(3):
                bands_f[rows_at(3 * k + b, chans), (k + a) * chans : (k + a + 1) * chans] = second[
                    3 * a + b
                ].astype(F32)
    bands[...] = bands_f[...].astype(BF16)

    def group(g, _):
        at = rows_at(part * height + g * POOL, chans, POOL + 2)
        parts = jnp.dot(bands[...], blended[at, :], preferred_element_type=F32)
        for k in range(POOL):
            row = conv_sum(parts[3 * k * chans : 3 * (k + 1) * chans], chans, 1)
            rows[rows_at(g * POOL + k, chans), :] = row[:, 0:span].astype(BF16)
        return 0

    lax.fori_loop(0, height // POOL, group, 0, unroll=2)
    for part in tiles_of(span):
        out[:, :, part] = to_planes(rows[:, part], chans)


def final_kernel(factor, mine, other, first, second):
    chans = first.shape[1]
    total = (mine[...] + other[...]) * factor
    turned = total[0 : 3 * chans].T
    for b in range(3):
        for a in range(3):
            first[3 * a + b] = turned[b * chans : (b + 1) * chans, a * chans : (a + 1) * chans]
    half = 3 * chans // 2
    low = total[3 * chans :]
    both = jnp.concatenate([low, turn(low, -(TILE // 2))], axis=0)
    for a in range(3):
        at = slice((2 - a) * chans, (3 - a) * chans)
        second[3 * a + 2] = turn(total[at], -3 * chans)[:, 0:chans]
        second[3 * a + 1] = both[at, 0:chans]
        second[3 * a + 0] = turn(both[at], -chans)[:, 0:chans]


def call(kernel, outs, scratch, n_in, limit, flops=0, smem_first=False, **more):
    specs = [VMEM] * n_in
    if smem_first:
        specs[0] = SMEM
    more.setdefault("in_specs", specs)
    more.setdefault("out_specs", jax.tree.map(lambda _: VMEM, outs))
    return pl.pallas_call(
        kernel,
        out_shape=outs,
        scratch_shapes=scratch,
        compiler_params=pltpu.CompilerParams(vmem_limit_bytes=limit * MIB),
        cost_estimate=pl.CostEstimate(flops=flops, bytes_accessed=4 * MIB, transcendentals=0),
        **more,
    )


def predict(blended, second, shape, parts, part, before):
    chans, height, span = shape
    rows = height // parts
    block = pl.BlockSpec((chans, rows, span), lambda i: (0, part, 0))
    whole = lambda a: pl.BlockSpec(a.shape, lambda i: (0,) * a.ndim)
    args = (blended, second)
    specs = [whole(a) for a in args]
    more = {}
    if before is not None:
        args += (before,)
        specs.append(pl.BlockSpec(memory_space=pl.ANY))
        more["input_output_aliases"] = {2: 0}
    return call(
        functools.partial(predict_kernel, part),
        jax.ShapeDtypeStruct(shape, BF16),
        [
            pltpu.VMEM((chans * rows, span), BF16),
            pltpu.VMEM((3 * POOL * chans, (POOL + 2) * chans), F32),
            pltpu.VMEM((3 * POOL * chans, (POOL + 2) * chans), BF16),
        ],
        len(args),
        12,
        flops=10**9,
        grid=(1,),
        in_specs=specs,
        out_specs=block,
        **more,
    )(*args)


def shards(features, shifts, first_kernel, bottle_kernel, second_kernel, cotangent):
    imgs, chans, height, span = features.shape
    rows, cols, dp = (lax.axis_size(a) for a in ("rows", "cols", "dp"))
    tiles = span // TILE
    width = span + TILE
    full = height * chans
    groups = height // POOL

    def bf(*shape):
        return jax.ShapeDtypeStruct(shape, BF16)

    def swapped(messages, axis):
        pairs = [p for p in swaps(lax.axis_size(axis)) if p]
        return [lax.ppermute(m, axis, p) for m, p in zip(messages, pairs)]

    halo = bf(FHALO * chans, span)
    messages = call(
        feature_kernel, (halo, halo), [pltpu.VMEM((full, span), BF16)], 1, 8
    )(features[0])
    feat_msgs = swapped(messages, "rows")
    packed = chans * (height * SLOT // TILE)
    cot_rows, *messages = call(
        column_kernel,
        (bf(full, span),) + (bf(packed, TILE),) * (1 if cols == 2 else 2),
        [],
        2,
        8,
        flops=2 * 10**10,
    )(features[0], cotangent[0])
    col_msgs = swapped(messages, "cols")
    ncols = len(col_msgs)
    halo = bf(CHALO * chans + ncols * packed * TILE // span, span)
    messages = call(edge_kernel, (halo, halo), [], 1 + ncols, 8)(cot_rows, *col_msgs)
    row_msgs = swapped(messages, "rows")

    tall_c = (height + 2 * CHALO) * chans
    view = bf((height + 2) * chans, span)
    band = 3 * (POOL + 2) * chans
    act_grad, *views = call(
        functools.partial(back_kernel, ncols),
        (jax.ShapeDtypeStruct((full, span), F32), view, view, view),
        [pltpu.VMEM((tall_c, width), BF16)] * 3
        + [pltpu.VMEM(((height + 2 * POOL) * chans, span), BF16)]
        + [pltpu.VMEM(((groups + 2) * chans, width), BF16)] * 3
        + [
            pltpu.VMEM((band, POOL * chans), F32),
            pltpu.VMEM((POOL * chans, band), BF16),
            pltpu.VMEM((9 * chans, TILE), F32),
            pltpu.VMEM((3 * chans, 3 * chans), BF16),
        ],
        5 + ncols,
        16,
    )(cot_rows, *row_msgs, *col_msgs, second_kernel, bottle_kernel)

    tall = pl.cdiv(height + 2 * EXT, 16) * 16
    grads, blended = call(
        functools.partial(main_kernel, ncols),
        (jax.ShapeDtypeStruct((9 * chans // 2, TILE), F32), bf((height + 2) * chans, width)),
        [
            pltpu.VMEM((chans, 3 * height, width), BF16),
            pltpu.VMEM((chans, tall, width), BF16),
        ]
        + [pltpu.VMEM((tall * chans, width), BF16)] * 3
        + [pltpu.VMEM(((height + 4 * POOL) * chans, width), BF16)]
        + [pltpu.VMEM(((groups + 4) * chans, width), BF16)] * 3
        + [
            pltpu.VMEM((full, span), BF16),
            pltpu.VMEM((band, POOL * chans), F32),
            pltpu.VMEM((POOL * chans, band), F32),
            pltpu.VMEM((POOL * chans, band), BF16),
            pltpu.VMEM((chans, 9 * chans), F32),
            pltpu.VMEM((3 * chans, 3 * chans), BF16),
        ],
        12 + ncols,
        32,
        flops=10**10,
        smem_first=True,
    )(
        shifts[0], features[0], *feat_msgs, *row_msgs, *col_msgs,
        act_grad, *views, first_kernel, bottle_kernel,
    )

    steps = []
    for axis, size in (("dp", dp), ("cols", cols), ("rows", rows)):
        bit = 1
        while bit < size:
            steps.append((axis, [(i, i ^ bit) for i in range(size)]))
            bit *= 2
    parts, prediction = 2, None
    for step, (axis, pairs) in enumerate(steps):
        other = lax.ppermute(grads, axis, pairs)
        if 1 <= step <= parts:
            prediction = predict(
                blended, second_kernel, (chans, height, span), parts, step - 1, prediction
            )
            other, prediction = lax.optimization_barrier((other, prediction))
        if step < len(steps) - 1:
            grads = grads + other
            if step < parts:
                grads, blended = lax.optimization_barrier((grads, blended))
    factor = 1.0 / math.sqrt(imgs * dp * height * rows * span * cols)
    shape = jax.ShapeDtypeStruct((9, chans, chans), F32)
    first_grad, second_grad = call(
        functools.partial(final_kernel, factor), (shape, shape), [], 2, 2
    )(grads, other)
    return (prediction[None], first_grad, second_grad)


def solution(mesh):
    placed = (
        P("dp", None, "rows", "cols"),
        P("dp", None, None),
        P(),
        P(),
        P(),
        P("dp", None, "rows", "cols"),
    )
    return jax.shard_map(
        shards,
        mesh=mesh,
        in_specs=placed,
        out_specs=(P("dp", None, "rows", "cols"), P(), P()),
        check_vma=False,
    )
```

```python
import functools
import math

import jax
import jax.numpy as jnp
from jax import lax
from jax.experimental import pallas as pl
from jax.experimental.pallas import tpu as pltpu
from jax.sharding import PartitionSpec as P


MAXSHIFT = 16
POOL = 4
TILE = 128
SLOT = 32
EXT = 9
FHALO = MAXSHIFT + EXT
CHALO = 5
F32 = jnp.float32
BF16 = jnp.bfloat16
VMEM = pl.BlockSpec(memory_space=pltpu.VMEM)
SMEM = pl.BlockSpec(memory_space=pltpu.SMEM)
MIB = 1024 * 1024


def lanes_of(shape):
    return lax.broadcasted_iota(jnp.int32, shape, len(shape) - 1)


def turn(values, shift):
    width = values.shape[-1]
    if isinstance(shift, int):
        shift = shift % width
        if shift == 0:
            return values
    return pltpu.roll(values, shift, values.ndim - 1)


def has_sides():
    row, col = lax.axis_index("rows"), lax.axis_index("cols")
    return (
        row > 0,
        row < lax.axis_size("rows") - 1,
        col > 0,
        col < lax.axis_size("cols") - 1,
    )


def rows_at(r, chans, count=1):
    if isinstance(r, int):
        return slice(r * chans, (r + count) * chans)
    return pl.ds(pl.multiple_of(r * chans, chans), count * chans)


def to_rows(block):
    chans, height, span = block.shape
    return jnp.transpose(block, (1, 0, 2)).reshape(height * chans, span)


def to_planes(block, chans):
    height = block.shape[0] // chans
    return jnp.transpose(block.reshape(height, chans, block.shape[1]), (1, 0, 2))


def tiles_of(span):
    return [slice(t, t + TILE) for t in range(0, span, TILE)]


def is_even(axis):
    return lax.rem(lax.axis_index(axis), 2) == 0


def swaps(size):
    first = [(i, i ^ 1) for i in range(size)]
    second = [(i, i + 1) for i in range(1, size - 1, 2)]
    return [first, second + [(j, i) for i, j in second]]


def feature_kernel(feat, msg_a, msg_b, rows):
    chans, height, span = feat.shape
    for part in tiles_of(span):
        rows[:, part] = to_rows(feat[:, :, part])
    edge = (height - FHALO) * chans
    low = jnp.where(is_even("rows"), edge, 0)
    msg_a[...] = rows[pl.ds(pl.multiple_of(low, chans), FHALO * chans), :]
    msg_b[...] = rows[pl.ds(pl.multiple_of(edge - low, chans), FHALO * chans), :]


def column_kernel(feat, cot, cot_rows, *col_msgs):
    chans, height, span = feat.shape
    first, last = tiles_of(span)[0], tiles_of(span)[-1]
    for part in tiles_of(span):
        cot_rows[:, part] = to_rows(cot[:, :, part])
    count = TILE // SLOT
    block = height // count
    lane = lanes_of((chans, block, TILE))
    for index, msg in enumerate(col_msgs):
        sends_right = is_even("cols") if index == 0 else jnp.logical_not(is_even("cols"))
        total = jnp.zeros((chans, block, TILE), F32)
        inner = jnp.where(sends_right, TILE - 1 - lane, lane) < FHALO
        for k in range(count):
            at = slice(k * block, (k + 1) * block)
            feats = jnp.where(sends_right, feat[:, at, last].astype(F32), feat[:, at, first].astype(F32))
            cots = jnp.where(sends_right, cot[:, at, last].astype(F32), cot[:, at, first].astype(F32))
            cots = turn(cots, jnp.where(sends_right, TILE - FHALO, FHALO))
            piece = jnp.where(inner, feats, cots)
            piece = turn(piece, jnp.where(sends_right, (k + 1) * SLOT % TILE, k * SLOT))
            inside = (lane >= k * SLOT) & (lane < (k + 1) * SLOT)
            total = jnp.where(inside, piece, total)
        msg[...] = total.reshape(chans * block, TILE).astype(BF16)


def edge_kernel(cot_rows, *rest):
    cols, (msg_a, msg_b) = rest[:-2], rest[-2:]
    span = cot_rows.shape[1]
    size = msg_a.shape[0] - sum(c.shape[0] * TILE // span for c in cols)
    edge = cot_rows.shape[0] - size
    chans = size // CHALO
    low = jnp.where(is_even("rows"), edge, 0)
    msg_a[0:size] = cot_rows[pl.ds(pl.multiple_of(low, chans), size), :]
    msg_b[0:size] = cot_rows[pl.ds(pl.multiple_of(edge - low, chans), size), :]
    at = size
    for col in cols:
        count = col.shape[0] * TILE // span
        for t, part in enumerate(tiles_of(span)):
            block = col[t * count : (t + 1) * count]
            msg_a[at : at + count, part] = block
            msg_b[at : at + count, part] = block
        at += count


def corner_views(msg, size, cols):
    span = msg.shape[1]
    views, at = [], size
    for col in cols:
        count = col.shape[0] * TILE // span
        views.append(
            jnp.concatenate([msg[at : at + count, part] for part in tiles_of(span)], axis=0)
        )
        at += count
    return views


def halo_block(sources, k, chans, kind):
    rows = sources[0].shape[0] // chans
    lane = lanes_of((chans * rows, TILE))
    total = jnp.zeros((chans * rows, TILE), F32)
    if kind == "features":
        count, shift_r, shift_l = FHALO, -k * SLOT, TILE - (k + 1) * SLOT
    else:
        count, shift_r, shift_l = CHALO, -k * SLOT - FHALO, TILE - (k + 1) * SLOT + FHALO
    for index, source in enumerate(sources):
        from_right = is_even("cols") if index == 0 else jnp.logical_not(is_even("cols"))
        moved = turn(
            source.astype(F32), jnp.where(from_right, shift_r % TILE, shift_l % TILE)
        )
        total = jnp.where(
            jnp.where(from_right, lane, TILE - 1 - lane) < count, moved, total
        )
    return total.astype(BF16).reshape(chans, rows, TILE)


def columns_seen(shape, span):
    _, _, has_left, has_right = has_sides()
    lane = lanes_of(shape)
    middle = span + TILE // 2
    return (lane < span) | ((lane < middle) & has_right) | ((lane >= middle) & has_left)


def block_ones(width):
    row = lax.broadcasted_iota(jnp.int32, (width, width), 0) // POOL
    col = lax.broadcasted_iota(jnp.int32, (width, width), 1) // POOL
    return jnp.where(row == col, 1.0, 0.0).astype(BF16)


def store_split(high, low, at, total):
    top = total.astype(BF16)
    high[at, :] = top
    low[at, :] = (total - top.astype(F32)).astype(BF16)


def block_sums(high, low, ones):
    return jnp.dot(high[...], ones, preferred_element_type=F32) + jnp.dot(
        low[...], ones, preferred_element_type=F32
    )


def fill_bands(out, kernel, count):
    chans = kernel.shape[1]
    out[...] = jnp.zeros(out.shape, out.dtype)
    for k in range(count):
        for b in range(3):
            for a in range(3):
                at = (b * (count + 2) + k + a) * chans
                out[k * chans : (k + 1) * chans, at : at + chans] = kernel[3 * a + b].astype(
                    out.dtype
                )


def fill_turned_bands(out, kernel, count):
    chans = kernel.shape[1]
    out[...] = jnp.zeros(out.shape, out.dtype)
    for k in range(count):
        for b in range(3):
            for a in range(3):
                at = (b * (count + 2) + k + a) * chans
                out[at : at + chans, k * chans : (k + 1) * chans] = kernel[8 - 3 * a - b].astype(
                    out.dtype
                )


def stacked(views, at):
    return jnp.concatenate([view[at, :] for view in views], axis=0)


def conv_sum(parts, chans, step):
    return (
        turn(parts[0:chans], step)
        + parts[chans : 2 * chans]
        + turn(parts[2 * chans : 3 * chans], -step)
    )


def back_kernel(
    ncols, cot, msg_a, msg_b, *rest,
):
    cols, (
        first, bottle, second,
        act_grad, view_m, view_0, view_p, sides, first_bands, bottle_bands, second_bands,
        cot_m, cot_0, cot_p, back, high, low, coarse, bands_f, bands, small_f, small, wide_f,
    ) = rest[:ncols], rest[ncols:]
    chans = second.shape[1]
    full, span = cot.shape
    height = full // chans
    width = span + TILE
    groups = height // POOL
    has_up, has_down, _, _ = has_sides()
    seen_cols = columns_seen((chans, width), span)

    fill_turned_bands(bands_f, second, POOL)
    bands[...] = bands_f[...].T.astype(BF16)
    fill_turned_bands(small_f, bottle, 1)
    small_t = small_f[...].T
    for b in range(3):
        small[rows_at(b, chans)] = small_t[0:chans, 3 * b * chans : 3 * (b + 1) * chans].astype(BF16)
    fill_bands(first_bands, first, POOL)
    fill_bands(wide_f, bottle, 1)
    for b in range(3):
        bottle_bands[rows_at(b, chans)] = wide_f[
            0:chans, 3 * b * chans : 3 * (b + 1) * chans
        ].astype(BF16)
    second_bands[...] = jnp.zeros(second_bands.shape, BF16)
    for k in range(POOL):
        for b in range(3):
            for a in range(3):
                second_bands[
                    rows_at(3 * k + b, chans), (k + a) * chans : (k + a + 1) * chans
                ] = second[3 * a + b]

    size = CHALO * chans
    count = TILE // SLOT
    block = height // count

    def halo_columns(sources, at):
        for k in range(count):
            sides[:, at + k * block : at + (k + 1) * block, :] = halo_block(
                sources, k, chans, "features"
            )

    halo_columns([c[...] for c in cols], height)
    cot_0[rows_at(CHALO, chans, height), 0:span] = cot[...]
    for k in range(count):
        cot_0[rows_at(CHALO + k * block, chans, block), span:width] = to_rows(
            halo_block([c[...] for c in cols], k, chans, "cotangent")
        )

    def vertical(up, down):
        cot_0[rows_at(0, chans, CHALO), 0:span] = up[0:size]
        cot_0[rows_at(CHALO + height, chans, CHALO), 0:span] = down[0:size]
        corner = to_rows(
            halo_block(corner_views(up, size, cols), count - 1, chans, "cotangent")
        )
        cot_0[rows_at(0, chans, CHALO), span:width] = corner[(block - CHALO) * chans :]
        corner = to_rows(halo_block(corner_views(down, size, cols), 0, chans, "cotangent"))
        cot_0[rows_at(CHALO + height, chans, CHALO), span:width] = corner[0:size]
        halo_columns(corner_views(up, size, cols), 0)
        halo_columns(corner_views(down, size, cols), 2 * height)

    pl.when(is_even("rows"))(lambda: vertical(msg_b, msg_a))
    pl.when(jnp.logical_not(is_even("rows")))(lambda: vertical(msg_a, msg_b))
    for j in range(height + 2 * CHALO):
        at = rows_at(j, chans)
        cot_m[at] = turn(cot_0[at], 1)
        cot_p[at] = turn(cot_0[at], -1)
    inner = rows_at(CHALO - 1, chans, height + 2)
    view_m[...] = cot_m[inner, 0:span]
    view_0[...] = cot_0[inner, 0:span]
    view_p[...] = cot_p[inner, 0:span]

    def group(g, _):
        at = rows_at(g * POOL, chans, POOL + 2)
        rows = jnp.dot(
            bands[...], stacked((cot_m, cot_0, cot_p), at), preferred_element_type=F32
        ).astype(BF16)
        back[rows_at(g * POOL, chans, POOL), :] = rows[:, 0:span]
        rows = rows.astype(F32)
        total = rows[0:chans]
        for k in range(1, POOL):
            total = total + rows[k * chans : (k + 1) * chans]
        store_split(high, low, rows_at(g, chans), total)
        return 0

    lax.fori_loop(0, groups + 2, group, 0, unroll=2)
    sums = block_sums(high, low, block_ones(width))
    for g in range(groups + 2):
        at = rows_at(g, chans)
        seen = seen_cols
        if g == 0:
            seen = seen & has_up
        elif g == groups + 1:
            seen = seen & has_down
        coarse[at] = jnp.where(seen, sums[at], 0.0).astype(BF16)
    for g in range(groups):
        parts = jnp.dot(small[...], coarse[rows_at(g, chans, 3), :], preferred_element_type=F32)
        mean = conv_sum(parts, chans, POOL)[:, 0:span] * (1.0 / POOL**2)
        for k in range(POOL):
            r = g * POOL + k
            act_grad[rows_at(r, chans), :] = back[rows_at(r + POOL, chans), :].astype(F32) + mean


def correlate(u, u0, views, v0, acc, height, chans, span):
    acc[...] = jnp.zeros(acc.shape, F32)

    def group(g, _):
        left = jnp.concatenate(
            [view[rows_at(v0 + g * POOL, chans, POOL + 2), 0:span] for view in views], axis=0
        )
        right = u[rows_at(u0 + g * POOL, chans, POOL), 0:span]
        acc[...] += lax.dot_general(
            left, right, (((1,), (1,)), ((), ())), preferred_element_type=F32
        )
        return 0

    lax.fori_loop(0, height // POOL, group, 0, unroll=2)


def folded(acc, chans):
    lane = lanes_of((3 * chans, TILE))
    result = jnp.zeros((3 * chans, TILE), F32)
    for b in range(3):
        total = None
        for k in range(POOL):
            block = turn(
                acc[rows_at(b * (POOL + 2) + k, chans, 3), 0:TILE], (b - k) * chans
            )
            total = block if total is None else total + block
        result = jnp.where((lane >= b * chans) & (lane < (b + 1) * chans), total, result)
    return result


def main_kernel(
    shifts, feat, feat_a, feat_b, sides, act_grad, view_m, view_0, view_p, bands, small,
    grads, blended,
    planes, moved, warp_m, warp_0, warp_p, act, high, low, pooled, pre_grad, acc,
):
    chans, height, span = feat.shape
    tiles = span // TILE
    width = span + TILE
    groups = height // POOL
    has_up, has_down, has_left, has_right = has_sides()
    seen_cols = columns_seen((chans, width), span)

    planes[:, height : 2 * height, 0:span] = feat[...]
    planes[:, :, span:width] = sides[...]
    fill = (height - FHALO) * chans

    def vertical(up, down):
        for part in tiles_of(span):
            none = jnp.zeros((fill, TILE), BF16)
            planes[:, 0:height, part] = to_planes(
                jnp.concatenate([none, up[:, part]], axis=0), chans
            )
            planes[:, 2 * height : 3 * height, part] = to_planes(
                jnp.concatenate([down[:, part], none], axis=0), chans
            )

    pl.when(is_even("rows"))(lambda: vertical(feat_b, feat_a))
    pl.when(jnp.logical_not(is_even("rows")))(lambda: vertical(feat_a, feat_b))

    tall = moved.shape[1]
    lane = lanes_of((tall, TILE))
    seen_halo = ((lane < TILE // 2) & has_right) | ((lane >= TILE // 2) & has_left)
    step = lanes_of((tall, 3 * height)) - lax.broadcasted_iota(jnp.int32, (tall, 3 * height), 0)

    def warp(c, _):
        pick = jnp.where(step == height - EXT + shifts[c, 0], 1.0, 0.0).astype(BF16)
        plane = jnp.dot(pick, planes[c], preferred_element_type=F32)
        move = shifts[c, 1]
        amount = jnp.where(move > 0, TILE - move, -move)
        parts = [turn(plane[:, part], amount) for part in tiles_of(width)]
        inside = jnp.where(move > 0, lane, TILE - 1 - lane) < TILE - jnp.abs(move)
        for t, part in enumerate(tiles_of(width)):
            after, before = parts[(t + 1) % (tiles + 1)], parts[t - 1]
            result = jnp.where(inside, parts[t], jnp.where(move > 0, after, before))
            if t == tiles:
                result = jnp.where(seen_halo, result, 0.0)
            moved[c, :, part] = result.astype(BF16)
        return 0

    lax.fori_loop(0, chans, warp, 0, unroll=4)
    chunk = 16
    for r in range(0, tall, chunk):
        for part in tiles_of(width):
            warp_0[rows_at(r, chans, chunk), part] = to_rows(moved[:, r : r + chunk, part])

    def clear(r, count):
        warp_0[rows_at(r, chans, count)] = jnp.zeros((count * chans, width), BF16)

    pl.when(jnp.logical_not(has_up))(lambda: clear(0, EXT))
    pl.when(jnp.logical_not(has_down))(lambda: clear(EXT + height, EXT))
    for j in range(height + 2 * EXT):
        at = rows_at(j, chans)
        warp_m[at] = turn(warp_0[at], 1)
        warp_p[at] = turn(warp_0[at], -1)

    def first_group(g, own):
        at = rows_at(g * POOL, chans, POOL + 2)
        pre = jnp.dot(
            bands[...], stacked((warp_m, warp_0, warp_p), at), preferred_element_type=F32
        )
        sigma = 0.5 * jnp.tanh(0.5 * pre) + 0.5
        rows = (pre * sigma).astype(BF16)
        act[rows_at(g * POOL, chans, POOL), :] = rows
        rows = rows.astype(F32)
        total = rows[0:chans]
        for k in range(1, POOL):
            total = total + rows[k * chans : (k + 1) * chans]
        store_split(high, low, rows_at(g, chans), total)
        if own:
            there = rows_at(g * POOL - 2 * POOL, chans, POOL)
            pre, sigma = pre[:, 0:span], sigma[:, 0:span]
            pre_grad[there, :] = (
                act_grad[there, :] * (sigma * (1.0 + pre * (1.0 - sigma)))
            ).astype(BF16)
        return 0

    for g in (0, 1, groups + 2, groups + 3):
        first_group(g, False)
    lax.fori_loop(2, groups + 2, lambda g, _: first_group(g, True), 0, unroll=2)
    sums = block_sums(high, low, block_ones(width))
    for g in range(groups + 4):
        at = rows_at(g, chans)
        seen = seen_cols
        if g < 2:
            seen = seen & has_up
        elif g >= groups + 2:
            seen = seen & has_down
        pooled[at] = jnp.where(seen, sums[at] * (1.0 / POOL**2), 0.0).astype(BF16)

    for g in range(groups + 2):
        parts = jnp.dot(small[...], pooled[rows_at(g, chans, 3), :], preferred_element_type=F32)
        bottle_row = conv_sum(parts, chans, POOL)
        rows, seen = range(POOL), seen_cols
        if g == 0:
            rows, seen = (POOL - 1,), seen & has_up
        elif g == groups + 1:
            rows, seen = (0,), seen & has_down
        for k in rows:
            row = act[rows_at((g + 1) * POOL + k, chans), :].astype(F32) + bottle_row
            blended[rows_at(g * POOL + k - POOL + 1, chans), :] = jnp.where(seen, row, 0.0).astype(
                BF16
            )

    correlate(pre_grad, 0, (warp_m, warp_0, warp_p), EXT - 1, acc, height, chans, span)
    first_part = folded(acc, chans)
    correlate(blended, 1, (view_m, view_0, view_p), 0, acc, height, chans, span)
    second_part = folded(acc, chans)
    lane = lanes_of((3 * chans, TILE))
    grads[0 : 3 * chans] = jnp.where(lane < 3 * chans, first_part, turn(second_part, 3 * chans))
    half = 3 * chans // 2
    grads[3 * chans :] = jnp.where(
        lane[0:half] < TILE // 2,
        turn(second_part[0:half], -chans),
        turn(second_part[half:], TILE // 2 - chans),
    )


def predict_kernel(part, blended, bands, *rest):
    out, rows = rest[-2:]
    chans, height, span = out.shape

    def group(g, _):
        at = rows_at(part * height + g * POOL, chans, POOL + 2)
        parts = jnp.dot(bands[...], blended[at, :], preferred_element_type=F32)
        for k in range(POOL):
            row = conv_sum(parts[3 * k * chans : 3 * (k + 1) * chans], chans, 1)
            rows[rows_at(g * POOL + k, chans), :] = row[:, 0:span].astype(BF16)
        return 0

    lax.fori_loop(0, height // POOL, group, 0, unroll=2)
    for part in tiles_of(span):
        out[:, :, part] = to_planes(rows[:, part], chans)


def final_kernel(factor, mine, other, first, second):
    chans = first.shape[1]
    total = (mine[...] + other[...]) * factor
    turned = total[0 : 3 * chans].T
    for b in range(3):
        for a in range(3):
            first[3 * a + b] = turned[b * chans : (b + 1) * chans, a * chans : (a + 1) * chans]
    half = 3 * chans // 2
    low = total[3 * chans :]
    both = jnp.concatenate([low, turn(low, -(TILE // 2))], axis=0)
    for a in range(3):
        at = slice((2 - a) * chans, (3 - a) * chans)
        second[3 * a + 2] = turn(total[at], -3 * chans)[:, 0:chans]
        second[3 * a + 1] = both[at, 0:chans]
        second[3 * a + 0] = turn(both[at], -chans)[:, 0:chans]


def call(kernel, outs, scratch, n_in, limit, flops=0, smem_first=False, **more):
    specs = [VMEM] * n_in
    if smem_first:
        specs[0] = SMEM
    more.setdefault("in_specs", specs)
    more.setdefault("out_specs", jax.tree.map(lambda _: VMEM, outs))
    return pl.pallas_call(
        kernel,
        out_shape=outs,
        scratch_shapes=scratch,
        compiler_params=pltpu.CompilerParams(vmem_limit_bytes=limit * MIB),
        cost_estimate=pl.CostEstimate(flops=flops, bytes_accessed=4 * MIB, transcendentals=0),
        **more,
    )


def predict(blended, bands, shape, parts, part, before):
    chans, height, span = shape
    rows = height // parts
    block = pl.BlockSpec((chans, rows, span), lambda i: (0, part, 0))
    whole = lambda a: pl.BlockSpec(a.shape, lambda i: (0,) * a.ndim)
    args = (blended, bands)
    specs = [whole(a) for a in args]
    more = {}
    if before is not None:
        args += (before,)
        specs.append(pl.BlockSpec(memory_space=pl.ANY))
        more["input_output_aliases"] = {2: 0}
    return call(
        functools.partial(predict_kernel, part),
        jax.ShapeDtypeStruct(shape, BF16),
        [
            pltpu.VMEM((chans * rows, span), BF16),
        ],
        len(args),
        12,
        flops=10**9,
        grid=(1,),
        in_specs=specs,
        out_specs=block,
        **more,
    )(*args)


def shards(features, shifts, first_kernel, bottle_kernel, second_kernel, cotangent):
    imgs, chans, height, span = features.shape
    rows, cols, dp = (lax.axis_size(a) for a in ("rows", "cols", "dp"))
    tiles = span // TILE
    width = span + TILE
    full = height * chans
    groups = height // POOL

    def bf(*shape):
        return jax.ShapeDtypeStruct(shape, BF16)

    def swapped(messages, axis):
        pairs = [p for p in swaps(lax.axis_size(axis)) if p]
        return [lax.ppermute(m, axis, p) for m, p in zip(messages, pairs)]

    halo = bf(FHALO * chans, span)
    feat_msgs = call(
        feature_kernel, (halo, halo), [pltpu.VMEM((full, span), BF16)], 1, 8
    )(features[0])
    row_pairs = swaps(rows)
    feat_a = lax.ppermute(feat_msgs[0], "rows", row_pairs[0])
    packed = chans * (height * SLOT // TILE)
    cot_rows, *messages = call(
        column_kernel,
        (bf(full, span),) + (bf(packed, TILE),) * (1 if cols == 2 else 2),
        [],
        2,
        8,
        flops=2 * 10**10,
    )(features[0], cotangent[0])
    col_msgs = swapped(messages, "cols")
    ncols = len(col_msgs)
    halo = bf(CHALO * chans + ncols * packed * TILE // span, span)
    messages = call(edge_kernel, (halo, halo), [], 1 + ncols, 8)(cot_rows, *col_msgs)
    messages, late = lax.optimization_barrier((messages, feat_msgs[1]))
    row_msgs = swapped(messages, "rows")
    feat_b = lax.ppermute(late, "rows", row_pairs[1])

    tall_c = (height + 2 * CHALO) * chans
    view = bf((height + 2) * chans, span)
    band = 3 * (POOL + 2) * chans
    act_grad, *rest = call(
        functools.partial(back_kernel, ncols),
        (
            jax.ShapeDtypeStruct((full, span), F32), view, view, view,
            bf(chans, 3 * height, TILE), bf(POOL * chans, band), bf(3 * chans, 3 * chans),
            bf(3 * POOL * chans, (POOL + 2) * chans),
        ),
        [pltpu.VMEM((tall_c, width), BF16)] * 3
        + [pltpu.VMEM(((height + 2 * POOL) * chans, span), BF16)]
        + [pltpu.VMEM(((groups + 2) * chans, width), BF16)] * 3
        + [
            pltpu.VMEM((band, POOL * chans), F32),
            pltpu.VMEM((POOL * chans, band), BF16),
            pltpu.VMEM((9 * chans, TILE), F32),
            pltpu.VMEM((3 * chans, 3 * chans), BF16),
            pltpu.VMEM((chans, 9 * chans), F32),
        ],
        6 + ncols,
        16,
        flops=8 * 10**9,
    )(cot_rows, *row_msgs, *col_msgs, first_kernel, bottle_kernel, second_kernel)
    views, sides, weights = rest[:3], rest[3], rest[4:]

    tall = pl.cdiv(height + 2 * EXT, 16) * 16
    grads, blended = call(
        main_kernel,
        (jax.ShapeDtypeStruct((9 * chans // 2, TILE), F32), bf((height + 2) * chans, width)),
        [
            pltpu.VMEM((chans, 3 * height, width), BF16),
            pltpu.VMEM((chans, tall, width), BF16),
        ]
        + [pltpu.VMEM((tall * chans, width), BF16)] * 3
        + [pltpu.VMEM(((height + 4 * POOL) * chans, width), BF16)]
        + [pltpu.VMEM(((groups + 4) * chans, width), BF16)] * 3
        + [
            pltpu.VMEM((full, span), BF16),
            pltpu.VMEM((band, POOL * chans), F32),
        ],
        11,
        32,
        flops=10**10,
        smem_first=True,
    )(
        shifts[0], features[0], feat_a, feat_b, sides, act_grad, *views, *weights[:2]
    )

    steps = []
    for axis, size in (("dp", dp), ("cols", cols), ("rows", rows)):
        bit = 1
        while bit < size:
            steps.append((axis, [(i, i ^ bit) for i in range(size)]))
            bit *= 2
    parts, prediction = 2, None
    for step, (axis, pairs) in enumerate(steps):
        other = lax.ppermute(grads, axis, pairs)
        if 1 <= step <= parts:
            prediction = predict(
                blended, weights[2], (chans, height, span), parts, step - 1, prediction
            )
            other, prediction = lax.optimization_barrier((other, prediction))
        if step < len(steps) - 1:
            grads = grads + other
            if step < parts:
                grads, blended = lax.optimization_barrier((grads, blended))
    factor = 1.0 / math.sqrt(imgs * dp * height * rows * span * cols)
    shape = jax.ShapeDtypeStruct((9, chans, chans), F32)
    first_grad, second_grad = call(
        functools.partial(final_kernel, factor), (shape, shape), [], 2, 2
    )(grads, other)
    return (prediction[None], first_grad, second_grad)


def solution(mesh):
    placed = (
        P("dp", None, "rows", "cols"),
        P("dp", None, None),
        P(),
        P(),
        P(),
        P("dp", None, "rows", "cols"),
    )
    return jax.shard_map(
        shards,
        mesh=mesh,
        in_specs=placed,
        out_specs=(P("dp", None, "rows", "cols"), P(), P()),
        check_vma=False,
    )
```

```python
import functools
import math

import jax
import jax.numpy as jnp
from jax import lax
from jax.experimental import pallas as pl
from jax.experimental.pallas import tpu as pltpu
from jax.sharding import PartitionSpec as P


MAXSHIFT = 16
POOL = 4
TILE = 128
SLOT = 32
EXT = 9
FHALO = MAXSHIFT + EXT
USUAL = 14
LARGEST = FHALO + 1
CHALO = 5
F32 = jnp.float32
BF16 = jnp.bfloat16
VMEM = pl.BlockSpec(memory_space=pltpu.VMEM)
SMEM = pl.BlockSpec(memory_space=pltpu.SMEM)
MIB = 1024 * 1024


def lanes_of(shape):
    return lax.broadcasted_iota(jnp.int32, shape, len(shape) - 1)


def turn(values, shift):
    width = values.shape[-1]
    if isinstance(shift, int):
        shift = shift % width
        if shift == 0:
            return values
    return pltpu.roll(values, shift, values.ndim - 1)


def has_sides():
    row, col = lax.axis_index("rows"), lax.axis_index("cols")
    return (
        row > 0,
        row < lax.axis_size("rows") - 1,
        col > 0,
        col < lax.axis_size("cols") - 1,
    )


def rows_at(r, chans, count=1):
    if isinstance(r, int):
        return slice(r * chans, (r + count) * chans)
    return pl.ds(pl.multiple_of(r * chans, chans), count * chans)


def to_rows(block):
    chans, height, span = block.shape
    return jnp.transpose(block, (1, 0, 2)).reshape(height * chans, span)


def to_planes(block, chans):
    height = block.shape[0] // chans
    return jnp.transpose(block.reshape(height, chans, block.shape[1]), (1, 0, 2))


def tiles_of(span):
    return [slice(t, t + TILE) for t in range(0, span, TILE)]


def is_even(axis):
    return lax.rem(lax.axis_index(axis), 2) == 0


def swaps(size):
    first = [(i, i ^ 1) for i in range(size)]
    second = [(i, i + 1) for i in range(1, size - 1, 2)]
    return [first, second + [(j, i) for i, j in second]]


def needed(shift, below):
    return jnp.maximum(EXT + shift if below else EXT - shift, 0)


def feature_kernel(shifts, feat, msg_a, msg_b):
    chans, height, span = feat.shape
    full = chans * height
    size = msg_a.shape[0]
    chunk = size // 4
    source = feat[...].reshape(full, span)
    lane = lanes_of((8, full))
    chan, row = lane // height, lane % height
    for msg, to_below in ((msg_a, is_even("rows")), (msg_b, jnp.logical_not(is_even("rows")))):
        target = jnp.full((8, full), -1, jnp.int32)
        at = jnp.int32(0)
        for c in range(chans):
            shift = shifts[c, 0]
            count = jnp.where(to_below, needed(shift, False), needed(shift, True))
            first = jnp.where(to_below, height - count, 0)
            mine = (chan == c) & (row >= first) & (row < first + count)
            target = jnp.where(mine, row + (at - first), target)
            at = at + count
        for p in range(0, size, chunk):
            place = lax.broadcasted_iota(jnp.int32, (chunk, full), 0) + p
            pick = jnp.where(place == target[0:1], 1.0, 0.0).astype(BF16)
            msg[p : p + chunk] = jnp.dot(pick, source, preferred_element_type=F32).astype(BF16)


def column_kernel(feat, cot, cot_rows, *col_msgs):
    chans, height, span = feat.shape
    first, last = tiles_of(span)[0], tiles_of(span)[-1]
    for part in tiles_of(span):
        cot_rows[:, part] = to_rows(cot[:, :, part])
    count = TILE // SLOT
    block = height // count
    lane = lanes_of((chans, block, TILE))
    for index, msg in enumerate(col_msgs):
        sends_right = is_even("cols") if index == 0 else jnp.logical_not(is_even("cols"))
        total = jnp.zeros((chans, block, TILE), F32)
        inner = jnp.where(sends_right, TILE - 1 - lane, lane) < FHALO
        for k in range(count):
            at = slice(k * block, (k + 1) * block)
            feats = jnp.where(sends_right, feat[:, at, last].astype(F32), feat[:, at, first].astype(F32))
            cots = jnp.where(sends_right, cot[:, at, last].astype(F32), cot[:, at, first].astype(F32))
            cots = turn(cots, jnp.where(sends_right, TILE - FHALO, FHALO))
            piece = jnp.where(inner, feats, cots)
            piece = turn(piece, jnp.where(sends_right, (k + 1) * SLOT % TILE, k * SLOT))
            inside = (lane >= k * SLOT) & (lane < (k + 1) * SLOT)
            total = jnp.where(inside, piece, total)
        msg[...] = total.reshape(chans * block, TILE).astype(BF16)


def edge_kernel(cot_rows, *rest):
    cols, (msg_a, msg_b) = rest[:-2], rest[-2:]
    span = cot_rows.shape[1]
    size = msg_a.shape[0] - sum(c.shape[0] * TILE // span for c in cols)
    edge = cot_rows.shape[0] - size
    chans = size // CHALO
    low = jnp.where(is_even("rows"), edge, 0)
    msg_a[0:size] = cot_rows[pl.ds(pl.multiple_of(low, chans), size), :]
    msg_b[0:size] = cot_rows[pl.ds(pl.multiple_of(edge - low, chans), size), :]
    at = size
    for col in cols:
        count = col.shape[0] * TILE // span
        for t, part in enumerate(tiles_of(span)):
            block = col[t * count : (t + 1) * count]
            msg_a[at : at + count, part] = block
            msg_b[at : at + count, part] = block
        at += count


def corner_views(msg, size, cols):
    span = msg.shape[1]
    views, at = [], size
    for col in cols:
        count = col.shape[0] * TILE // span
        views.append(
            jnp.concatenate([msg[at : at + count, part] for part in tiles_of(span)], axis=0)
        )
        at += count
    return views


def halo_block(sources, k, chans, kind):
    rows = sources[0].shape[0] // chans
    lane = lanes_of((chans * rows, TILE))
    total = jnp.zeros((chans * rows, TILE), F32)
    if kind == "features":
        count, shift_r, shift_l = FHALO, -k * SLOT, TILE - (k + 1) * SLOT
    else:
        count, shift_r, shift_l = CHALO, -k * SLOT - FHALO, TILE - (k + 1) * SLOT + FHALO
    for index, source in enumerate(sources):
        from_right = is_even("cols") if index == 0 else jnp.logical_not(is_even("cols"))
        moved = turn(
            source.astype(F32), jnp.where(from_right, shift_r % TILE, shift_l % TILE)
        )
        total = jnp.where(
            jnp.where(from_right, lane, TILE - 1 - lane) < count, moved, total
        )
    return total.astype(BF16).reshape(chans, rows, TILE)


def columns_seen(shape, span):
    _, _, has_left, has_right = has_sides()
    lane = lanes_of(shape)
    middle = span + TILE // 2
    return (lane < span) | ((lane < middle) & has_right) | ((lane >= middle) & has_left)


def block_ones(width):
    row = lax.broadcasted_iota(jnp.int32, (width, width), 0) // POOL
    col = lax.broadcasted_iota(jnp.int32, (width, width), 1) // POOL
    return jnp.where(row == col, 1.0, 0.0).astype(BF16)


def store_split(high, low, at, total):
    top = total.astype(BF16)
    high[at, :] = top
    low[at, :] = (total - top.astype(F32)).astype(BF16)


def block_sums(high, low, ones):
    return jnp.dot(high[...], ones, preferred_element_type=F32) + jnp.dot(
        low[...], ones, preferred_element_type=F32
    )


def fill_bands(out, kernel, count):
    chans = kernel.shape[1]
    out[...] = jnp.zeros(out.shape, out.dtype)
    for k in range(count):
        for b in range(3):
            for a in range(3):
                at = (b * (count + 2) + k + a) * chans
                out[k * chans : (k + 1) * chans, at : at + chans] = kernel[3 * a + b].astype(
                    out.dtype
                )


def fill_turned_bands(out, kernel, count):
    chans = kernel.shape[1]
    out[...] = jnp.zeros(out.shape, out.dtype)
    for k in range(count):
        for b in range(3):
            for a in range(3):
                at = (b * (count + 2) + k + a) * chans
                out[at : at + chans, k * chans : (k + 1) * chans] = kernel[8 - 3 * a - b].astype(
                    out.dtype
                )


def stacked(views, at):
    return jnp.concatenate([view[at, :] for view in views], axis=0)


def conv_sum(parts, chans, step):
    return (
        turn(parts[0:chans], step)
        + parts[chans : 2 * chans]
        + turn(parts[2 * chans : 3 * chans], -step)
    )


def back_kernel(
    ncols, cot, msg_a, msg_b, *rest,
):
    cols, (
        first, bottle, second,
        act_grad, view_m, view_0, view_p, sides, first_bands, bottle_bands, second_bands,
        cot_m, cot_0, cot_p, back, high, low, coarse, bands_f, bands, small_f, small, wide_f,
    ) = rest[:ncols], rest[ncols:]
    chans = second.shape[1]
    full, span = cot.shape
    height = full // chans
    width = span + TILE
    groups = height // POOL
    has_up, has_down, _, _ = has_sides()
    seen_cols = columns_seen((chans, width), span)

    fill_turned_bands(bands_f, second, POOL)
    bands[...] = bands_f[...].T.astype(BF16)
    fill_turned_bands(small_f, bottle, 1)
    small_t = small_f[...].T
    for b in range(3):
        small[rows_at(b, chans)] = small_t[0:chans, 3 * b * chans : 3 * (b + 1) * chans].astype(BF16)
    fill_bands(first_bands, first, POOL)
    fill_bands(wide_f, bottle, 1)
    for b in range(3):
        bottle_bands[rows_at(b, chans)] = wide_f[
            0:chans, 3 * b * chans : 3 * (b + 1) * chans
        ].astype(BF16)
    second_bands[...] = jnp.zeros(second_bands.shape, BF16)
    for k in range(POOL):
        for b in range(3):
            for a in range(3):
                second_bands[
                    rows_at(3 * k + b, chans), (k + a) * chans : (k + a + 1) * chans
                ] = second[3 * a + b]

    size = CHALO * chans
    count = TILE // SLOT
    block = height // count

    def halo_columns(sources, at):
        for k in range(count):
            sides[:, at + k * block : at + (k + 1) * block, :] = halo_block(
                sources, k, chans, "features"
            )

    halo_columns([c[...] for c in cols], height)
    cot_0[rows_at(CHALO, chans, height), 0:span] = cot[...]
    for k in range(count):
        cot_0[rows_at(CHALO + k * block, chans, block), span:width] = to_rows(
            halo_block([c[...] for c in cols], k, chans, "cotangent")
        )

    def vertical(up, down):
        cot_0[rows_at(0, chans, CHALO), 0:span] = up[0:size]
        cot_0[rows_at(CHALO + height, chans, CHALO), 0:span] = down[0:size]
        corner = to_rows(
            halo_block(corner_views(up, size, cols), count - 1, chans, "cotangent")
        )
        cot_0[rows_at(0, chans, CHALO), span:width] = corner[(block - CHALO) * chans :]
        corner = to_rows(halo_block(corner_views(down, size, cols), 0, chans, "cotangent"))
        cot_0[rows_at(CHALO + height, chans, CHALO), span:width] = corner[0:size]
        halo_columns(corner_views(up, size, cols), 0)
        halo_columns(corner_views(down, size, cols), 2 * height)

    pl.when(is_even("rows"))(lambda: vertical(msg_b, msg_a))
    pl.when(jnp.logical_not(is_even("rows")))(lambda: vertical(msg_a, msg_b))
    for j in range(height + 2 * CHALO):
        at = rows_at(j, chans)
        cot_m[at] = turn(cot_0[at], 1)
        cot_p[at] = turn(cot_0[at], -1)
    inner = rows_at(CHALO - 1, chans, height + 2)
    view_m[...] = cot_m[inner, 0:span]
    view_0[...] = cot_0[inner, 0:span]
    view_p[...] = cot_p[inner, 0:span]

    def group(g, _):
        at = rows_at(g * POOL, chans, POOL + 2)
        rows = jnp.dot(
            bands[...], stacked((cot_m, cot_0, cot_p), at), preferred_element_type=F32
        ).astype(BF16)
        back[rows_at(g * POOL, chans, POOL), :] = rows[:, 0:span]
        rows = rows.astype(F32)
        total = rows[0:chans]
        for k in range(1, POOL):
            total = total + rows[k * chans : (k + 1) * chans]
        store_split(high, low, rows_at(g, chans), total)
        return 0

    lax.fori_loop(0, groups + 2, group, 0, unroll=2)
    sums = block_sums(high, low, block_ones(width))
    for g in range(groups + 2):
        at = rows_at(g, chans)
        seen = seen_cols
        if g == 0:
            seen = seen & has_up
        elif g == groups + 1:
            seen = seen & has_down
        coarse[at] = jnp.where(seen, sums[at], 0.0).astype(BF16)
    for g in range(groups):
        parts = jnp.dot(small[...], coarse[rows_at(g, chans, 3), :], preferred_element_type=F32)
        mean = conv_sum(parts, chans, POOL)[:, 0:span] * (1.0 / POOL**2)
        for k in range(POOL):
            r = g * POOL + k
            act_grad[rows_at(r, chans), :] = back[rows_at(r + POOL, chans), :].astype(F32) + mean


def correlate(u, u0, views, v0, acc, height, chans, span):
    acc[...] = jnp.zeros(acc.shape, F32)

    def group(g, _):
        left = jnp.concatenate(
            [view[rows_at(v0 + g * POOL, chans, POOL + 2), 0:span] for view in views], axis=0
        )
        right = u[rows_at(u0 + g * POOL, chans, POOL), 0:span]
        acc[...] += lax.dot_general(
            left, right, (((1,), (1,)), ((), ())), preferred_element_type=F32
        )
        return 0

    lax.fori_loop(0, height // POOL, group, 0, unroll=2)


def folded(acc, chans):
    lane = lanes_of((3 * chans, TILE))
    result = jnp.zeros((3 * chans, TILE), F32)
    for b in range(3):
        total = None
        for k in range(POOL):
            block = turn(
                acc[rows_at(b * (POOL + 2) + k, chans, 3), 0:TILE], (b - k) * chans
            )
            total = block if total is None else total + block
        result = jnp.where((lane >= b * chans) & (lane < (b + 1) * chans), total, result)
    return result


def main_kernel(
    shifts, feat, feat_a, feat_b, sides, act_grad, view_m, view_0, view_p, bands, small,
    grads, blended,
    lent, moved, warp_m, warp_0, warp_p, act, high, low, pooled, pre_grad, acc,
):
    chans, height, span = feat.shape
    tiles = span // TILE
    width = span + TILE
    groups = height // POOL
    has_up, has_down, has_left, has_right = has_sides()
    seen_cols = columns_seen((chans, width), span)

    size = feat_a.shape[0]
    window = lent.shape[1] - size
    lent[:, size:, :] = jnp.zeros((2, window, span), BF16)

    def borrow(up, down):
        lent[0, 0:size] = up[...]
        lent[1, 0:size] = down[...]

    pl.when(is_even("rows"))(lambda: borrow(feat_b, feat_a))
    pl.when(jnp.logical_not(is_even("rows")))(lambda: borrow(feat_a, feat_b))

    tall = moved.shape[1]
    lane = lanes_of((tall, TILE))
    seen_halo = ((lane < TILE // 2) & has_right) | ((lane >= TILE // 2) & has_left)
    step = lanes_of((tall, 3 * height)) - lax.broadcasted_iota(jnp.int32, (tall, 3 * height), 0)
    depth = 2 * window + height
    source = lanes_of((1, depth))
    apart = lax.broadcasted_iota(jnp.int32, (tall, depth), 0) - lanes_of((tall, depth))
    align = 16

    def warp(c, ats):
        at_up, at_down = ats
        shift, move = shifts[c, 0], shifts[c, 1]
        n_up, n_down = needed(shift, False), needed(shift, True)
        base_up, base_down = (
            pl.multiple_of(lax.div(at, align) * align, align) for at in (at_up, at_down)
        )
        skip_up, skip_down = at_up - base_up, at_down - base_down
        own = EXT - window - shift
        below = own - skip_down
        above = EXT - skip_up - n_up - shift
        in_up = (source >= skip_up) & (source < skip_up + n_up)
        first_down = window + height + skip_down
        in_down = (source >= first_down) & (source < first_down + n_down)
        none = 4 * depth
        offset = jnp.where(
            source < window,
            jnp.where(in_up, above, none),
            jnp.where(source < window + height, own, jnp.where(in_down, below, none)),
        )
        pick = jnp.where(apart == offset, 1.0, 0.0).astype(BF16)
        rows = jnp.concatenate(
            [lent[0, pl.ds(base_up, window), :], feat[c], lent[1, pl.ds(base_down, window), :]], axis=0
        )
        plane = jnp.dot(pick, rows, preferred_element_type=F32)
        pick = jnp.where(step == height - EXT + shift, 1.0, 0.0).astype(BF16)
        plane = [plane[:, part] for part in tiles_of(span)]
        plane.append(jnp.dot(pick, sides[c], preferred_element_type=F32))
        amount = jnp.where(move > 0, TILE - move, -move)
        parts = [turn(part, amount) for part in plane]
        inside = jnp.where(move > 0, lane, TILE - 1 - lane) < TILE - jnp.abs(move)
        for t, part in enumerate(tiles_of(width)):
            after, before = parts[(t + 1) % (tiles + 1)], parts[t - 1]
            result = jnp.where(inside, parts[t], jnp.where(move > 0, after, before))
            if t == tiles:
                result = jnp.where(seen_halo, result, 0.0)
            moved[c, :, part] = result.astype(BF16)
        return at_up + n_up, at_down + n_down

    lax.fori_loop(0, chans, warp, (jnp.int32(0), jnp.int32(0)), unroll=4)
    chunk = 16
    for r in range(0, tall, chunk):
        for part in tiles_of(width):
            warp_0[rows_at(r, chans, chunk), part] = to_rows(moved[:, r : r + chunk, part])

    def clear(r, count):
        warp_0[rows_at(r, chans, count)] = jnp.zeros((count * chans, width), BF16)

    pl.when(jnp.logical_not(has_up))(lambda: clear(0, EXT))
    pl.when(jnp.logical_not(has_down))(lambda: clear(EXT + height, EXT))
    for j in range(height + 2 * EXT):
        at = rows_at(j, chans)
        warp_m[at] = turn(warp_0[at], 1)
        warp_p[at] = turn(warp_0[at], -1)

    def first_group(g, own):
        at = rows_at(g * POOL, chans, POOL + 2)
        pre = jnp.dot(
            bands[...], stacked((warp_m, warp_0, warp_p), at), preferred_element_type=F32
        )
        sigma = 0.5 * jnp.tanh(0.5 * pre) + 0.5
        rows = (pre * sigma).astype(BF16)
        act[rows_at(g * POOL, chans, POOL), :] = rows
        rows = rows.astype(F32)
        total = rows[0:chans]
        for k in range(1, POOL):
            total = total + rows[k * chans : (k + 1) * chans]
        store_split(high, low, rows_at(g, chans), total)
        if own:
            there = rows_at(g * POOL - 2 * POOL, chans, POOL)
            pre, sigma = pre[:, 0:span], sigma[:, 0:span]
            pre_grad[there, :] = (
                act_grad[there, :] * (sigma * (1.0 + pre * (1.0 - sigma)))
            ).astype(BF16)
        return 0

    for g in (0, 1, groups + 2, groups + 3):
        first_group(g, False)
    lax.fori_loop(2, groups + 2, lambda g, _: first_group(g, True), 0, unroll=2)
    sums = block_sums(high, low, block_ones(width))
    for g in range(groups + 4):
        at = rows_at(g, chans)
        seen = seen_cols
        if g < 2:
            seen = seen & has_up
        elif g >= groups + 2:
            seen = seen & has_down
        pooled[at] = jnp.where(seen, sums[at] * (1.0 / POOL**2), 0.0).astype(BF16)

    for g in range(groups + 2):
        parts = jnp.dot(small[...], pooled[rows_at(g, chans, 3), :], preferred_element_type=F32)
        bottle_row = conv_sum(parts, chans, POOL)
        rows, seen = range(POOL), seen_cols
        if g == 0:
            rows, seen = (POOL - 1,), seen & has_up
        elif g == groups + 1:
            rows, seen = (0,), seen & has_down
        for k in rows:
            row = act[rows_at((g + 1) * POOL + k, chans), :].astype(F32) + bottle_row
            blended[rows_at(g * POOL + k - POOL + 1, chans), :] = jnp.where(seen, row, 0.0).astype(
                BF16
            )

    correlate(pre_grad, 0, (warp_m, warp_0, warp_p), EXT - 1, acc, height, chans, span)
    first_part = folded(acc, chans)
    correlate(blended, 1, (view_m, view_0, view_p), 0, acc, height, chans, span)
    second_part = folded(acc, chans)
    lane = lanes_of((3 * chans, TILE))
    grads[0 : 3 * chans] = jnp.where(lane < 3 * chans, first_part, turn(second_part, 3 * chans))
    half = 3 * chans // 2
    grads[3 * chans :] = jnp.where(
        lane[0:half] < TILE // 2,
        turn(second_part[0:half], -chans),
        turn(second_part[half:], TILE // 2 - chans),
    )


def predict_kernel(part, blended, bands, *rest):
    out, rows = rest[-2:]
    chans, height, span = out.shape

    def group(g, _):
        at = rows_at(part * height + g * POOL, chans, POOL + 2)
        parts = jnp.dot(bands[...], blended[at, :], preferred_element_type=F32)
        for k in range(POOL):
            row = conv_sum(parts[3 * k * chans : 3 * (k + 1) * chans], chans, 1)
            rows[rows_at(g * POOL + k, chans), :] = row[:, 0:span].astype(BF16)
        return 0

    lax.fori_loop(0, height // POOL, group, 0, unroll=2)
    for part in tiles_of(span):
        out[:, :, part] = to_planes(rows[:, part], chans)


def final_kernel(factor, mine, other, first, second):
    chans = first.shape[1]
    total = (mine[...] + other[...]) * factor
    turned = total[0 : 3 * chans].T
    for b in range(3):
        for a in range(3):
            first[3 * a + b] = turned[b * chans : (b + 1) * chans, a * chans : (a + 1) * chans]
    half = 3 * chans // 2
    low = total[3 * chans :]
    both = jnp.concatenate([low, turn(low, -(TILE // 2))], axis=0)
    for a in range(3):
        at = slice((2 - a) * chans, (3 - a) * chans)
        second[3 * a + 2] = turn(total[at], -3 * chans)[:, 0:chans]
        second[3 * a + 1] = both[at, 0:chans]
        second[3 * a + 0] = turn(both[at], -chans)[:, 0:chans]


def call(kernel, outs, scratch, n_in, limit, flops=0, smem_first=False, **more):
    specs = [VMEM] * n_in
    if smem_first:
        specs[0] = SMEM
    more.setdefault("in_specs", specs)
    more.setdefault("out_specs", jax.tree.map(lambda _: VMEM, outs))
    return pl.pallas_call(
        kernel,
        out_shape=outs,
        scratch_shapes=scratch,
        compiler_params=pltpu.CompilerParams(vmem_limit_bytes=limit * MIB),
        cost_estimate=pl.CostEstimate(flops=flops, bytes_accessed=4 * MIB, transcendentals=0),
        **more,
    )


def predict(blended, bands, shape, parts, part, before):
    chans, height, span = shape
    rows = height // parts
    block = pl.BlockSpec((chans, rows, span), lambda i: (0, part, 0))
    whole = lambda a: pl.BlockSpec(a.shape, lambda i: (0,) * a.ndim)
    args = (blended, bands)
    specs = [whole(a) for a in args]
    more = {}
    if before is not None:
        args += (before,)
        specs.append(pl.BlockSpec(memory_space=pl.ANY))
        more["input_output_aliases"] = {2: 0}
    return call(
        functools.partial(predict_kernel, part),
        jax.ShapeDtypeStruct(shape, BF16),
        [
            pltpu.VMEM((chans * rows, span), BF16),
        ],
        len(args),
        12,
        flops=10**9,
        grid=(1,),
        in_specs=specs,
        out_specs=block,
        **more,
    )(*args)


def bf(*shape):
    return jax.ShapeDtypeStruct(shape, BF16)


def swapped(messages, axis):
    pairs = [p for p in swaps(lax.axis_size(axis)) if p]
    return [lax.ppermute(m, axis, p) for m, p in zip(messages, pairs)]


def both_passes(size, feat, shifts, cot_rows, col_msgs, first_kernel, bottle_kernel, second_kernel):
    chans, height, span = feat.shape
    width = span + TILE
    full = height * chans
    groups = height // POOL
    ncols = len(col_msgs)
    packed = col_msgs[0].shape[0]

    halo = bf(CHALO * chans + ncols * packed * TILE // span, span)
    messages = call(edge_kernel, (halo, halo), [], 1 + ncols, 8)(cot_rows, *col_msgs)
    row_msgs = swapped(messages, "rows")
    messages = call(
        feature_kernel, (bf(size, span), bf(size, span)), [], 2, 16, smem_first=True
    )(shifts, feat)
    feat_msgs = swapped(messages, "rows")

    tall_c = (height + 2 * CHALO) * chans
    view = bf((height + 2) * chans, span)
    band = 3 * (POOL + 2) * chans
    act_grad, *rest = call(
        functools.partial(back_kernel, ncols),
        (
            jax.ShapeDtypeStruct((full, span), F32), view, view, view,
            bf(chans, 3 * height, TILE), bf(POOL * chans, band), bf(3 * chans, 3 * chans),
            bf(3 * POOL * chans, (POOL + 2) * chans),
        ),
        [pltpu.VMEM((tall_c, width), BF16)] * 3
        + [pltpu.VMEM(((height + 2 * POOL) * chans, span), BF16)]
        + [pltpu.VMEM(((groups + 2) * chans, width), BF16)] * 3
        + [
            pltpu.VMEM((band, POOL * chans), F32),
            pltpu.VMEM((POOL * chans, band), BF16),
            pltpu.VMEM((9 * chans, TILE), F32),
            pltpu.VMEM((3 * chans, 3 * chans), BF16),
            pltpu.VMEM((chans, 9 * chans), F32),
        ],
        6 + ncols,
        16,
        flops=8 * 10**9,
    )(cot_rows, *row_msgs, *col_msgs, first_kernel, bottle_kernel, second_kernel)
    views, sides, weights = rest[:3], rest[3], rest[4:]

    tall = pl.cdiv(height + 2 * EXT, 16) * 16
    grads, blended = call(
        main_kernel,
        (jax.ShapeDtypeStruct((9 * chans // 2, TILE), F32), bf((height + 2) * chans, width)),
        [
            pltpu.VMEM((2, size + 48, span), BF16),
            pltpu.VMEM((chans, tall, width), BF16),
        ]
        + [pltpu.VMEM((tall * chans, width), BF16)] * 3
        + [pltpu.VMEM(((height + 4 * POOL) * chans, width), BF16)]
        + [pltpu.VMEM(((groups + 4) * chans, width), BF16)] * 3
        + [
            pltpu.VMEM((full, span), BF16),
            pltpu.VMEM((band, POOL * chans), F32),
        ],
        11,
        32,
        flops=10**10,
        smem_first=True,
    )(
        shifts, feat, *feat_msgs, sides, act_grad, *views, *weights[:2]
    )

    return grads, blended, weights[2]


def shards(features, shifts, first_kernel, bottle_kernel, second_kernel, cotangent):
    imgs, chans, height, span = features.shape
    rows, cols, dp = (lax.axis_size(a) for a in ("rows", "cols", "dp"))
    full = height * chans

    packed = chans * (height * SLOT // TILE)
    cot_rows, *messages = call(
        column_kernel,
        (bf(full, span),) + (bf(packed, TILE),) * (1 if cols == 2 else 2),
        [],
        2,
        8,
    )(features[0], cotangent[0])
    col_msgs = swapped(messages, "cols")
    ncols = len(col_msgs)
    moves = shifts[0, :, 0]
    total = jnp.maximum(jnp.sum(needed(moves, False)), jnp.sum(needed(moves, True)))
    bit = 1
    while bit < dp:
        total = jnp.maximum(total, lax.ppermute(total, "dp", [(i, i ^ bit) for i in range(dp)]))
        bit *= 2

    def passes(size):
        return functools.partial(both_passes, size)

    grads, blended, second_bands = lax.cond(
        total <= USUAL * chans,
        passes(USUAL * chans),
        passes(LARGEST * chans),
        features[0], shifts[0], cot_rows, tuple(col_msgs), first_kernel, bottle_kernel, second_kernel,
    )

    steps = []
    for axis, size in (("dp", dp), ("cols", cols), ("rows", rows)):
        bit = 1
        while bit < size:
            steps.append((axis, [(i, i ^ bit) for i in range(size)]))
            bit *= 2
    parts, prediction = 2, None
    for step, (axis, pairs) in enumerate(steps):
        other = lax.ppermute(grads, axis, pairs)
        if 1 <= step <= parts:
            prediction = predict(
                blended, second_bands, (chans, height, span), parts, step - 1, prediction
            )
            other, prediction = lax.optimization_barrier((other, prediction))
        if step < len(steps) - 1:
            grads = grads + other
            if step < parts:
                grads, blended = lax.optimization_barrier((grads, blended))
    factor = 1.0 / math.sqrt(imgs * dp * height * rows * span * cols)
    shape = jax.ShapeDtypeStruct((9, chans, chans), F32)
    first_grad, second_grad = call(
        functools.partial(final_kernel, factor), (shape, shape), [], 2, 2
    )(grads, other)
    return (prediction[None], first_grad, second_grad)


def solution(mesh):
    placed = (
        P("dp", None, "rows", "cols"),
        P("dp", None, None),
        P(),
        P(),
        P(),
        P("dp", None, "rows", "cols"),
    )
    return jax.shard_map(
        shards,
        mesh=mesh,
        in_specs=placed,
        out_specs=(P("dp", None, "rows", "cols"), P(), P()),
        check_vma=False,
    )
```

```python
import functools
import math

import jax
import jax.numpy as jnp
from jax import lax
from jax.experimental import pallas as pl
from jax.experimental.pallas import tpu as pltpu
from jax.sharding import PartitionSpec as P


MAXSHIFT = 16
POOL = 4
TILE = 128
SLOT = 32
EXT = 9
FHALO = MAXSHIFT + EXT
USUAL = 14
LARGEST = FHALO + 1
CHALO = 5
F32 = jnp.float32
BF16 = jnp.bfloat16
VMEM = pl.BlockSpec(memory_space=pltpu.VMEM)
SMEM = pl.BlockSpec(memory_space=pltpu.SMEM)
MIB = 1024 * 1024


def lanes_of(shape):
    return lax.broadcasted_iota(jnp.int32, shape, len(shape) - 1)


def turn(values, shift):
    width = values.shape[-1]
    if isinstance(shift, int):
        shift = shift % width
        if shift == 0:
            return values
    return pltpu.roll(values, shift, values.ndim - 1)


def has_sides():
    row, col = lax.axis_index("rows"), lax.axis_index("cols")
    return (
        row > 0,
        row < lax.axis_size("rows") - 1,
        col > 0,
        col < lax.axis_size("cols") - 1,
    )


def rows_at(r, chans, count=1):
    if isinstance(r, int):
        return slice(r * chans, (r + count) * chans)
    return pl.ds(pl.multiple_of(r * chans, chans), count * chans)


def to_rows(block):
    chans, height, span = block.shape
    return jnp.transpose(block, (1, 0, 2)).reshape(height * chans, span)


def to_planes(block, chans):
    height = block.shape[0] // chans
    return jnp.transpose(block.reshape(height, chans, block.shape[1]), (1, 0, 2))


def tiles_of(span):
    return [slice(t, t + TILE) for t in range(0, span, TILE)]


def is_even(axis):
    return lax.rem(lax.axis_index(axis), 2) == 0


def swaps(size):
    first = [(i, i ^ 1) for i in range(size)]
    second = [(i, i + 1) for i in range(1, size - 1, 2)]
    return [first, second + [(j, i) for i, j in second]]


def needed(shift, below):
    return jnp.maximum(EXT + shift if below else EXT - shift, 0)


def feature_kernel(shifts, feat, msg_a, msg_b):
    chans, height, span = feat.shape
    full = chans * height
    size = msg_a.shape[0]
    chunk = size // 4
    source = feat[...].reshape(full, span)
    lane = lanes_of((8, full))
    chan, row = lane // height, lane % height
    for msg, to_below in ((msg_a, is_even("rows")), (msg_b, jnp.logical_not(is_even("rows")))):
        target = jnp.full((8, full), -1, jnp.int32)
        at = jnp.int32(0)
        for c in range(chans):
            shift = shifts[c, 0]
            count = jnp.where(to_below, needed(shift, False), needed(shift, True))
            first = jnp.where(to_below, height - count, 0)
            mine = (chan == c) & (row >= first) & (row < first + count)
            target = jnp.where(mine, row + (at - first), target)
            at = at + count
        for p in range(0, size, chunk):
            place = lax.broadcasted_iota(jnp.int32, (chunk, full), 0) + p
            pick = jnp.where(place == target[0:1], 1.0, 0.0).astype(BF16)
            msg[p : p + chunk] = jnp.dot(pick, source, preferred_element_type=F32).astype(BF16)


def column_kernel(feat, cot, cot_rows, *col_msgs):
    chans, height, span = feat.shape
    first, last = tiles_of(span)[0], tiles_of(span)[-1]
    for part in tiles_of(span):
        cot_rows[:, part] = to_rows(cot[:, :, part])
    count = TILE // SLOT
    block = height // count
    lane = lanes_of((chans, block, TILE))
    for index, msg in enumerate(col_msgs):
        sends_right = is_even("cols") if index == 0 else jnp.logical_not(is_even("cols"))
        total = jnp.zeros((chans, block, TILE), F32)
        inner = jnp.where(sends_right, TILE - 1 - lane, lane) < FHALO
        for k in range(count):
            at = slice(k * block, (k + 1) * block)
            feats = jnp.where(sends_right, feat[:, at, last].astype(F32), feat[:, at, first].astype(F32))
            cots = jnp.where(sends_right, cot[:, at, last].astype(F32), cot[:, at, first].astype(F32))
            cots = turn(cots, jnp.where(sends_right, TILE - FHALO, FHALO))
            piece = jnp.where(inner, feats, cots)
            piece = turn(piece, jnp.where(sends_right, (k + 1) * SLOT % TILE, k * SLOT))
            inside = (lane >= k * SLOT) & (lane < (k + 1) * SLOT)
            total = jnp.where(inside, piece, total)
        msg[...] = total.reshape(chans * block, TILE).astype(BF16)


def edge_kernel(cot_rows, *rest):
    cols, (msg_a, msg_b) = rest[:-2], rest[-2:]
    span = cot_rows.shape[1]
    size = msg_a.shape[0] - sum(c.shape[0] * TILE // span for c in cols)
    edge = cot_rows.shape[0] - size
    chans = size // CHALO
    low = jnp.where(is_even("rows"), edge, 0)
    msg_a[0:size] = cot_rows[pl.ds(pl.multiple_of(low, chans), size), :]
    msg_b[0:size] = cot_rows[pl.ds(pl.multiple_of(edge - low, chans), size), :]
    at = size
    for col in cols:
        count = col.shape[0] * TILE // span
        for t, part in enumerate(tiles_of(span)):
            block = col[t * count : (t + 1) * count]
            msg_a[at : at + count, part] = block
            msg_b[at : at + count, part] = block
        at += count


def corner_views(msg, size, cols):
    span = msg.shape[1]
    views, at = [], size
    for col in cols:
        count = col.shape[0] * TILE // span
        views.append(
            jnp.concatenate([msg[at : at + count, part] for part in tiles_of(span)], axis=0)
        )
        at += count
    return views


def halo_block(sources, k, chans, kind):
    rows = sources[0].shape[0] // chans
    lane = lanes_of((chans * rows, TILE))
    total = jnp.zeros((chans * rows, TILE), F32)
    if kind == "features":
        count, shift_r, shift_l = FHALO, -k * SLOT, TILE - (k + 1) * SLOT
    else:
        count, shift_r, shift_l = CHALO, -k * SLOT - FHALO, TILE - (k + 1) * SLOT + FHALO
    for index, source in enumerate(sources):
        from_right = is_even("cols") if index == 0 else jnp.logical_not(is_even("cols"))
        moved = turn(
            source.astype(F32), jnp.where(from_right, shift_r % TILE, shift_l % TILE)
        )
        total = jnp.where(
            jnp.where(from_right, lane, TILE - 1 - lane) < count, moved, total
        )
    return total.astype(BF16).reshape(chans, rows, TILE)


def columns_seen(shape, span):
    _, _, has_left, has_right = has_sides()
    lane = lanes_of(shape)
    middle = span + TILE // 2
    return (lane < span) | ((lane < middle) & has_right) | ((lane >= middle) & has_left)


def block_ones(width):
    row = lax.broadcasted_iota(jnp.int32, (width, width), 0) // POOL
    col = lax.broadcasted_iota(jnp.int32, (width, width), 1) // POOL
    return jnp.where(row == col, 1.0, 0.0).astype(BF16)


def store_split(high, low, at, total):
    top = total.astype(BF16)
    high[at, :] = top
    low[at, :] = (total - top.astype(F32)).astype(BF16)


def block_sums(high, low, ones):
    return jnp.dot(high[...], ones, preferred_element_type=F32) + jnp.dot(
        low[...], ones, preferred_element_type=F32
    )


def fill_bands(out, kernel, count):
    chans = kernel.shape[1]
    out[...] = jnp.zeros(out.shape, out.dtype)
    for k in range(count):
        for b in range(3):
            for a in range(3):
                at = (b * (count + 2) + k + a) * chans
                out[k * chans : (k + 1) * chans, at : at + chans] = kernel[3 * a + b].astype(
                    out.dtype
                )


def fill_turned_bands(out, kernel, count):
    chans = kernel.shape[1]
    out[...] = jnp.zeros(out.shape, out.dtype)
    for k in range(count):
        for b in range(3):
            for a in range(3):
                at = (b * (count + 2) + k + a) * chans
                out[at : at + chans, k * chans : (k + 1) * chans] = kernel[8 - 3 * a - b].astype(
                    out.dtype
                )


def stacked(views, at):
    return jnp.concatenate([view[at, :] for view in views], axis=0)


def conv_sum(parts, chans, step):
    return (
        turn(parts[0:chans], step)
        + parts[chans : 2 * chans]
        + turn(parts[2 * chans : 3 * chans], -step)
    )


def back_kernel(
    ncols, cot, msg_a, msg_b, *rest,
):
    cols, (
        first, bottle, second,
        act_grad, view_m, view_0, view_p, sides, first_bands, bottle_bands, second_bands,
        cot_m, cot_0, cot_p, back, high, low, coarse, bands_f, bands, small_f, small, wide_f,
    ) = rest[:ncols], rest[ncols:]
    chans = second.shape[1]
    full, span = cot.shape
    height = full // chans
    width = span + TILE
    groups = height // POOL
    has_up, has_down, _, _ = has_sides()
    seen_cols = columns_seen((chans, width), span)

    fill_turned_bands(bands_f, second, POOL)
    bands[...] = bands_f[...].T.astype(BF16)
    fill_turned_bands(small_f, bottle, 1)
    small_t = small_f[...].T
    for b in range(3):
        small[rows_at(b, chans)] = small_t[0:chans, 3 * b * chans : 3 * (b + 1) * chans].astype(BF16)
    fill_bands(first_bands, first, POOL)
    fill_bands(wide_f, bottle, 1)
    for b in range(3):
        bottle_bands[rows_at(b, chans)] = wide_f[
            0:chans, 3 * b * chans : 3 * (b + 1) * chans
        ].astype(BF16)
    second_bands[...] = jnp.zeros(second_bands.shape, BF16)
    for k in range(POOL):
        for b in range(3):
            for a in range(3):
                second_bands[
                    rows_at(3 * k + b, chans), (k + a) * chans : (k + a + 1) * chans
                ] = second[3 * a + b]

    size = CHALO * chans
    count = TILE // SLOT
    block = height // count

    def halo_columns(sources, at):
        for k in range(count):
            sides[:, at + k * block : at + (k + 1) * block, :] = halo_block(
                sources, k, chans, "features"
            )

    halo_columns([c[...] for c in cols], height)
    cot_0[rows_at(CHALO, chans, height), 0:span] = cot[...]
    for k in range(count):
        cot_0[rows_at(CHALO + k * block, chans, block), span:width] = to_rows(
            halo_block([c[...] for c in cols], k, chans, "cotangent")
        )

    def vertical(up, down):
        cot_0[rows_at(0, chans, CHALO), 0:span] = up[0:size]
        cot_0[rows_at(CHALO + height, chans, CHALO), 0:span] = down[0:size]
        corner = to_rows(
            halo_block(corner_views(up, size, cols), count - 1, chans, "cotangent")
        )
        cot_0[rows_at(0, chans, CHALO), span:width] = corner[(block - CHALO) * chans :]
        corner = to_rows(halo_block(corner_views(down, size, cols), 0, chans, "cotangent"))
        cot_0[rows_at(CHALO + height, chans, CHALO), span:width] = corner[0:size]
        halo_columns(corner_views(up, size, cols), 0)
        halo_columns(corner_views(down, size, cols), 2 * height)

    pl.when(is_even("rows"))(lambda: vertical(msg_b, msg_a))
    pl.when(jnp.logical_not(is_even("rows")))(lambda: vertical(msg_a, msg_b))
    for j in range(height + 2 * CHALO):
        at = rows_at(j, chans)
        cot_m[at] = turn(cot_0[at], 1)
        cot_p[at] = turn(cot_0[at], -1)
    inner = rows_at(CHALO - 1, chans, height + 2)
    view_m[...] = cot_m[inner, 0:span]
    view_0[...] = cot_0[inner, 0:span]
    view_p[...] = cot_p[inner, 0:span]

    def group(g, _):
        at = rows_at(g * POOL, chans, POOL + 2)
        rows = jnp.dot(
            bands[...], stacked((cot_m, cot_0, cot_p), at), preferred_element_type=F32
        ).astype(BF16)
        back[rows_at(g * POOL, chans, POOL), :] = rows[:, 0:span]
        rows = rows.astype(F32)
        total = rows[0:chans]
        for k in range(1, POOL):
            total = total + rows[k * chans : (k + 1) * chans]
        store_split(high, low, rows_at(g, chans), total)
        return 0

    lax.fori_loop(0, groups + 2, group, 0, unroll=2)
    sums = block_sums(high, low, block_ones(width))
    for g in range(groups + 2):
        at = rows_at(g, chans)
        seen = seen_cols
        if g == 0:
            seen = seen & has_up
        elif g == groups + 1:
            seen = seen & has_down
        coarse[at] = jnp.where(seen, sums[at], 0.0).astype(BF16)
    for g in range(groups):
        parts = jnp.dot(small[...], coarse[rows_at(g, chans, 3), :], preferred_element_type=F32)
        mean = conv_sum(parts, chans, POOL)[:, 0:span] * (1.0 / POOL**2)
        for k in range(POOL):
            r = g * POOL + k
            act_grad[rows_at(r, chans), :] = back[rows_at(r + POOL, chans), :].astype(F32) + mean


def correlate(u, u0, views, v0, acc, height, chans, span):
    acc[...] = jnp.zeros(acc.shape, F32)

    def group(g, _):
        left = jnp.concatenate(
            [view[rows_at(v0 + g * POOL, chans, POOL + 2), 0:span] for view in views], axis=0
        )
        right = u[rows_at(u0 + g * POOL, chans, POOL), 0:span]
        acc[...] += lax.dot_general(
            left, right, (((1,), (1,)), ((), ())), preferred_element_type=F32
        )
        return 0

    lax.fori_loop(0, height // POOL, group, 0, unroll=2)


def folded(acc, chans):
    lane = lanes_of((3 * chans, TILE))
    result = jnp.zeros((3 * chans, TILE), F32)
    for b in range(3):
        total = None
        for k in range(POOL):
            block = turn(
                acc[rows_at(b * (POOL + 2) + k, chans, 3), 0:TILE], (b - k) * chans
            )
            total = block if total is None else total + block
        result = jnp.where((lane >= b * chans) & (lane < (b + 1) * chans), total, result)
    return result


def main_kernel(
    shifts, feat, feat_a, feat_b, sides, act_grad, view_m, view_0, view_p, bands, small,
    grads, blended,
    lent, moved, warp_m, warp_0, warp_p, act, high, low, pooled, pre_grad, acc,
):
    chans, height, span = feat.shape
    tiles = span // TILE
    width = span + TILE
    groups = height // POOL
    has_up, has_down, has_left, has_right = has_sides()
    seen_cols = columns_seen((chans, width), span)

    size = feat_a.shape[0]
    window = lent.shape[1] - size
    lent[:, size:, :] = jnp.zeros((2, window, span), BF16)

    def borrow(up, down):
        lent[0, 0:size] = up[...]
        lent[1, 0:size] = down[...]

    pl.when(is_even("rows"))(lambda: borrow(feat_b, feat_a))
    pl.when(jnp.logical_not(is_even("rows")))(lambda: borrow(feat_a, feat_b))

    tall = moved.shape[1]
    lane = lanes_of((tall, TILE))
    seen_halo = ((lane < TILE // 2) & has_right) | ((lane >= TILE // 2) & has_left)
    step = lanes_of((tall, 3 * height)) - lax.broadcasted_iota(jnp.int32, (tall, 3 * height), 0)
    depth = 2 * window + height
    source = lanes_of((1, depth))
    apart = lax.broadcasted_iota(jnp.int32, (tall, depth), 0) - lanes_of((tall, depth))
    align = 16

    def warp(c, ats):
        at_up, at_down = ats
        shift, move = shifts[c, 0], shifts[c, 1]
        n_up, n_down = needed(shift, False), needed(shift, True)
        base_up, base_down = (
            pl.multiple_of(lax.div(at, align) * align, align) for at in (at_up, at_down)
        )
        skip_up, skip_down = at_up - base_up, at_down - base_down
        own = EXT - window - shift
        below = own - skip_down
        above = EXT - skip_up - n_up - shift
        in_up = (source >= skip_up) & (source < skip_up + n_up)
        first_down = window + height + skip_down
        in_down = (source >= first_down) & (source < first_down + n_down)
        none = 4 * depth
        offset = jnp.where(
            source < window,
            jnp.where(in_up, above, none),
            jnp.where(source < window + height, own, jnp.where(in_down, below, none)),
        )
        pick = jnp.where(apart == offset, 1.0, 0.0).astype(BF16)
        rows = jnp.concatenate(
            [lent[0, pl.ds(base_up, window), :], feat[c], lent[1, pl.ds(base_down, window), :]], axis=0
        )
        plane = jnp.dot(pick, rows, preferred_element_type=F32)
        pick = jnp.where(step == height - EXT + shift, 1.0, 0.0).astype(BF16)
        plane = [plane[:, part] for part in tiles_of(span)]
        plane.append(jnp.dot(pick, sides[c], preferred_element_type=F32))
        amount = jnp.where(move > 0, TILE - move, -move)
        parts = [turn(part, amount) for part in plane]
        inside = jnp.where(move > 0, lane, TILE - 1 - lane) < TILE - jnp.abs(move)
        for t, part in enumerate(tiles_of(width)):
            after, before = parts[(t + 1) % (tiles + 1)], parts[t - 1]
            result = jnp.where(inside, parts[t], jnp.where(move > 0, after, before))
            if t == tiles:
                result = jnp.where(seen_halo, result, 0.0)
            moved[c, :, part] = result.astype(BF16)
        return at_up + n_up, at_down + n_down

    lax.fori_loop(0, chans, warp, (jnp.int32(0), jnp.int32(0)), unroll=4)
    chunk = 16
    for r in range(0, tall, chunk):
        for part in tiles_of(width):
            warp_0[rows_at(r, chans, chunk), part] = to_rows(moved[:, r : r + chunk, part])

    def clear(r, count):
        warp_0[rows_at(r, chans, count)] = jnp.zeros((count * chans, width), BF16)

    pl.when(jnp.logical_not(has_up))(lambda: clear(0, EXT))
    pl.when(jnp.logical_not(has_down))(lambda: clear(EXT + height, EXT))
    for j in range(height + 2 * EXT):
        at = rows_at(j, chans)
        warp_m[at] = turn(warp_0[at], 1)
        warp_p[at] = turn(warp_0[at], -1)

    def first_group(g, own):
        at = rows_at(g * POOL, chans, POOL + 2)
        pre = jnp.dot(
            bands[...], stacked((warp_m, warp_0, warp_p), at), preferred_element_type=F32
        )
        sigma = 0.5 * jnp.tanh(0.5 * pre) + 0.5
        rows = (pre * sigma).astype(BF16)
        act[rows_at(g * POOL, chans, POOL), :] = rows
        rows = rows.astype(F32)
        total = rows[0:chans]
        for k in range(1, POOL):
            total = total + rows[k * chans : (k + 1) * chans]
        store_split(high, low, rows_at(g, chans), total)
        if own:
            there = rows_at(g * POOL - 2 * POOL, chans, POOL)
            pre, sigma = pre[:, 0:span], sigma[:, 0:span]
            pre_grad[there, :] = (
                act_grad[there, :] * (sigma * (1.0 + pre * (1.0 - sigma)))
            ).astype(BF16)
        return 0

    for g in (0, 1, groups + 2, groups + 3):
        first_group(g, False)
    lax.fori_loop(2, groups + 2, lambda g, _: first_group(g, True), 0, unroll=2)
    sums = block_sums(high, low, block_ones(width))
    for g in range(groups + 4):
        at = rows_at(g, chans)
        seen = seen_cols
        if g < 2:
            seen = seen & has_up
        elif g >= groups + 2:
            seen = seen & has_down
        pooled[at] = jnp.where(seen, sums[at] * (1.0 / POOL**2), 0.0).astype(BF16)

    for g in range(groups + 2):
        parts = jnp.dot(small[...], pooled[rows_at(g, chans, 3), :], preferred_element_type=F32)
        bottle_row = conv_sum(parts, chans, POOL)
        rows, seen = range(POOL), seen_cols
        if g == 0:
            rows, seen = (POOL - 1,), seen & has_up
        elif g == groups + 1:
            rows, seen = (0,), seen & has_down
        for k in rows:
            row = act[rows_at((g + 1) * POOL + k, chans), :].astype(F32) + bottle_row
            blended[rows_at(g * POOL + k - POOL + 1, chans), :] = jnp.where(seen, row, 0.0).astype(
                BF16
            )

    correlate(pre_grad, 0, (warp_m, warp_0, warp_p), EXT - 1, acc, height, chans, span)
    first_part = folded(acc, chans)
    correlate(blended, 1, (view_m, view_0, view_p), 0, acc, height, chans, span)
    second_part = folded(acc, chans)
    lane = lanes_of((3 * chans, TILE))
    grads[0 : 3 * chans] = jnp.where(lane < 3 * chans, first_part, turn(second_part, 3 * chans))
    half = 3 * chans // 2
    grads[3 * chans :] = jnp.where(
        lane[0:half] < TILE // 2,
        turn(second_part[0:half], -chans),
        turn(second_part[half:], TILE // 2 - chans),
    )


def predict_kernel(part, blended, bands, *rest):
    out, rows = rest[-2:]
    chans, height, span = out.shape

    def group(g, _):
        at = rows_at(part * height + g * POOL, chans, POOL + 2)
        parts = jnp.dot(bands[...], blended[at, :], preferred_element_type=F32)
        for k in range(POOL):
            row = conv_sum(parts[3 * k * chans : 3 * (k + 1) * chans], chans, 1)
            rows[rows_at(g * POOL + k, chans), :] = row[:, 0:span].astype(BF16)
        return 0

    lax.fori_loop(0, height // POOL, group, 0, unroll=2)
    for part in tiles_of(span):
        out[:, :, part] = to_planes(rows[:, part], chans)


def final_kernel(factor, mine, other, first, second):
    chans = first.shape[1]
    total = (mine[...] + other[...]) * factor
    turned = total[0 : 3 * chans].T
    for b in range(3):
        for a in range(3):
            first[3 * a + b] = turned[b * chans : (b + 1) * chans, a * chans : (a + 1) * chans]
    half = 3 * chans // 2
    low = total[3 * chans :]
    both = jnp.concatenate([low, turn(low, -(TILE // 2))], axis=0)
    for a in range(3):
        at = slice((2 - a) * chans, (3 - a) * chans)
        second[3 * a + 2] = turn(total[at], -3 * chans)[:, 0:chans]
        second[3 * a + 1] = both[at, 0:chans]
        second[3 * a + 0] = turn(both[at], -chans)[:, 0:chans]


def call(kernel, outs, scratch, n_in, limit, flops=0, smem_first=False, **more):
    specs = [VMEM] * n_in
    if smem_first:
        specs[0] = SMEM
    more.setdefault("in_specs", specs)
    more.setdefault("out_specs", jax.tree.map(lambda _: VMEM, outs))
    return pl.pallas_call(
        kernel,
        out_shape=outs,
        scratch_shapes=scratch,
        compiler_params=pltpu.CompilerParams(vmem_limit_bytes=limit * MIB),
        cost_estimate=pl.CostEstimate(flops=flops, bytes_accessed=4 * MIB, transcendentals=0),
        **more,
    )


def predict(blended, bands, shape, parts, part, before):
    chans, height, span = shape
    rows = height // parts
    block = pl.BlockSpec((chans, rows, span), lambda i: (0, part, 0))
    whole = lambda a: pl.BlockSpec(a.shape, lambda i: (0,) * a.ndim)
    args = (blended, bands)
    specs = [whole(a) for a in args]
    more = {}
    if before is not None:
        args += (before,)
        specs.append(pl.BlockSpec(memory_space=pl.ANY))
        more["input_output_aliases"] = {2: 0}
    return call(
        functools.partial(predict_kernel, part),
        jax.ShapeDtypeStruct(shape, BF16),
        [
            pltpu.VMEM((chans * rows, span), BF16),
        ],
        len(args),
        12,
        flops=10**9,
        grid=(1,),
        in_specs=specs,
        out_specs=block,
        **more,
    )(*args)


def bf(*shape):
    return jax.ShapeDtypeStruct(shape, BF16)


def swapped(messages, axis):
    pairs = [p for p in swaps(lax.axis_size(axis)) if p]
    return [lax.ppermute(m, axis, p) for m, p in zip(messages, pairs)]


def both_passes(size, feat, shifts, cot_rows, col_msgs, first_kernel, bottle_kernel, second_kernel):
    chans, height, span = feat.shape
    width = span + TILE
    full = height * chans
    groups = height // POOL
    ncols = len(col_msgs)
    packed = col_msgs[0].shape[0]

    halo = bf(CHALO * chans + ncols * packed * TILE // span, span)
    messages = call(edge_kernel, (halo, halo), [], 1 + ncols, 8)(cot_rows, *col_msgs)
    row_msgs = swapped(messages, "rows")
    messages = call(
        feature_kernel, (bf(size, span), bf(size, span)), [], 2, 16, smem_first=True
    )(shifts, feat)
    feat_msgs = swapped(messages, "rows")

    tall_c = (height + 2 * CHALO) * chans
    view = bf((height + 2) * chans, span)
    band = 3 * (POOL + 2) * chans
    act_grad, *rest = call(
        functools.partial(back_kernel, ncols),
        (
            jax.ShapeDtypeStruct((full, span), F32), view, view, view,
            bf(chans, 3 * height, TILE), bf(POOL * chans, band), bf(3 * chans, 3 * chans),
            bf(3 * POOL * chans, (POOL + 2) * chans),
        ),
        [pltpu.VMEM((tall_c, width), BF16)] * 3
        + [pltpu.VMEM(((height + 2 * POOL) * chans, span), BF16)]
        + [pltpu.VMEM(((groups + 2) * chans, width), BF16)] * 3
        + [
            pltpu.VMEM((band, POOL * chans), F32),
            pltpu.VMEM((POOL * chans, band), BF16),
            pltpu.VMEM((9 * chans, TILE), F32),
            pltpu.VMEM((3 * chans, 3 * chans), BF16),
            pltpu.VMEM((chans, 9 * chans), F32),
        ],
        6 + ncols,
        16,
        flops=8 * 10**9,
    )(cot_rows, *row_msgs, *col_msgs, first_kernel, bottle_kernel, second_kernel)
    views, sides, weights = rest[:3], rest[3], rest[4:]

    tall = pl.cdiv(height + 2 * EXT, 16) * 16
    grads, blended = call(
        main_kernel,
        (jax.ShapeDtypeStruct((9 * chans // 2, TILE), F32), bf((height + 2) * chans, width)),
        [
            pltpu.VMEM((2, size + 48, span), BF16),
            pltpu.VMEM((chans, tall, width), BF16),
        ]
        + [pltpu.VMEM((tall * chans, width), BF16)] * 3
        + [pltpu.VMEM(((height + 4 * POOL) * chans, width), BF16)]
        + [pltpu.VMEM(((groups + 4) * chans, width), BF16)] * 3
        + [
            pltpu.VMEM((full, span), BF16),
            pltpu.VMEM((band, POOL * chans), F32),
        ],
        11,
        32,
        flops=10**10,
        smem_first=True,
    )(
        shifts, feat, *feat_msgs, sides, act_grad, *views, *weights[:2]
    )

    return grads, blended, weights[2]


def shards(features, shifts, first_kernel, bottle_kernel, second_kernel, cotangent):
    imgs, chans, height, span = features.shape
    rows, cols, dp = (lax.axis_size(a) for a in ("rows", "cols", "dp"))
    full = height * chans

    packed = chans * (height * SLOT // TILE)
    cot_rows, *messages = call(
        column_kernel,
        (bf(full, span),) + (bf(packed, TILE),) * (1 if cols == 2 else 2),
        [],
        2,
        8,
    )(features[0], cotangent[0])
    col_msgs = swapped(messages, "cols")
    ncols = len(col_msgs)
    moves = shifts[0, :, 0]
    total = jnp.maximum(jnp.sum(needed(moves, False)), jnp.sum(needed(moves, True)))
    bit = 1
    while bit < dp:
        total = jnp.maximum(total, lax.ppermute(total, "dp", [(i, i ^ bit) for i in range(dp)]))
        bit *= 2

    def passes(size):
        return functools.partial(both_passes, size)

    grads, blended, second_bands = lax.cond(
        total <= USUAL * chans,
        passes(USUAL * chans),
        passes(LARGEST * chans),
        features[0], shifts[0], cot_rows, tuple(col_msgs), first_kernel, bottle_kernel, second_kernel,
    )

    everyone = ("rows", "cols", "dp")
    devices = rows * cols * dp
    pieces = lax.all_to_all(
        jnp.pad(grads, ((0, 8 * devices - grads.shape[0]), (0, 0))).reshape(devices, 8, TILE),
        everyone, 0, 0,
    )
    total = jnp.sum(pieces, axis=0)
    pieces = lax.all_to_all(jnp.broadcast_to(total, pieces.shape), everyone, 0, 0)
    grads = pieces.reshape(8 * devices, TILE)[: grads.shape[0]]
    other = jnp.zeros_like(grads)
    prediction = None
    for step in range(2):
        prediction = predict(blended, second_bands, (chans, height, span), 2, step, prediction)
    factor = 1.0 / math.sqrt(imgs * dp * height * rows * span * cols)
    shape = jax.ShapeDtypeStruct((9, chans, chans), F32)
    first_grad, second_grad = call(
        functools.partial(final_kernel, factor), (shape, shape), [], 2, 2
    )(grads, other)
    return (prediction[None], first_grad, second_grad)


def solution(mesh):
    placed = (
        P("dp", None, "rows", "cols"),
        P("dp", None, None),
        P(),
        P(),
        P(),
        P("dp", None, "rows", "cols"),
    )
    return jax.shard_map(
        shards,
        mesh=mesh,
        in_specs=placed,
        out_specs=(P("dp", None, "rows", "cols"), P(), P()),
        check_vma=False,
    )
```

```python
import functools
import math

import jax
import jax.numpy as jnp
from jax import lax
from jax.experimental import pallas as pl
from jax.experimental.pallas import tpu as pltpu
from jax.sharding import PartitionSpec as P


MAXSHIFT = 16
POOL = 4
TILE = 128
SLOT = 32
EXT = 9
FHALO = MAXSHIFT + EXT
USUAL = 14
LARGEST = FHALO + 1
CHALO = 5
F32 = jnp.float32
BF16 = jnp.bfloat16
VMEM = pl.BlockSpec(memory_space=pltpu.VMEM)
SMEM = pl.BlockSpec(memory_space=pltpu.SMEM)
MIB = 1024 * 1024


def lanes_of(shape):
    return lax.broadcasted_iota(jnp.int32, shape, len(shape) - 1)


def turn(values, shift):
    width = values.shape[-1]
    if isinstance(shift, int):
        shift = shift % width
        if shift == 0:
            return values
    return pltpu.roll(values, shift, values.ndim - 1)


def has_sides():
    row, col = lax.axis_index("rows"), lax.axis_index("cols")
    return (
        row > 0,
        row < lax.axis_size("rows") - 1,
        col > 0,
        col < lax.axis_size("cols") - 1,
    )


def rows_at(r, chans, count=1):
    if isinstance(r, int):
        return slice(r * chans, (r + count) * chans)
    return pl.ds(pl.multiple_of(r * chans, chans), count * chans)


def to_rows(block):
    chans, height, span = block.shape
    return jnp.transpose(block, (1, 0, 2)).reshape(height * chans, span)


def to_planes(block, chans):
    height = block.shape[0] // chans
    return jnp.transpose(block.reshape(height, chans, block.shape[1]), (1, 0, 2))


def tiles_of(span):
    return [slice(t, t + TILE) for t in range(0, span, TILE)]


def is_even(axis):
    return lax.rem(lax.axis_index(axis), 2) == 0


def swaps(size):
    first = [(i, i ^ 1) for i in range(size)]
    second = [(i, i + 1) for i in range(1, size - 1, 2)]
    return [first, second + [(j, i) for i, j in second]]


def needed(shift, below):
    return jnp.maximum(EXT + shift if below else EXT - shift, 0)


def feature_kernel(shifts, feat, msg_a, msg_b):
    chans, height, span = feat.shape
    full = chans * height
    size = msg_a.shape[0]
    chunk = size // 4
    source = feat[...].reshape(full, span)
    lane = lanes_of((8, full))
    chan, row = lane // height, lane % height
    for msg, to_below in ((msg_a, is_even("rows")), (msg_b, jnp.logical_not(is_even("rows")))):
        target = jnp.full((8, full), -1, jnp.int32)
        at = jnp.int32(0)
        for c in range(chans):
            shift = shifts[c, 0]
            count = jnp.where(to_below, needed(shift, False), needed(shift, True))
            first = jnp.where(to_below, height - count, 0)
            mine = (chan == c) & (row >= first) & (row < first + count)
            target = jnp.where(mine, row + (at - first), target)
            at = at + count
        for p in range(0, size, chunk):
            place = lax.broadcasted_iota(jnp.int32, (chunk, full), 0) + p
            pick = jnp.where(place == target[0:1], 1.0, 0.0).astype(BF16)
            msg[p : p + chunk] = jnp.dot(pick, source, preferred_element_type=F32).astype(BF16)


def rows_kernel(source, out):
    for part in tiles_of(source.shape[2]):
        out[:, part] = to_rows(source[:, :, part])


def count_kernel(shifts, out):
    down = up = jnp.int32(0)
    for c in range(shifts.shape[0]):
        up = up + needed(shifts[c, 0], False)
        down = down + needed(shifts[c, 0], True)
    out[...] = jnp.full(out.shape, jnp.maximum(up, down), jnp.int32)


def column_kernel(feat, cot, *col_msgs):
    chans, height, span = feat.shape
    first, last = tiles_of(span)[0], tiles_of(span)[-1]
    count = TILE // SLOT
    block = height // count
    lane = lanes_of((chans, block, TILE))
    for index, msg in enumerate(col_msgs):
        sends_right = is_even("cols") if index == 0 else jnp.logical_not(is_even("cols"))
        total = jnp.zeros((chans, block, TILE), F32)
        inner = jnp.where(sends_right, TILE - 1 - lane, lane) < FHALO
        for k in range(count):
            at = slice(k * block, (k + 1) * block)
            feats = jnp.where(sends_right, feat[:, at, last].astype(F32), feat[:, at, first].astype(F32))
            cots = jnp.where(sends_right, cot[:, at, last].astype(F32), cot[:, at, first].astype(F32))
            cots = turn(cots, jnp.where(sends_right, TILE - FHALO, FHALO))
            piece = jnp.where(inner, feats, cots)
            piece = turn(piece, jnp.where(sends_right, (k + 1) * SLOT % TILE, k * SLOT))
            inside = (lane >= k * SLOT) & (lane < (k + 1) * SLOT)
            total = jnp.where(inside, piece, total)
        msg[...] = total.reshape(chans * block, TILE).astype(BF16)


def edge_kernel(cot_rows, *rest):
    cols, (msg_a, msg_b) = rest[:-2], rest[-2:]
    span = cot_rows.shape[1]
    size = msg_a.shape[0] - sum(c.shape[0] * TILE // span for c in cols)
    edge = cot_rows.shape[0] - size
    chans = size // CHALO
    low = jnp.where(is_even("rows"), edge, 0)
    msg_a[0:size] = cot_rows[pl.ds(pl.multiple_of(low, chans), size), :]
    msg_b[0:size] = cot_rows[pl.ds(pl.multiple_of(edge - low, chans), size), :]
    at = size
    for col in cols:
        count = col.shape[0] * TILE // span
        for t, part in enumerate(tiles_of(span)):
            block = col[t * count : (t + 1) * count]
            msg_a[at : at + count, part] = block
            msg_b[at : at + count, part] = block
        at += count


def corner_views(msg, size, cols):
    span = msg.shape[1]
    views, at = [], size
    for col in cols:
        count = col.shape[0] * TILE // span
        views.append(
            jnp.concatenate([msg[at : at + count, part] for part in tiles_of(span)], axis=0)
        )
        at += count
    return views


def halo_block(sources, k, chans, kind):
    rows = sources[0].shape[0] // chans
    lane = lanes_of((chans * rows, TILE))
    total = jnp.zeros((chans * rows, TILE), F32)
    if kind == "features":
        count, shift_r, shift_l = FHALO, -k * SLOT, TILE - (k + 1) * SLOT
    else:
        count, shift_r, shift_l = CHALO, -k * SLOT - FHALO, TILE - (k + 1) * SLOT + FHALO
    for index, source in enumerate(sources):
        from_right = is_even("cols") if index == 0 else jnp.logical_not(is_even("cols"))
        moved = turn(
            source.astype(F32), jnp.where(from_right, shift_r % TILE, shift_l % TILE)
        )
        total = jnp.where(
            jnp.where(from_right, lane, TILE - 1 - lane) < count, moved, total
        )
    return total.astype(BF16).reshape(chans, rows, TILE)


def columns_seen(shape, span):
    _, _, has_left, has_right = has_sides()
    lane = lanes_of(shape)
    middle = span + TILE // 2
    return (lane < span) | ((lane < middle) & has_right) | ((lane >= middle) & has_left)


def block_ones(width):
    row = lax.broadcasted_iota(jnp.int32, (width, width), 0) // POOL
    col = lax.broadcasted_iota(jnp.int32, (width, width), 1) // POOL
    return jnp.where(row == col, 1.0, 0.0).astype(BF16)


def store_split(high, low, at, total):
    top = total.astype(BF16)
    high[at, :] = top
    low[at, :] = (total - top.astype(F32)).astype(BF16)


def block_sums(high, low, ones):
    return jnp.dot(high[...], ones, preferred_element_type=F32) + jnp.dot(
        low[...], ones, preferred_element_type=F32
    )


def fill_bands(out, kernel, count):
    chans = kernel.shape[1]
    out[...] = jnp.zeros(out.shape, out.dtype)
    for k in range(count):
        for b in range(3):
            for a in range(3):
                at = (b * (count + 2) + k + a) * chans
                out[k * chans : (k + 1) * chans, at : at + chans] = kernel[3 * a + b].astype(
                    out.dtype
                )


def fill_turned_bands(out, kernel, count):
    chans = kernel.shape[1]
    out[...] = jnp.zeros(out.shape, out.dtype)
    for k in range(count):
        for b in range(3):
            for a in range(3):
                at = (b * (count + 2) + k + a) * chans
                out[at : at + chans, k * chans : (k + 1) * chans] = kernel[8 - 3 * a - b].astype(
                    out.dtype
                )


def stacked(views, at):
    return jnp.concatenate([view[at, :] for view in views], axis=0)


def conv_sum(parts, chans, step):
    return (
        turn(parts[0:chans], step)
        + parts[chans : 2 * chans]
        + turn(parts[2 * chans : 3 * chans], -step)
    )


def back_kernel(
    ncols, cot, msg_a, msg_b, *rest,
):
    cols, (
        first, bottle, second,
        act_grad, view_m, view_0, view_p, sides, first_bands, bottle_bands, second_bands,
        cot_m, cot_0, cot_p, back, high, low, coarse, bands_f, bands, small_f, small, wide_f,
    ) = rest[:ncols], rest[ncols:]
    chans = second.shape[1]
    full, span = cot.shape
    height = full // chans
    width = span + TILE
    groups = height // POOL
    has_up, has_down, _, _ = has_sides()
    seen_cols = columns_seen((chans, width), span)

    fill_turned_bands(bands_f, second, POOL)
    bands[...] = bands_f[...].T.astype(BF16)
    fill_turned_bands(small_f, bottle, 1)
    small_t = small_f[...].T
    for b in range(3):
        small[rows_at(b, chans)] = small_t[0:chans, 3 * b * chans : 3 * (b + 1) * chans].astype(BF16)
    fill_bands(first_bands, first, POOL)
    fill_bands(wide_f, bottle, 1)
    for b in range(3):
        bottle_bands[rows_at(b, chans)] = wide_f[
            0:chans, 3 * b * chans : 3 * (b + 1) * chans
        ].astype(BF16)
    second_bands[...] = jnp.zeros(second_bands.shape, BF16)
    for k in range(POOL):
        for b in range(3):
            for a in range(3):
                second_bands[
                    rows_at(3 * k + b, chans), (k + a) * chans : (k + a + 1) * chans
                ] = second[3 * a + b]

    size = CHALO * chans
    count = TILE // SLOT
    block = height // count

    def halo_columns(sources, at):
        for k in range(count):
            sides[:, at + k * block : at + (k + 1) * block, :] = halo_block(
                sources, k, chans, "features"
            )

    halo_columns([c[...] for c in cols], height)
    cot_0[rows_at(CHALO, chans, height), 0:span] = cot[...]
    for k in range(count):
        cot_0[rows_at(CHALO + k * block, chans, block), span:width] = to_rows(
            halo_block([c[...] for c in cols], k, chans, "cotangent")
        )

    def vertical(up, down):
        cot_0[rows_at(0, chans, CHALO), 0:span] = up[0:size]
        cot_0[rows_at(CHALO + height, chans, CHALO), 0:span] = down[0:size]
        corner = to_rows(
            halo_block(corner_views(up, size, cols), count - 1, chans, "cotangent")
        )
        cot_0[rows_at(0, chans, CHALO), span:width] = corner[(block - CHALO) * chans :]
        corner = to_rows(halo_block(corner_views(down, size, cols), 0, chans, "cotangent"))
        cot_0[rows_at(CHALO + height, chans, CHALO), span:width] = corner[0:size]
        halo_columns(corner_views(up, size, cols), 0)
        halo_columns(corner_views(down, size, cols), 2 * height)

    pl.when(is_even("rows"))(lambda: vertical(msg_b, msg_a))
    pl.when(jnp.logical_not(is_even("rows")))(lambda: vertical(msg_a, msg_b))
    for j in range(height + 2 * CHALO):
        at = rows_at(j, chans)
        cot_m[at] = turn(cot_0[at], 1)
        cot_p[at] = turn(cot_0[at], -1)
    inner = rows_at(CHALO - 1, chans, height + 2)
    view_m[...] = cot_m[inner, 0:span]
    view_0[...] = cot_0[inner, 0:span]
    view_p[...] = cot_p[inner, 0:span]

    def group(g, _):
        at = rows_at(g * POOL, chans, POOL + 2)
        rows = jnp.dot(
            bands[...], stacked((cot_m, cot_0, cot_p), at), preferred_element_type=F32
        ).astype(BF16)
        back[rows_at(g * POOL, chans, POOL), :] = rows[:, 0:span]
        rows = rows.astype(F32)
        total = rows[0:chans]
        for k in range(1, POOL):
            total = total + rows[k * chans : (k + 1) * chans]
        store_split(high, low, rows_at(g, chans), total)
        return 0

    lax.fori_loop(0, groups + 2, group, 0, unroll=2)
    sums = block_sums(high, low, block_ones(width))
    for g in range(groups + 2):
        at = rows_at(g, chans)
        seen = seen_cols
        if g == 0:
            seen = seen & has_up
        elif g == groups + 1:
            seen = seen & has_down
        coarse[at] = jnp.where(seen, sums[at], 0.0).astype(BF16)
    for g in range(groups):
        parts = jnp.dot(small[...], coarse[rows_at(g, chans, 3), :], preferred_element_type=F32)
        mean = conv_sum(parts, chans, POOL)[:, 0:span] * (1.0 / POOL**2)
        for k in range(POOL):
            r = g * POOL + k
            act_grad[rows_at(r, chans), :] = back[rows_at(r + POOL, chans), :].astype(F32) + mean


def correlate(u, u0, views, v0, acc, height, chans, span):
    groups = range(0, height, POOL)
    left = jnp.concatenate(
        [
            jnp.concatenate(
                [view[rows_at(v0 + g, chans, POOL + 2), 0:span] for view in views], axis=0
            )
            for g in groups
        ],
        axis=1,
    )
    right = jnp.concatenate([u[rows_at(u0 + g, chans, POOL), 0:span] for g in groups], axis=1)
    acc[...] = lax.dot_general(
        left, right, (((1,), (1,)), ((), ())), preferred_element_type=F32
    )


def folded(acc, chans):
    lane = lanes_of((3 * chans, TILE))
    result = jnp.zeros((3 * chans, TILE), F32)
    for b in range(3):
        total = None
        for k in range(POOL):
            block = turn(
                acc[rows_at(b * (POOL + 2) + k, chans, 3), 0:TILE], (b - k) * chans
            )
            total = block if total is None else total + block
        result = jnp.where((lane >= b * chans) & (lane < (b + 1) * chans), total, result)
    return result


def main_kernel(
    shifts, feat, feat_a, feat_b, sides, act_grad, view_m, view_0, view_p, bands, small,
    grads, blended,
    lent, moved, warp_m, warp_0, warp_p, act, high, low, pooled, pre_grad, acc,
):
    chans, height, span = feat.shape
    tiles = span // TILE
    width = span + TILE
    groups = height // POOL
    has_up, has_down, has_left, has_right = has_sides()
    seen_cols = columns_seen((chans, width), span)

    size = feat_a.shape[0]
    window = lent.shape[1] - size
    lent[:, size:, :] = jnp.zeros((2, window, span), BF16)

    def borrow(up, down):
        lent[0, 0:size] = up[...]
        lent[1, 0:size] = down[...]

    pl.when(is_even("rows"))(lambda: borrow(feat_b, feat_a))
    pl.when(jnp.logical_not(is_even("rows")))(lambda: borrow(feat_a, feat_b))

    tall = moved.shape[1]
    lane = lanes_of((tall, TILE))
    seen_halo = ((lane < TILE // 2) & has_right) | ((lane >= TILE // 2) & has_left)
    step = lanes_of((tall, 3 * height)) - lax.broadcasted_iota(jnp.int32, (tall, 3 * height), 0)
    depth = 2 * window + height
    source = lanes_of((1, depth))
    apart = lax.broadcasted_iota(jnp.int32, (tall, depth), 0) - lanes_of((tall, depth))
    align = 16

    def warp(c, ats):
        at_up, at_down = ats
        shift, move = shifts[c, 0], shifts[c, 1]
        n_up, n_down = needed(shift, False), needed(shift, True)
        base_up, base_down = (
            pl.multiple_of(lax.div(at, align) * align, align) for at in (at_up, at_down)
        )
        skip_up, skip_down = at_up - base_up, at_down - base_down
        own = EXT - window - shift
        below = own - skip_down
        above = EXT - skip_up - n_up - shift
        in_up = (source >= skip_up) & (source < skip_up + n_up)
        first_down = window + height + skip_down
        in_down = (source >= first_down) & (source < first_down + n_down)
        none = 4 * depth
        offset = jnp.where(
            source < window,
            jnp.where(in_up, above, none),
            jnp.where(source < window + height, own, jnp.where(in_down, below, none)),
        )
        pick = jnp.where(apart == offset, 1.0, 0.0).astype(BF16)
        rows = jnp.concatenate(
            [lent[0, pl.ds(base_up, window), :], feat[c], lent[1, pl.ds(base_down, window), :]], axis=0
        )
        plane = jnp.dot(pick, rows, preferred_element_type=F32)
        pick = jnp.where(step == height - EXT + shift, 1.0, 0.0).astype(BF16)
        plane = [plane[:, part] for part in tiles_of(span)]
        plane.append(jnp.dot(pick, sides[c], preferred_element_type=F32))
        amount = jnp.where(move > 0, TILE - move, -move)
        parts = [turn(part, amount) for part in plane]
        inside = jnp.where(move > 0, lane, TILE - 1 - lane) < TILE - jnp.abs(move)
        for t, part in enumerate(tiles_of(width)):
            after, before = parts[(t + 1) % (tiles + 1)], parts[t - 1]
            result = jnp.where(inside, parts[t], jnp.where(move > 0, after, before))
            if t == tiles:
                result = jnp.where(seen_halo, result, 0.0)
            moved[c, :, part] = result.astype(BF16)
        return at_up + n_up, at_down + n_down

    lax.fori_loop(0, chans, warp, (jnp.int32(0), jnp.int32(0)), unroll=8)
    chunk = 16
    for r in range(0, tall, chunk):
        for part in tiles_of(width):
            warp_0[rows_at(r, chans, chunk), part] = to_rows(moved[:, r : r + chunk, part])

    def clear(r, count):
        warp_0[rows_at(r, chans, count)] = jnp.zeros((count * chans, width), BF16)

    pl.when(jnp.logical_not(has_up))(lambda: clear(0, EXT))
    pl.when(jnp.logical_not(has_down))(lambda: clear(EXT + height, EXT))
    for j in range(height + 2 * EXT):
        at = rows_at(j, chans)
        warp_m[at] = turn(warp_0[at], 1)
        warp_p[at] = turn(warp_0[at], -1)

    def first_group(g, own):
        at = rows_at(g * POOL, chans, POOL + 2)
        pre = jnp.dot(
            bands[...], stacked((warp_m, warp_0, warp_p), at), preferred_element_type=F32
        )
        sigma = 0.5 * jnp.tanh(0.5 * pre) + 0.5
        rows = (pre * sigma).astype(BF16)
        act[rows_at(g * POOL, chans, POOL), :] = rows
        rows = rows.astype(F32)
        total = rows[0:chans]
        for k in range(1, POOL):
            total = total + rows[k * chans : (k + 1) * chans]
        store_split(high, low, rows_at(g, chans), total)
        if own:
            there = rows_at(g * POOL - 2 * POOL, chans, POOL)
            pre, sigma = pre[:, 0:span], sigma[:, 0:span]
            pre_grad[there, :] = (
                act_grad[there, :] * (sigma * (1.0 + pre * (1.0 - sigma)))
            ).astype(BF16)
        return 0

    for g in (0, 1, groups + 2, groups + 3):
        first_group(g, False)
    lax.fori_loop(2, groups + 2, lambda g, _: first_group(g, True), 0, unroll=4)
    sums = block_sums(high, low, block_ones(width))
    for g in range(groups + 4):
        at = rows_at(g, chans)
        seen = seen_cols
        if g < 2:
            seen = seen & has_up
        elif g >= groups + 2:
            seen = seen & has_down
        pooled[at] = jnp.where(seen, sums[at] * (1.0 / POOL**2), 0.0).astype(BF16)

    for g in range(groups + 2):
        parts = jnp.dot(small[...], pooled[rows_at(g, chans, 3), :], preferred_element_type=F32)
        bottle_row = conv_sum(parts, chans, POOL)
        rows, seen = range(POOL), seen_cols
        if g == 0:
            rows, seen = (POOL - 1,), seen & has_up
        elif g == groups + 1:
            rows, seen = (0,), seen & has_down
        for k in rows:
            row = act[rows_at((g + 1) * POOL + k, chans), :].astype(F32) + bottle_row
            blended[rows_at(g * POOL + k - POOL + 1, chans), :] = jnp.where(seen, row, 0.0).astype(
                BF16
            )

    correlate(pre_grad, 0, (warp_m, warp_0, warp_p), EXT - 1, acc, height, chans, span)
    first_part = folded(acc, chans)
    correlate(blended, 1, (view_m, view_0, view_p), 0, acc, height, chans, span)
    second_part = folded(acc, chans)
    lane = lanes_of((3 * chans, TILE))
    grads[0 : 3 * chans] = jnp.where(lane < 3 * chans, first_part, turn(second_part, 3 * chans))
    half = 3 * chans // 2
    grads[3 * chans :] = jnp.where(
        lane[0:half] < TILE // 2,
        turn(second_part[0:half], -chans),
        turn(second_part[half:], TILE // 2 - chans),
    )


def predict_kernel(part, blended, bands, *rest):
    out, rows = rest[-2:]
    chans, height, span = out.shape

    def group(g, _):
        at = rows_at(part * height + g * POOL, chans, POOL + 2)
        parts = jnp.dot(bands[...], blended[at, :], preferred_element_type=F32)
        for k in range(POOL):
            row = conv_sum(parts[3 * k * chans : 3 * (k + 1) * chans], chans, 1)
            rows[rows_at(g * POOL + k, chans), :] = row[:, 0:span].astype(BF16)
        return 0

    lax.fori_loop(0, height // POOL, group, 0, unroll=2)
    for part in tiles_of(span):
        out[:, :, part] = to_planes(rows[:, part], chans)


def final_kernel(factor, mine, other, first, second):
    chans = first.shape[1]
    total = (mine[...] + other[...]) * factor
    turned = total[0 : 3 * chans].T
    for b in range(3):
        for a in range(3):
            first[3 * a + b] = turned[b * chans : (b + 1) * chans, a * chans : (a + 1) * chans]
    half = 3 * chans // 2
    low = total[3 * chans :]
    both = jnp.concatenate([low, turn(low, -(TILE // 2))], axis=0)
    for a in range(3):
        at = slice((2 - a) * chans, (3 - a) * chans)
        second[3 * a + 2] = turn(total[at], -3 * chans)[:, 0:chans]
        second[3 * a + 1] = both[at, 0:chans]
        second[3 * a + 0] = turn(both[at], -chans)[:, 0:chans]


def call(kernel, outs, scratch, n_in, limit, flops=0, smem_first=False, **more):
    specs = [VMEM] * n_in
    if smem_first:
        specs[0] = SMEM
    more.setdefault("in_specs", specs)
    more.setdefault("out_specs", jax.tree.map(lambda _: VMEM, outs))
    return pl.pallas_call(
        kernel,
        out_shape=outs,
        scratch_shapes=scratch,
        compiler_params=pltpu.CompilerParams(vmem_limit_bytes=limit * MIB),
        cost_estimate=pl.CostEstimate(flops=flops, bytes_accessed=4 * MIB, transcendentals=0),
        **more,
    )


def predict(blended, bands, shape, parts, part, before):
    chans, height, span = shape
    rows = height // parts
    block = pl.BlockSpec((chans, rows, span), lambda i: (0, part, 0))
    whole = lambda a: pl.BlockSpec(a.shape, lambda i: (0,) * a.ndim)
    args = (blended, bands)
    specs = [whole(a) for a in args]
    more = {}
    if before is not None:
        args += (before,)
        specs.append(pl.BlockSpec(memory_space=pl.ANY))
        more["input_output_aliases"] = {2: 0}
    return call(
        functools.partial(predict_kernel, part),
        jax.ShapeDtypeStruct(shape, BF16),
        [
            pltpu.VMEM((chans * rows, span), BF16),
        ],
        len(args),
        12,
        flops=10**9,
        grid=(1,),
        in_specs=specs,
        out_specs=block,
        **more,
    )(*args)


def bf(*shape):
    return jax.ShapeDtypeStruct(shape, BF16)


def swapped(messages, axis):
    pairs = [p for p in swaps(lax.axis_size(axis)) if p]
    return [lax.ppermute(m, axis, p) for m, p in zip(messages, pairs)]


def pack_rows(size, shifts, feat):
    message = bf(size, feat.shape[2])
    return call(
        feature_kernel, (message, message), [], 2, 16, flops=10**9, smem_first=True
    )(shifts, feat)


def both_passes(size, usual, feat, shifts, cot_rows, col_msgs, first_kernel, bottle_kernel, second_kernel):
    chans, height, span = feat.shape
    width = span + TILE
    full = height * chans
    groups = height // POOL
    ncols = len(col_msgs)
    packed = col_msgs[0].shape[0]

    halo = bf(CHALO * chans + ncols * packed * TILE // span, span)
    messages = call(edge_kernel, (halo, halo), [], 1 + ncols, 8)(cot_rows, *col_msgs)
    row_msgs = swapped(messages, "rows")
    if usual[0].shape[0] != size:
        usual = pack_rows(size, shifts, feat)
    feat_msgs = swapped(usual, "rows")

    tall_c = (height + 2 * CHALO) * chans
    view = bf((height + 2) * chans, span)
    band = 3 * (POOL + 2) * chans
    act_grad, *rest = call(
        functools.partial(back_kernel, ncols),
        (
            jax.ShapeDtypeStruct((full, span), F32), view, view, view,
            bf(chans, 3 * height, TILE), bf(POOL * chans, band), bf(3 * chans, 3 * chans),
            bf(3 * POOL * chans, (POOL + 2) * chans),
        ),
        [pltpu.VMEM((tall_c, width), BF16)] * 3
        + [pltpu.VMEM(((height + 2 * POOL) * chans, span), BF16)]
        + [pltpu.VMEM(((groups + 2) * chans, width), BF16)] * 3
        + [
            pltpu.VMEM((band, POOL * chans), F32),
            pltpu.VMEM((POOL * chans, band), BF16),
            pltpu.VMEM((9 * chans, TILE), F32),
            pltpu.VMEM((3 * chans, 3 * chans), BF16),
            pltpu.VMEM((chans, 9 * chans), F32),
        ],
        6 + ncols,
        16,
        flops=8 * 10**9,
    )(cot_rows, *row_msgs, *col_msgs, first_kernel, bottle_kernel, second_kernel)
    views, sides, weights = rest[:3], rest[3], rest[4:]

    tall = pl.cdiv(height + 2 * EXT, 16) * 16
    grads, blended = call(
        main_kernel,
        (jax.ShapeDtypeStruct((9 * chans // 2, TILE), F32), bf((height + 2) * chans, width)),
        [
            pltpu.VMEM((2, size + 48, span), BF16),
            pltpu.VMEM((chans, tall, width), BF16),
        ]
        + [pltpu.VMEM((tall * chans, width), BF16)] * 3
        + [pltpu.VMEM(((height + 4 * POOL) * chans, width), BF16)]
        + [pltpu.VMEM(((groups + 4) * chans, width), BF16)] * 3
        + [
            pltpu.VMEM((full, span), BF16),
            pltpu.VMEM((band, POOL * chans), F32),
        ],
        11,
        32,
        flops=10**10,
        smem_first=True,
    )(
        shifts, feat, *feat_msgs, sides, act_grad, *views, *weights[:2]
    )

    return grads, blended, weights[2]


def shards(features, shifts, first_kernel, bottle_kernel, second_kernel, cotangent):
    imgs, chans, height, span = features.shape
    rows, cols, dp = (lax.axis_size(a) for a in ("rows", "cols", "dp"))
    full = height * chans

    packed = chans * (height * SLOT // TILE)
    shifts = shifts[0]
    total = call(
        count_kernel, jax.ShapeDtypeStruct((8, TILE), jnp.int32), [], 1, 2, smem_first=True
    )(shifts)
    bit = 1
    while bit < dp:
        total = jnp.maximum(total, lax.ppermute(total, "dp", [(i, i ^ bit) for i in range(dp)]))
        bit *= 2
    messages = call(
        column_kernel, (bf(packed, TILE),) * (1 if cols == 2 else 2), [], 2, 8, flops=10**9
    )(features[0], cotangent[0])
    col_msgs = swapped(messages, "cols")
    ncols = len(col_msgs)
    usual = pack_rows(USUAL * chans, shifts, features[0])
    cot_rows = call(rows_kernel, bf(full, span), [], 1, 4, flops=10**9)(cotangent[0])

    def passes(size):
        return functools.partial(both_passes, size)

    grads, blended, second_bands = lax.cond(
        total[0, 0] <= USUAL * chans,
        passes(USUAL * chans),
        passes(LARGEST * chans),
        usual, features[0], shifts, cot_rows, tuple(col_msgs), first_kernel, bottle_kernel, second_kernel,
    )

    steps = []
    for axis, size in (("dp", dp), ("cols", cols), ("rows", rows)):
        bit = 1
        while bit < size:
            steps.append((axis, [(i, i ^ bit) for i in range(size)]))
            bit *= 2
    parts, prediction = 2, None
    for step, (axis, pairs) in enumerate(steps):
        other = lax.ppermute(grads, axis, pairs)
        if 1 <= step <= parts:
            prediction = predict(
                blended, second_bands, (chans, height, span), parts, step - 1, prediction
            )
            other, prediction = lax.optimization_barrier((other, prediction))
        if step < len(steps) - 1:
            grads = grads + other
            if step < parts:
                grads, blended = lax.optimization_barrier((grads, blended))
    factor = 1.0 / math.sqrt(imgs * dp * height * rows * span * cols)
    shape = jax.ShapeDtypeStruct((9, chans, chans), F32)
    first_grad, second_grad = call(
        functools.partial(final_kernel, factor), (shape, shape), [], 2, 2
    )(grads, other)
    return (prediction[None], first_grad, second_grad)


def solution(mesh):
    placed = (
        P("dp", None, "rows", "cols"),
        P("dp", None, None),
        P(),
        P(),
        P(),
        P("dp", None, "rows", "cols"),
    )
    return jax.shard_map(
        shards,
        mesh=mesh,
        in_specs=placed,
        out_specs=(P("dp", None, "rows", "cols"), P(), P()),
        check_vma=False,
    )
```

```python
import functools
import math

import jax
import jax.numpy as jnp
from jax import lax
from jax.experimental import pallas as pl
from jax.experimental.pallas import tpu as pltpu
from jax.sharding import PartitionSpec as P


MAXSHIFT = 16
POOL = 4
TILE = 128
SLOT = 32
EXT = 9
FHALO = MAXSHIFT + EXT
USUAL = 14
LARGEST = FHALO + 1
CHALO = 5
F32 = jnp.float32
BF16 = jnp.bfloat16
VMEM = pl.BlockSpec(memory_space=pltpu.VMEM)
SMEM = pl.BlockSpec(memory_space=pltpu.SMEM)
MIB = 1024 * 1024


def lanes_of(shape):
    return lax.broadcasted_iota(jnp.int32, shape, len(shape) - 1)


def turn(values, shift):
    width = values.shape[-1]
    if isinstance(shift, int):
        shift = shift % width
        if shift == 0:
            return values
    return pltpu.roll(values, shift, values.ndim - 1)


def has_sides():
    row, col = lax.axis_index("rows"), lax.axis_index("cols")
    return (
        row > 0,
        row < lax.axis_size("rows") - 1,
        col > 0,
        col < lax.axis_size("cols") - 1,
    )


def rows_at(r, chans, count=1):
    if isinstance(r, int):
        return slice(r * chans, (r + count) * chans)
    return pl.ds(pl.multiple_of(r * chans, chans), count * chans)


def to_rows(block):
    chans, height, span = block.shape
    return jnp.transpose(block, (1, 0, 2)).reshape(height * chans, span)


def to_planes(block, chans):
    height = block.shape[0] // chans
    return jnp.transpose(block.reshape(height, chans, block.shape[1]), (1, 0, 2))


def tiles_of(span):
    return [slice(t, t + TILE) for t in range(0, span, TILE)]


def is_even(axis):
    return lax.rem(lax.axis_index(axis), 2) == 0


def swaps(size):
    first = [(i, i ^ 1) for i in range(size)]
    second = [(i, i + 1) for i in range(1, size - 1, 2)]
    return [first, second + [(j, i) for i, j in second]]


def needed(shift, below):
    return jnp.maximum(EXT + shift if below else EXT - shift, 0)


def feature_kernel(index, skip, shifts, feat, msg, *counts):
    chans, height, span = feat.shape
    full = chans * height
    size = msg.shape[0]
    chunk = size // 4
    source = feat[...].reshape(full, span)
    lane = lanes_of((8, full))
    chan, row = lane // height, lane % height
    to_below = is_even("rows") if index == 0 else jnp.logical_not(is_even("rows"))
    target = jnp.full((8, full), -1, jnp.int32)
    at, up, down = jnp.int32(-skip), jnp.int32(0), jnp.int32(0)
    for c in range(chans):
        shift = shifts[c, 0]
        n_up, n_down = needed(shift, False), needed(shift, True)
        count = jnp.where(to_below, n_up, n_down)
        first = jnp.where(to_below, height - count, 0)
        mine = (chan == c) & (row >= first) & (row < first + count)
        target = jnp.where(mine, row + (at - first), target)
        at, up, down = at + count, up + n_up, down + n_down
    for out in counts:
        out[...] = jnp.full(out.shape, jnp.maximum(up, down), jnp.int32)
    for p in range(0, size, chunk):
        place = lax.broadcasted_iota(jnp.int32, (chunk, full), 0) + p
        pick = jnp.where(place == target[0:1], 1.0, 0.0).astype(BF16)
        msg[p : p + chunk] = jnp.dot(pick, source, preferred_element_type=F32).astype(BF16)


def rows_kernel(source, out):
    for part in tiles_of(source.shape[2]):
        out[:, part] = to_rows(source[:, :, part])


def column_kernel(feat, cot, *col_msgs):
    chans, height, span = feat.shape
    first, last = tiles_of(span)[0], tiles_of(span)[-1]
    count = TILE // SLOT
    block = height // count
    lane = lanes_of((chans, block, TILE))
    for index, msg in enumerate(col_msgs):
        sends_right = is_even("cols") if index == 0 else jnp.logical_not(is_even("cols"))
        total = jnp.zeros((chans, block, TILE), F32)
        inner = jnp.where(sends_right, TILE - 1 - lane, lane) < FHALO
        for k in range(count):
            at = slice(k * block, (k + 1) * block)
            feats = jnp.where(sends_right, feat[:, at, last].astype(F32), feat[:, at, first].astype(F32))
            cots = jnp.where(sends_right, cot[:, at, last].astype(F32), cot[:, at, first].astype(F32))
            cots = turn(cots, jnp.where(sends_right, TILE - FHALO, FHALO))
            piece = jnp.where(inner, feats, cots)
            piece = turn(piece, jnp.where(sends_right, (k + 1) * SLOT % TILE, k * SLOT))
            inside = (lane >= k * SLOT) & (lane < (k + 1) * SLOT)
            total = jnp.where(inside, piece, total)
        msg[...] = total.reshape(chans * block, TILE).astype(BF16)


def edge_kernel(cot_rows, *rest):
    cols, (msg_a, msg_b) = rest[:-2], rest[-2:]
    span = cot_rows.shape[1]
    size = msg_a.shape[0] - sum(c.shape[0] * TILE // span for c in cols)
    edge = cot_rows.shape[0] - size
    chans = size // CHALO
    low = jnp.where(is_even("rows"), edge, 0)
    msg_a[0:size] = cot_rows[pl.ds(pl.multiple_of(low, chans), size), :]
    msg_b[0:size] = cot_rows[pl.ds(pl.multiple_of(edge - low, chans), size), :]
    at = size
    for col in cols:
        count = col.shape[0] * TILE // span
        for t, part in enumerate(tiles_of(span)):
            block = col[t * count : (t + 1) * count]
            msg_a[at : at + count, part] = block
            msg_b[at : at + count, part] = block
        at += count


def corner_views(msg, size, cols):
    span = msg.shape[1]
    views, at = [], size
    for col in cols:
        count = col.shape[0] * TILE // span
        views.append(
            jnp.concatenate([msg[at : at + count, part] for part in tiles_of(span)], axis=0)
        )
        at += count
    return views


def halo_block(sources, k, chans, kind):
    rows = sources[0].shape[0] // chans
    lane = lanes_of((chans * rows, TILE))
    total = jnp.zeros((chans * rows, TILE), F32)
    if kind == "features":
        count, shift_r, shift_l = FHALO, -k * SLOT, TILE - (k + 1) * SLOT
    else:
        count, shift_r, shift_l = CHALO, -k * SLOT - FHALO, TILE - (k + 1) * SLOT + FHALO
    for index, source in enumerate(sources):
        from_right = is_even("cols") if index == 0 else jnp.logical_not(is_even("cols"))
        moved = turn(
            source.astype(F32), jnp.where(from_right, shift_r % TILE, shift_l % TILE)
        )
        total = jnp.where(
            jnp.where(from_right, lane, TILE - 1 - lane) < count, moved, total
        )
    return total.astype(BF16).reshape(chans, rows, TILE)


def columns_seen(shape, span):
    _, _, has_left, has_right = has_sides()
    lane = lanes_of(shape)
    middle = span + TILE // 2
    return (lane < span) | ((lane < middle) & has_right) | ((lane >= middle) & has_left)


def block_ones(width):
    row = lax.broadcasted_iota(jnp.int32, (width, width), 0) // POOL
    col = lax.broadcasted_iota(jnp.int32, (width, width), 1) // POOL
    return jnp.where(row == col, 1.0, 0.0).astype(BF16)


def store_split(high, low, at, total):
    top = total.astype(BF16)
    high[at, :] = top
    low[at, :] = (total - top.astype(F32)).astype(BF16)


def block_sums(high, low, ones):
    return jnp.dot(high[...], ones, preferred_element_type=F32) + jnp.dot(
        low[...], ones, preferred_element_type=F32
    )


def fill_bands(out, kernel, count):
    chans = kernel.shape[1]
    out[...] = jnp.zeros(out.shape, out.dtype)
    for k in range(count):
        for b in range(3):
            for a in range(3):
                at = (b * (count + 2) + k + a) * chans
                out[k * chans : (k + 1) * chans, at : at + chans] = kernel[3 * a + b].astype(
                    out.dtype
                )


def fill_turned_bands(out, kernel, count):
    chans = kernel.shape[1]
    out[...] = jnp.zeros(out.shape, out.dtype)
    for k in range(count):
        for b in range(3):
            for a in range(3):
                at = (b * (count + 2) + k + a) * chans
                out[at : at + chans, k * chans : (k + 1) * chans] = kernel[8 - 3 * a - b].astype(
                    out.dtype
                )


def stacked(views, at):
    return jnp.concatenate([view[at, :] for view in views], axis=0)


def conv_sum(parts, chans, step):
    return (
        turn(parts[0:chans], step)
        + parts[chans : 2 * chans]
        + turn(parts[2 * chans : 3 * chans], -step)
    )


def back_kernel(
    ncols, cot, msg_a, msg_b, *rest,
):
    cols, (
        first, bottle, second,
        act_grad, view_m, view_0, view_p, sides, first_bands, bottle_bands, second_bands,
        cot_m, cot_0, cot_p, back, high, low, coarse, bands_f, bands, small_f, small, wide_f,
    ) = rest[:ncols], rest[ncols:]
    chans = second.shape[1]
    full, span = cot.shape
    height = full // chans
    width = span + TILE
    groups = height // POOL
    has_up, has_down, _, _ = has_sides()
    seen_cols = columns_seen((chans, width), span)

    fill_turned_bands(bands_f, second, POOL)
    bands[...] = bands_f[...].T.astype(BF16)
    fill_turned_bands(small_f, bottle, 1)
    small_t = small_f[...].T
    for b in range(3):
        small[rows_at(b, chans)] = small_t[0:chans, 3 * b * chans : 3 * (b + 1) * chans].astype(BF16)
    fill_bands(first_bands, first, POOL)
    fill_bands(wide_f, bottle, 1)
    for b in range(3):
        bottle_bands[rows_at(b, chans)] = wide_f[
            0:chans, 3 * b * chans : 3 * (b + 1) * chans
        ].astype(BF16)
    second_bands[...] = jnp.zeros(second_bands.shape, BF16)
    for k in range(POOL):
        for b in range(3):
            for a in range(3):
                second_bands[
                    rows_at(3 * k + b, chans), (k + a) * chans : (k + a + 1) * chans
                ] = second[3 * a + b]

    size = CHALO * chans
    count = TILE // SLOT
    block = height // count

    def halo_columns(sources, at):
        for k in range(count):
            sides[:, at + k * block : at + (k + 1) * block, :] = halo_block(
                sources, k, chans, "features"
            )

    halo_columns([c[...] for c in cols], height)
    cot_0[rows_at(CHALO, chans, height), 0:span] = cot[...]
    for k in range(count):
        cot_0[rows_at(CHALO + k * block, chans, block), span:width] = to_rows(
            halo_block([c[...] for c in cols], k, chans, "cotangent")
        )

    def vertical(up, down):
        cot_0[rows_at(0, chans, CHALO), 0:span] = up[0:size]
        cot_0[rows_at(CHALO + height, chans, CHALO), 0:span] = down[0:size]
        corner = to_rows(
            halo_block(corner_views(up, size, cols), count - 1, chans, "cotangent")
        )
        cot_0[rows_at(0, chans, CHALO), span:width] = corner[(block - CHALO) * chans :]
        corner = to_rows(halo_block(corner_views(down, size, cols), 0, chans, "cotangent"))
        cot_0[rows_at(CHALO + height, chans, CHALO), span:width] = corner[0:size]
        halo_columns(corner_views(up, size, cols), 0)
        halo_columns(corner_views(down, size, cols), 2 * height)

    pl.when(is_even("rows"))(lambda: vertical(msg_b, msg_a))
    pl.when(jnp.logical_not(is_even("rows")))(lambda: vertical(msg_a, msg_b))
    for j in range(height + 2 * CHALO):
        at = rows_at(j, chans)
        cot_m[at] = turn(cot_0[at], 1)
        cot_p[at] = turn(cot_0[at], -1)
    inner = rows_at(CHALO - 1, chans, height + 2)
    view_m[...] = cot_m[inner, 0:span]
    view_0[...] = cot_0[inner, 0:span]
    view_p[...] = cot_p[inner, 0:span]

    def group(g, _):
        at = rows_at(g * POOL, chans, POOL + 2)
        rows = jnp.dot(
            bands[...], stacked((cot_m, cot_0, cot_p), at), preferred_element_type=F32
        ).astype(BF16)
        back[rows_at(g * POOL, chans, POOL), :] = rows[:, 0:span]
        rows = rows.astype(F32)
        total = rows[0:chans]
        for k in range(1, POOL):
            total = total + rows[k * chans : (k + 1) * chans]
        store_split(high, low, rows_at(g, chans), total)
        return 0

    lax.fori_loop(0, groups + 2, group, 0, unroll=2)
    sums = block_sums(high, low, block_ones(width))
    for g in range(groups + 2):
        at = rows_at(g, chans)
        seen = seen_cols
        if g == 0:
            seen = seen & has_up
        elif g == groups + 1:
            seen = seen & has_down
        coarse[at] = jnp.where(seen, sums[at], 0.0).astype(BF16)
    for g in range(groups):
        parts = jnp.dot(small[...], coarse[rows_at(g, chans, 3), :], preferred_element_type=F32)
        mean = conv_sum(parts, chans, POOL)[:, 0:span] * (1.0 / POOL**2)
        for k in range(POOL):
            r = g * POOL + k
            act_grad[rows_at(r, chans), :] = back[rows_at(r + POOL, chans), :].astype(F32) + mean


def correlate(u, u0, views, v0, acc, height, chans, span):
    groups = range(0, height, POOL)
    left = jnp.concatenate(
        [
            jnp.concatenate(
                [view[rows_at(v0 + g, chans, POOL + 2), 0:span] for view in views], axis=0
            )
            for g in groups
        ],
        axis=1,
    )
    right = jnp.concatenate([u[rows_at(u0 + g, chans, POOL), 0:span] for g in groups], axis=1)
    acc[...] = lax.dot_general(
        left, right, (((1,), (1,)), ((), ())), preferred_element_type=F32
    )


def folded(acc, chans):
    lane = lanes_of((3 * chans, TILE))
    result = jnp.zeros((3 * chans, TILE), F32)
    for b in range(3):
        total = None
        for k in range(POOL):
            block = turn(
                acc[rows_at(b * (POOL + 2) + k, chans, 3), 0:TILE], (b - k) * chans
            )
            total = block if total is None else total + block
        result = jnp.where((lane >= b * chans) & (lane < (b + 1) * chans), total, result)
    return result


def main_kernel(
    shifts, feat, feat_a, feat_b, sides, act_grad, view_m, view_0, view_p, bands, small,
    grads, blended,
    lent, moved, warp_m, warp_0, warp_p, act, high, low, pooled, pre_grad, acc,
):
    chans, height, span = feat.shape
    tiles = span // TILE
    width = span + TILE
    groups = height // POOL
    has_up, has_down, has_left, has_right = has_sides()
    seen_cols = columns_seen((chans, width), span)

    size = feat_a.shape[0]
    window = lent.shape[1] - size
    lent[:, size:, :] = jnp.zeros((2, window, span), BF16)

    def borrow(up, down):
        lent[0, 0:size] = up[...]
        lent[1, 0:size] = down[...]

    pl.when(is_even("rows"))(lambda: borrow(feat_b, feat_a))
    pl.when(jnp.logical_not(is_even("rows")))(lambda: borrow(feat_a, feat_b))

    tall = moved.shape[1]
    lane = lanes_of((tall, TILE))
    seen_halo = ((lane < TILE // 2) & has_right) | ((lane >= TILE // 2) & has_left)
    step = lanes_of((tall, 3 * height)) - lax.broadcasted_iota(jnp.int32, (tall, 3 * height), 0)
    depth = 2 * window + height
    source = lanes_of((1, depth))
    apart = lax.broadcasted_iota(jnp.int32, (tall, depth), 0) - lanes_of((tall, depth))
    align = 16

    def warp(c, ats):
        at_up, at_down = ats
        shift, move = shifts[c, 0], shifts[c, 1]
        n_up, n_down = needed(shift, False), needed(shift, True)
        base_up, base_down = (
            pl.multiple_of(lax.div(at, align) * align, align) for at in (at_up, at_down)
        )
        skip_up, skip_down = at_up - base_up, at_down - base_down
        own = EXT - window - shift
        below = own - skip_down
        above = EXT - skip_up - n_up - shift
        in_up = (source >= skip_up) & (source < skip_up + n_up)
        first_down = window + height + skip_down
        in_down = (source >= first_down) & (source < first_down + n_down)
        none = 4 * depth
        offset = jnp.where(
            source < window,
            jnp.where(in_up, above, none),
            jnp.where(source < window + height, own, jnp.where(in_down, below, none)),
        )
        pick = jnp.where(apart == offset, 1.0, 0.0).astype(BF16)
        rows = jnp.concatenate(
            [lent[0, pl.ds(base_up, window), :], feat[c], lent[1, pl.ds(base_down, window), :]], axis=0
        )
        plane = jnp.dot(pick, rows, preferred_element_type=F32)
        pick = jnp.where(step == height - EXT + shift, 1.0, 0.0).astype(BF16)
        plane = [plane[:, part] for part in tiles_of(span)]
        plane.append(jnp.dot(pick, sides[c], preferred_element_type=F32))
        amount = jnp.where(move > 0, TILE - move, -move)
        parts = [turn(part, amount) for part in plane]
        inside = jnp.where(move > 0, lane, TILE - 1 - lane) < TILE - jnp.abs(move)
        for t, part in enumerate(tiles_of(width)):
            after, before = parts[(t + 1) % (tiles + 1)], parts[t - 1]
            result = jnp.where(inside, parts[t], jnp.where(move > 0, after, before))
            if t == tiles:
                result = jnp.where(seen_halo, result, 0.0)
            moved[c, :, part] = result.astype(BF16)
        return at_up + n_up, at_down + n_down

    lax.fori_loop(0, chans, warp, (jnp.int32(0), jnp.int32(0)), unroll=8)
    chunk = 16
    for r in range(0, tall, chunk):
        for part in tiles_of(width):
            warp_0[rows_at(r, chans, chunk), part] = to_rows(moved[:, r : r + chunk, part])

    def clear(r, count):
        warp_0[rows_at(r, chans, count)] = jnp.zeros((count * chans, width), BF16)

    pl.when(jnp.logical_not(has_up))(lambda: clear(0, EXT))
    pl.when(jnp.logical_not(has_down))(lambda: clear(EXT + height, EXT))
    for j in range(height + 2 * EXT):
        at = rows_at(j, chans)
        warp_m[at] = turn(warp_0[at], 1)
        warp_p[at] = turn(warp_0[at], -1)

    def first_group(g, own):
        at = rows_at(g * POOL, chans, POOL + 2)
        pre = jnp.dot(
            bands[...], stacked((warp_m, warp_0, warp_p), at), preferred_element_type=F32
        )
        sigma = 0.5 * jnp.tanh(0.5 * pre) + 0.5
        rows = (pre * sigma).astype(BF16)
        act[rows_at(g * POOL, chans, POOL), :] = rows
        rows = rows.astype(F32)
        total = rows[0:chans]
        for k in range(1, POOL):
            total = total + rows[k * chans : (k + 1) * chans]
        store_split(high, low, rows_at(g, chans), total)
        if own:
            there = rows_at(g * POOL - 2 * POOL, chans, POOL)
            pre, sigma = pre[:, 0:span], sigma[:, 0:span]
            pre_grad[there, :] = (
                act_grad[there, :] * (sigma * (1.0 + pre * (1.0 - sigma)))
            ).astype(BF16)
        return 0

    for g in (0, 1, groups + 2, groups + 3):
        first_group(g, False)
    lax.fori_loop(2, groups + 2, lambda g, _: first_group(g, True), 0, unroll=4)
    sums = block_sums(high, low, block_ones(width))
    for g in range(groups + 4):
        at = rows_at(g, chans)
        seen = seen_cols
        if g < 2:
            seen = seen & has_up
        elif g >= groups + 2:
            seen = seen & has_down
        pooled[at] = jnp.where(seen, sums[at] * (1.0 / POOL**2), 0.0).astype(BF16)

    for g in range(groups + 2):
        parts = jnp.dot(small[...], pooled[rows_at(g, chans, 3), :], preferred_element_type=F32)
        bottle_row = conv_sum(parts, chans, POOL)
        rows, seen = range(POOL), seen_cols
        if g == 0:
            rows, seen = (POOL - 1,), seen & has_up
        elif g == groups + 1:
            rows, seen = (0,), seen & has_down
        for k in rows:
            row = act[rows_at((g + 1) * POOL + k, chans), :].astype(F32) + bottle_row
            blended[rows_at(g * POOL + k - POOL + 1, chans), :] = jnp.where(seen, row, 0.0).astype(
                BF16
            )

    correlate(pre_grad, 0, (warp_m, warp_0, warp_p), EXT - 1, acc, height, chans, span)
    first_part = folded(acc, chans)
    correlate(blended, 1, (view_m, view_0, view_p), 0, acc, height, chans, span)
    second_part = folded(acc, chans)
    lane = lanes_of((3 * chans, TILE))
    grads[0 : 3 * chans] = jnp.where(lane < 3 * chans, first_part, turn(second_part, 3 * chans))
    half = 3 * chans // 2
    grads[3 * chans :] = jnp.where(
        lane[0:half] < TILE // 2,
        turn(second_part[0:half], -chans),
        turn(second_part[half:], TILE // 2 - chans),
    )


def predict_kernel(part, blended, bands, *rest):
    out, rows = rest[-2:]
    chans, height, span = out.shape

    def group(g, _):
        at = rows_at(part * height + g * POOL, chans, POOL + 2)
        parts = jnp.dot(bands[...], blended[at, :], preferred_element_type=F32)
        for k in range(POOL):
            row = conv_sum(parts[3 * k * chans : 3 * (k + 1) * chans], chans, 1)
            rows[rows_at(g * POOL + k, chans), :] = row[:, 0:span].astype(BF16)
        return 0

    lax.fori_loop(0, height // POOL, group, 0, unroll=2)
    for part in tiles_of(span):
        out[:, :, part] = to_planes(rows[:, part], chans)


def final_kernel(factor, mine, other, first, second):
    chans = first.shape[1]
    total = (mine[...] + other[...]) * factor
    turned = total[0 : 3 * chans].T
    for b in range(3):
        for a in range(3):
            first[3 * a + b] = turned[b * chans : (b + 1) * chans, a * chans : (a + 1) * chans]
    half = 3 * chans // 2
    low = total[3 * chans :]
    both = jnp.concatenate([low, turn(low, -(TILE // 2))], axis=0)
    for a in range(3):
        at = slice((2 - a) * chans, (3 - a) * chans)
        second[3 * a + 2] = turn(total[at], -3 * chans)[:, 0:chans]
        second[3 * a + 1] = both[at, 0:chans]
        second[3 * a + 0] = turn(both[at], -chans)[:, 0:chans]


def call(kernel, outs, scratch, n_in, limit, flops=0, smem_first=False, **more):
    specs = [VMEM] * n_in
    if smem_first:
        specs[0] = SMEM
    more.setdefault("in_specs", specs)
    more.setdefault("out_specs", jax.tree.map(lambda _: VMEM, outs))
    return pl.pallas_call(
        kernel,
        out_shape=outs,
        scratch_shapes=scratch,
        compiler_params=pltpu.CompilerParams(vmem_limit_bytes=limit * MIB),
        cost_estimate=pl.CostEstimate(flops=flops, bytes_accessed=4 * MIB, transcendentals=0),
        **more,
    )


def predict(blended, bands, shape, parts, part, before):
    chans, height, span = shape
    rows = height // parts
    block = pl.BlockSpec((chans, rows, span), lambda i: (0, part, 0))
    whole = lambda a: pl.BlockSpec(a.shape, lambda i: (0,) * a.ndim)
    args = (blended, bands)
    specs = [whole(a) for a in args]
    more = {}
    if before is not None:
        args += (before,)
        specs.append(pl.BlockSpec(memory_space=pl.ANY))
        more["input_output_aliases"] = {2: 0}
    return call(
        functools.partial(predict_kernel, part),
        jax.ShapeDtypeStruct(shape, BF16),
        [
            pltpu.VMEM((chans * rows, span), BF16),
        ],
        len(args),
        12,
        flops=10**9,
        grid=(1,),
        in_specs=specs,
        out_specs=block,
        **more,
    )(*args)


def bf(*shape):
    return jax.ShapeDtypeStruct(shape, BF16)


def swapped(messages, axis):
    pairs = [p for p in swaps(lax.axis_size(axis)) if p]
    return [lax.ppermute(m, axis, p) for m, p in zip(messages, pairs)]


def pack_rows(index, skip, size, shifts, feat, counted=False):
    message = bf(size, feat.shape[2])
    if counted:
        message = (message, jax.ShapeDtypeStruct((8, TILE), jnp.int32))
    return call(
        functools.partial(feature_kernel, index, skip),
        message, [], 2, 16, smem_first=True,
    )(shifts, feat)


def main_pass(rest, lent, shifts, feat, sides, act_grad, views, bands):
    chans, height, span = feat.shape
    width = span + TILE
    full = height * chans
    groups = height // POOL
    band = 3 * (POOL + 2) * chans
    if rest:
        size = lent[0].shape[0]
        more = swapped([pack_rows(i, size, rest, shifts, feat) for i in (0, 1)], "rows")
        lent = [jnp.concatenate(pair, axis=0) for pair in zip(lent, more)]
    size = lent[0].shape[0]
    tall = pl.cdiv(height + 2 * EXT, 16) * 16
    grads, blended = call(
        main_kernel,
        (jax.ShapeDtypeStruct((9 * chans // 2, TILE), F32), bf((height + 2) * chans, width)),
        [
            pltpu.VMEM((2, size + 48, span), BF16),
            pltpu.VMEM((chans, tall, width), BF16),
        ]
        + [pltpu.VMEM((tall * chans, width), BF16)] * 3
        + [pltpu.VMEM(((height + 4 * POOL) * chans, width), BF16)]
        + [pltpu.VMEM(((groups + 4) * chans, width), BF16)] * 3
        + [
            pltpu.VMEM((full, span), BF16),
            pltpu.VMEM((band, POOL * chans), F32),
        ],
        11,
        32,
        flops=10**10,
        smem_first=True,
    )(
        shifts, feat, *lent, sides, act_grad, *views, *bands
    )

    return grads, blended


def shards(features, shifts, first_kernel, bottle_kernel, second_kernel, cotangent):
    imgs, chans, height, span = features.shape
    rows, cols, dp = (lax.axis_size(a) for a in ("rows", "cols", "dp"))
    full = height * chans

    width = span + TILE
    groups = height // POOL
    feat, cot, shifts = features[0], cotangent[0], shifts[0]
    row_pairs = swaps(rows)

    usual = USUAL * chans
    message, total = pack_rows(0, 0, usual, shifts, feat, counted=True)
    message, total, cot = lax.optimization_barrier((message, total, cot))
    feat_a = lax.ppermute(message, "rows", row_pairs[0])
    bit = 1
    while bit < dp:
        total = jnp.maximum(total, lax.ppermute(total, "dp", [(i, i ^ bit) for i in range(dp)]))
        bit *= 2

    packed = chans * (height * SLOT // TILE)
    messages = call(
        column_kernel, (bf(packed, TILE),) * (1 if cols == 2 else 2), [], 2, 8, flops=2 * 10**10
    )(feat, cot)
    col_msgs = swapped(messages, "cols")
    ncols = len(col_msgs)
    feat_b = lax.ppermute(pack_rows(1, 0, usual, shifts, feat), "rows", row_pairs[1])
    cot_rows = call(rows_kernel, bf(full, span), [], 1, 4)(cot)
    halo = bf(CHALO * chans + ncols * packed * TILE // span, span)
    messages = call(edge_kernel, (halo, halo), [], 1 + ncols, 8)(cot_rows, *col_msgs)
    row_msgs = swapped(messages, "rows")
    row_msgs, feat_a = lax.optimization_barrier((row_msgs, feat_a))

    tall_c = (height + 2 * CHALO) * chans
    view = bf((height + 2) * chans, span)
    band = 3 * (POOL + 2) * chans
    act_grad, *rest = call(
        functools.partial(back_kernel, ncols),
        (
            jax.ShapeDtypeStruct((full, span), F32), view, view, view,
            bf(chans, 3 * height, TILE), bf(POOL * chans, band), bf(3 * chans, 3 * chans),
            bf(3 * POOL * chans, (POOL + 2) * chans),
        ),
        [pltpu.VMEM((tall_c, width), BF16)] * 3
        + [pltpu.VMEM(((height + 2 * POOL) * chans, span), BF16)]
        + [pltpu.VMEM(((groups + 2) * chans, width), BF16)] * 3
        + [
            pltpu.VMEM((band, POOL * chans), F32),
            pltpu.VMEM((POOL * chans, band), BF16),
            pltpu.VMEM((9 * chans, TILE), F32),
            pltpu.VMEM((3 * chans, 3 * chans), BF16),
            pltpu.VMEM((chans, 9 * chans), F32),
        ],
        6 + ncols,
        16,
        flops=8 * 10**9,
    )(cot_rows, *row_msgs, *col_msgs, first_kernel, bottle_kernel, second_kernel)
    views, sides, weights = rest[:3], rest[3], rest[4:]

    grads, blended = lax.cond(
        total[0, 0] <= usual,
        functools.partial(main_pass, 0),
        functools.partial(main_pass, LARGEST * chans - usual),
        (feat_a, feat_b), shifts, feat, sides, act_grad, tuple(views), tuple(weights[:2]),
    )

    steps = []
    for axis, size in (("dp", dp), ("cols", cols), ("rows", rows)):
        bit = 1
        while bit < size:
            steps.append((axis, [(i, i ^ bit) for i in range(size)]))
            bit *= 2
    parts, prediction = 2, None
    for step, (axis, pairs) in enumerate(steps):
        other = lax.ppermute(grads, axis, pairs)
        if 1 <= step <= parts:
            prediction = predict(
                blended, weights[2], (chans, height, span), parts, step - 1, prediction
            )
            other, prediction = lax.optimization_barrier((other, prediction))
        if step < len(steps) - 1:
            grads = grads + other
            if step < parts:
                grads, blended = lax.optimization_barrier((grads, blended))
    factor = 1.0 / math.sqrt(imgs * dp * height * rows * span * cols)
    shape = jax.ShapeDtypeStruct((9, chans, chans), F32)
    first_grad, second_grad = call(
        functools.partial(final_kernel, factor), (shape, shape), [], 2, 2
    )(grads, other)
    return (prediction[None], first_grad, second_grad)


def solution(mesh):
    placed = (
        P("dp", None, "rows", "cols"),
        P("dp", None, None),
        P(),
        P(),
        P(),
        P("dp", None, "rows", "cols"),
    )
    return jax.shard_map(
        shards,
        mesh=mesh,
        in_specs=placed,
        out_specs=(P("dp", None, "rows", "cols"), P(), P()),
        check_vma=False,
    )
```

```python
import functools
import math

import jax
import jax.numpy as jnp
from jax import lax
from jax.experimental import pallas as pl
from jax.experimental.pallas import tpu as pltpu
from jax.sharding import PartitionSpec as P


MAXSHIFT = 16
POOL = 4
TILE = 128
SLOT = 32
EXT = 9
FHALO = MAXSHIFT + EXT
USUAL = 14
LARGEST = FHALO + 1
CHALO = 5
F32 = jnp.float32
BF16 = jnp.bfloat16
VMEM = pl.BlockSpec(memory_space=pltpu.VMEM)
SMEM = pl.BlockSpec(memory_space=pltpu.SMEM)
MIB = 1024 * 1024


def lanes_of(shape):
    return lax.broadcasted_iota(jnp.int32, shape, len(shape) - 1)


def turn(values, shift):
    width = values.shape[-1]
    if isinstance(shift, int):
        shift = shift % width
        if shift == 0:
            return values
    return pltpu.roll(values, shift, values.ndim - 1)


def has_sides():
    row, col = lax.axis_index("rows"), lax.axis_index("cols")
    return (
        row > 0,
        row < lax.axis_size("rows") - 1,
        col > 0,
        col < lax.axis_size("cols") - 1,
    )


def rows_at(r, chans, count=1):
    if isinstance(r, int):
        return slice(r * chans, (r + count) * chans)
    return pl.ds(pl.multiple_of(r * chans, chans), count * chans)


def to_rows(block):
    chans, height, span = block.shape
    return jnp.transpose(block, (1, 0, 2)).reshape(height * chans, span)


def to_planes(block, chans):
    height = block.shape[0] // chans
    return jnp.transpose(block.reshape(height, chans, block.shape[1]), (1, 0, 2))


def tiles_of(span):
    return [slice(t, t + TILE) for t in range(0, span, TILE)]


def is_even(axis):
    return lax.rem(lax.axis_index(axis), 2) == 0


def swaps(size):
    first = [(i, i ^ 1) for i in range(size)]
    second = [(i, i + 1) for i in range(1, size - 1, 2)]
    return [first, second + [(j, i) for i, j in second]]


def needed(shift, below):
    return jnp.maximum(EXT + shift if below else EXT - shift, 0)


def feature_kernel(index, skip, shifts, feat, msg, *counts):
    chans, height, span = feat.shape
    full = chans * height
    size = msg.shape[0]
    chunk = size // 4
    source = feat[...].reshape(full, span)
    lane = lanes_of((8, full))
    chan, row = lane // height, lane % height
    to_below = is_even("rows") if index == 0 else jnp.logical_not(is_even("rows"))
    target = jnp.full((8, full), -1, jnp.int32)
    at, up, down = jnp.int32(-skip), jnp.int32(0), jnp.int32(0)
    for c in range(chans):
        shift = shifts[c, 0]
        n_up, n_down = needed(shift, False), needed(shift, True)
        count = jnp.where(to_below, n_up, n_down)
        first = jnp.where(to_below, height - count, 0)
        mine = (chan == c) & (row >= first) & (row < first + count)
        target = jnp.where(mine, row + (at - first), target)
        at, up, down = at + count, up + n_up, down + n_down
    for out in counts:
        out[...] = jnp.full(out.shape, jnp.maximum(up, down), jnp.int32)
    for p in range(0, size, chunk):
        place = lax.broadcasted_iota(jnp.int32, (chunk, full), 0) + p
        pick = jnp.where(place == target[0:1], 1.0, 0.0).astype(BF16)
        msg[p : p + chunk] = jnp.dot(pick, source, preferred_element_type=F32).astype(BF16)


def rows_kernel(source, out):
    for part in tiles_of(source.shape[2]):
        out[:, part] = to_rows(source[:, :, part])


def column_kernel(feat, cot, *col_msgs):
    chans, height, span = feat.shape
    first, last = tiles_of(span)[0], tiles_of(span)[-1]
    count = TILE // SLOT
    block = height // count
    lane = lanes_of((chans, block, TILE))
    for index, msg in enumerate(col_msgs):
        sends_right = is_even("cols") if index == 0 else jnp.logical_not(is_even("cols"))
        total = jnp.zeros((chans, block, TILE), F32)
        inner = jnp.where(sends_right, TILE - 1 - lane, lane) < FHALO
        for k in range(count):
            at = slice(k * block, (k + 1) * block)
            feats = jnp.where(sends_right, feat[:, at, last].astype(F32), feat[:, at, first].astype(F32))
            cots = jnp.where(sends_right, cot[:, at, last].astype(F32), cot[:, at, first].astype(F32))
            cots = turn(cots, jnp.where(sends_right, TILE - FHALO, FHALO))
            piece = jnp.where(inner, feats, cots)
            piece = turn(piece, jnp.where(sends_right, (k + 1) * SLOT % TILE, k * SLOT))
            inside = (lane >= k * SLOT) & (lane < (k + 1) * SLOT)
            total = jnp.where(inside, piece, total)
        msg[...] = total.reshape(chans * block, TILE).astype(BF16)


def edge_kernel(cot_rows, *rest):
    cols, (msg_a, msg_b) = rest[:-2], rest[-2:]
    span = cot_rows.shape[1]
    size = msg_a.shape[0] - sum(c.shape[0] * TILE // span for c in cols)
    edge = cot_rows.shape[0] - size
    chans = size // CHALO
    low = jnp.where(is_even("rows"), edge, 0)
    msg_a[0:size] = cot_rows[pl.ds(pl.multiple_of(low, chans), size), :]
    msg_b[0:size] = cot_rows[pl.ds(pl.multiple_of(edge - low, chans), size), :]
    at = size
    for col in cols:
        count = col.shape[0] * TILE // span
        for t, part in enumerate(tiles_of(span)):
            block = col[t * count : (t + 1) * count]
            msg_a[at : at + count, part] = block
            msg_b[at : at + count, part] = block
        at += count


def corner_views(msg, size, cols):
    span = msg.shape[1]
    views, at = [], size
    for col in cols:
        count = col.shape[0] * TILE // span
        views.append(
            jnp.concatenate([msg[at : at + count, part] for part in tiles_of(span)], axis=0)
        )
        at += count
    return views


def halo_block(sources, k, chans, kind):
    rows = sources[0].shape[0] // chans
    lane = lanes_of((chans * rows, TILE))
    total = jnp.zeros((chans * rows, TILE), F32)
    if kind == "features":
        count, shift_r, shift_l = FHALO, -k * SLOT, TILE - (k + 1) * SLOT
    else:
        count, shift_r, shift_l = CHALO, -k * SLOT - FHALO, TILE - (k + 1) * SLOT + FHALO
    for index, source in enumerate(sources):
        from_right = is_even("cols") if index == 0 else jnp.logical_not(is_even("cols"))
        moved = turn(
            source.astype(F32), jnp.where(from_right, shift_r % TILE, shift_l % TILE)
        )
        total = jnp.where(
            jnp.where(from_right, lane, TILE - 1 - lane) < count, moved, total
        )
    return total.astype(BF16).reshape(chans, rows, TILE)


def columns_seen(shape, span):
    _, _, has_left, has_right = has_sides()
    lane = lanes_of(shape)
    middle = span + TILE // 2
    return (lane < span) | ((lane < middle) & has_right) | ((lane >= middle) & has_left)


def block_ones(width):
    row = lax.broadcasted_iota(jnp.int32, (width, width), 0) // POOL
    col = lax.broadcasted_iota(jnp.int32, (width, width), 1) // POOL
    return jnp.where(row == col, 1.0, 0.0).astype(BF16)


def store_split(high, low, at, total):
    top = total.astype(BF16)
    high[at, :] = top
    low[at, :] = (total - top.astype(F32)).astype(BF16)


def block_sums(high, low, ones):
    return jnp.dot(high[...], ones, preferred_element_type=F32) + jnp.dot(
        low[...], ones, preferred_element_type=F32
    )


def fill_bands(out, kernel, count):
    chans = kernel.shape[1]
    out[...] = jnp.zeros(out.shape, out.dtype)
    for k in range(count):
        for b in range(3):
            for a in range(3):
                at = (b * (count + 2) + k + a) * chans
                out[k * chans : (k + 1) * chans, at : at + chans] = kernel[3 * a + b].astype(
                    out.dtype
                )


def fill_turned_bands(out, kernel, count):
    chans = kernel.shape[1]
    out[...] = jnp.zeros(out.shape, out.dtype)
    for k in range(count):
        for b in range(3):
            for a in range(3):
                at = (b * (count + 2) + k + a) * chans
                out[at : at + chans, k * chans : (k + 1) * chans] = kernel[8 - 3 * a - b].astype(
                    out.dtype
                )


def stacked(views, at):
    return jnp.concatenate([view[at, :] for view in views], axis=0)


def conv_sum(parts, chans, step):
    return (
        turn(parts[0:chans], step)
        + parts[chans : 2 * chans]
        + turn(parts[2 * chans : 3 * chans], -step)
    )


def back_kernel(
    ncols, cot, msg_a, msg_b, *rest,
):
    cols, (
        first, bottle, second,
        act_grad, view_m, view_0, view_p, sides, first_bands, bottle_bands, second_bands,
        cot_m, cot_0, cot_p, back, high, low, coarse, bands_f, bands, small_f, small, wide_f,
    ) = rest[:ncols], rest[ncols:]
    chans = second.shape[1]
    full, span = cot.shape
    height = full // chans
    width = span + TILE
    groups = height // POOL
    has_up, has_down, _, _ = has_sides()
    seen_cols = columns_seen((chans, width), span)

    fill_turned_bands(bands_f, second, POOL)
    bands[...] = bands_f[...].T.astype(BF16)
    fill_turned_bands(small_f, bottle, 1)
    small_t = small_f[...].T
    for b in range(3):
        small[rows_at(b, chans)] = small_t[0:chans, 3 * b * chans : 3 * (b + 1) * chans].astype(BF16)
    fill_bands(first_bands, first, POOL)
    fill_bands(wide_f, bottle, 1)
    for b in range(3):
        bottle_bands[rows_at(b, chans)] = wide_f[
            0:chans, 3 * b * chans : 3 * (b + 1) * chans
        ].astype(BF16)
    second_bands[...] = jnp.zeros(second_bands.shape, BF16)
    for k in range(POOL):
        for b in range(3):
            for a in range(3):
                second_bands[
                    rows_at(3 * k + b, chans), (k + a) * chans : (k + a + 1) * chans
                ] = second[3 * a + b]

    size = CHALO * chans
    count = TILE // SLOT
    block = height // count

    def halo_columns(sources, at):
        for k in range(count):
            sides[:, at + k * block : at + (k + 1) * block, :] = halo_block(
                sources, k, chans, "features"
            )

    halo_columns([c[...] for c in cols], height)
    cot_0[rows_at(CHALO, chans, height), 0:span] = cot[...]
    for k in range(count):
        cot_0[rows_at(CHALO + k * block, chans, block), span:width] = to_rows(
            halo_block([c[...] for c in cols], k, chans, "cotangent")
        )

    def vertical(up, down):
        cot_0[rows_at(0, chans, CHALO), 0:span] = up[0:size]
        cot_0[rows_at(CHALO + height, chans, CHALO), 0:span] = down[0:size]
        corner = to_rows(
            halo_block(corner_views(up, size, cols), count - 1, chans, "cotangent")
        )
        cot_0[rows_at(0, chans, CHALO), span:width] = corner[(block - CHALO) * chans :]
        corner = to_rows(halo_block(corner_views(down, size, cols), 0, chans, "cotangent"))
        cot_0[rows_at(CHALO + height, chans, CHALO), span:width] = corner[0:size]
        halo_columns(corner_views(up, size, cols), 0)
        halo_columns(corner_views(down, size, cols), 2 * height)

    pl.when(is_even("rows"))(lambda: vertical(msg_b, msg_a))
    pl.when(jnp.logical_not(is_even("rows")))(lambda: vertical(msg_a, msg_b))
    for j in range(height + 2 * CHALO):
        at = rows_at(j, chans)
        cot_m[at] = turn(cot_0[at], 1)
        cot_p[at] = turn(cot_0[at], -1)
    inner = rows_at(CHALO - 1, chans, height + 2)
    view_m[...] = cot_m[inner, 0:span]
    view_0[...] = cot_0[inner, 0:span]
    view_p[...] = cot_p[inner, 0:span]

    def group(g, _):
        at = rows_at(g * POOL, chans, POOL + 2)
        rows = jnp.dot(
            bands[...], stacked((cot_m, cot_0, cot_p), at), preferred_element_type=F32
        ).astype(BF16)
        back[rows_at(g * POOL, chans, POOL), :] = rows[:, 0:span]
        rows = rows.astype(F32)
        total = rows[0:chans]
        for k in range(1, POOL):
            total = total + rows[k * chans : (k + 1) * chans]
        store_split(high, low, rows_at(g, chans), total)
        return 0

    lax.fori_loop(0, groups + 2, group, 0, unroll=2)
    sums = block_sums(high, low, block_ones(width))
    for g in range(groups + 2):
        at = rows_at(g, chans)
        seen = seen_cols
        if g == 0:
            seen = seen & has_up
        elif g == groups + 1:
            seen = seen & has_down
        coarse[at] = jnp.where(seen, sums[at], 0.0).astype(BF16)
    for g in range(groups):
        parts = jnp.dot(small[...], coarse[rows_at(g, chans, 3), :], preferred_element_type=F32)
        mean = conv_sum(parts, chans, POOL)[:, 0:span] * (1.0 / POOL**2)
        for k in range(POOL):
            r = g * POOL + k
            act_grad[rows_at(r, chans), :] = back[rows_at(r + POOL, chans), :].astype(F32) + mean


def correlate(u, u0, views, v0, acc, height, chans, span):
    groups = range(0, height, POOL)
    left = jnp.concatenate(
        [
            jnp.concatenate(
                [view[rows_at(v0 + g, chans, POOL + 2), 0:span] for view in views], axis=0
            )
            for g in groups
        ],
        axis=1,
    )
    right = jnp.concatenate([u[rows_at(u0 + g, chans, POOL), 0:span] for g in groups], axis=1)
    acc[...] = lax.dot_general(
        left, right, (((1,), (1,)), ((), ())), preferred_element_type=F32
    )


def folded(acc, chans):
    lane = lanes_of((3 * chans, TILE))
    result = jnp.zeros((3 * chans, TILE), F32)
    for b in range(3):
        total = None
        for k in range(POOL):
            block = turn(
                acc[rows_at(b * (POOL + 2) + k, chans, 3), 0:TILE], (b - k) * chans
            )
            total = block if total is None else total + block
        result = jnp.where((lane >= b * chans) & (lane < (b + 1) * chans), total, result)
    return result


def main_kernel(
    shifts, feat, feat_a, feat_b, sides, act_grad, view_m, view_0, view_p, bands, small,
    grads, blended,
    lent, moved, warp_m, warp_0, warp_p, act, high, low, pooled, pre_grad, acc,
):
    chans, height, span = feat.shape
    tiles = span // TILE
    width = span + TILE
    groups = height // POOL
    has_up, has_down, has_left, has_right = has_sides()
    seen_cols = columns_seen((chans, width), span)

    size = feat_a.shape[0]
    window = lent.shape[1] - size
    lent[:, size:, :] = jnp.zeros((2, window, span), BF16)

    def borrow(up, down):
        lent[0, 0:size] = up[...]
        lent[1, 0:size] = down[...]

    pl.when(is_even("rows"))(lambda: borrow(feat_b, feat_a))
    pl.when(jnp.logical_not(is_even("rows")))(lambda: borrow(feat_a, feat_b))

    tall = moved.shape[1]
    lane = lanes_of((tall, TILE))
    seen_halo = ((lane < TILE // 2) & has_right) | ((lane >= TILE // 2) & has_left)
    step = lanes_of((tall, 3 * height)) - lax.broadcasted_iota(jnp.int32, (tall, 3 * height), 0)
    depth = 2 * window + height
    source = lanes_of((1, depth))
    apart = lax.broadcasted_iota(jnp.int32, (tall, depth), 0) - lanes_of((tall, depth))
    align = 16

    def warp(c, ats):
        at_up, at_down = ats
        shift, move = shifts[c, 0], shifts[c, 1]
        n_up, n_down = needed(shift, False), needed(shift, True)
        base_up, base_down = (
            pl.multiple_of(lax.div(at, align) * align, align) for at in (at_up, at_down)
        )
        skip_up, skip_down = at_up - base_up, at_down - base_down
        own = EXT - window - shift
        below = own - skip_down
        above = EXT - skip_up - n_up - shift
        in_up = (source >= skip_up) & (source < skip_up + n_up)
        first_down = window + height + skip_down
        in_down = (source >= first_down) & (source < first_down + n_down)
        none = 4 * depth
        offset = jnp.where(
            source < window,
            jnp.where(in_up, above, none),
            jnp.where(source < window + height, own, jnp.where(in_down, below, none)),
        )
        pick = jnp.where(apart == offset, 1.0, 0.0).astype(BF16)
        rows = jnp.concatenate(
            [lent[0, pl.ds(base_up, window), :], feat[c], lent[1, pl.ds(base_down, window), :]], axis=0
        )
        plane = jnp.dot(pick, rows, preferred_element_type=F32)
        pick = jnp.where(step == height - EXT + shift, 1.0, 0.0).astype(BF16)
        plane = [plane[:, part] for part in tiles_of(span)]
        plane.append(jnp.dot(pick, sides[c], preferred_element_type=F32))
        amount = jnp.where(move > 0, TILE - move, -move)
        parts = [turn(part, amount) for part in plane]
        inside = jnp.where(move > 0, lane, TILE - 1 - lane) < TILE - jnp.abs(move)
        for t, part in enumerate(tiles_of(width)):
            after, before = parts[(t + 1) % (tiles + 1)], parts[t - 1]
            result = jnp.where(inside, parts[t], jnp.where(move > 0, after, before))
            if t == tiles:
                result = jnp.where(seen_halo, result, 0.0)
            moved[c, :, part] = result.astype(BF16)
        return at_up + n_up, at_down + n_down

    lax.fori_loop(0, chans, warp, (jnp.int32(0), jnp.int32(0)), unroll=8)
    chunk = 16
    for r in range(0, tall, chunk):
        for part in tiles_of(width):
            warp_0[rows_at(r, chans, chunk), part] = to_rows(moved[:, r : r + chunk, part])

    def clear(r, count):
        warp_0[rows_at(r, chans, count)] = jnp.zeros((count * chans, width), BF16)

    pl.when(jnp.logical_not(has_up))(lambda: clear(0, EXT))
    pl.when(jnp.logical_not(has_down))(lambda: clear(EXT + height, EXT))
    for j in range(height + 2 * EXT):
        at = rows_at(j, chans)
        warp_m[at] = turn(warp_0[at], 1)
        warp_p[at] = turn(warp_0[at], -1)

    def first_group(g, own):
        at = rows_at(g * POOL, chans, POOL + 2)
        pre = jnp.dot(
            bands[...], stacked((warp_m, warp_0, warp_p), at), preferred_element_type=F32
        )
        sigma = 0.5 * jnp.tanh(0.5 * pre) + 0.5
        rows = (pre * sigma).astype(BF16)
        act[rows_at(g * POOL, chans, POOL), :] = rows
        rows = rows.astype(F32)
        total = rows[0:chans]
        for k in range(1, POOL):
            total = total + rows[k * chans : (k + 1) * chans]
        store_split(high, low, rows_at(g, chans), total)
        if own:
            there = rows_at(g * POOL - 2 * POOL, chans, POOL)
            pre, sigma = pre[:, 0:span], sigma[:, 0:span]
            pre_grad[there, :] = (
                act_grad[there, :] * (sigma * (1.0 + pre * (1.0 - sigma)))
            ).astype(BF16)
        return 0

    for g in (0, 1, groups + 2, groups + 3):
        first_group(g, False)
    lax.fori_loop(2, groups + 2, lambda g, _: first_group(g, True), 0, unroll=4)
    sums = block_sums(high, low, block_ones(width))
    for g in range(groups + 4):
        at = rows_at(g, chans)
        seen = seen_cols
        if g < 2:
            seen = seen & has_up
        elif g >= groups + 2:
            seen = seen & has_down
        pooled[at] = jnp.where(seen, sums[at] * (1.0 / POOL**2), 0.0).astype(BF16)

    for g in range(groups + 2):
        parts = jnp.dot(small[...], pooled[rows_at(g, chans, 3), :], preferred_element_type=F32)
        bottle_row = conv_sum(parts, chans, POOL)
        rows, seen = range(POOL), seen_cols
        if g == 0:
            rows, seen = (POOL - 1,), seen & has_up
        elif g == groups + 1:
            rows, seen = (0,), seen & has_down
        for k in rows:
            row = act[rows_at((g + 1) * POOL + k, chans), :].astype(F32) + bottle_row
            blended[rows_at(g * POOL + k - POOL + 1, chans), :] = jnp.where(seen, row, 0.0).astype(
                BF16
            )

    correlate(pre_grad, 0, (warp_m, warp_0, warp_p), EXT - 1, acc, height, chans, span)
    first_part = folded(acc, chans)
    correlate(blended, 1, (view_m, view_0, view_p), 0, acc, height, chans, span)
    second_part = folded(acc, chans)
    lane = lanes_of((3 * chans, TILE))
    grads[0 : 3 * chans] = jnp.where(lane < 3 * chans, first_part, turn(second_part, 3 * chans))
    half = 3 * chans // 2
    grads[3 * chans :] = jnp.where(
        lane[0:half] < TILE // 2,
        turn(second_part[0:half], -chans),
        turn(second_part[half:], TILE // 2 - chans),
    )


def predict_kernel(part, blended, bands, *rest):
    out, rows = rest[-2:]
    chans, height, span = out.shape

    def group(g, _):
        at = rows_at(part * height + g * POOL, chans, POOL + 2)
        parts = jnp.dot(bands[...], blended[at, :], preferred_element_type=F32)
        for k in range(POOL):
            row = conv_sum(parts[3 * k * chans : 3 * (k + 1) * chans], chans, 1)
            rows[rows_at(g * POOL + k, chans), :] = row[:, 0:span].astype(BF16)
        return 0

    lax.fori_loop(0, height // POOL, group, 0, unroll=2)
    for part in tiles_of(span):
        out[:, :, part] = to_planes(rows[:, part], chans)


def final_kernel(factor, mine, other, first, second):
    chans = first.shape[1]
    total = (mine[...] + other[...]) * factor
    turned = total[0 : 3 * chans].T
    for b in range(3):
        for a in range(3):
            first[3 * a + b] = turned[b * chans : (b + 1) * chans, a * chans : (a + 1) * chans]
    half = 3 * chans // 2
    low = total[3 * chans :]
    both = jnp.concatenate([low, turn(low, -(TILE // 2))], axis=0)
    for a in range(3):
        at = slice((2 - a) * chans, (3 - a) * chans)
        second[3 * a + 2] = turn(total[at], -3 * chans)[:, 0:chans]
        second[3 * a + 1] = both[at, 0:chans]
        second[3 * a + 0] = turn(both[at], -chans)[:, 0:chans]


def call(kernel, outs, scratch, n_in, limit, flops=0, smem_first=False, **more):
    specs = [VMEM] * n_in
    if smem_first:
        specs[0] = SMEM
    more.setdefault("in_specs", specs)
    more.setdefault("out_specs", jax.tree.map(lambda _: VMEM, outs))
    return pl.pallas_call(
        kernel,
        out_shape=outs,
        scratch_shapes=scratch,
        compiler_params=pltpu.CompilerParams(vmem_limit_bytes=limit * MIB),
        cost_estimate=pl.CostEstimate(flops=flops, bytes_accessed=4 * MIB, transcendentals=0),
        **more,
    )


def predict(blended, bands, shape, parts, part, before):
    chans, height, span = shape
    rows = height // parts
    block = pl.BlockSpec((chans, rows, span), lambda i: (0, part, 0))
    whole = lambda a: pl.BlockSpec(a.shape, lambda i: (0,) * a.ndim)
    args = (blended, bands)
    specs = [whole(a) for a in args]
    more = {}
    if before is not None:
        args += (before,)
        specs.append(pl.BlockSpec(memory_space=pl.ANY))
        more["input_output_aliases"] = {2: 0}
    return call(
        functools.partial(predict_kernel, part),
        jax.ShapeDtypeStruct(shape, BF16),
        [
            pltpu.VMEM((chans * rows, span), BF16),
        ],
        len(args),
        12,
        flops=10**9,
        grid=(1,),
        in_specs=specs,
        out_specs=block,
        **more,
    )(*args)


def bf(*shape):
    return jax.ShapeDtypeStruct(shape, BF16)


def swapped(messages, axis):
    pairs = [p for p in swaps(lax.axis_size(axis)) if p]
    return [lax.ppermute(m, axis, p) for m, p in zip(messages, pairs)]


def pack_rows(index, skip, size, shifts, feat, counted=False):
    message = bf(size, feat.shape[2])
    if counted:
        message = (message, jax.ShapeDtypeStruct((8, TILE), jnp.int32))
    return call(
        functools.partial(feature_kernel, index, skip),
        message, [], 2, 16, smem_first=True,
    )(shifts, feat)


def main_pass(rest, lent, shifts, feat, sides, act_grad, views, bands):
    chans, height, span = feat.shape
    width = span + TILE
    full = height * chans
    groups = height // POOL
    band = 3 * (POOL + 2) * chans
    if rest:
        size = lent[0].shape[0]
        more = swapped([pack_rows(i, size, rest, shifts, feat) for i in (0, 1)], "rows")
        lent = [jnp.concatenate(pair, axis=0) for pair in zip(lent, more)]
    size = lent[0].shape[0]
    tall = pl.cdiv(height + 2 * EXT, 16) * 16
    grads, blended = call(
        main_kernel,
        (jax.ShapeDtypeStruct((9 * chans // 2, TILE), F32), bf((height + 2) * chans, width)),
        [
            pltpu.VMEM((2, size + 48, span), BF16),
            pltpu.VMEM((chans, tall, width), BF16),
        ]
        + [pltpu.VMEM((tall * chans, width), BF16)] * 3
        + [pltpu.VMEM(((height + 4 * POOL) * chans, width), BF16)]
        + [pltpu.VMEM(((groups + 4) * chans, width), BF16)] * 3
        + [
            pltpu.VMEM((full, span), BF16),
            pltpu.VMEM((band, POOL * chans), F32),
        ],
        11,
        32,
        flops=10**10,
        smem_first=True,
    )(
        shifts, feat, *lent, sides, act_grad, *views, *bands
    )

    return grads, blended


def shards(features, shifts, first_kernel, bottle_kernel, second_kernel, cotangent):
    imgs, chans, height, span = features.shape
    rows, cols, dp = (lax.axis_size(a) for a in ("rows", "cols", "dp"))
    full = height * chans

    width = span + TILE
    groups = height // POOL
    feat, cot, shifts = features[0], cotangent[0], shifts[0]
    row_pairs = swaps(rows)

    usual = USUAL * chans
    message, total = pack_rows(0, 0, usual, shifts, feat, counted=True)
    message, total, cot = lax.optimization_barrier((message, total, cot))
    feat_a = lax.ppermute(message, "rows", row_pairs[0])
    bit = 1
    while bit < dp:
        total = jnp.maximum(total, lax.ppermute(total, "dp", [(i, i ^ bit) for i in range(dp)]))
        bit *= 2

    packed = chans * (height * SLOT // TILE)
    messages = call(
        column_kernel, (bf(packed, TILE),) * (1 if cols == 2 else 2), [], 2, 8, flops=2 * 10**10
    )(feat, cot)
    col_msgs = swapped(messages, "cols")
    ncols = len(col_msgs)
    message = pack_rows(1, 0, usual, shifts, feat)
    col_msgs, message, total = lax.optimization_barrier((col_msgs, message, total))
    feat_b = lax.ppermute(message, "rows", row_pairs[1])
    cot_rows = call(rows_kernel, bf(full, span), [], 1, 4)(cot)
    halo = bf(CHALO * chans + ncols * packed * TILE // span, span)
    messages = call(edge_kernel, (halo, halo), [], 1 + ncols, 8)(cot_rows, *col_msgs)
    row_msgs = swapped(messages, "rows")
    row_msgs, feat_a = lax.optimization_barrier((row_msgs, feat_a))

    tall_c = (height + 2 * CHALO) * chans
    view = bf((height + 2) * chans, span)
    band = 3 * (POOL + 2) * chans
    act_grad, *rest = call(
        functools.partial(back_kernel, ncols),
        (
            jax.ShapeDtypeStruct((full, span), F32), view, view, view,
            bf(chans, 3 * height, TILE), bf(POOL * chans, band), bf(3 * chans, 3 * chans),
            bf(3 * POOL * chans, (POOL + 2) * chans),
        ),
        [pltpu.VMEM((tall_c, width), BF16)] * 3
        + [pltpu.VMEM(((height + 2 * POOL) * chans, span), BF16)]
        + [pltpu.VMEM(((groups + 2) * chans, width), BF16)] * 3
        + [
            pltpu.VMEM((band, POOL * chans), F32),
            pltpu.VMEM((POOL * chans, band), BF16),
            pltpu.VMEM((9 * chans, TILE), F32),
            pltpu.VMEM((3 * chans, 3 * chans), BF16),
            pltpu.VMEM((chans, 9 * chans), F32),
        ],
        6 + ncols,
        16,
        flops=8 * 10**9,
    )(cot_rows, *row_msgs, *col_msgs, first_kernel, bottle_kernel, second_kernel)
    views, sides, weights = rest[:3], rest[3], rest[4:]

    grads, blended = lax.cond(
        total[0, 0] <= usual,
        functools.partial(main_pass, 0),
        functools.partial(main_pass, LARGEST * chans - usual),
        (feat_a, feat_b), shifts, feat, sides, act_grad, tuple(views), tuple(weights[:2]),
    )

    steps = []
    for axis, size in (("dp", dp), ("cols", cols), ("rows", rows)):
        bit = 1
        while bit < size:
            steps.append((axis, [(i, i ^ bit) for i in range(size)]))
            bit *= 2
    parts, prediction = 2, None
    for step, (axis, pairs) in enumerate(steps):
        other = lax.ppermute(grads, axis, pairs)
        if 1 <= step <= parts:
            prediction = predict(
                blended, weights[2], (chans, height, span), parts, step - 1, prediction
            )
            other, prediction = lax.optimization_barrier((other, prediction))
        if step < len(steps) - 1:
            grads = grads + other
            if step < parts:
                grads, blended = lax.optimization_barrier((grads, blended))
    factor = 1.0 / math.sqrt(imgs * dp * height * rows * span * cols)
    shape = jax.ShapeDtypeStruct((9, chans, chans), F32)
    first_grad, second_grad = call(
        functools.partial(final_kernel, factor), (shape, shape), [], 2, 2
    )(grads, other)
    return (prediction[None], first_grad, second_grad)


def solution(mesh):
    placed = (
        P("dp", None, "rows", "cols"),
        P("dp", None, None),
        P(),
        P(),
        P(),
        P("dp", None, "rows", "cols"),
    )
    return jax.shard_map(
        shards,
        mesh=mesh,
        in_specs=placed,
        out_specs=(P("dp", None, "rows", "cols"), P(), P()),
        check_vma=False,
    )
```

```python
import functools
import math

import jax
import jax.numpy as jnp
from jax import lax
from jax.experimental import pallas as pl
from jax.experimental.pallas import tpu as pltpu
from jax.sharding import PartitionSpec as P


MAXSHIFT = 16
POOL = 4
TILE = 128
SLOT = 32
EXT = 9
FHALO = MAXSHIFT + EXT
USUAL = 14
LARGEST = FHALO + 1
CHALO = 5
F32 = jnp.float32
BF16 = jnp.bfloat16
VMEM = pl.BlockSpec(memory_space=pltpu.VMEM)
SMEM = pl.BlockSpec(memory_space=pltpu.SMEM)
MIB = 1024 * 1024


def lanes_of(shape):
    return lax.broadcasted_iota(jnp.int32, shape, len(shape) - 1)


def turn(values, shift):
    width = values.shape[-1]
    if isinstance(shift, int):
        shift = shift % width
        if shift == 0:
            return values
    return pltpu.roll(values, shift, values.ndim - 1)


def has_sides():
    row, col = lax.axis_index("rows"), lax.axis_index("cols")
    return (
        row > 0,
        row < lax.axis_size("rows") - 1,
        col > 0,
        col < lax.axis_size("cols") - 1,
    )


def rows_at(r, chans, count=1):
    if isinstance(r, int):
        return slice(r * chans, (r + count) * chans)
    return pl.ds(pl.multiple_of(r * chans, chans), count * chans)


def to_rows(block):
    chans, height, span = block.shape
    return jnp.transpose(block, (1, 0, 2)).reshape(height * chans, span)


def to_planes(block, chans):
    height = block.shape[0] // chans
    return jnp.transpose(block.reshape(height, chans, block.shape[1]), (1, 0, 2))


def tiles_of(span):
    return [slice(t, t + TILE) for t in range(0, span, TILE)]


def is_even(axis):
    return lax.rem(lax.axis_index(axis), 2) == 0


def swaps(size):
    first = [(i, i ^ 1) for i in range(size)]
    second = [(i, i + 1) for i in range(1, size - 1, 2)]
    return [first, second + [(j, i) for i, j in second]]


def needed(shift, below):
    return jnp.maximum(EXT + shift if below else EXT - shift, 0)


def feature_kernel(index, skip, shifts, feat, msg, *counts):
    chans, height, span = feat.shape
    full = chans * height
    size = msg.shape[0]
    chunk = size // 4
    source = feat[...].reshape(full, span)
    lane = lanes_of((8, full))
    chan, row = lane // height, lane % height
    to_below = is_even("rows") if index == 0 else jnp.logical_not(is_even("rows"))
    target = jnp.full((8, full), -1, jnp.int32)
    at, up, down = jnp.int32(-skip), jnp.int32(0), jnp.int32(0)
    for c in range(chans):
        shift = shifts[0, c]
        n_up, n_down = needed(shift, False), needed(shift, True)
        count = jnp.where(to_below, n_up, n_down)
        first = jnp.where(to_below, height - count, 0)
        mine = (chan == c) & (row >= first) & (row < first + count)
        target = jnp.where(mine, row + (at - first), target)
        at, up, down = at + count, up + n_up, down + n_down
    for out in counts:
        out[...] = jnp.full(out.shape, jnp.maximum(up, down), jnp.int32)
    for p in range(0, size, chunk):
        place = lax.broadcasted_iota(jnp.int32, (chunk, full), 0) + p
        pick = jnp.where(place == target[0:1], 1.0, 0.0).astype(BF16)
        msg[p : p + chunk] = jnp.dot(pick, source, preferred_element_type=F32).astype(BF16)


def rows_kernel(source, out):
    for part in tiles_of(source.shape[2]):
        out[:, part] = to_rows(source[:, :, part])


def edge_lanes(shape, right, count):
    lane = lanes_of(shape)
    return jnp.where(jnp.where(right, TILE - 1 - lane, lane) < count, 1.0, 0.0).astype(BF16)


def slots(chans, height):
    half, block = chans // 2, height // 2
    for h in (0, 1):
        for m in (0, 1):
            yield 2 * h + m, slice(h * half, (h + 1) * half), slice(m * block, (m + 1) * block)


def column_kernel(feat, cot, *col_msgs):
    chans, height, span = feat.shape
    for index, msg in enumerate(col_msgs):
        right = is_even("cols") if index == 0 else jnp.logical_not(is_even("cols"))
        part = pl.ds(pl.multiple_of(jnp.where(right, span - TILE, 0), TILE), TILE)
        shape = (1, height // 2, TILE)
        inner = edge_lanes(shape, right, FHALO)
        outer = edge_lanes(shape, right, SLOT) - inner
        total = None
        for q, channels, rows in slots(chans, height):
            cots = turn(cot[channels, rows, part], jnp.where(right, TILE - FHALO, FHALO))
            piece = feat[channels, rows, part] * inner + cots * outer
            piece = turn(piece, jnp.where(right, (q + 1) * SLOT % TILE, q * SLOT))
            total = piece if total is None else total + piece
        msg[...] = total.reshape(msg.shape)


def edge_kernel(cot_rows, *rest):
    cols, (msg_a, msg_b) = rest[:-2], rest[-2:]
    span = cot_rows.shape[1]
    size = msg_a.shape[0] - sum(c.shape[0] * TILE // span for c in cols)
    edge = cot_rows.shape[0] - size
    chans = size // CHALO
    low = jnp.where(is_even("rows"), edge, 0)
    msg_a[0:size] = cot_rows[pl.ds(pl.multiple_of(low, chans), size), :]
    msg_b[0:size] = cot_rows[pl.ds(pl.multiple_of(edge - low, chans), size), :]
    at = size
    for col in cols:
        count = col.shape[0] * TILE // span
        for t, part in enumerate(tiles_of(span)):
            block = col[t * count : (t + 1) * count]
            msg_a[at : at + count, part] = block
            msg_b[at : at + count, part] = block
        at += count


def corner_views(msg, size, cols):
    span = msg.shape[1]
    views, at = [], size
    for col in cols:
        count = col.shape[0] * TILE // span
        views.append(
            jnp.concatenate([msg[at : at + count, part] for part in tiles_of(span)], axis=0)
        )
        at += count
    return views


def halo_block(sources, slot, rows, kind):
    total = None
    if kind == "features":
        count, shift_r, shift_l = FHALO, -slot * SLOT, TILE - (slot + 1) * SLOT
    else:
        count = CHALO
        shift_r, shift_l = -slot * SLOT - FHALO, TILE - (slot + 1) * SLOT + FHALO
    for index, source in enumerate(sources):
        from_right = is_even("cols") if index == 0 else jnp.logical_not(is_even("cols"))
        block = source.reshape(source.shape[0] // rows, rows, TILE)
        block = turn(block, jnp.where(from_right, shift_r % TILE, shift_l % TILE))
        block = block * edge_lanes((1, rows, TILE), jnp.logical_not(from_right), count)
        total = block if total is None else total + block
    return total


def halo_rows(sources, m, rows, kind):
    return to_rows(
        jnp.concatenate([halo_block(sources, 2 * h + m, rows, kind) for h in (0, 1)], axis=0)
    )


def columns_seen(shape, span):
    _, _, has_left, has_right = has_sides()
    lane = lanes_of(shape)
    middle = span + TILE // 2
    return (lane < span) | ((lane < middle) & has_right) | ((lane >= middle) & has_left)


def block_ones(width):
    row = lax.broadcasted_iota(jnp.int32, (width, width), 0) // POOL
    col = lax.broadcasted_iota(jnp.int32, (width, width), 1) // POOL
    return jnp.where(row == col, 1.0, 0.0).astype(BF16)


def store_split(high, low, at, total):
    top = total.astype(BF16)
    high[at, :] = top
    low[at, :] = (total - top.astype(F32)).astype(BF16)


def block_sums(high, low, ones):
    return jnp.dot(high[...], ones, preferred_element_type=F32) + jnp.dot(
        low[...], ones, preferred_element_type=F32
    )


def fill_bands(out, kernel, count):
    chans = kernel.shape[1]
    out[...] = jnp.zeros(out.shape, out.dtype)
    for k in range(count):
        for b in range(3):
            for a in range(3):
                at = (b * (count + 2) + k + a) * chans
                out[k * chans : (k + 1) * chans, at : at + chans] = kernel[3 * a + b].astype(
                    out.dtype
                )


def fill_turned_bands(out, kernel, count):
    chans = kernel.shape[1]
    out[...] = jnp.zeros(out.shape, out.dtype)
    for k in range(count):
        for b in range(3):
            for a in range(3):
                at = (b * (count + 2) + k + a) * chans
                out[at : at + chans, k * chans : (k + 1) * chans] = kernel[8 - 3 * a - b].astype(
                    out.dtype
                )


def stacked(views, at):
    return jnp.concatenate([view[at, :] for view in views], axis=0)


def conv_sum(parts, chans, step):
    return (
        turn(parts[0:chans], step)
        + parts[chans : 2 * chans]
        + turn(parts[2 * chans : 3 * chans], -step)
    )


def back_kernel(
    ncols, cot, msg_a, msg_b, *rest,
):
    cols, (
        first, bottle, second,
        act_grad, cot_m, cot_0, cot_p, sides, first_bands, bottle_bands, second_bands,
        back, high, low, coarse, bands_f, bands, small_f, small, wide_f,
    ) = rest[:ncols], rest[ncols:]
    chans = second.shape[1]
    full, span = cot.shape
    height = full // chans
    width = span + TILE
    groups = height // POOL
    has_up, has_down, _, _ = has_sides()
    seen_cols = columns_seen((chans, width), span)

    fill_turned_bands(bands_f, second, POOL)
    bands[...] = bands_f[...].T.astype(BF16)
    fill_turned_bands(small_f, bottle, 1)
    small_t = small_f[...].T
    for b in range(3):
        small[rows_at(b, chans)] = small_t[0:chans, 3 * b * chans : 3 * (b + 1) * chans].astype(BF16)
    fill_bands(first_bands, first, POOL)
    fill_bands(wide_f, bottle, 1)
    for b in range(3):
        bottle_bands[rows_at(b, chans)] = wide_f[
            0:chans, 3 * b * chans : 3 * (b + 1) * chans
        ].astype(BF16)
    second_bands[...] = jnp.zeros(second_bands.shape, BF16)
    for k in range(POOL):
        for b in range(3):
            for a in range(3):
                second_bands[
                    rows_at(3 * k + b, chans), (k + a) * chans : (k + a + 1) * chans
                ] = second[3 * a + b]

    size = CHALO * chans
    block = height // 2

    def halo_columns(sources, at):
        for q, channels, rows in slots(chans, height):
            sides[channels, at + rows.start : at + rows.stop, :] = halo_block(
                sources, q, block, "features"
            )

    own = [c[...] for c in cols]
    halo_columns(own, height)
    cot_0[rows_at(CHALO, chans, height), 0:span] = cot[...]
    for m in (0, 1):
        cot_0[rows_at(CHALO + m * block, chans, block), span:width] = halo_rows(
            own, m, block, "cotangent"
        )

    def vertical(up, down):
        cot_0[rows_at(0, chans, CHALO), 0:span] = up[0:size]
        cot_0[rows_at(CHALO + height, chans, CHALO), 0:span] = down[0:size]
        above, below = corner_views(up, size, cols), corner_views(down, size, cols)
        cot_0[rows_at(0, chans, CHALO), span:width] = halo_rows(above, 1, block, "cotangent")[
            (block - CHALO) * chans :
        ]
        cot_0[rows_at(CHALO + height, chans, CHALO), span:width] = halo_rows(
            below, 0, block, "cotangent"
        )[0:size]
        halo_columns(above, 0)
        halo_columns(below, 2 * height)

    pl.when(is_even("rows"))(lambda: vertical(msg_b, msg_a))
    pl.when(jnp.logical_not(is_even("rows")))(lambda: vertical(msg_a, msg_b))
    for j in range(height + 2 * CHALO):
        at = rows_at(j, chans)
        cot_m[at] = turn(cot_0[at], 1)
        cot_p[at] = turn(cot_0[at], -1)
    def group(g, _):
        at = rows_at(g * POOL, chans, POOL + 2)
        rows = jnp.dot(
            bands[...], stacked((cot_m, cot_0, cot_p), at), preferred_element_type=F32
        ).astype(BF16)
        back[rows_at(g * POOL, chans, POOL), :] = rows[:, 0:span]
        rows = rows.astype(F32)
        total = rows[0:chans]
        for k in range(1, POOL):
            total = total + rows[k * chans : (k + 1) * chans]
        store_split(high, low, rows_at(g, chans), total)
        return 0

    lax.fori_loop(0, groups + 2, group, 0, unroll=5)
    sums = block_sums(high, low, block_ones(width))
    for g in range(groups + 2):
        at = rows_at(g, chans)
        seen = seen_cols
        if g == 0:
            seen = seen & has_up
        elif g == groups + 1:
            seen = seen & has_down
        coarse[at] = jnp.where(seen, sums[at], 0.0).astype(BF16)
    for g in range(groups):
        parts = jnp.dot(small[...], coarse[rows_at(g, chans, 3), :], preferred_element_type=F32)
        mean = conv_sum(parts, chans, POOL)[:, 0:span] * (1.0 / POOL**2)
        for k in range(POOL):
            r = g * POOL + k
            act_grad[rows_at(r, chans), :] = back[rows_at(r + POOL, chans), :].astype(F32) + mean


def correlate(u, u0, views, v0, acc, height, chans, span):
    groups = range(0, height, POOL)
    left = jnp.concatenate(
        [
            jnp.concatenate(
                [view[rows_at(v0 + g, chans, POOL + 2), 0:span] for view in views], axis=0
            )
            for g in groups
        ],
        axis=1,
    )
    right = jnp.concatenate([u[rows_at(u0 + g, chans, POOL), 0:span] for g in groups], axis=1)
    acc[...] = lax.dot_general(
        left, right, (((1,), (1,)), ((), ())), preferred_element_type=F32
    )


def folded(acc, chans):
    lane = lanes_of((3 * chans, TILE))
    result = jnp.zeros((3 * chans, TILE), F32)
    for b in range(3):
        total = None
        for k in range(POOL):
            block = turn(
                acc[rows_at(b * (POOL + 2) + k, chans, 3), 0:TILE], (b - k) * chans
            )
            total = block if total is None else total + block
        result = jnp.where((lane >= b * chans) & (lane < (b + 1) * chans), total, result)
    return result


def main_kernel(
    shifts, feat, feat_a, feat_b, sides, act_grad, view_m, view_0, view_p, bands, small,
    grads, blended,
    lent, moved, warp_m, warp_0, warp_p, act, high, low, pooled, pre_grad, acc,
):
    chans, height, span = feat.shape
    tiles = span // TILE
    width = span + TILE
    groups = height // POOL
    has_up, has_down, has_left, has_right = has_sides()
    seen_cols = columns_seen((chans, width), span)

    size = feat_a.shape[0]
    window = lent.shape[1] - size
    lent[:, size:, :] = jnp.zeros((2, window, span), BF16)

    def borrow(up, down):
        lent[0, 0:size] = up[...]
        lent[1, 0:size] = down[...]

    pl.when(is_even("rows"))(lambda: borrow(feat_b, feat_a))
    pl.when(jnp.logical_not(is_even("rows")))(lambda: borrow(feat_a, feat_b))

    tall = moved.shape[1]
    lane = lanes_of((tall, TILE))
    seen_halo = ((lane < TILE // 2) & has_right) | ((lane >= TILE // 2) & has_left)
    step = lanes_of((tall, 3 * height)) - lax.broadcasted_iota(jnp.int32, (tall, 3 * height), 0)
    depth = 2 * window + height
    source = lanes_of((1, depth))
    apart = lax.broadcasted_iota(jnp.int32, (tall, depth), 0) - lanes_of((tall, depth))
    align = 16

    def warp(c, ats):
        at_up, at_down = ats
        shift, move = shifts[0, c], shifts[1, c]
        n_up, n_down = needed(shift, False), needed(shift, True)
        base_up, base_down = (
            pl.multiple_of(lax.div(at, align) * align, align) for at in (at_up, at_down)
        )
        skip_up, skip_down = at_up - base_up, at_down - base_down
        own = EXT - window - shift
        below = own - skip_down
        above = EXT - skip_up - n_up - shift
        in_up = (source >= skip_up) & (source < skip_up + n_up)
        first_down = window + height + skip_down
        in_down = (source >= first_down) & (source < first_down + n_down)
        none = 4 * depth
        offset = jnp.where(
            source < window,
            jnp.where(in_up, above, none),
            jnp.where(source < window + height, own, jnp.where(in_down, below, none)),
        )
        pick = jnp.where(apart == offset, 1.0, 0.0).astype(BF16)
        rows = jnp.concatenate(
            [lent[0, pl.ds(base_up, window), :], feat[c], lent[1, pl.ds(base_down, window), :]], axis=0
        )
        plane = jnp.dot(pick, rows, preferred_element_type=F32)
        pick = jnp.where(step == height - EXT + shift, 1.0, 0.0).astype(BF16)
        plane = [plane[:, part] for part in tiles_of(span)]
        plane.append(jnp.dot(pick, sides[c], preferred_element_type=F32))
        amount = jnp.where(move > 0, TILE - move, -move)
        parts = [turn(part, amount) for part in plane]
        inside = jnp.where(move > 0, lane, TILE - 1 - lane) < TILE - jnp.abs(move)
        for t, part in enumerate(tiles_of(width)):
            after, before = parts[(t + 1) % (tiles + 1)], parts[t - 1]
            result = jnp.where(inside, parts[t], jnp.where(move > 0, after, before))
            if t == tiles:
                result = jnp.where(seen_halo, result, 0.0)
            moved[c, :, part] = result.astype(BF16)
        return at_up + n_up, at_down + n_down

    lax.fori_loop(0, chans, warp, (jnp.int32(0), jnp.int32(0)), unroll=8)
    chunk = 16
    for r in range(0, tall, chunk):
        for part in tiles_of(width):
            warp_0[rows_at(r, chans, chunk), part] = to_rows(moved[:, r : r + chunk, part])

    def clear(r, count):
        warp_0[rows_at(r, chans, count)] = jnp.zeros((count * chans, width), BF16)

    pl.when(jnp.logical_not(has_up))(lambda: clear(0, EXT))
    pl.when(jnp.logical_not(has_down))(lambda: clear(EXT + height, EXT))
    for j in range(height + 2 * EXT):
        at = rows_at(j, chans)
        warp_m[at] = turn(warp_0[at], 1)
        warp_p[at] = turn(warp_0[at], -1)

    def first_group(g, own):
        at = rows_at(g * POOL, chans, POOL + 2)
        pre = jnp.dot(
            bands[...], stacked((warp_m, warp_0, warp_p), at), preferred_element_type=F32
        )
        sigma = 0.5 * jnp.tanh(0.5 * pre) + 0.5
        rows = (pre * sigma).astype(BF16)
        act[rows_at(g * POOL, chans, POOL), :] = rows
        rows = rows.astype(F32)
        total = rows[0:chans]
        for k in range(1, POOL):
            total = total + rows[k * chans : (k + 1) * chans]
        store_split(high, low, rows_at(g, chans), total)
        if own:
            there = rows_at(g * POOL - 2 * POOL, chans, POOL)
            pre, sigma = pre[:, 0:span], sigma[:, 0:span]
            pre_grad[there, :] = (
                act_grad[there, :] * (sigma * (1.0 + pre * (1.0 - sigma)))
            ).astype(BF16)
        return 0

    for g in (0, 1, groups + 2, groups + 3):
        first_group(g, False)
    lax.fori_loop(2, groups + 2, lambda g, _: first_group(g, True), 0, unroll=4)
    sums = block_sums(high, low, block_ones(width))
    for g in range(groups + 4):
        at = rows_at(g, chans)
        seen = seen_cols
        if g < 2:
            seen = seen & has_up
        elif g >= groups + 2:
            seen = seen & has_down
        pooled[at] = jnp.where(seen, sums[at] * (1.0 / POOL**2), 0.0).astype(BF16)

    for g in range(groups + 2):
        parts = jnp.dot(small[...], pooled[rows_at(g, chans, 3), :], preferred_element_type=F32)
        bottle_row = conv_sum(parts, chans, POOL)
        rows, seen = range(POOL), seen_cols
        if g == 0:
            rows, seen = (POOL - 1,), seen & has_up
        elif g == groups + 1:
            rows, seen = (0,), seen & has_down
        for k in rows:
            row = act[rows_at((g + 1) * POOL + k, chans), :].astype(F32) + bottle_row
            blended[rows_at(g * POOL + k - POOL + 1, chans), :] = jnp.where(seen, row, 0.0).astype(
                BF16
            )

    correlate(pre_grad, 0, (warp_m, warp_0, warp_p), EXT - 1, acc, height, chans, span)
    first_part = folded(acc, chans)
    correlate(blended, 1, (view_m, view_0, view_p), CHALO - 1, acc, height, chans, span)
    second_part = folded(acc, chans)
    lane = lanes_of((3 * chans, TILE))
    grads[0 : 3 * chans] = jnp.where(lane < 3 * chans, first_part, turn(second_part, 3 * chans))
    half = 3 * chans // 2
    grads[3 * chans :] = jnp.where(
        lane[0:half] < TILE // 2,
        turn(second_part[0:half], -chans),
        turn(second_part[half:], TILE // 2 - chans),
    )


def predict_kernel(part, blended, bands, *rest):
    out, rows = rest[-2:]
    chans, height, span = out.shape

    def group(g, _):
        at = rows_at(part * height + g * POOL, chans, POOL + 2)
        parts = jnp.dot(bands[...], blended[at, :], preferred_element_type=F32)
        for k in range(POOL):
            row = conv_sum(parts[3 * k * chans : 3 * (k + 1) * chans], chans, 1)
            rows[rows_at(g * POOL + k, chans), :] = row[:, 0:span].astype(BF16)
        return 0

    lax.fori_loop(0, height // POOL, group, 0, unroll=2)
    for part in tiles_of(span):
        out[:, :, part] = to_planes(rows[:, part], chans)


def final_kernel(factor, mine, other, first, second):
    chans = first.shape[1]
    total = (mine[...] + other[...]) * factor
    turned = total[0 : 3 * chans].T
    for b in range(3):
        for a in range(3):
            first[3 * a + b] = turned[b * chans : (b + 1) * chans, a * chans : (a + 1) * chans]
    half = 3 * chans // 2
    low = total[3 * chans :]
    both = jnp.concatenate([low, turn(low, -(TILE // 2))], axis=0)
    for a in range(3):
        at = slice((2 - a) * chans, (3 - a) * chans)
        second[3 * a + 2] = turn(total[at], -3 * chans)[:, 0:chans]
        second[3 * a + 1] = both[at, 0:chans]
        second[3 * a + 0] = turn(both[at], -chans)[:, 0:chans]


def call(kernel, outs, scratch, n_in, limit, flops=0, smem_first=False, **more):
    specs = [VMEM] * n_in
    if smem_first:
        specs[0] = SMEM
    more.setdefault("in_specs", specs)
    more.setdefault("out_specs", jax.tree.map(lambda _: VMEM, outs))
    return pl.pallas_call(
        kernel,
        out_shape=outs,
        scratch_shapes=scratch,
        compiler_params=pltpu.CompilerParams(vmem_limit_bytes=limit * MIB),
        cost_estimate=pl.CostEstimate(flops=flops, bytes_accessed=4 * MIB, transcendentals=0),
        **more,
    )


def predict(blended, bands, shape, parts, part, before):
    chans, height, span = shape
    rows = height // parts
    block = pl.BlockSpec((chans, rows, span), lambda i: (0, part, 0))
    whole = lambda a: pl.BlockSpec(a.shape, lambda i: (0,) * a.ndim)
    args = (blended, bands)
    specs = [whole(a) for a in args]
    more = {}
    if before is not None:
        args += (before,)
        specs.append(pl.BlockSpec(memory_space=pl.ANY))
        more["input_output_aliases"] = {2: 0}
    return call(
        functools.partial(predict_kernel, part),
        jax.ShapeDtypeStruct(shape, BF16),
        [
            pltpu.VMEM((chans * rows, span), BF16),
        ],
        len(args),
        12,
        flops=10**9,
        grid=(1,),
        in_specs=specs,
        out_specs=block,
        **more,
    )(*args)


def bf(*shape):
    return jax.ShapeDtypeStruct(shape, BF16)


def swapped(messages, axis):
    pairs = [p for p in swaps(lax.axis_size(axis)) if p]
    return [lax.ppermute(m, axis, p) for m, p in zip(messages, pairs)]


def pack_rows(index, skip, size, shifts, feat, counted=False):
    message = bf(size, feat.shape[2])
    if counted:
        message = (message, jax.ShapeDtypeStruct((8, TILE), jnp.int32))
    return call(
        functools.partial(feature_kernel, index, skip),
        message, [], 2, 16, smem_first=True,
    )(shifts, feat)


def main_pass(rest, lent, shifts, feat, sides, act_grad, views, bands):
    chans, height, span = feat.shape
    width = span + TILE
    full = height * chans
    groups = height // POOL
    band = 3 * (POOL + 2) * chans
    if rest:
        size = lent[0].shape[0]
        more = swapped([pack_rows(i, size, rest, shifts, feat) for i in (0, 1)], "rows")
        lent = [jnp.concatenate(pair, axis=0) for pair in zip(lent, more)]
    size = lent[0].shape[0]
    tall = pl.cdiv(height + 2 * EXT, 16) * 16
    grads, blended = call(
        main_kernel,
        (jax.ShapeDtypeStruct((9 * chans // 2, TILE), F32), bf((height + 2) * chans, width)),
        [
            pltpu.VMEM((2, size + 48, span), BF16),
            pltpu.VMEM((chans, tall, width), BF16),
        ]
        + [pltpu.VMEM((tall * chans, width), BF16)] * 3
        + [pltpu.VMEM(((height + 4 * POOL) * chans, width), BF16)]
        + [pltpu.VMEM(((groups + 4) * chans, width), BF16)] * 3
        + [
            pltpu.VMEM((full, span), BF16),
            pltpu.VMEM((band, POOL * chans), F32),
        ],
        11,
        20,
        flops=10**10,
        smem_first=True,
    )(
        shifts, feat, *lent, sides, act_grad, *views, *bands
    )

    return grads, blended


def shards(features, shifts, first_kernel, bottle_kernel, second_kernel, cotangent):
    imgs, chans, height, span = features.shape
    rows, cols, dp = (lax.axis_size(a) for a in ("rows", "cols", "dp"))
    full = height * chans

    width = span + TILE
    groups = height // POOL
    feat, cot, shifts = features[0], cotangent[0], shifts[0].T
    row_pairs = swaps(rows)

    usual = USUAL * chans
    message, total = pack_rows(0, 0, usual, shifts, feat, counted=True)
    message, total, cot = lax.optimization_barrier((message, total, cot))
    feat_a = lax.ppermute(message, "rows", row_pairs[0])
    bit = 1
    while bit < dp:
        total = jnp.maximum(total, lax.ppermute(total, "dp", [(i, i ^ bit) for i in range(dp)]))
        bit *= 2

    packed = chans * (height * SLOT // TILE)
    messages = call(
        column_kernel, (bf(packed, TILE),) * (1 if cols == 2 else 2), [], 2, 8, flops=2 * 10**10
    )(feat, cot)
    col_msgs = swapped(messages, "cols")
    ncols = len(col_msgs)
    message = pack_rows(1, 0, usual, shifts, feat)
    col_msgs, message, total = lax.optimization_barrier((col_msgs, message, total))
    feat_b = lax.ppermute(message, "rows", row_pairs[1])
    cot_rows = call(rows_kernel, bf(full, span), [], 1, 4)(cot)
    halo = bf(CHALO * chans + ncols * packed * TILE // span, span)
    messages = call(edge_kernel, (halo, halo), [], 1 + ncols, 8)(cot_rows, *col_msgs)
    row_msgs = swapped(messages, "rows")
    row_msgs, feat_a = lax.optimization_barrier((row_msgs, feat_a))

    tall_c = (height + 2 * CHALO) * chans
    view = bf(tall_c, width)
    band = 3 * (POOL + 2) * chans
    act_grad, *rest = call(
        functools.partial(back_kernel, ncols),
        (
            jax.ShapeDtypeStruct((full, span), F32), view, view, view,
            bf(chans, 3 * height, TILE), bf(POOL * chans, band), bf(3 * chans, 3 * chans),
            bf(3 * POOL * chans, (POOL + 2) * chans),
        ),
        [pltpu.VMEM(((height + 2 * POOL) * chans, span), BF16)]
        + [pltpu.VMEM(((groups + 2) * chans, width), BF16)] * 3
        + [
            pltpu.VMEM((band, POOL * chans), F32),
            pltpu.VMEM((POOL * chans, band), BF16),
            pltpu.VMEM((9 * chans, TILE), F32),
            pltpu.VMEM((3 * chans, 3 * chans), BF16),
            pltpu.VMEM((chans, 9 * chans), F32),
        ],
        6 + ncols,
        16,
        flops=8 * 10**9,
    )(cot_rows, *row_msgs, *col_msgs, first_kernel, bottle_kernel, second_kernel)
    views, sides, weights = rest[:3], rest[3], rest[4:]

    grads, blended = lax.cond(
        total[0, 0] <= usual,
        functools.partial(main_pass, 0),
        functools.partial(main_pass, LARGEST * chans - usual),
        (feat_a, feat_b), shifts, feat, sides, act_grad, tuple(views), tuple(weights[:2]),
    )

    steps = []
    for axis, size in (("dp", dp), ("cols", cols), ("rows", rows)):
        bit = 1
        while bit < size:
            steps.append((axis, [(i, i ^ bit) for i in range(size)]))
            bit *= 2
    parts, prediction = 2, None
    for step, (axis, pairs) in enumerate(steps):
        other = lax.ppermute(grads, axis, pairs)
        if 1 <= step <= parts:
            prediction = predict(
                blended, weights[2], (chans, height, span), parts, step - 1, prediction
            )
            other, prediction = lax.optimization_barrier((other, prediction))
        if step < len(steps) - 1:
            grads = grads + other
            if step < parts:
                grads, blended = lax.optimization_barrier((grads, blended))
    factor = 1.0 / math.sqrt(imgs * dp * height * rows * span * cols)
    shape = jax.ShapeDtypeStruct((9, chans, chans), F32)
    first_grad, second_grad = call(
        functools.partial(final_kernel, factor), (shape, shape), [], 2, 2
    )(grads, other)
    return (prediction[None], first_grad, second_grad)


def solution(mesh):
    placed = (
        P("dp", None, "rows", "cols"),
        P("dp", None, None),
        P(),
        P(),
        P(),
        P("dp", None, "rows", "cols"),
    )
    return jax.shard_map(
        shards,
        mesh=mesh,
        in_specs=placed,
        out_specs=(P("dp", None, "rows", "cols"), P(), P()),
        check_vma=False,
    )
```

```python
import functools
import math

import jax
import jax.numpy as jnp
from jax import lax
from jax.experimental import pallas as pl
from jax.experimental.pallas import tpu as pltpu
from jax.sharding import PartitionSpec as P


MAXSHIFT = 16
POOL = 4
TILE = 128
SLOT = 32
EXT = 9
FHALO = MAXSHIFT + EXT
USUAL = 14
LARGEST = FHALO + 1
CHALO = 5
F32 = jnp.float32
BF16 = jnp.bfloat16
VMEM = pl.BlockSpec(memory_space=pltpu.VMEM)
SMEM = pl.BlockSpec(memory_space=pltpu.SMEM)
MIB = 1024 * 1024


def lanes_of(shape):
    return lax.broadcasted_iota(jnp.int32, shape, len(shape) - 1)


def turn(values, shift):
    width = values.shape[-1]
    if isinstance(shift, int):
        shift = shift % width
        if shift == 0:
            return values
    return pltpu.roll(values, shift, values.ndim - 1)


def has_sides():
    row, col = lax.axis_index("rows"), lax.axis_index("cols")
    return (
        row > 0,
        row < lax.axis_size("rows") - 1,
        col > 0,
        col < lax.axis_size("cols") - 1,
    )


def rows_at(r, chans, count=1):
    if isinstance(r, int):
        return slice(r * chans, (r + count) * chans)
    return pl.ds(pl.multiple_of(r * chans, chans), count * chans)


def to_rows(block):
    chans, height, span = block.shape
    return jnp.transpose(block, (1, 0, 2)).reshape(height * chans, span)


def to_planes(block, chans):
    height = block.shape[0] // chans
    return jnp.transpose(block.reshape(height, chans, block.shape[1]), (1, 0, 2))


def tiles_of(span):
    return [slice(t, t + TILE) for t in range(0, span, TILE)]


def is_even(axis):
    return lax.rem(lax.axis_index(axis), 2) == 0


def swaps(size):
    first = [(i, i ^ 1) for i in range(size)]
    second = [(i, i + 1) for i in range(1, size - 1, 2)]
    return [first, second + [(j, i) for i, j in second]]


def needed(shift, below):
    return jnp.maximum(EXT + shift if below else EXT - shift, 0)


def feature_kernel(index, skip, shifts, feat, msg, *counts):
    chans, height, span = feat.shape
    full = chans * height
    size = msg.shape[0]
    chunk = size // 4
    source = feat[...].reshape(full, span)
    lane = lanes_of((8, full))
    chan, row = lane // height, lane % height
    to_below = is_even("rows") if index == 0 else jnp.logical_not(is_even("rows"))
    target = jnp.full((8, full), -1, jnp.int32)
    at, up, down = jnp.int32(-skip), jnp.int32(0), jnp.int32(0)
    for c in range(chans):
        shift = shifts[0, c]
        n_up, n_down = needed(shift, False), needed(shift, True)
        count = jnp.where(to_below, n_up, n_down)
        first = jnp.where(to_below, height - count, 0)
        mine = (chan == c) & (row >= first) & (row < first + count)
        target = jnp.where(mine, row + (at - first), target)
        at, up, down = at + count, up + n_up, down + n_down
    for out in counts:
        out[...] = jnp.full(out.shape, jnp.maximum(up, down), jnp.int32)
    for p in range(0, size, chunk):
        place = lax.broadcasted_iota(jnp.int32, (chunk, full), 0) + p
        pick = jnp.where(place == target[0:1], 1.0, 0.0).astype(BF16)
        msg[p : p + chunk] = jnp.dot(pick, source, preferred_element_type=F32).astype(BF16)


def rows_kernel(source, out):
    for part in tiles_of(source.shape[2]):
        out[:, part] = to_rows(source[:, :, part])


def edge_lanes(shape, right, count):
    lane = lanes_of(shape)
    return jnp.where(jnp.where(right, TILE - 1 - lane, lane) < count, 1.0, 0.0).astype(BF16)


def slots(chans, height):
    half, block = chans // 2, height // 2
    for h in (0, 1):
        for m in (0, 1):
            yield 2 * h + m, slice(h * half, (h + 1) * half), slice(m * block, (m + 1) * block)


def column_kernel(feat, cot, *col_msgs):
    chans, height, span = feat.shape
    for index, msg in enumerate(col_msgs):
        right = is_even("cols") if index == 0 else jnp.logical_not(is_even("cols"))
        part = pl.ds(pl.multiple_of(jnp.where(right, span - TILE, 0), TILE), TILE)
        shape = (1, height // 2, TILE)
        inner = edge_lanes(shape, right, FHALO)
        outer = edge_lanes(shape, right, SLOT) - inner
        total = None
        for q, channels, rows in slots(chans, height):
            cots = turn(cot[channels, rows, part], jnp.where(right, TILE - FHALO, FHALO))
            piece = feat[channels, rows, part] * inner + cots * outer
            piece = turn(piece, jnp.where(right, (q + 1) * SLOT % TILE, q * SLOT))
            total = piece if total is None else total + piece
        msg[...] = total.reshape(msg.shape)


def edge_kernel(cot_rows, *rest):
    cols, (msg_a, msg_b) = rest[:-2], rest[-2:]
    span = cot_rows.shape[1]
    size = msg_a.shape[0] - sum(c.shape[0] * TILE // span for c in cols)
    edge = cot_rows.shape[0] - size
    chans = size // CHALO
    low = jnp.where(is_even("rows"), edge, 0)
    msg_a[0:size] = cot_rows[pl.ds(pl.multiple_of(low, chans), size), :]
    msg_b[0:size] = cot_rows[pl.ds(pl.multiple_of(edge - low, chans), size), :]
    at = size
    for col in cols:
        count = col.shape[0] * TILE // span
        for t, part in enumerate(tiles_of(span)):
            block = col[t * count : (t + 1) * count]
            msg_a[at : at + count, part] = block
            msg_b[at : at + count, part] = block
        at += count


def corner_views(msg, size, cols):
    span = msg.shape[1]
    views, at = [], size
    for col in cols:
        count = col.shape[0] * TILE // span
        views.append(
            jnp.concatenate([msg[at : at + count, part] for part in tiles_of(span)], axis=0)
        )
        at += count
    return views


def halo_block(sources, slot, rows, kind):
    total = None
    if kind == "features":
        count, shift_r, shift_l = FHALO, -slot * SLOT, TILE - (slot + 1) * SLOT
    else:
        count = CHALO
        shift_r, shift_l = -slot * SLOT - FHALO, TILE - (slot + 1) * SLOT + FHALO
    for index, source in enumerate(sources):
        from_right = is_even("cols") if index == 0 else jnp.logical_not(is_even("cols"))
        block = source.reshape(source.shape[0] // rows, rows, TILE)
        block = turn(block, jnp.where(from_right, shift_r % TILE, shift_l % TILE))
        block = block * edge_lanes((1, rows, TILE), jnp.logical_not(from_right), count)
        total = block if total is None else total + block
    return total


def halo_rows(sources, m, rows, kind):
    return to_rows(
        jnp.concatenate([halo_block(sources, 2 * h + m, rows, kind) for h in (0, 1)], axis=0)
    )


def columns_seen(shape, span):
    _, _, has_left, has_right = has_sides()
    lane = lanes_of(shape)
    middle = span + TILE // 2
    return (lane < span) | ((lane < middle) & has_right) | ((lane >= middle) & has_left)


def block_ones(width):
    row = lax.broadcasted_iota(jnp.int32, (width, width), 0) // POOL
    col = lax.broadcasted_iota(jnp.int32, (width, width), 1) // POOL
    return jnp.where(row == col, 1.0, 0.0).astype(BF16)


def store_split(high, low, at, total):
    top = total.astype(BF16)
    high[at, :] = top
    low[at, :] = (total - top.astype(F32)).astype(BF16)


def block_sums(high, low, ones):
    return jnp.dot(high[...], ones, preferred_element_type=F32) + jnp.dot(
        low[...], ones, preferred_element_type=F32
    )


def fill_bands(out, kernel, count):
    chans = kernel.shape[1]
    out[...] = jnp.zeros(out.shape, out.dtype)
    for k in range(count):
        for b in range(3):
            for a in range(3):
                at = (b * (count + 2) + k + a) * chans
                out[k * chans : (k + 1) * chans, at : at + chans] = kernel[3 * a + b].astype(
                    out.dtype
                )


def fill_turned_bands(out, kernel, count):
    chans = kernel.shape[1]
    out[...] = jnp.zeros(out.shape, out.dtype)
    for k in range(count):
        for b in range(3):
            for a in range(3):
                at = (b * (count + 2) + k + a) * chans
                out[at : at + chans, k * chans : (k + 1) * chans] = kernel[8 - 3 * a - b].astype(
                    out.dtype
                )


def stacked(views, at):
    return jnp.concatenate([view[at, :] for view in views], axis=0)


def conv_sum(parts, chans, step):
    return (
        turn(parts[0:chans], step)
        + parts[chans : 2 * chans]
        + turn(parts[2 * chans : 3 * chans], -step)
    )


def back_kernel(
    ncols, cot, msg_a, msg_b, *rest,
):
    cols, (
        first, bottle, second,
        act_grad, cot_m, cot_0, cot_p, sides, first_bands, bottle_bands, second_bands,
        back, high, low, coarse, bands_f, bands, small_f, small, wide_f,
    ) = rest[:ncols], rest[ncols:]
    chans = second.shape[1]
    full, span = cot.shape
    height = full // chans
    width = span + TILE
    groups = height // POOL
    has_up, has_down, _, _ = has_sides()
    seen_cols = columns_seen((chans, width), span)

    fill_turned_bands(bands_f, second, POOL)
    bands[...] = bands_f[...].T.astype(BF16)
    fill_turned_bands(small_f, bottle, 1)
    small_t = small_f[...].T
    for b in range(3):
        small[rows_at(b, chans)] = small_t[0:chans, 3 * b * chans : 3 * (b + 1) * chans].astype(BF16)
    fill_bands(first_bands, first, POOL)
    fill_bands(wide_f, bottle, 1)
    for b in range(3):
        bottle_bands[rows_at(b, chans)] = wide_f[
            0:chans, 3 * b * chans : 3 * (b + 1) * chans
        ].astype(BF16)
    second_bands[...] = jnp.zeros(second_bands.shape, BF16)
    for k in range(POOL):
        for b in range(3):
            for a in range(3):
                second_bands[
                    rows_at(3 * k + b, chans), (k + a) * chans : (k + a + 1) * chans
                ] = second[3 * a + b]

    size = CHALO * chans
    block = height // 2

    def halo_columns(sources, at):
        for q, channels, rows in slots(chans, height):
            sides[channels, at + rows.start : at + rows.stop, :] = halo_block(
                sources, q, block, "features"
            )

    own = [c[...] for c in cols]
    halo_columns(own, height)
    cot_0[rows_at(CHALO, chans, height), 0:span] = cot[...]
    for m in (0, 1):
        cot_0[rows_at(CHALO + m * block, chans, block), span:width] = halo_rows(
            own, m, block, "cotangent"
        )

    def vertical(up, down):
        cot_0[rows_at(0, chans, CHALO), 0:span] = up[0:size]
        cot_0[rows_at(CHALO + height, chans, CHALO), 0:span] = down[0:size]
        above, below = corner_views(up, size, cols), corner_views(down, size, cols)
        cot_0[rows_at(0, chans, CHALO), span:width] = halo_rows(above, 1, block, "cotangent")[
            (block - CHALO) * chans :
        ]
        cot_0[rows_at(CHALO + height, chans, CHALO), span:width] = halo_rows(
            below, 0, block, "cotangent"
        )[0:size]
        halo_columns(above, 0)
        halo_columns(below, 2 * height)

    pl.when(is_even("rows"))(lambda: vertical(msg_b, msg_a))
    pl.when(jnp.logical_not(is_even("rows")))(lambda: vertical(msg_a, msg_b))
    for j in range(height + 2 * CHALO):
        at = rows_at(j, chans)
        cot_m[at] = turn(cot_0[at], 1)
        cot_p[at] = turn(cot_0[at], -1)
    def group(g, _):
        at = rows_at(g * POOL, chans, POOL + 2)
        rows = jnp.dot(
            bands[...], stacked((cot_m, cot_0, cot_p), at), preferred_element_type=F32
        ).astype(BF16)
        back[rows_at(g * POOL, chans, POOL), :] = rows[:, 0:span]
        rows = rows.astype(F32)
        total = rows[0:chans]
        for k in range(1, POOL):
            total = total + rows[k * chans : (k + 1) * chans]
        store_split(high, low, rows_at(g, chans), total)
        return 0

    lax.fori_loop(0, groups + 2, group, 0, unroll=5)
    sums = block_sums(high, low, block_ones(width))
    for g in range(groups + 2):
        at = rows_at(g, chans)
        seen = seen_cols
        if g == 0:
            seen = seen & has_up
        elif g == groups + 1:
            seen = seen & has_down
        coarse[at] = jnp.where(seen, sums[at], 0.0).astype(BF16)
    for g in range(groups):
        parts = jnp.dot(small[...], coarse[rows_at(g, chans, 3), :], preferred_element_type=F32)
        mean = conv_sum(parts, chans, POOL)[:, 0:span] * (1.0 / POOL**2)
        for k in range(POOL):
            r = g * POOL + k
            act_grad[rows_at(r, chans), :] = back[rows_at(r + POOL, chans), :].astype(F32) + mean


def correlate(u, u0, views, v0, acc, height, chans, span):
    groups = range(0, height, POOL)
    left = jnp.concatenate(
        [
            jnp.concatenate(
                [view[rows_at(v0 + g, chans, POOL + 2), 0:span] for view in views], axis=0
            )
            for g in groups
        ],
        axis=1,
    )
    right = jnp.concatenate([u[rows_at(u0 + g, chans, POOL), 0:span] for g in groups], axis=1)
    acc[...] = lax.dot_general(
        left, right, (((1,), (1,)), ((), ())), preferred_element_type=F32
    )


def folded(acc, chans):
    lane = lanes_of((3 * chans, TILE))
    result = jnp.zeros((3 * chans, TILE), F32)
    for b in range(3):
        total = None
        for k in range(POOL):
            block = turn(
                acc[rows_at(b * (POOL + 2) + k, chans, 3), 0:TILE], (b - k) * chans
            )
            total = block if total is None else total + block
        result = jnp.where((lane >= b * chans) & (lane < (b + 1) * chans), total, result)
    return result


def main_kernel(
    shifts, feat, feat_a, feat_b, sides, act_grad, view_m, view_0, view_p, bands, small,
    grads, blended,
    lent, moved, warp_m, warp_0, warp_p, act, high, low, pooled, pre_grad, acc,
):
    chans, height, span = feat.shape
    tiles = span // TILE
    width = span + TILE
    groups = height // POOL
    has_up, has_down, has_left, has_right = has_sides()
    seen_cols = columns_seen((chans, width), span)

    size = feat_a.shape[0]
    window = lent.shape[1] - size
    lent[:, size:, :] = jnp.zeros((2, window, span), BF16)

    def borrow(up, down):
        lent[0, 0:size] = up[...]
        lent[1, 0:size] = down[...]

    pl.when(is_even("rows"))(lambda: borrow(feat_b, feat_a))
    pl.when(jnp.logical_not(is_even("rows")))(lambda: borrow(feat_a, feat_b))

    tall = moved.shape[1]
    lane = lanes_of((tall, TILE))
    seen_halo = ((lane < TILE // 2) & has_right) | ((lane >= TILE // 2) & has_left)
    step = lanes_of((tall, 3 * height)) - lax.broadcasted_iota(jnp.int32, (tall, 3 * height), 0)
    depth = 2 * window + height
    source = lanes_of((1, depth))
    apart = lax.broadcasted_iota(jnp.int32, (tall, depth), 0) - lanes_of((tall, depth))
    align = 16

    def warp(c, ats):
        at_up, at_down = ats
        shift, move = shifts[0, c], shifts[1, c]
        n_up, n_down = needed(shift, False), needed(shift, True)
        base_up, base_down = (
            pl.multiple_of(lax.div(at, align) * align, align) for at in (at_up, at_down)
        )
        skip_up, skip_down = at_up - base_up, at_down - base_down
        own = EXT - window - shift
        below = own - skip_down
        above = EXT - skip_up - n_up - shift
        in_up = (source >= skip_up) & (source < skip_up + n_up)
        first_down = window + height + skip_down
        in_down = (source >= first_down) & (source < first_down + n_down)
        none = 4 * depth
        offset = jnp.where(
            source < window,
            jnp.where(in_up, above, none),
            jnp.where(source < window + height, own, jnp.where(in_down, below, none)),
        )
        pick = jnp.where(apart == offset, 1.0, 0.0).astype(BF16)
        rows = jnp.concatenate(
            [lent[0, pl.ds(base_up, window), :], feat[c], lent[1, pl.ds(base_down, window), :]], axis=0
        )
        plane = jnp.dot(pick, rows, preferred_element_type=F32)
        pick = jnp.where(step == height - EXT + shift, 1.0, 0.0).astype(BF16)
        plane = [plane[:, part] for part in tiles_of(span)]
        plane.append(jnp.dot(pick, sides[c], preferred_element_type=F32))
        amount = jnp.where(move > 0, TILE - move, -move)
        parts = [turn(part, amount) for part in plane]
        inside = jnp.where(move > 0, lane, TILE - 1 - lane) < TILE - jnp.abs(move)
        for t, part in enumerate(tiles_of(width)):
            after, before = parts[(t + 1) % (tiles + 1)], parts[t - 1]
            result = jnp.where(inside, parts[t], jnp.where(move > 0, after, before))
            if t == tiles:
                result = jnp.where(seen_halo, result, 0.0)
            moved[c, :, part] = result.astype(BF16)
        return at_up + n_up, at_down + n_down

    lax.fori_loop(0, chans, warp, (jnp.int32(0), jnp.int32(0)), unroll=8)
    chunk = 16
    for r in range(0, tall, chunk):
        for part in tiles_of(width):
            warp_0[rows_at(r, chans, chunk), part] = to_rows(moved[:, r : r + chunk, part])

    def clear(r, count):
        warp_0[rows_at(r, chans, count)] = jnp.zeros((count * chans, width), BF16)

    pl.when(jnp.logical_not(has_up))(lambda: clear(0, EXT))
    pl.when(jnp.logical_not(has_down))(lambda: clear(EXT + height, EXT))
    for j in range(height + 2 * EXT):
        at = rows_at(j, chans)
        warp_m[at] = turn(warp_0[at], 1)
        warp_p[at] = turn(warp_0[at], -1)

    def first_group(g, own):
        at = rows_at(g * POOL, chans, POOL + 2)
        pre = jnp.dot(
            bands[...], stacked((warp_m, warp_0, warp_p), at), preferred_element_type=F32
        )
        sigma = 0.5 * jnp.tanh(0.5 * pre) + 0.5
        rows = (pre * sigma).astype(BF16)
        act[rows_at(g * POOL, chans, POOL), :] = rows
        rows = rows.astype(F32)
        total = rows[0:chans]
        for k in range(1, POOL):
            total = total + rows[k * chans : (k + 1) * chans]
        store_split(high, low, rows_at(g, chans), total)
        if own:
            there = rows_at(g * POOL - 2 * POOL, chans, POOL)
            pre, sigma = pre[:, 0:span], sigma[:, 0:span]
            pre_grad[there, :] = (
                act_grad[there, :] * (sigma * (1.0 + pre * (1.0 - sigma)))
            ).astype(BF16)
        return 0

    for g in (0, 1, groups + 2, groups + 3):
        first_group(g, False)
    lax.fori_loop(2, groups + 2, lambda g, _: first_group(g, True), 0, unroll=4)
    sums = block_sums(high, low, block_ones(width))
    for g in range(groups + 4):
        at = rows_at(g, chans)
        seen = seen_cols
        if g < 2:
            seen = seen & has_up
        elif g >= groups + 2:
            seen = seen & has_down
        pooled[at] = jnp.where(seen, sums[at] * (1.0 / POOL**2), 0.0).astype(BF16)

    for g in range(groups + 2):
        parts = jnp.dot(small[...], pooled[rows_at(g, chans, 3), :], preferred_element_type=F32)
        bottle_row = conv_sum(parts, chans, POOL)
        rows, seen = range(POOL), seen_cols
        if g == 0:
            rows, seen = (POOL - 1,), seen & has_up
        elif g == groups + 1:
            rows, seen = (0,), seen & has_down
        for k in rows:
            row = act[rows_at((g + 1) * POOL + k, chans), :].astype(F32) + bottle_row
            blended[rows_at(g * POOL + k - POOL + 1, chans), :] = jnp.where(seen, row, 0.0).astype(
                BF16
            )

    correlate(pre_grad, 0, (warp_m, warp_0, warp_p), EXT - 1, acc, height, chans, span)
    first_part = folded(acc, chans)
    correlate(blended, 1, (view_m, view_0, view_p), CHALO - 1, acc, height, chans, span)
    second_part = folded(acc, chans)
    lane = lanes_of((3 * chans, TILE))
    grads[0 : 3 * chans] = jnp.where(lane < 3 * chans, first_part, turn(second_part, 3 * chans))
    half = 3 * chans // 2
    grads[3 * chans :] = jnp.where(
        lane[0:half] < TILE // 2,
        turn(second_part[0:half], -chans),
        turn(second_part[half:], TILE // 2 - chans),
    )


def predict_kernel(part, blended, bands, *rest):
    out, rows = rest[-2:]
    chans, height, span = out.shape

    def group(g, _):
        at = rows_at(part * height + g * POOL, chans, POOL + 2)
        parts = jnp.dot(bands[...], blended[at, :], preferred_element_type=F32)
        for k in range(POOL):
            row = conv_sum(parts[3 * k * chans : 3 * (k + 1) * chans], chans, 1)
            rows[rows_at(g * POOL + k, chans), :] = row[:, 0:span].astype(BF16)
        return 0

    lax.fori_loop(0, height // POOL, group, 0, unroll=2)
    for part in tiles_of(span):
        out[:, :, part] = to_planes(rows[:, part], chans)


def final_kernel(factor, sums, first, second):
    chans = first.shape[1]
    total = sums[...] * factor
    turned = total[0 : 3 * chans].T
    for b in range(3):
        for a in range(3):
            first[3 * a + b] = turned[b * chans : (b + 1) * chans, a * chans : (a + 1) * chans]
    half = 3 * chans // 2
    low = total[3 * chans :]
    both = jnp.concatenate([low, turn(low, -(TILE // 2))], axis=0)
    for a in range(3):
        at = slice((2 - a) * chans, (3 - a) * chans)
        second[3 * a + 2] = turn(total[at], -3 * chans)[:, 0:chans]
        second[3 * a + 1] = both[at, 0:chans]
        second[3 * a + 0] = turn(both[at], -chans)[:, 0:chans]


def call(kernel, outs, scratch, n_in, limit, flops=0, smem_first=False, **more):
    specs = [VMEM] * n_in
    if smem_first:
        specs[0] = SMEM
    more.setdefault("in_specs", specs)
    more.setdefault("out_specs", jax.tree.map(lambda _: VMEM, outs))
    return pl.pallas_call(
        kernel,
        out_shape=outs,
        scratch_shapes=scratch,
        compiler_params=pltpu.CompilerParams(vmem_limit_bytes=limit * MIB),
        cost_estimate=pl.CostEstimate(flops=flops, bytes_accessed=4 * MIB, transcendentals=0),
        **more,
    )


def predict(blended, bands, shape, parts, part, before):
    chans, height, span = shape
    rows = height // parts
    block = pl.BlockSpec((chans, rows, span), lambda i: (0, part, 0))
    whole = lambda a: pl.BlockSpec(a.shape, lambda i: (0,) * a.ndim)
    args = (blended, bands)
    specs = [whole(a) for a in args]
    more = {}
    if before is not None:
        args += (before,)
        specs.append(pl.BlockSpec(memory_space=pl.ANY))
        more["input_output_aliases"] = {2: 0}
    return call(
        functools.partial(predict_kernel, part),
        jax.ShapeDtypeStruct(shape, BF16),
        [
            pltpu.VMEM((chans * rows, span), BF16),
        ],
        len(args),
        12,
        flops=10**9,
        grid=(1,),
        in_specs=specs,
        out_specs=block,
        **more,
    )(*args)


def bf(*shape):
    return jax.ShapeDtypeStruct(shape, BF16)


def swapped(messages, axis):
    pairs = [p for p in swaps(lax.axis_size(axis)) if p]
    return [lax.ppermute(m, axis, p) for m, p in zip(messages, pairs)]


def pack_rows(index, skip, size, shifts, feat, counted=False):
    message = bf(size, feat.shape[2])
    if counted:
        message = (message, jax.ShapeDtypeStruct((8, TILE), jnp.int32))
    return call(
        functools.partial(feature_kernel, index, skip),
        message, [], 2, 16, smem_first=True,
    )(shifts, feat)


def main_pass(rest, lent, shifts, feat, sides, act_grad, views, bands):
    chans, height, span = feat.shape
    width = span + TILE
    full = height * chans
    groups = height // POOL
    band = 3 * (POOL + 2) * chans
    if rest:
        size = lent[0].shape[0]
        more = swapped([pack_rows(i, size, rest, shifts, feat) for i in (0, 1)], "rows")
        lent = [jnp.concatenate(pair, axis=0) for pair in zip(lent, more)]
    size = lent[0].shape[0]
    tall = pl.cdiv(height + 2 * EXT, 16) * 16
    grads, blended = call(
        main_kernel,
        (jax.ShapeDtypeStruct((9 * chans // 2, TILE), F32), bf((height + 2) * chans, width)),
        [
            pltpu.VMEM((2, size + 48, span), BF16),
            pltpu.VMEM((chans, tall, width), BF16),
        ]
        + [pltpu.VMEM((tall * chans, width), BF16)] * 3
        + [pltpu.VMEM(((height + 4 * POOL) * chans, width), BF16)]
        + [pltpu.VMEM(((groups + 4) * chans, width), BF16)] * 3
        + [
            pltpu.VMEM((full, span), BF16),
            pltpu.VMEM((band, POOL * chans), F32),
        ],
        11,
        20,
        flops=10**10,
        smem_first=True,
    )(
        shifts, feat, *lent, sides, act_grad, *views, *bands
    )

    return grads, blended


def shards(features, shifts, first_kernel, bottle_kernel, second_kernel, cotangent):
    imgs, chans, height, span = features.shape
    rows, cols, dp = (lax.axis_size(a) for a in ("rows", "cols", "dp"))
    full = height * chans

    width = span + TILE
    groups = height // POOL
    feat, cot, shifts = features[0], cotangent[0], shifts[0].T
    row_pairs = swaps(rows)

    usual = USUAL * chans
    message, total = pack_rows(0, 0, usual, shifts, feat, counted=True)
    message, total, cot = lax.optimization_barrier((message, total, cot))
    feat_a = lax.ppermute(message, "rows", row_pairs[0])
    bit = 1
    while bit < dp:
        total = jnp.maximum(total, lax.ppermute(total, "dp", [(i, i ^ bit) for i in range(dp)]))
        bit *= 2

    packed = chans * (height * SLOT // TILE)
    messages = call(
        column_kernel, (bf(packed, TILE),) * (1 if cols == 2 else 2), [], 2, 8, flops=2 * 10**10
    )(feat, cot)
    col_msgs = swapped(messages, "cols")
    ncols = len(col_msgs)
    message = pack_rows(1, 0, usual, shifts, feat)
    col_msgs, message, total = lax.optimization_barrier((col_msgs, message, total))
    feat_b = lax.ppermute(message, "rows", row_pairs[1])
    cot_rows = call(rows_kernel, bf(full, span), [], 1, 4)(cot)
    halo = bf(CHALO * chans + ncols * packed * TILE // span, span)
    messages = call(edge_kernel, (halo, halo), [], 1 + ncols, 8)(cot_rows, *col_msgs)
    row_msgs = swapped(messages, "rows")
    row_msgs, feat_a = lax.optimization_barrier((row_msgs, feat_a))

    tall_c = (height + 2 * CHALO) * chans
    view = bf(tall_c, width)
    band = 3 * (POOL + 2) * chans
    act_grad, *rest = call(
        functools.partial(back_kernel, ncols),
        (
            jax.ShapeDtypeStruct((full, span), F32), view, view, view,
            bf(chans, 3 * height, TILE), bf(POOL * chans, band), bf(3 * chans, 3 * chans),
            bf(3 * POOL * chans, (POOL + 2) * chans),
        ),
        [pltpu.VMEM(((height + 2 * POOL) * chans, span), BF16)]
        + [pltpu.VMEM(((groups + 2) * chans, width), BF16)] * 3
        + [
            pltpu.VMEM((band, POOL * chans), F32),
            pltpu.VMEM((POOL * chans, band), BF16),
            pltpu.VMEM((9 * chans, TILE), F32),
            pltpu.VMEM((3 * chans, 3 * chans), BF16),
            pltpu.VMEM((chans, 9 * chans), F32),
        ],
        6 + ncols,
        16,
        flops=8 * 10**9,
    )(cot_rows, *row_msgs, *col_msgs, first_kernel, bottle_kernel, second_kernel)
    views, sides, weights = rest[:3], rest[3], rest[4:]

    grads, blended = lax.cond(
        total[0, 0] <= usual,
        functools.partial(main_pass, 0),
        functools.partial(main_pass, LARGEST * chans - usual),
        (feat_a, feat_b), shifts, feat, sides, act_grad, tuple(views), tuple(weights[:2]),
    )

    lead = dp - 1
    steps = []
    for axis, size in (("cols", cols), ("rows", rows)):
        bit = 1
        while bit < size:
            steps.append(
                ((axis, "dp"), [(i * dp + lead, (i ^ bit) * dp + lead) for i in range(size)])
            )
            bit *= 2
    for i in range(lead):
        grads = grads + lax.ppermute(grads, "dp", [(i, lead)])
    parts, prediction = 2, None
    for step, (axes, pairs) in enumerate(steps):
        if step < parts:
            grads, blended = lax.optimization_barrier((grads, blended))
        other = lax.ppermute(grads, axes, pairs)
        if step < parts:
            prediction = predict(
                blended, weights[2], (chans, height, span), parts, step, prediction
            )
            other, prediction = lax.optimization_barrier((other, prediction))
        grads = grads + other
    result = grads
    for i in range(lead):
        back = lax.ppermute(grads, "dp", [(lead, i)])
        result = jnp.where(lax.axis_index("dp") == i, back, result)
    factor = 1.0 / math.sqrt(imgs * dp * height * rows * span * cols)
    shape = jax.ShapeDtypeStruct((9, chans, chans), F32)
    first_grad, second_grad = call(
        functools.partial(final_kernel, factor), (shape, shape), [], 1, 2
    )(result)
    return (prediction[None], first_grad, second_grad)


def solution(mesh):
    placed = (
        P("dp", None, "rows", "cols"),
        P("dp", None, None),
        P(),
        P(),
        P(),
        P("dp", None, "rows", "cols"),
    )
    return jax.shard_map(
        shards,
        mesh=mesh,
        in_specs=placed,
        out_specs=(P("dp", None, "rows", "cols"), P(), P()),
        check_vma=False,
    )
```

```python
import functools
import math

import jax
import jax.numpy as jnp
from jax import lax
from jax.experimental import pallas as pl
from jax.experimental.pallas import tpu as pltpu
from jax.sharding import PartitionSpec as P


MAXSHIFT = 16
POOL = 4
TILE = 128
SLOT = 32
EXT = 9
FHALO = MAXSHIFT + EXT
USUAL = 14
LARGEST = FHALO + 1
CHALO = 5
F32 = jnp.float32
BF16 = jnp.bfloat16
VMEM = pl.BlockSpec(memory_space=pltpu.VMEM)
SMEM = pl.BlockSpec(memory_space=pltpu.SMEM)
MIB = 1024 * 1024


def lanes_of(shape):
    return lax.broadcasted_iota(jnp.int32, shape, len(shape) - 1)


def turn(values, shift):
    width = values.shape[-1]
    if isinstance(shift, int):
        shift = shift % width
        if shift == 0:
            return values
    return pltpu.roll(values, shift, values.ndim - 1)


def has_sides():
    row, col = lax.axis_index("rows"), lax.axis_index("cols")
    return (
        row > 0,
        row < lax.axis_size("rows") - 1,
        col > 0,
        col < lax.axis_size("cols") - 1,
    )


def rows_at(r, chans, count=1):
    if isinstance(r, int):
        return slice(r * chans, (r + count) * chans)
    return pl.ds(pl.multiple_of(r * chans, chans), count * chans)


def to_rows(block):
    chans, height, span = block.shape
    return jnp.transpose(block, (1, 0, 2)).reshape(height * chans, span)


def to_planes(block, chans):
    height = block.shape[0] // chans
    return jnp.transpose(block.reshape(height, chans, block.shape[1]), (1, 0, 2))


def tiles_of(span):
    return [slice(t, t + TILE) for t in range(0, span, TILE)]


def is_even(axis):
    return lax.rem(lax.axis_index(axis), 2) == 0


def swaps(size):
    first = [(i, i ^ 1) for i in range(size)]
    second = [(i, i + 1) for i in range(1, size - 1, 2)]
    return [first, second + [(j, i) for i, j in second]]


def needed(shift, below):
    return jnp.maximum(EXT + shift if below else EXT - shift, 0)


def feature_kernel(index, skip, shifts, feat, msg, *counts):
    chans, height, span = feat.shape
    full = chans * height
    size = msg.shape[0]
    chunk = size // 4
    source = feat[...].reshape(full, span)
    lane = lanes_of((8, full))
    chan, row = lane // height, lane % height
    to_below = is_even("rows") if index == 0 else jnp.logical_not(is_even("rows"))
    target = jnp.full((8, full), -1, jnp.int32)
    at, up, down = jnp.int32(-skip), jnp.int32(0), jnp.int32(0)
    for c in range(chans):
        shift = shifts[0, c]
        n_up, n_down = needed(shift, False), needed(shift, True)
        count = jnp.where(to_below, n_up, n_down)
        first = jnp.where(to_below, height - count, 0)
        mine = (chan == c) & (row >= first) & (row < first + count)
        target = jnp.where(mine, row + (at - first), target)
        at, up, down = at + count, up + n_up, down + n_down
    for out in counts:
        out[...] = jnp.full(out.shape, jnp.maximum(up, down), jnp.int32)
    for p in range(0, size, chunk):
        place = lax.broadcasted_iota(jnp.int32, (chunk, full), 0) + p
        pick = jnp.where(place == target[0:1], 1.0, 0.0).astype(BF16)
        msg[p : p + chunk] = jnp.dot(pick, source, preferred_element_type=F32).astype(BF16)


def rows_kernel(source, out):
    for part in tiles_of(source.shape[2]):
        out[:, part] = to_rows(source[:, :, part])


def edge_lanes(shape, right, count):
    lane = lanes_of(shape)
    return jnp.where(jnp.where(right, TILE - 1 - lane, lane) < count, 1.0, 0.0).astype(BF16)


def slots(chans, height):
    half, block = chans // 2, height // 2
    for h in (0, 1):
        for m in (0, 1):
            yield 2 * h + m, slice(h * half, (h + 1) * half), slice(m * block, (m + 1) * block)


def column_kernel(feat, cot, *col_msgs):
    chans, height, span = feat.shape
    for index, msg in enumerate(col_msgs):
        right = is_even("cols") if index == 0 else jnp.logical_not(is_even("cols"))
        part = pl.ds(pl.multiple_of(jnp.where(right, span - TILE, 0), TILE), TILE)
        shape = (1, height // 2, TILE)
        inner = edge_lanes(shape, right, FHALO)
        outer = edge_lanes(shape, right, SLOT) - inner
        total = None
        for q, channels, rows in slots(chans, height):
            cots = turn(cot[channels, rows, part], jnp.where(right, TILE - FHALO, FHALO))
            piece = feat[channels, rows, part] * inner + cots * outer
            piece = turn(piece, jnp.where(right, (q + 1) * SLOT % TILE, q * SLOT))
            total = piece if total is None else total + piece
        msg[...] = total.reshape(msg.shape)


def edge_kernel(cot_rows, *rest):
    cols, (msg_a, msg_b) = rest[:-2], rest[-2:]
    span = cot_rows.shape[1]
    size = msg_a.shape[0] - sum(c.shape[0] * TILE // span for c in cols)
    edge = cot_rows.shape[0] - size
    chans = size // CHALO
    low = jnp.where(is_even("rows"), edge, 0)
    msg_a[0:size] = cot_rows[pl.ds(pl.multiple_of(low, chans), size), :]
    msg_b[0:size] = cot_rows[pl.ds(pl.multiple_of(edge - low, chans), size), :]
    at = size
    for col in cols:
        count = col.shape[0] * TILE // span
        for t, part in enumerate(tiles_of(span)):
            block = col[t * count : (t + 1) * count]
            msg_a[at : at + count, part] = block
            msg_b[at : at + count, part] = block
        at += count


def corner_views(msg, size, cols):
    span = msg.shape[1]
    views, at = [], size
    for col in cols:
        count = col.shape[0] * TILE // span
        views.append(
            jnp.concatenate([msg[at : at + count, part] for part in tiles_of(span)], axis=0)
        )
        at += count
    return views


def halo_block(sources, slot, rows, kind):
    total = None
    if kind == "features":
        count, shift_r, shift_l = FHALO, -slot * SLOT, TILE - (slot + 1) * SLOT
    else:
        count = CHALO
        shift_r, shift_l = -slot * SLOT - FHALO, TILE - (slot + 1) * SLOT + FHALO
    for index, source in enumerate(sources):
        from_right = is_even("cols") if index == 0 else jnp.logical_not(is_even("cols"))
        block = source.reshape(source.shape[0] // rows, rows, TILE)
        block = turn(block, jnp.where(from_right, shift_r % TILE, shift_l % TILE))
        block = block * edge_lanes((1, rows, TILE), jnp.logical_not(from_right), count)
        total = block if total is None else total + block
    return total


def halo_rows(sources, m, rows, kind):
    return to_rows(
        jnp.concatenate([halo_block(sources, 2 * h + m, rows, kind) for h in (0, 1)], axis=0)
    )


def columns_seen(shape, span):
    _, _, has_left, has_right = has_sides()
    lane = lanes_of(shape)
    middle = span + TILE // 2
    return (lane < span) | ((lane < middle) & has_right) | ((lane >= middle) & has_left)


def block_ones(width):
    row = lax.broadcasted_iota(jnp.int32, (width, width), 0) // POOL
    col = lax.broadcasted_iota(jnp.int32, (width, width), 1) // POOL
    return jnp.where(row == col, 1.0, 0.0).astype(BF16)


def store_split(high, low, at, total):
    top = total.astype(BF16)
    high[at, :] = top
    low[at, :] = (total - top.astype(F32)).astype(BF16)


def block_sums(high, low, ones):
    return jnp.dot(high[...], ones, preferred_element_type=F32) + jnp.dot(
        low[...], ones, preferred_element_type=F32
    )


def fill_bands(out, kernel, count):
    chans = kernel.shape[1]
    out[...] = jnp.zeros(out.shape, out.dtype)
    for k in range(count):
        for b in range(3):
            for a in range(3):
                at = (b * (count + 2) + k + a) * chans
                out[k * chans : (k + 1) * chans, at : at + chans] = kernel[3 * a + b].astype(
                    out.dtype
                )


def fill_turned_bands(out, kernel, count):
    chans = kernel.shape[1]
    out[...] = jnp.zeros(out.shape, out.dtype)
    for k in range(count):
        for b in range(3):
            for a in range(3):
                at = (b * (count + 2) + k + a) * chans
                out[at : at + chans, k * chans : (k + 1) * chans] = kernel[8 - 3 * a - b].astype(
                    out.dtype
                )


def stacked(views, at):
    return jnp.concatenate([view[at, :] for view in views], axis=0)


def conv_sum(parts, chans, step):
    return (
        turn(parts[0:chans], step)
        + parts[chans : 2 * chans]
        + turn(parts[2 * chans : 3 * chans], -step)
    )


def back_kernel(
    ncols, cot, msg_a, msg_b, *rest,
):
    cols, (
        first, bottle, second,
        act_grad, cot_m, cot_0, cot_p, sides, first_bands, bottle_bands, second_bands,
        back, high, low, coarse, bands_f, bands, small_f, small, wide_f,
    ) = rest[:ncols], rest[ncols:]
    chans = second.shape[1]
    full, span = cot.shape
    height = full // chans
    width = span + TILE
    groups = height // POOL
    has_up, has_down, _, _ = has_sides()
    seen_cols = columns_seen((chans, width), span)

    fill_turned_bands(bands_f, second, POOL)
    bands[...] = bands_f[...].T.astype(BF16)
    fill_turned_bands(small_f, bottle, 1)
    small_t = small_f[...].T
    for b in range(3):
        small[rows_at(b, chans)] = small_t[0:chans, 3 * b * chans : 3 * (b + 1) * chans].astype(BF16)
    fill_bands(first_bands, first, POOL)
    fill_bands(wide_f, bottle, 1)
    for b in range(3):
        bottle_bands[rows_at(b, chans)] = wide_f[
            0:chans, 3 * b * chans : 3 * (b + 1) * chans
        ].astype(BF16)
    second_bands[...] = jnp.zeros(second_bands.shape, BF16)
    for k in range(POOL):
        for b in range(3):
            for a in range(3):
                second_bands[
                    rows_at(3 * k + b, chans), (k + a) * chans : (k + a + 1) * chans
                ] = second[3 * a + b]

    size = CHALO * chans
    block = height // 2

    def halo_columns(sources, at):
        for q, channels, rows in slots(chans, height):
            sides[channels, at + rows.start : at + rows.stop, :] = halo_block(
                sources, q, block, "features"
            )

    own = [c[...] for c in cols]
    halo_columns(own, height)
    cot_0[rows_at(CHALO, chans, height), 0:span] = cot[...]
    for m in (0, 1):
        cot_0[rows_at(CHALO + m * block, chans, block), span:width] = halo_rows(
            own, m, block, "cotangent"
        )

    def vertical(up, down):
        cot_0[rows_at(0, chans, CHALO), 0:span] = up[0:size]
        cot_0[rows_at(CHALO + height, chans, CHALO), 0:span] = down[0:size]
        above, below = corner_views(up, size, cols), corner_views(down, size, cols)
        cot_0[rows_at(0, chans, CHALO), span:width] = halo_rows(above, 1, block, "cotangent")[
            (block - CHALO) * chans :
        ]
        cot_0[rows_at(CHALO + height, chans, CHALO), span:width] = halo_rows(
            below, 0, block, "cotangent"
        )[0:size]
        halo_columns(above, 0)
        halo_columns(below, 2 * height)

    pl.when(is_even("rows"))(lambda: vertical(msg_b, msg_a))
    pl.when(jnp.logical_not(is_even("rows")))(lambda: vertical(msg_a, msg_b))
    for j in range(height + 2 * CHALO):
        at = rows_at(j, chans)
        cot_m[at] = turn(cot_0[at], 1)
        cot_p[at] = turn(cot_0[at], -1)
    def group(g, _):
        at = rows_at(g * POOL, chans, POOL + 2)
        rows = jnp.dot(
            bands[...], stacked((cot_m, cot_0, cot_p), at), preferred_element_type=F32
        ).astype(BF16)
        back[rows_at(g * POOL, chans, POOL), :] = rows[:, 0:span]
        rows = rows.astype(F32)
        total = rows[0:chans]
        for k in range(1, POOL):
            total = total + rows[k * chans : (k + 1) * chans]
        store_split(high, low, rows_at(g, chans), total)
        return 0

    lax.fori_loop(0, groups + 2, group, 0, unroll=5)
    sums = block_sums(high, low, block_ones(width))
    for g in range(groups + 2):
        at = rows_at(g, chans)
        seen = seen_cols
        if g == 0:
            seen = seen & has_up
        elif g == groups + 1:
            seen = seen & has_down
        coarse[at] = jnp.where(seen, sums[at], 0.0).astype(BF16)
    for g in range(groups):
        parts = jnp.dot(small[...], coarse[rows_at(g, chans, 3), :], preferred_element_type=F32)
        mean = conv_sum(parts, chans, POOL)[:, 0:span] * (1.0 / POOL**2)
        for k in range(POOL):
            r = g * POOL + k
            act_grad[rows_at(r, chans), :] = back[rows_at(r + POOL, chans), :].astype(F32) + mean


def correlate(u, u0, views, v0, acc, height, chans, span):
    groups = range(0, height, POOL)
    left = jnp.concatenate(
        [
            jnp.concatenate(
                [view[rows_at(v0 + g, chans, POOL + 2), 0:span] for view in views], axis=0
            )
            for g in groups
        ],
        axis=1,
    )
    right = jnp.concatenate([u[rows_at(u0 + g, chans, POOL), 0:span] for g in groups], axis=1)
    acc[...] = lax.dot_general(
        left, right, (((1,), (1,)), ((), ())), preferred_element_type=F32
    )


def folded(acc, chans):
    lane = lanes_of((3 * chans, TILE))
    result = jnp.zeros((3 * chans, TILE), F32)
    for b in range(3):
        total = None
        for k in range(POOL):
            block = turn(
                acc[rows_at(b * (POOL + 2) + k, chans, 3), 0:TILE], (b - k) * chans
            )
            total = block if total is None else total + block
        result = jnp.where((lane >= b * chans) & (lane < (b + 1) * chans), total, result)
    return result


def main_kernel(
    shifts, feat, feat_a, feat_b, sides, act_grad, view_m, view_0, view_p, bands, small,
    grads, blended,
    lent, moved, warp_m, warp_0, warp_p, act, high, low, pooled, pre_grad, acc,
):
    chans, height, span = feat.shape
    tiles = span // TILE
    width = span + TILE
    groups = height // POOL
    has_up, has_down, has_left, has_right = has_sides()
    seen_cols = columns_seen((chans, width), span)

    size = feat_a.shape[0]
    window = lent.shape[1] - size
    lent[:, size:, :] = jnp.zeros((2, window, span), BF16)

    def borrow(up, down):
        lent[0, 0:size] = up[...]
        lent[1, 0:size] = down[...]

    pl.when(is_even("rows"))(lambda: borrow(feat_b, feat_a))
    pl.when(jnp.logical_not(is_even("rows")))(lambda: borrow(feat_a, feat_b))

    tall = moved.shape[1]
    lane = lanes_of((tall, TILE))
    seen_halo = ((lane < TILE // 2) & has_right) | ((lane >= TILE // 2) & has_left)
    step = lanes_of((tall, 3 * height)) - lax.broadcasted_iota(jnp.int32, (tall, 3 * height), 0)
    depth = 2 * window + height
    source = lanes_of((1, depth))
    apart = lax.broadcasted_iota(jnp.int32, (tall, depth), 0) - lanes_of((tall, depth))
    align = 16

    def warp(c, ats):
        at_up, at_down = ats
        shift, move = shifts[0, c], shifts[1, c]
        n_up, n_down = needed(shift, False), needed(shift, True)
        base_up, base_down = (
            pl.multiple_of(lax.div(at, align) * align, align) for at in (at_up, at_down)
        )
        skip_up, skip_down = at_up - base_up, at_down - base_down
        own = EXT - window - shift
        below = own - skip_down
        above = EXT - skip_up - n_up - shift
        in_up = (source >= skip_up) & (source < skip_up + n_up)
        first_down = window + height + skip_down
        in_down = (source >= first_down) & (source < first_down + n_down)
        none = 4 * depth
        offset = jnp.where(
            source < window,
            jnp.where(in_up, above, none),
            jnp.where(source < window + height, own, jnp.where(in_down, below, none)),
        )
        pick = jnp.where(apart == offset, 1.0, 0.0).astype(BF16)
        rows = jnp.concatenate(
            [lent[0, pl.ds(base_up, window), :], feat[c], lent[1, pl.ds(base_down, window), :]], axis=0
        )
        plane = jnp.dot(pick, rows, preferred_element_type=F32)
        pick = jnp.where(step == height - EXT + shift, 1.0, 0.0).astype(BF16)
        plane = [plane[:, part] for part in tiles_of(span)]
        plane.append(jnp.dot(pick, sides[c], preferred_element_type=F32))
        amount = jnp.where(move > 0, TILE - move, -move)
        parts = [turn(part, amount) for part in plane]
        inside = jnp.where(move > 0, lane, TILE - 1 - lane) < TILE - jnp.abs(move)
        for t, part in enumerate(tiles_of(width)):
            after, before = parts[(t + 1) % (tiles + 1)], parts[t - 1]
            result = jnp.where(inside, parts[t], jnp.where(move > 0, after, before))
            if t == tiles:
                result = jnp.where(seen_halo, result, 0.0)
            moved[c, :, part] = result.astype(BF16)
        return at_up + n_up, at_down + n_down

    lax.fori_loop(0, chans, warp, (jnp.int32(0), jnp.int32(0)), unroll=8)
    chunk = 16
    for r in range(0, tall, chunk):
        for part in tiles_of(width):
            warp_0[rows_at(r, chans, chunk), part] = to_rows(moved[:, r : r + chunk, part])

    def clear(r, count):
        warp_0[rows_at(r, chans, count)] = jnp.zeros((count * chans, width), BF16)

    pl.when(jnp.logical_not(has_up))(lambda: clear(0, EXT))
    pl.when(jnp.logical_not(has_down))(lambda: clear(EXT + height, EXT))
    for j in range(height + 2 * EXT):
        at = rows_at(j, chans)
        warp_m[at] = turn(warp_0[at], 1)
        warp_p[at] = turn(warp_0[at], -1)

    def first_group(g, own):
        at = rows_at(g * POOL, chans, POOL + 2)
        pre = jnp.dot(
            bands[...], stacked((warp_m, warp_0, warp_p), at), preferred_element_type=F32
        )
        sigma = 0.5 * jnp.tanh(0.5 * pre) + 0.5
        rows = (pre * sigma).astype(BF16)
        act[rows_at(g * POOL, chans, POOL), :] = rows
        rows = rows.astype(F32)
        total = rows[0:chans]
        for k in range(1, POOL):
            total = total + rows[k * chans : (k + 1) * chans]
        store_split(high, low, rows_at(g, chans), total)
        if own:
            there = rows_at(g * POOL - 2 * POOL, chans, POOL)
            pre, sigma = pre[:, 0:span], sigma[:, 0:span]
            pre_grad[there, :] = (
                act_grad[there, :] * (sigma * (1.0 + pre * (1.0 - sigma)))
            ).astype(BF16)
        return 0

    for g in (0, 1, groups + 2, groups + 3):
        first_group(g, False)
    lax.fori_loop(2, groups + 2, lambda g, _: first_group(g, True), 0, unroll=4)
    sums = block_sums(high, low, block_ones(width))
    for g in range(groups + 4):
        at = rows_at(g, chans)
        seen = seen_cols
        if g < 2:
            seen = seen & has_up
        elif g >= groups + 2:
            seen = seen & has_down
        pooled[at] = jnp.where(seen, sums[at] * (1.0 / POOL**2), 0.0).astype(BF16)

    for g in range(groups + 2):
        parts = jnp.dot(small[...], pooled[rows_at(g, chans, 3), :], preferred_element_type=F32)
        bottle_row = conv_sum(parts, chans, POOL)
        rows, seen = range(POOL), seen_cols
        if g == 0:
            rows, seen = (POOL - 1,), seen & has_up
        elif g == groups + 1:
            rows, seen = (0,), seen & has_down
        for k in rows:
            row = act[rows_at((g + 1) * POOL + k, chans), :].astype(F32) + bottle_row
            blended[rows_at(g * POOL + k - POOL + 1, chans), :] = jnp.where(seen, row, 0.0).astype(
                BF16
            )

    correlate(pre_grad, 0, (warp_m, warp_0, warp_p), EXT - 1, acc, height, chans, span)
    first_part = folded(acc, chans)
    correlate(blended, 1, (view_m, view_0, view_p), CHALO - 1, acc, height, chans, span)
    second_part = folded(acc, chans)
    lane = lanes_of((3 * chans, TILE))
    grads[0 : 3 * chans] = jnp.where(lane < 3 * chans, first_part, turn(second_part, 3 * chans))
    half = 3 * chans // 2
    grads[3 * chans :] = jnp.where(
        lane[0:half] < TILE // 2,
        turn(second_part[0:half], -chans),
        turn(second_part[half:], TILE // 2 - chans),
    )


def predict_kernel(part, blended, bands, *rest):
    out, rows = rest[-2:]
    chans, height, span = out.shape

    def group(g, _):
        at = rows_at(part * height + g * POOL, chans, POOL + 2)
        parts = jnp.dot(bands[...], blended[at, :], preferred_element_type=F32)
        for k in range(POOL):
            row = conv_sum(parts[3 * k * chans : 3 * (k + 1) * chans], chans, 1)
            rows[rows_at(g * POOL + k, chans), :] = row[:, 0:span].astype(BF16)
        return 0

    lax.fori_loop(0, height // POOL, group, 0, unroll=2)
    for part in tiles_of(span):
        out[:, :, part] = to_planes(rows[:, part], chans)


def final_kernel(factor, mine, other, first, second):
    chans = first.shape[1]
    total = (mine[...].astype(F32) + other[...].astype(F32)) * factor
    turned = total[0 : 3 * chans].T
    for b in range(3):
        for a in range(3):
            first[3 * a + b] = turned[b * chans : (b + 1) * chans, a * chans : (a + 1) * chans]
    half = 3 * chans // 2
    low = total[3 * chans :]
    both = jnp.concatenate([low, turn(low, -(TILE // 2))], axis=0)
    for a in range(3):
        at = slice((2 - a) * chans, (3 - a) * chans)
        second[3 * a + 2] = turn(total[at], -3 * chans)[:, 0:chans]
        second[3 * a + 1] = both[at, 0:chans]
        second[3 * a + 0] = turn(both[at], -chans)[:, 0:chans]


def call(kernel, outs, scratch, n_in, limit, flops=0, smem_first=False, **more):
    specs = [VMEM] * n_in
    if smem_first:
        specs[0] = SMEM
    more.setdefault("in_specs", specs)
    more.setdefault("out_specs", jax.tree.map(lambda _: VMEM, outs))
    return pl.pallas_call(
        kernel,
        out_shape=outs,
        scratch_shapes=scratch,
        compiler_params=pltpu.CompilerParams(vmem_limit_bytes=limit * MIB),
        cost_estimate=pl.CostEstimate(flops=flops, bytes_accessed=4 * MIB, transcendentals=0),
        **more,
    )


def predict(blended, bands, shape, parts, part, before):
    chans, height, span = shape
    rows = height // parts
    block = pl.BlockSpec((chans, rows, span), lambda i: (0, part, 0))
    whole = lambda a: pl.BlockSpec(a.shape, lambda i: (0,) * a.ndim)
    args = (blended, bands)
    specs = [whole(a) for a in args]
    more = {}
    if before is not None:
        args += (before,)
        specs.append(pl.BlockSpec(memory_space=pl.ANY))
        more["input_output_aliases"] = {2: 0}
    return call(
        functools.partial(predict_kernel, part),
        jax.ShapeDtypeStruct(shape, BF16),
        [
            pltpu.VMEM((chans * rows, span), BF16),
        ],
        len(args),
        12,
        flops=10**9,
        grid=(1,),
        in_specs=specs,
        out_specs=block,
        **more,
    )(*args)


def bf(*shape):
    return jax.ShapeDtypeStruct(shape, BF16)


def swapped(messages, axis):
    pairs = [p for p in swaps(lax.axis_size(axis)) if p]
    return [lax.ppermute(m, axis, p) for m, p in zip(messages, pairs)]


def pack_rows(index, skip, size, shifts, feat, counted=False):
    message = bf(size, feat.shape[2])
    if counted:
        message = (message, jax.ShapeDtypeStruct((8, TILE), jnp.int32))
    return call(
        functools.partial(feature_kernel, index, skip),
        message, [], 2, 16, smem_first=True,
    )(shifts, feat)


def main_pass(rest, lent, shifts, feat, sides, act_grad, views, bands):
    chans, height, span = feat.shape
    width = span + TILE
    full = height * chans
    groups = height // POOL
    band = 3 * (POOL + 2) * chans
    if rest:
        size = lent[0].shape[0]
        more = swapped([pack_rows(i, size, rest, shifts, feat) for i in (0, 1)], "rows")
        lent = [jnp.concatenate(pair, axis=0) for pair in zip(lent, more)]
    size = lent[0].shape[0]
    tall = pl.cdiv(height + 2 * EXT, 16) * 16
    grads, blended = call(
        main_kernel,
        (jax.ShapeDtypeStruct((9 * chans // 2, TILE), F32), bf((height + 2) * chans, width)),
        [
            pltpu.VMEM((2, size + 48, span), BF16),
            pltpu.VMEM((chans, tall, width), BF16),
        ]
        + [pltpu.VMEM((tall * chans, width), BF16)] * 3
        + [pltpu.VMEM(((height + 4 * POOL) * chans, width), BF16)]
        + [pltpu.VMEM(((groups + 4) * chans, width), BF16)] * 3
        + [
            pltpu.VMEM((full, span), BF16),
            pltpu.VMEM((band, POOL * chans), F32),
        ],
        11,
        20,
        flops=10**10,
        smem_first=True,
    )(
        shifts, feat, *lent, sides, act_grad, *views, *bands
    )

    return grads, blended


def shards(features, shifts, first_kernel, bottle_kernel, second_kernel, cotangent):
    imgs, chans, height, span = features.shape
    rows, cols, dp = (lax.axis_size(a) for a in ("rows", "cols", "dp"))
    full = height * chans

    width = span + TILE
    groups = height // POOL
    feat, cot, shifts = features[0], cotangent[0], shifts[0].T
    row_pairs = swaps(rows)

    usual = USUAL * chans
    message, total = pack_rows(0, 0, usual, shifts, feat, counted=True)
    message, total, cot = lax.optimization_barrier((message, total, cot))
    feat_a = lax.ppermute(message, "rows", row_pairs[0])
    bit = 1
    while bit < dp:
        total = jnp.maximum(total, lax.ppermute(total, "dp", [(i, i ^ bit) for i in range(dp)]))
        bit *= 2

    packed = chans * (height * SLOT // TILE)
    messages = call(
        column_kernel, (bf(packed, TILE),) * (1 if cols == 2 else 2), [], 2, 8, flops=2 * 10**10
    )(feat, cot)
    col_msgs = swapped(messages, "cols")
    ncols = len(col_msgs)
    message = pack_rows(1, 0, usual, shifts, feat)
    col_msgs, message, total = lax.optimization_barrier((col_msgs, message, total))
    feat_b = lax.ppermute(message, "rows", row_pairs[1])
    cot_rows = call(rows_kernel, bf(full, span), [], 1, 4)(cot)
    halo = bf(CHALO * chans + ncols * packed * TILE // span, span)
    messages = call(edge_kernel, (halo, halo), [], 1 + ncols, 8)(cot_rows, *col_msgs)
    row_msgs = swapped(messages, "rows")
    row_msgs, feat_a, total = lax.optimization_barrier((row_msgs, feat_a, total))

    tall_c = (height + 2 * CHALO) * chans
    view = bf(tall_c, width)
    band = 3 * (POOL + 2) * chans
    act_grad, *rest = call(
        functools.partial(back_kernel, ncols),
        (
            jax.ShapeDtypeStruct((full, span), F32), view, view, view,
            bf(chans, 3 * height, TILE), bf(POOL * chans, band), bf(3 * chans, 3 * chans),
            bf(3 * POOL * chans, (POOL + 2) * chans),
        ),
        [pltpu.VMEM(((height + 2 * POOL) * chans, span), BF16)]
        + [pltpu.VMEM(((groups + 2) * chans, width), BF16)] * 3
        + [
            pltpu.VMEM((band, POOL * chans), F32),
            pltpu.VMEM((POOL * chans, band), BF16),
            pltpu.VMEM((9 * chans, TILE), F32),
            pltpu.VMEM((3 * chans, 3 * chans), BF16),
            pltpu.VMEM((chans, 9 * chans), F32),
        ],
        6 + ncols,
        16,
        flops=8 * 10**9,
    )(cot_rows, *row_msgs, *col_msgs, first_kernel, bottle_kernel, second_kernel)
    views, sides, weights = rest[:3], rest[3], rest[4:]

    grads, blended = lax.cond(
        total[0, 0] <= usual,
        functools.partial(main_pass, 0),
        functools.partial(main_pass, LARGEST * chans - usual),
        (feat_a, feat_b), shifts, feat, sides, act_grad, tuple(views), tuple(weights[:2]),
    )

    steps = []
    for axis, size in (("dp", dp), ("cols", cols), ("rows", rows)):
        bit = 1
        while bit < size:
            steps.append((axis, [(i, i ^ bit) for i in range(size)]))
            bit *= 2
    parts, prediction = 2, None
    for step, (axis, pairs) in enumerate(steps):
        if axis != "dp":
            grads = lax.optimization_barrier(grads.astype(BF16))
        other = lax.ppermute(grads, axis, pairs)
        if 1 <= step <= parts:
            prediction = predict(
                blended, weights[2], (chans, height, span), parts, step - 1, prediction
            )
            other, prediction = lax.optimization_barrier((other, prediction))
        if step < len(steps) - 1:
            grads = grads.astype(F32) + other.astype(F32)
            if step < parts:
                grads, blended = lax.optimization_barrier((grads, blended))
    factor = 1.0 / math.sqrt(imgs * dp * height * rows * span * cols)
    shape = jax.ShapeDtypeStruct((9, chans, chans), F32)
    first_grad, second_grad = call(
        functools.partial(final_kernel, factor), (shape, shape), [], 2, 2
    )(grads, other)
    return (prediction[None], first_grad, second_grad)


def solution(mesh):
    placed = (
        P("dp", None, "rows", "cols"),
        P("dp", None, None),
        P(),
        P(),
        P(),
        P("dp", None, "rows", "cols"),
    )
    return jax.shard_map(
        shards,
        mesh=mesh,
        in_specs=placed,
        out_specs=(P("dp", None, "rows", "cols"), P(), P()),
        check_vma=False,
    )
```

```python
import functools
import math

import jax
import jax.numpy as jnp
from jax import lax
from jax.experimental import pallas as pl
from jax.experimental.pallas import tpu as pltpu
from jax.sharding import PartitionSpec as P


MAXSHIFT = 16
POOL = 4
TILE = 128
SLOT = 32
EXT = 9
FHALO = MAXSHIFT + EXT
USUAL = 14
LARGEST = FHALO + 1
CHALO = 5
F32 = jnp.float32
BF16 = jnp.bfloat16
VMEM = pl.BlockSpec(memory_space=pltpu.VMEM)
SMEM = pl.BlockSpec(memory_space=pltpu.SMEM)
MIB = 1024 * 1024


def lanes_of(shape):
    return lax.broadcasted_iota(jnp.int32, shape, len(shape) - 1)


def turn(values, shift):
    width = values.shape[-1]
    if isinstance(shift, int):
        shift = shift % width
        if shift == 0:
            return values
    return pltpu.roll(values, shift, values.ndim - 1)


def has_sides():
    row, col = lax.axis_index("rows"), lax.axis_index("cols")
    return (
        row > 0,
        row < lax.axis_size("rows") - 1,
        col > 0,
        col < lax.axis_size("cols") - 1,
    )


def rows_at(r, chans, count=1):
    if isinstance(r, int):
        return slice(r * chans, (r + count) * chans)
    return pl.ds(pl.multiple_of(r * chans, chans), count * chans)


def to_rows(block):
    chans, height, span = block.shape
    return jnp.transpose(block, (1, 0, 2)).reshape(height * chans, span)


def to_planes(block, chans):
    height = block.shape[0] // chans
    return jnp.transpose(block.reshape(height, chans, block.shape[1]), (1, 0, 2))


def tiles_of(span):
    return [slice(t, t + TILE) for t in range(0, span, TILE)]


def is_even(axis):
    return lax.rem(lax.axis_index(axis), 2) == 0


def swaps(size):
    first = [(i, i ^ 1) for i in range(size)]
    second = [(i, i + 1) for i in range(1, size - 1, 2)]
    return [first, second + [(j, i) for i, j in second]]


def needed(shift, below):
    return jnp.maximum(EXT + shift if below else EXT - shift, 0)


def feature_kernel(index, skip, shifts, feat, msg, *counts):
    chans, height, span = feat.shape
    full = chans * height
    size = msg.shape[0]
    chunk = size // 4
    source = feat[...].reshape(full, span)
    lane = lanes_of((8, full))
    chan, row = lane // height, lane % height
    to_below = is_even("rows") if index == 0 else jnp.logical_not(is_even("rows"))
    target = jnp.full((8, full), -1, jnp.int32)
    at, up, down = jnp.int32(-skip), jnp.int32(0), jnp.int32(0)
    for c in range(chans):
        shift = shifts[0, c]
        n_up, n_down = needed(shift, False), needed(shift, True)
        count = jnp.where(to_below, n_up, n_down)
        first = jnp.where(to_below, height - count, 0)
        mine = (chan == c) & (row >= first) & (row < first + count)
        target = jnp.where(mine, row + (at - first), target)
        at, up, down = at + count, up + n_up, down + n_down
    for out in counts:
        out[...] = jnp.full(out.shape, jnp.maximum(up, down), jnp.int32)
    for p in range(0, size, chunk):
        place = lax.broadcasted_iota(jnp.int32, (chunk, full), 0) + p
        pick = jnp.where(place == target[0:1], 1.0, 0.0).astype(BF16)
        msg[p : p + chunk] = jnp.dot(pick, source, preferred_element_type=F32).astype(BF16)


def rows_kernel(source, out):
    for part in tiles_of(source.shape[2]):
        out[:, part] = to_rows(source[:, :, part])


def edge_lanes(shape, right, count):
    lane = lanes_of(shape)
    return jnp.where(jnp.where(right, TILE - 1 - lane, lane) < count, 1.0, 0.0).astype(BF16)


def slots(chans, height):
    half, block = chans // 2, height // 2
    for h in (0, 1):
        for m in (0, 1):
            yield 2 * h + m, slice(h * half, (h + 1) * half), slice(m * block, (m + 1) * block)


def column_kernel(feat, cot, *col_msgs):
    chans, height, span = feat.shape
    for index, msg in enumerate(col_msgs):
        right = is_even("cols") if index == 0 else jnp.logical_not(is_even("cols"))
        part = pl.ds(pl.multiple_of(jnp.where(right, span - TILE, 0), TILE), TILE)
        shape = (1, height // 2, TILE)
        inner = edge_lanes(shape, right, FHALO)
        outer = edge_lanes(shape, right, SLOT) - inner
        total = None
        for q, channels, rows in slots(chans, height):
            cots = turn(cot[channels, rows, part], jnp.where(right, TILE - FHALO, FHALO))
            piece = feat[channels, rows, part] * inner + cots * outer
            piece = turn(piece, jnp.where(right, (q + 1) * SLOT % TILE, q * SLOT))
            total = piece if total is None else total + piece
        msg[...] = total.reshape(msg.shape)


def edge_kernel(cot_rows, *rest):
    cols, (msg_a, msg_b) = rest[:-2], rest[-2:]
    span = cot_rows.shape[1]
    size = msg_a.shape[0] - sum(c.shape[0] * TILE // span for c in cols)
    edge = cot_rows.shape[0] - size
    chans = size // CHALO
    low = jnp.where(is_even("rows"), edge, 0)
    msg_a[0:size] = cot_rows[pl.ds(pl.multiple_of(low, chans), size), :]
    msg_b[0:size] = cot_rows[pl.ds(pl.multiple_of(edge - low, chans), size), :]
    at = size
    for col in cols:
        count = col.shape[0] * TILE // span
        for t, part in enumerate(tiles_of(span)):
            block = col[t * count : (t + 1) * count]
            msg_a[at : at + count, part] = block
            msg_b[at : at + count, part] = block
        at += count


def corner_views(msg, size, cols):
    span = msg.shape[1]
    views, at = [], size
    for col in cols:
        count = col.shape[0] * TILE // span
        views.append(
            jnp.concatenate([msg[at : at + count, part] for part in tiles_of(span)], axis=0)
        )
        at += count
    return views


def halo_block(sources, slot, rows, kind):
    total = None
    if kind == "features":
        count, shift_r, shift_l = FHALO, -slot * SLOT, TILE - (slot + 1) * SLOT
    else:
        count = CHALO
        shift_r, shift_l = -slot * SLOT - FHALO, TILE - (slot + 1) * SLOT + FHALO
    for index, source in enumerate(sources):
        from_right = is_even("cols") if index == 0 else jnp.logical_not(is_even("cols"))
        block = source.reshape(source.shape[0] // rows, rows, TILE)
        block = turn(block, jnp.where(from_right, shift_r % TILE, shift_l % TILE))
        block = block * edge_lanes((1, rows, TILE), jnp.logical_not(from_right), count)
        total = block if total is None else total + block
    return total


def halo_rows(sources, m, rows, kind):
    return to_rows(
        jnp.concatenate([halo_block(sources, 2 * h + m, rows, kind) for h in (0, 1)], axis=0)
    )


def columns_seen(shape, span):
    _, _, has_left, has_right = has_sides()
    lane = lanes_of(shape)
    middle = span + TILE // 2
    return (lane < span) | ((lane < middle) & has_right) | ((lane >= middle) & has_left)


def cell_matrix(width, by_cell):
    shape = (TILE, width) if by_cell else (width, TILE)
    lane = lax.broadcasted_iota(jnp.int32, shape, 1 if by_cell else 0)
    cell = lax.broadcasted_iota(jnp.int32, shape, 0 if by_cell else 1)
    place = lane // POOL + jnp.where(lane >= width - TILE // 2, TILE - width // POOL, 0)
    return jnp.where(place == cell, 1.0, 0.0).astype(BF16)


def cells_seen(shape, span):
    _, _, has_left, has_right = has_sides()
    lane = lanes_of(shape)
    count = span // POOL
    middle = (count + TILE) // 2
    return (lane < count) | ((lane < middle) & has_right) | ((lane >= middle) & has_left)


def store_split(high, low, at, total):
    top = total.astype(BF16)
    high[at, :] = top
    low[at, :] = (total - top.astype(F32)).astype(BF16)


def block_sums(high, low):
    matrix = cell_matrix(high.shape[1], False)
    return jnp.dot(high[...], matrix, preferred_element_type=F32) + jnp.dot(
        low[...], matrix, preferred_element_type=F32
    )


def spread(rows, width, count):
    values = jnp.concatenate(rows, axis=0)
    top = values.astype(BF16)
    rest = (values - top.astype(F32)).astype(BF16)
    matrix = cell_matrix(width, True)[:, 0:count]
    return jnp.dot(
        jnp.concatenate([top, rest], axis=1),
        jnp.concatenate([matrix, matrix], axis=0),
        preferred_element_type=F32,
    )


def fill_bands(out, kernel, count):
    chans = kernel.shape[1]
    out[...] = jnp.zeros(out.shape, out.dtype)
    for k in range(count):
        for b in range(3):
            for a in range(3):
                at = (b * (count + 2) + k + a) * chans
                out[k * chans : (k + 1) * chans, at : at + chans] = kernel[3 * a + b].astype(
                    out.dtype
                )


def fill_turned_bands(out, kernel, count):
    chans = kernel.shape[1]
    out[...] = jnp.zeros(out.shape, out.dtype)
    for k in range(count):
        for b in range(3):
            for a in range(3):
                at = (b * (count + 2) + k + a) * chans
                out[at : at + chans, k * chans : (k + 1) * chans] = kernel[8 - 3 * a - b].astype(
                    out.dtype
                )


def stacked(views, at):
    return jnp.concatenate([view[at, :] for view in views], axis=0)


def conv_sum(parts, chans, step):
    return (
        turn(parts[0:chans], step)
        + parts[chans : 2 * chans]
        + turn(parts[2 * chans : 3 * chans], -step)
    )


def back_kernel(
    ncols, cot, msg_a, msg_b, *rest,
):
    cols, (
        first, bottle, second,
        act_grad, cot_m, cot_0, cot_p, sides, first_bands, bottle_bands, second_bands,
        back, high, low, coarse, bands_f, bands, small_f, small, wide_f,
    ) = rest[:ncols], rest[ncols:]
    chans = second.shape[1]
    full, span = cot.shape
    height = full // chans
    width = span + TILE
    groups = height // POOL
    has_up, has_down, _, _ = has_sides()

    fill_turned_bands(bands_f, second, POOL)
    bands[...] = bands_f[...].T.astype(BF16)
    fill_turned_bands(small_f, bottle, 1)
    small_t = small_f[...].T
    for b in range(3):
        small[rows_at(b, chans)] = small_t[0:chans, 3 * b * chans : 3 * (b + 1) * chans].astype(BF16)
    fill_bands(first_bands, first, POOL)
    fill_bands(wide_f, bottle, 1)
    for b in range(3):
        bottle_bands[rows_at(b, chans)] = wide_f[
            0:chans, 3 * b * chans : 3 * (b + 1) * chans
        ].astype(BF16)
    second_bands[...] = jnp.zeros(second_bands.shape, BF16)
    for k in range(POOL):
        for b in range(3):
            for a in range(3):
                second_bands[
                    rows_at(3 * k + b, chans), (k + a) * chans : (k + a + 1) * chans
                ] = second[3 * a + b]

    size = CHALO * chans
    block = height // 2

    def halo_columns(sources, at):
        for q, channels, rows in slots(chans, height):
            sides[channels, at + rows.start : at + rows.stop, :] = halo_block(
                sources, q, block, "features"
            )

    own = [c[...] for c in cols]
    halo_columns(own, height)
    cot_0[rows_at(CHALO, chans, height), 0:span] = cot[...]
    for m in (0, 1):
        cot_0[rows_at(CHALO + m * block, chans, block), span:width] = halo_rows(
            own, m, block, "cotangent"
        )

    def vertical(up, down):
        cot_0[rows_at(0, chans, CHALO), 0:span] = up[0:size]
        cot_0[rows_at(CHALO + height, chans, CHALO), 0:span] = down[0:size]
        above, below = corner_views(up, size, cols), corner_views(down, size, cols)
        cot_0[rows_at(0, chans, CHALO), span:width] = halo_rows(above, 1, block, "cotangent")[
            (block - CHALO) * chans :
        ]
        cot_0[rows_at(CHALO + height, chans, CHALO), span:width] = halo_rows(
            below, 0, block, "cotangent"
        )[0:size]
        halo_columns(above, 0)
        halo_columns(below, 2 * height)

    pl.when(is_even("rows"))(lambda: vertical(msg_b, msg_a))
    pl.when(jnp.logical_not(is_even("rows")))(lambda: vertical(msg_a, msg_b))
    for j in range(height + 2 * CHALO):
        at = rows_at(j, chans)
        cot_m[at] = turn(cot_0[at], 1)
        cot_p[at] = turn(cot_0[at], -1)
    def group(g, _):
        at = rows_at(g * POOL, chans, POOL + 2)
        rows = jnp.dot(
            bands[...], stacked((cot_m, cot_0, cot_p), at), preferred_element_type=F32
        ).astype(BF16)
        back[rows_at(g * POOL, chans, POOL), :] = rows[:, 0:span]
        rows = rows.astype(F32)
        total = rows[0:chans]
        for k in range(1, POOL):
            total = total + rows[k * chans : (k + 1) * chans]
        store_split(high, low, rows_at(g, chans), total)
        return 0

    lax.fori_loop(0, groups + 2, group, 0, unroll=5)
    sums = block_sums(high, low)
    seen_cells = cells_seen((chans, TILE), span)
    for g in range(groups + 2):
        at = rows_at(g, chans)
        seen = seen_cells
        if g == 0:
            seen = seen & has_up
        elif g == groups + 1:
            seen = seen & has_down
        coarse[at] = jnp.where(seen, sums[at], 0.0).astype(BF16)
    means = []
    for g in range(groups):
        parts = jnp.dot(small[...], coarse[rows_at(g, chans, 3), :], preferred_element_type=F32)
        means.append(conv_sum(parts, chans, 1) * (1.0 / POOL**2))
    mean = spread(means, width, span)
    for r in range(height):
        act_grad[rows_at(r, chans), :] = (
            back[rows_at(r + POOL, chans), :].astype(F32) + mean[rows_at(r // POOL, chans)]
        )


def correlate(u, u0, views, v0, acc, height, chans, span):
    groups = range(0, height, POOL)
    left = jnp.concatenate(
        [
            jnp.concatenate(
                [view[rows_at(v0 + g, chans, POOL + 2), 0:span] for view in views], axis=0
            )
            for g in groups
        ],
        axis=1,
    )
    right = jnp.concatenate([u[rows_at(u0 + g, chans, POOL), 0:span] for g in groups], axis=1)
    acc[...] = lax.dot_general(
        left, right, (((1,), (1,)), ((), ())), preferred_element_type=F32
    )


def folded(acc, chans):
    lane = lanes_of((3 * chans, TILE))
    result = jnp.zeros((3 * chans, TILE), F32)
    for b in range(3):
        total = None
        for k in range(POOL):
            block = turn(
                acc[rows_at(b * (POOL + 2) + k, chans, 3), 0:TILE], (b - k) * chans
            )
            total = block if total is None else total + block
        result = jnp.where((lane >= b * chans) & (lane < (b + 1) * chans), total, result)
    return result


def main_kernel(
    shifts, feat, feat_a, feat_b, sides, act_grad, view_m, view_0, view_p, bands, small,
    grads, blended,
    lent, moved, warp_m, warp_0, warp_p, act, high, low, pooled, pre_grad, acc,
):
    chans, height, span = feat.shape
    tiles = span // TILE
    width = span + TILE
    groups = height // POOL
    has_up, has_down, has_left, has_right = has_sides()
    seen_cols = columns_seen((chans, width), span)

    size = feat_a.shape[0]
    window = lent.shape[1] - size
    lent[:, size:, :] = jnp.zeros((2, window, span), BF16)

    def borrow(up, down):
        lent[0, 0:size] = up[...]
        lent[1, 0:size] = down[...]

    pl.when(is_even("rows"))(lambda: borrow(feat_b, feat_a))
    pl.when(jnp.logical_not(is_even("rows")))(lambda: borrow(feat_a, feat_b))

    tall = moved.shape[1]
    lane = lanes_of((tall, TILE))
    seen_halo = ((lane < TILE // 2) & has_right) | ((lane >= TILE // 2) & has_left)
    step = lanes_of((tall, 3 * height)) - lax.broadcasted_iota(jnp.int32, (tall, 3 * height), 0)
    depth = 2 * window + height
    source = lanes_of((1, depth))
    apart = lax.broadcasted_iota(jnp.int32, (tall, depth), 0) - lanes_of((tall, depth))
    align = 16

    def warp(c, ats):
        at_up, at_down = ats
        shift, move = shifts[0, c], shifts[1, c]
        n_up, n_down = needed(shift, False), needed(shift, True)
        base_up, base_down = (
            pl.multiple_of(lax.div(at, align) * align, align) for at in (at_up, at_down)
        )
        skip_up, skip_down = at_up - base_up, at_down - base_down
        own = EXT - window - shift
        below = own - skip_down
        above = EXT - skip_up - n_up - shift
        in_up = (source >= skip_up) & (source < skip_up + n_up)
        first_down = window + height + skip_down
        in_down = (source >= first_down) & (source < first_down + n_down)
        none = 4 * depth
        offset = jnp.where(
            source < window,
            jnp.where(in_up, above, none),
            jnp.where(source < window + height, own, jnp.where(in_down, below, none)),
        )
        pick = jnp.where(apart == offset, 1.0, 0.0).astype(BF16)
        rows = jnp.concatenate(
            [lent[0, pl.ds(base_up, window), :], feat[c], lent[1, pl.ds(base_down, window), :]], axis=0
        )
        plane = jnp.dot(pick, rows, preferred_element_type=F32)
        pick = jnp.where(step == height - EXT + shift, 1.0, 0.0).astype(BF16)
        plane = [plane[:, part] for part in tiles_of(span)]
        plane.append(jnp.dot(pick, sides[c], preferred_element_type=F32))
        amount = jnp.where(move > 0, TILE - move, -move)
        parts = [turn(part, amount) for part in plane]
        inside = jnp.where(move > 0, lane, TILE - 1 - lane) < TILE - jnp.abs(move)
        for t, part in enumerate(tiles_of(width)):
            after, before = parts[(t + 1) % (tiles + 1)], parts[t - 1]
            result = jnp.where(inside, parts[t], jnp.where(move > 0, after, before))
            if t == tiles:
                result = jnp.where(seen_halo, result, 0.0)
            moved[c, :, part] = result.astype(BF16)
        return at_up + n_up, at_down + n_down

    lax.fori_loop(0, chans, warp, (jnp.int32(0), jnp.int32(0)), unroll=8)
    chunk = 16
    for r in range(0, tall, chunk):
        for part in tiles_of(width):
            warp_0[rows_at(r, chans, chunk), part] = to_rows(moved[:, r : r + chunk, part])

    def clear(r, count):
        warp_0[rows_at(r, chans, count)] = jnp.zeros((count * chans, width), BF16)

    pl.when(jnp.logical_not(has_up))(lambda: clear(0, EXT))
    pl.when(jnp.logical_not(has_down))(lambda: clear(EXT + height, EXT))
    for j in range(height + 2 * EXT):
        at = rows_at(j, chans)
        warp_m[at] = turn(warp_0[at], 1)
        warp_p[at] = turn(warp_0[at], -1)

    def first_group(g, own):
        at = rows_at(g * POOL, chans, POOL + 2)
        pre = jnp.dot(
            bands[...], stacked((warp_m, warp_0, warp_p), at), preferred_element_type=F32
        )
        sigma = 0.5 * jnp.tanh(0.5 * pre) + 0.5
        rows = (pre * sigma).astype(BF16)
        act[rows_at(g * POOL, chans, POOL), :] = rows
        rows = rows.astype(F32)
        total = rows[0:chans]
        for k in range(1, POOL):
            total = total + rows[k * chans : (k + 1) * chans]
        store_split(high, low, rows_at(g, chans), total)
        if own:
            there = rows_at(g * POOL - 2 * POOL, chans, POOL)
            pre, sigma = pre[:, 0:span], sigma[:, 0:span]
            pre_grad[there, :] = (
                act_grad[there, :] * (sigma * (1.0 + pre * (1.0 - sigma)))
            ).astype(BF16)
        return 0

    for g in (0, 1, groups + 2, groups + 3):
        first_group(g, False)
    lax.fori_loop(2, groups + 2, lambda g, _: first_group(g, True), 0, unroll=4)
    sums = block_sums(high, low)
    seen_cells = cells_seen((chans, TILE), span)
    for g in range(groups + 4):
        at = rows_at(g, chans)
        seen = seen_cells
        if g < 2:
            seen = seen & has_up
        elif g >= groups + 2:
            seen = seen & has_down
        pooled[at] = jnp.where(seen, sums[at] * (1.0 / POOL**2), 0.0).astype(BF16)

    bottles = []
    for g in range(groups + 2):
        parts = jnp.dot(small[...], pooled[rows_at(g, chans, 3), :], preferred_element_type=F32)
        bottles.append(conv_sum(parts, chans, 1))
    bottle = spread(bottles, width, width)
    for g in range(groups + 2):
        rows, seen = range(POOL), seen_cols
        if g == 0:
            rows, seen = (POOL - 1,), seen & has_up
        elif g == groups + 1:
            rows, seen = (0,), seen & has_down
        for k in rows:
            row = act[rows_at((g + 1) * POOL + k, chans), :].astype(F32) + bottle[rows_at(g, chans)]
            blended[rows_at(g * POOL + k - POOL + 1, chans), :] = jnp.where(seen, row, 0.0).astype(
                BF16
            )

    correlate(pre_grad, 0, (warp_m, warp_0, warp_p), EXT - 1, acc, height, chans, span)
    first_part = folded(acc, chans)
    correlate(blended, 1, (view_m, view_0, view_p), CHALO - 1, acc, height, chans, span)
    second_part = folded(acc, chans)
    lane = lanes_of((3 * chans, TILE))
    grads[0 : 3 * chans] = jnp.where(lane < 3 * chans, first_part, turn(second_part, 3 * chans))
    half = 3 * chans // 2
    grads[3 * chans :] = jnp.where(
        lane[0:half] < TILE // 2,
        turn(second_part[0:half], -chans),
        turn(second_part[half:], TILE // 2 - chans),
    )


def predict_kernel(part, blended, bands, *rest):
    out, rows = rest[-2:]
    chans, height, span = out.shape

    def group(g, _):
        at = rows_at(part * height + g * POOL, chans, POOL + 2)
        parts = jnp.dot(bands[...], blended[at, :], preferred_element_type=F32)
        for k in range(POOL):
            row = conv_sum(parts[3 * k * chans : 3 * (k + 1) * chans], chans, 1)
            rows[rows_at(g * POOL + k, chans), :] = row[:, 0:span].astype(BF16)
        return 0

    lax.fori_loop(0, height // POOL, group, 0, unroll=2)
    for part in tiles_of(span):
        out[:, :, part] = to_planes(rows[:, part], chans)


def final_kernel(factor, mine, other, first, second):
    chans = first.shape[1]
    total = (mine[...].astype(F32) + other[...].astype(F32)) * factor
    turned = total[0 : 3 * chans].T
    for b in range(3):
        for a in range(3):
            first[3 * a + b] = turned[b * chans : (b + 1) * chans, a * chans : (a + 1) * chans]
    half = 3 * chans // 2
    low = total[3 * chans :]
    both = jnp.concatenate([low, turn(low, -(TILE // 2))], axis=0)
    for a in range(3):
        at = slice((2 - a) * chans, (3 - a) * chans)
        second[3 * a + 2] = turn(total[at], -3 * chans)[:, 0:chans]
        second[3 * a + 1] = both[at, 0:chans]
        second[3 * a + 0] = turn(both[at], -chans)[:, 0:chans]


def call(kernel, outs, scratch, n_in, limit, flops=0, smem_first=False, **more):
    specs = [VMEM] * n_in
    if smem_first:
        specs[0] = SMEM
    more.setdefault("in_specs", specs)
    more.setdefault("out_specs", jax.tree.map(lambda _: VMEM, outs))
    return pl.pallas_call(
        kernel,
        out_shape=outs,
        scratch_shapes=scratch,
        compiler_params=pltpu.CompilerParams(vmem_limit_bytes=limit * MIB),
        cost_estimate=pl.CostEstimate(flops=flops, bytes_accessed=4 * MIB, transcendentals=0),
        **more,
    )


def predict(blended, bands, shape, parts, part, before):
    chans, height, span = shape
    rows = height // parts
    block = pl.BlockSpec((chans, rows, span), lambda i: (0, part, 0))
    whole = lambda a: pl.BlockSpec(a.shape, lambda i: (0,) * a.ndim)
    args = (blended, bands)
    specs = [whole(a) for a in args]
    more = {}
    if before is not None:
        args += (before,)
        specs.append(pl.BlockSpec(memory_space=pl.ANY))
        more["input_output_aliases"] = {2: 0}
    return call(
        functools.partial(predict_kernel, part),
        jax.ShapeDtypeStruct(shape, BF16),
        [
            pltpu.VMEM((chans * rows, span), BF16),
        ],
        len(args),
        12,
        flops=10**9,
        grid=(1,),
        in_specs=specs,
        out_specs=block,
        **more,
    )(*args)


def bf(*shape):
    return jax.ShapeDtypeStruct(shape, BF16)


def swapped(messages, axis):
    pairs = [p for p in swaps(lax.axis_size(axis)) if p]
    return [lax.ppermute(m, axis, p) for m, p in zip(messages, pairs)]


def pack_rows(index, skip, size, shifts, feat, counted=False):
    message = bf(size, feat.shape[2])
    if counted:
        message = (message, jax.ShapeDtypeStruct((8, TILE), jnp.int32))
    return call(
        functools.partial(feature_kernel, index, skip),
        message, [], 2, 16, smem_first=True,
    )(shifts, feat)


def main_pass(rest, lent, shifts, feat, sides, act_grad, views, bands):
    chans, height, span = feat.shape
    width = span + TILE
    full = height * chans
    groups = height // POOL
    band = 3 * (POOL + 2) * chans
    if rest:
        size = lent[0].shape[0]
        more = swapped([pack_rows(i, size, rest, shifts, feat) for i in (0, 1)], "rows")
        lent = [jnp.concatenate(pair, axis=0) for pair in zip(lent, more)]
    size = lent[0].shape[0]
    tall = pl.cdiv(height + 2 * EXT, 16) * 16
    grads, blended = call(
        main_kernel,
        (jax.ShapeDtypeStruct((9 * chans // 2, TILE), F32), bf((height + 2) * chans, width)),
        [
            pltpu.VMEM((2, size + 48, span), BF16),
            pltpu.VMEM((chans, tall, width), BF16),
        ]
        + [pltpu.VMEM((tall * chans, width), BF16)] * 3
        + [pltpu.VMEM(((height + 4 * POOL) * chans, width), BF16)]
        + [pltpu.VMEM(((groups + 4) * chans, width), BF16)] * 2
        + [pltpu.VMEM(((groups + 4) * chans, TILE), BF16)]
        + [
            pltpu.VMEM((full, span), BF16),
            pltpu.VMEM((band, POOL * chans), F32),
        ],
        11,
        20,
        flops=10**10,
        smem_first=True,
    )(
        shifts, feat, *lent, sides, act_grad, *views, *bands
    )

    return grads, blended


def shards(features, shifts, first_kernel, bottle_kernel, second_kernel, cotangent):
    imgs, chans, height, span = features.shape
    rows, cols, dp = (lax.axis_size(a) for a in ("rows", "cols", "dp"))
    full = height * chans

    width = span + TILE
    groups = height // POOL
    feat, cot, shifts = features[0], cotangent[0], shifts[0].T
    row_pairs = swaps(rows)

    usual = USUAL * chans
    message, total = pack_rows(0, 0, usual, shifts, feat, counted=True)
    message, total, cot = lax.optimization_barrier((message, total, cot))
    feat_a = lax.ppermute(message, "rows", row_pairs[0])
    bit = 1
    while bit < dp:
        total = jnp.maximum(total, lax.ppermute(total, "dp", [(i, i ^ bit) for i in range(dp)]))
        bit *= 2

    packed = chans * (height * SLOT // TILE)
    messages = call(
        column_kernel, (bf(packed, TILE),) * (1 if cols == 2 else 2), [], 2, 8, flops=2 * 10**10
    )(feat, cot)
    col_msgs = swapped(messages, "cols")
    ncols = len(col_msgs)
    message = pack_rows(1, 0, usual, shifts, feat)
    col_msgs, message, total = lax.optimization_barrier((col_msgs, message, total))
    feat_b = lax.ppermute(message, "rows", row_pairs[1])
    cot_rows = call(rows_kernel, bf(full, span), [], 1, 4)(cot)
    halo = bf(CHALO * chans + ncols * packed * TILE // span, span)
    messages = call(edge_kernel, (halo, halo), [], 1 + ncols, 8)(cot_rows, *col_msgs)
    row_msgs = swapped(messages, "rows")
    row_msgs, feat_a = lax.optimization_barrier((row_msgs, feat_a))
    row_msgs[0], total = lax.optimization_barrier((row_msgs[0], total))

    tall_c = (height + 2 * CHALO) * chans
    view = bf(tall_c, width)
    band = 3 * (POOL + 2) * chans
    act_grad, *rest = call(
        functools.partial(back_kernel, ncols),
        (
            jax.ShapeDtypeStruct((full, span), F32), view, view, view,
            bf(chans, 3 * height, TILE), bf(POOL * chans, band), bf(3 * chans, 3 * chans),
            bf(3 * POOL * chans, (POOL + 2) * chans),
        ),
        [pltpu.VMEM(((height + 2 * POOL) * chans, span), BF16)]
        + [pltpu.VMEM(((groups + 2) * chans, width), BF16)] * 2
        + [pltpu.VMEM(((groups + 2) * chans, TILE), BF16)]
        + [
            pltpu.VMEM((band, POOL * chans), F32),
            pltpu.VMEM((POOL * chans, band), BF16),
            pltpu.VMEM((9 * chans, TILE), F32),
            pltpu.VMEM((3 * chans, 3 * chans), BF16),
            pltpu.VMEM((chans, 9 * chans), F32),
        ],
        6 + ncols,
        16,
        flops=8 * 10**9,
    )(cot_rows, *row_msgs, *col_msgs, first_kernel, bottle_kernel, second_kernel)
    views, sides, weights = rest[:3], rest[3], rest[4:]

    grads, blended = lax.cond(
        total[0, 0] <= usual,
        functools.partial(main_pass, 0),
        functools.partial(main_pass, LARGEST * chans - usual),
        (feat_a, feat_b), shifts, feat, sides, act_grad, tuple(views), tuple(weights[:2]),
    )

    steps = []
    for axis, size in (("dp", dp), ("cols", cols), ("rows", rows)):
        bit = 1
        while bit < size:
            steps.append((axis, [(i, i ^ bit) for i in range(size)]))
            bit *= 2
    parts, prediction = 2, None
    for step, (axis, pairs) in enumerate(steps):
        if step == len(steps) - 1:
            grads = lax.optimization_barrier(grads.astype(BF16))
        other = lax.ppermute(grads, axis, pairs)
        if 1 <= step <= parts:
            prediction = predict(
                blended, weights[2], (chans, height, span), parts, step - 1, prediction
            )
            other, prediction = lax.optimization_barrier((other, prediction))
        if step < len(steps) - 1:
            grads = grads + other
            if step < parts:
                grads, blended = lax.optimization_barrier((grads, blended))
    factor = 1.0 / math.sqrt(imgs * dp * height * rows * span * cols)
    shape = jax.ShapeDtypeStruct((9, chans, chans), F32)
    first_grad, second_grad = call(
        functools.partial(final_kernel, factor), (shape, shape), [], 2, 2
    )(grads, other)
    return (prediction[None], first_grad, second_grad)


def solution(mesh):
    placed = (
        P("dp", None, "rows", "cols"),
        P("dp", None, None),
        P(),
        P(),
        P(),
        P("dp", None, "rows", "cols"),
    )
    return jax.shard_map(
        shards,
        mesh=mesh,
        in_specs=placed,
        out_specs=(P("dp", None, "rows", "cols"), P(), P()),
        check_vma=False,
    )
```

```python
import functools
import math

import jax
import jax.numpy as jnp
from jax import lax
from jax.experimental import pallas as pl
from jax.experimental.pallas import tpu as pltpu
from jax.sharding import PartitionSpec as P


MAXSHIFT = 16
POOL = 4
TILE = 128
SLOT = 32
EXT = 9
FHALO = MAXSHIFT + EXT
USUAL = 14
LARGEST = FHALO + 1
CHALO = 5
F32 = jnp.float32
BF16 = jnp.bfloat16
VMEM = pl.BlockSpec(memory_space=pltpu.VMEM)
SMEM = pl.BlockSpec(memory_space=pltpu.SMEM)
MIB = 1024 * 1024


def lanes_of(shape):
    return lax.broadcasted_iota(jnp.int32, shape, len(shape) - 1)


def turn(values, shift):
    width = values.shape[-1]
    if isinstance(shift, int):
        shift = shift % width
        if shift == 0:
            return values
    return pltpu.roll(values, shift, values.ndim - 1)


def has_sides():
    row, col = lax.axis_index("rows"), lax.axis_index("cols")
    return (
        row > 0,
        row < lax.axis_size("rows") - 1,
        col > 0,
        col < lax.axis_size("cols") - 1,
    )


def as_bf(values):
    return values.astype(F32).astype(BF16)


def one_hot(mask):
    return jnp.where(mask, jnp.ones((), BF16), jnp.zeros((), BF16))


def rows_at(r, chans, count=1):
    if isinstance(r, int):
        return slice(r * chans, (r + count) * chans)
    return pl.ds(pl.multiple_of(r * chans, chans), count * chans)


def to_rows(block):
    chans, height, span = block.shape
    return jnp.transpose(block, (1, 0, 2)).reshape(height * chans, span)


def to_planes(block, chans):
    height = block.shape[0] // chans
    return jnp.transpose(block.reshape(height, chans, block.shape[1]), (1, 0, 2))


def tiles_of(span):
    return [slice(t, t + TILE) for t in range(0, span, TILE)]


def is_even(axis):
    return lax.rem(lax.axis_index(axis), 2) == 0


def swaps(size):
    first = [(i, i ^ 1) for i in range(size)]
    second = [(i, i + 1) for i in range(1, size - 1, 2)]
    return [first, second + [(j, i) for i, j in second]]


def needed(shift, below):
    return jnp.maximum(EXT + shift if below else EXT - shift, 0)


def feature_kernel(index, skip, shifts, feat, msg, *counts):
    chans, height, span = feat.shape
    full = chans * height
    size = msg.shape[0]
    chunk = size // 4
    source = feat[...].reshape(full, span)
    lane = lanes_of((8, full))
    chan, row = lane // height, lane % height
    to_below = is_even("rows") if index == 0 else jnp.logical_not(is_even("rows"))
    target = jnp.full((8, full), -1, jnp.int32)
    at, up, down = jnp.int32(-skip), jnp.int32(0), jnp.int32(0)
    for c in range(chans):
        shift = shifts[0, c]
        n_up, n_down = needed(shift, False), needed(shift, True)
        count = jnp.where(to_below, n_up, n_down)
        first = jnp.where(to_below, height - count, 0)
        mine = (chan == c) & (row >= first) & (row < first + count)
        target = jnp.where(mine, row + (at - first), target)
        at, up, down = at + count, up + n_up, down + n_down
    for out in counts:
        out[...] = jnp.full(out.shape, jnp.maximum(up, down), jnp.int32)
    place = as_bf(lax.broadcasted_iota(jnp.int32, (chunk, full), 0))
    for p in range(0, size, chunk):
        pick = one_hot(place == as_bf(target[0:1] - p))
        msg[p : p + chunk] = jnp.dot(pick, source, preferred_element_type=F32).astype(BF16)


def rows_kernel(source, out):
    for part in tiles_of(source.shape[2]):
        out[:, part] = to_rows(source[:, :, part])


def edge_lanes(shape, right, count):
    lane = lanes_of(shape)
    return jnp.where(jnp.where(right, TILE - 1 - lane, lane) < count, 1.0, 0.0).astype(BF16)


def slots(chans, height):
    half, block = chans // 2, height // 2
    for h in (0, 1):
        for m in (0, 1):
            yield 2 * h + m, slice(h * half, (h + 1) * half), slice(m * block, (m + 1) * block)


def column_kernel(feat, cot, *col_msgs):
    chans, height, span = feat.shape
    for index, msg in enumerate(col_msgs):
        right = is_even("cols") if index == 0 else jnp.logical_not(is_even("cols"))
        part = pl.ds(pl.multiple_of(jnp.where(right, span - TILE, 0), TILE), TILE)
        shape = (1, height // 2, TILE)
        inner = edge_lanes(shape, right, FHALO)
        outer = edge_lanes(shape, right, SLOT) - inner
        total = None
        for q, channels, rows in slots(chans, height):
            cots = turn(cot[channels, rows, part], jnp.where(right, TILE - FHALO, FHALO))
            piece = feat[channels, rows, part] * inner + cots * outer
            piece = turn(piece, jnp.where(right, (q + 1) * SLOT % TILE, q * SLOT))
            total = piece if total is None else total + piece
        msg[...] = total.reshape(msg.shape)


def edge_kernel(cot_rows, *rest):
    cols, (msg_a, msg_b) = rest[:-2], rest[-2:]
    span = cot_rows.shape[1]
    size = msg_a.shape[0] - sum(c.shape[0] * TILE // span for c in cols)
    edge = cot_rows.shape[0] - size
    chans = size // CHALO
    low = jnp.where(is_even("rows"), edge, 0)
    msg_a[0:size] = cot_rows[pl.ds(pl.multiple_of(low, chans), size), :]
    msg_b[0:size] = cot_rows[pl.ds(pl.multiple_of(edge - low, chans), size), :]
    at = size
    for col in cols:
        count = col.shape[0] * TILE // span
        for t, part in enumerate(tiles_of(span)):
            block = col[t * count : (t + 1) * count]
            msg_a[at : at + count, part] = block
            msg_b[at : at + count, part] = block
        at += count


def corner_views(msg, size, cols):
    span = msg.shape[1]
    views, at = [], size
    for col in cols:
        count = col.shape[0] * TILE // span
        views.append(
            jnp.concatenate([msg[at : at + count, part] for part in tiles_of(span)], axis=0)
        )
        at += count
    return views


def halo_block(sources, slot, rows, kind):
    total = None
    if kind == "features":
        count, shift_r, shift_l = FHALO, -slot * SLOT, TILE - (slot + 1) * SLOT
    else:
        count = CHALO
        shift_r, shift_l = -slot * SLOT - FHALO, TILE - (slot + 1) * SLOT + FHALO
    for index, source in enumerate(sources):
        from_right = is_even("cols") if index == 0 else jnp.logical_not(is_even("cols"))
        block = source.reshape(source.shape[0] // rows, rows, TILE)
        block = turn(block, jnp.where(from_right, shift_r % TILE, shift_l % TILE))
        block = block * edge_lanes((1, rows, TILE), jnp.logical_not(from_right), count)
        total = block if total is None else total + block
    return total


def halo_rows(sources, m, rows, kind):
    return to_rows(
        jnp.concatenate([halo_block(sources, 2 * h + m, rows, kind) for h in (0, 1)], axis=0)
    )


def columns_seen(shape, span):
    _, _, has_left, has_right = has_sides()
    lane = lanes_of(shape)
    middle = span + TILE // 2
    return (lane < span) | ((lane < middle) & has_right) | ((lane >= middle) & has_left)


def cell_matrix(width, by_cell):
    shape = (TILE, width) if by_cell else (width, TILE)
    lane = lax.broadcasted_iota(jnp.int32, shape, 1 if by_cell else 0)
    cell = lax.broadcasted_iota(jnp.int32, shape, 0 if by_cell else 1)
    place = lane // POOL + jnp.where(lane >= width - TILE // 2, TILE - width // POOL, 0)
    return jnp.where(place == cell, 1.0, 0.0).astype(BF16)


def cells_seen(shape, span):
    _, _, has_left, has_right = has_sides()
    lane = lanes_of(shape)
    count = span // POOL
    middle = (count + TILE) // 2
    return (lane < count) | ((lane < middle) & has_right) | ((lane >= middle) & has_left)


def store_split(high, low, at, total):
    top = total.astype(BF16)
    high[at, :] = top
    low[at, :] = (total - top.astype(F32)).astype(BF16)


def block_sums(high, low):
    matrix = cell_matrix(high.shape[1], False)
    return jnp.dot(high[...], matrix, preferred_element_type=F32) + jnp.dot(
        low[...], matrix, preferred_element_type=F32
    )


def spread(rows, width, count):
    values = jnp.concatenate(rows, axis=0)
    top = values.astype(BF16)
    rest = (values - top.astype(F32)).astype(BF16)
    matrix = cell_matrix(width, True)[:, 0:count]
    return jnp.dot(
        jnp.concatenate([top, rest], axis=1),
        jnp.concatenate([matrix, matrix], axis=0),
        preferred_element_type=F32,
    )


def fill_bands(out, kernel, count):
    chans = kernel.shape[1]
    out[...] = jnp.zeros(out.shape, out.dtype)
    for k in range(count):
        for b in range(3):
            for a in range(3):
                at = (b * (count + 2) + k + a) * chans
                out[k * chans : (k + 1) * chans, at : at + chans] = kernel[3 * a + b].astype(
                    out.dtype
                )


def fill_turned_bands(out, kernel, count):
    chans = kernel.shape[1]
    out[...] = jnp.zeros(out.shape, out.dtype)
    for k in range(count):
        for b in range(3):
            for a in range(3):
                at = (b * (count + 2) + k + a) * chans
                out[at : at + chans, k * chans : (k + 1) * chans] = kernel[8 - 3 * a - b].astype(
                    out.dtype
                )


def stacked(views, at):
    return jnp.concatenate([view[at, :] for view in views], axis=0)


def conv_sum(parts, chans, step):
    return (
        turn(parts[0:chans], step)
        + parts[chans : 2 * chans]
        + turn(parts[2 * chans : 3 * chans], -step)
    )


def back_kernel(
    ncols, cot, msg_a, msg_b, *rest,
):
    cols, (
        first, bottle, second,
        act_grad, cot_m, cot_0, cot_p, sides, first_bands, bottle_bands, second_bands,
        back, high, low, coarse, bands_f, bands, small_f, small, wide_f,
    ) = rest[:ncols], rest[ncols:]
    chans = second.shape[1]
    full, span = cot.shape
    height = full // chans
    width = span + TILE
    groups = height // POOL
    has_up, has_down, _, _ = has_sides()

    fill_turned_bands(bands_f, second, POOL)
    bands[...] = bands_f[...].T.astype(BF16)
    fill_turned_bands(small_f, bottle, 1)
    small_t = small_f[...].T
    for b in range(3):
        small[rows_at(b, chans)] = small_t[0:chans, 3 * b * chans : 3 * (b + 1) * chans].astype(BF16)
    fill_bands(first_bands, first, POOL)
    fill_bands(wide_f, bottle, 1)
    for b in range(3):
        bottle_bands[rows_at(b, chans)] = wide_f[
            0:chans, 3 * b * chans : 3 * (b + 1) * chans
        ].astype(BF16)
    second_bands[...] = jnp.zeros(second_bands.shape, BF16)
    for k in range(POOL):
        for b in range(3):
            for a in range(3):
                second_bands[
                    rows_at(3 * k + b, chans), (k + a) * chans : (k + a + 1) * chans
                ] = second[3 * a + b]

    size = CHALO * chans
    block = height // 2

    def halo_columns(sources, at):
        for q, channels, rows in slots(chans, height):
            sides[channels, at + rows.start : at + rows.stop, :] = halo_block(
                sources, q, block, "features"
            )

    own = [c[...] for c in cols]
    halo_columns(own, height)
    cot_0[rows_at(CHALO, chans, height), 0:span] = cot[...]
    for m in (0, 1):
        cot_0[rows_at(CHALO + m * block, chans, block), span:width] = halo_rows(
            own, m, block, "cotangent"
        )

    def vertical(up, down):
        cot_0[rows_at(0, chans, CHALO), 0:span] = up[0:size]
        cot_0[rows_at(CHALO + height, chans, CHALO), 0:span] = down[0:size]
        above, below = corner_views(up, size, cols), corner_views(down, size, cols)
        cot_0[rows_at(0, chans, CHALO), span:width] = halo_rows(above, 1, block, "cotangent")[
            (block - CHALO) * chans :
        ]
        cot_0[rows_at(CHALO + height, chans, CHALO), span:width] = halo_rows(
            below, 0, block, "cotangent"
        )[0:size]
        halo_columns(above, 0)
        halo_columns(below, 2 * height)

    pl.when(is_even("rows"))(lambda: vertical(msg_b, msg_a))
    pl.when(jnp.logical_not(is_even("rows")))(lambda: vertical(msg_a, msg_b))
    for j in range(height + 2 * CHALO):
        at = rows_at(j, chans)
        cot_m[at] = turn(cot_0[at], 1)
        cot_p[at] = turn(cot_0[at], -1)
    def group(g, _):
        at = rows_at(g * POOL, chans, POOL + 2)
        rows = jnp.dot(
            bands[...], stacked((cot_m, cot_0, cot_p), at), preferred_element_type=F32
        ).astype(BF16)
        back[rows_at(g * POOL, chans, POOL), :] = rows[:, 0:span]
        rows = rows.astype(F32)
        total = rows[0:chans]
        for k in range(1, POOL):
            total = total + rows[k * chans : (k + 1) * chans]
        store_split(high, low, rows_at(g, chans), total)
        return 0

    lax.fori_loop(0, groups + 2, group, 0, unroll=5)
    sums = block_sums(high, low)
    seen_cells = cells_seen((chans, TILE), span)
    for g in range(groups + 2):
        at = rows_at(g, chans)
        seen = seen_cells
        if g == 0:
            seen = seen & has_up
        elif g == groups + 1:
            seen = seen & has_down
        coarse[at] = jnp.where(seen, sums[at], 0.0).astype(BF16)
    means = []
    for g in range(groups):
        parts = jnp.dot(small[...], coarse[rows_at(g, chans, 3), :], preferred_element_type=F32)
        means.append(conv_sum(parts, chans, 1) * (1.0 / POOL**2))
    mean = spread(means, width, span)
    for r in range(height):
        act_grad[rows_at(r, chans), :] = (
            back[rows_at(r + POOL, chans), :].astype(F32) + mean[rows_at(r // POOL, chans)]
        )


def correlate(u, u0, views, v0, acc, height, chans, span):
    groups = range(0, height, POOL)
    left = jnp.concatenate(
        [
            jnp.concatenate(
                [view[rows_at(v0 + g, chans, POOL + 2), 0:span] for view in views], axis=0
            )
            for g in groups
        ],
        axis=1,
    )
    right = jnp.concatenate([u[rows_at(u0 + g, chans, POOL), 0:span] for g in groups], axis=1)
    acc[...] = lax.dot_general(
        left, right, (((1,), (1,)), ((), ())), preferred_element_type=F32
    )


def folded(acc, chans):
    lane = lanes_of((3 * chans, TILE))
    result = jnp.zeros((3 * chans, TILE), F32)
    for b in range(3):
        total = None
        for k in range(POOL):
            block = turn(
                acc[rows_at(b * (POOL + 2) + k, chans, 3), 0:TILE], (b - k) * chans
            )
            total = block if total is None else total + block
        result = jnp.where((lane >= b * chans) & (lane < (b + 1) * chans), total, result)
    return result


def main_kernel(
    shifts, feat, feat_a, feat_b, sides, act_grad, view_m, view_0, view_p, bands, small,
    grads, blended,
    lent, moved, warp_m, warp_0, warp_p, act, high, low, pooled, pre_grad, acc,
):
    chans, height, span = feat.shape
    tiles = span // TILE
    width = span + TILE
    groups = height // POOL
    has_up, has_down, has_left, has_right = has_sides()
    seen_cols = columns_seen((chans, width), span)

    size = feat_a.shape[0]
    window = lent.shape[1] - size
    lent[:, size:, :] = jnp.zeros((2, window, span), BF16)

    def borrow(up, down):
        lent[0, 0:size] = up[...]
        lent[1, 0:size] = down[...]

    pl.when(is_even("rows"))(lambda: borrow(feat_b, feat_a))
    pl.when(jnp.logical_not(is_even("rows")))(lambda: borrow(feat_a, feat_b))

    tall = moved.shape[1]
    lane = lanes_of((tall, TILE))
    seen_halo = one_hot(((lane < TILE // 2) & has_right) | ((lane >= TILE // 2) & has_left))
    lane, mirrored = as_bf(lane), as_bf(TILE - 1 - lane)
    step = as_bf(
        lanes_of((tall, 3 * height)) - lax.broadcasted_iota(jnp.int32, (tall, 3 * height), 0)
    )
    depth = 2 * window + height
    source = lanes_of((1, depth))
    apart = as_bf(lax.broadcasted_iota(jnp.int32, (tall, depth), 0) - lanes_of((tall, depth)))
    align = 16

    def warp(c, ats):
        at_up, at_down = ats
        shift, move = shifts[0, c], shifts[1, c]
        n_up, n_down = needed(shift, False), needed(shift, True)
        base_up, base_down = (
            pl.multiple_of(lax.div(at, align) * align, align) for at in (at_up, at_down)
        )
        skip_up, skip_down = at_up - base_up, at_down - base_down
        own = EXT - window - shift
        below = own - skip_down
        above = EXT - skip_up - n_up - shift
        in_up = (source >= skip_up) & (source < skip_up + n_up)
        first_down = window + height + skip_down
        in_down = (source >= first_down) & (source < first_down + n_down)
        none = 4 * depth
        offset = jnp.where(
            source < window,
            jnp.where(in_up, above, none),
            jnp.where(source < window + height, own, jnp.where(in_down, below, none)),
        )
        pick = one_hot(apart == as_bf(offset))
        rows = jnp.concatenate(
            [lent[0, pl.ds(base_up, window), :], feat[c], lent[1, pl.ds(base_down, window), :]], axis=0
        )
        plane = jnp.dot(pick, rows, preferred_element_type=F32).astype(BF16)
        pick = one_hot(step == as_bf(height - EXT + shift))
        plane = [plane[:, part] for part in tiles_of(span)]
        plane.append(jnp.dot(pick, sides[c], preferred_element_type=F32).astype(BF16))
        amount = jnp.where(move > 0, TILE - move, -move)
        parts = [turn(part, amount) for part in plane]
        inside = jnp.where(move > 0, lane, mirrored) < as_bf(TILE - jnp.abs(move))
        for t, part in enumerate(tiles_of(width)):
            after, before = parts[(t + 1) % (tiles + 1)], parts[t - 1]
            result = jnp.where(inside, parts[t], jnp.where(move > 0, after, before))
            moved[c, :, part] = result * seen_halo if t == tiles else result
        return at_up + n_up, at_down + n_down

    lax.fori_loop(0, chans, warp, (jnp.int32(0), jnp.int32(0)), unroll=8)
    chunk = 16
    for r in range(0, tall, chunk):
        for part in tiles_of(width):
            warp_0[rows_at(r, chans, chunk), part] = to_rows(moved[:, r : r + chunk, part])

    def clear(r, count):
        warp_0[rows_at(r, chans, count)] = jnp.zeros((count * chans, width), BF16)

    pl.when(jnp.logical_not(has_up))(lambda: clear(0, EXT))
    pl.when(jnp.logical_not(has_down))(lambda: clear(EXT + height, EXT))
    for j in range(height + 2 * EXT):
        at = rows_at(j, chans)
        warp_m[at] = turn(warp_0[at], 1)
        warp_p[at] = turn(warp_0[at], -1)

    def first_group(g, own):
        at = rows_at(g * POOL, chans, POOL + 2)
        pre = jnp.dot(
            bands[...], stacked((warp_m, warp_0, warp_p), at), preferred_element_type=F32
        )
        sigma = 0.5 * jnp.tanh(0.5 * pre) + 0.5
        rows = (pre * sigma).astype(BF16)
        act[rows_at(g * POOL, chans, POOL), :] = rows
        rows = rows.astype(F32)
        total = rows[0:chans]
        for k in range(1, POOL):
            total = total + rows[k * chans : (k + 1) * chans]
        store_split(high, low, rows_at(g, chans), total)
        if own:
            there = rows_at(g * POOL - 2 * POOL, chans, POOL)
            pre, sigma = pre[:, 0:span], sigma[:, 0:span]
            pre_grad[there, :] = (
                act_grad[there, :] * (sigma * (1.0 + pre * (1.0 - sigma)))
            ).astype(BF16)
        return 0

    for g in (0, 1, groups + 2, groups + 3):
        first_group(g, False)
    lax.fori_loop(2, groups + 2, lambda g, _: first_group(g, True), 0, unroll=4)
    sums = block_sums(high, low)
    seen_cells = cells_seen((chans, TILE), span)
    for g in range(groups + 4):
        at = rows_at(g, chans)
        seen = seen_cells
        if g < 2:
            seen = seen & has_up
        elif g >= groups + 2:
            seen = seen & has_down
        pooled[at] = jnp.where(seen, sums[at] * (1.0 / POOL**2), 0.0).astype(BF16)

    bottles = []
    for g in range(groups + 2):
        parts = jnp.dot(small[...], pooled[rows_at(g, chans, 3), :], preferred_element_type=F32)
        bottles.append(conv_sum(parts, chans, 1))
    bottle = spread(bottles, width, width)
    for g in range(groups + 2):
        rows, seen = range(POOL), seen_cols
        if g == 0:
            rows, seen = (POOL - 1,), seen & has_up
        elif g == groups + 1:
            rows, seen = (0,), seen & has_down
        for k in rows:
            row = act[rows_at((g + 1) * POOL + k, chans), :].astype(F32) + bottle[rows_at(g, chans)]
            blended[rows_at(g * POOL + k - POOL + 1, chans), :] = jnp.where(seen, row, 0.0).astype(
                BF16
            )

    correlate(pre_grad, 0, (warp_m, warp_0, warp_p), EXT - 1, acc, height, chans, span)
    first_part = folded(acc, chans)
    correlate(blended, 1, (view_m, view_0, view_p), CHALO - 1, acc, height, chans, span)
    second_part = folded(acc, chans)
    lane = lanes_of((3 * chans, TILE))
    grads[0 : 3 * chans] = jnp.where(lane < 3 * chans, first_part, turn(second_part, 3 * chans))
    half = 3 * chans // 2
    grads[3 * chans :] = jnp.where(
        lane[0:half] < TILE // 2,
        turn(second_part[0:half], -chans),
        turn(second_part[half:], TILE // 2 - chans),
    )


def predict_kernel(part, blended, bands, *rest):
    out, rows = rest[-2:]
    chans, height, span = out.shape

    def group(g, _):
        at = rows_at(part * height + g * POOL, chans, POOL + 2)
        parts = jnp.dot(bands[...], blended[at, :], preferred_element_type=F32)
        for k in range(POOL):
            row = conv_sum(parts[3 * k * chans : 3 * (k + 1) * chans], chans, 1)
            rows[rows_at(g * POOL + k, chans), :] = row[:, 0:span].astype(BF16)
        return 0

    lax.fori_loop(0, height // POOL, group, 0, unroll=2)
    for part in tiles_of(span):
        out[:, :, part] = to_planes(rows[:, part], chans)


def final_kernel(factor, mine, other, first, second):
    chans = first.shape[1]
    total = (mine[...].astype(F32) + other[...].astype(F32)) * factor
    turned = total[0 : 3 * chans].T
    for b in range(3):
        for a in range(3):
            first[3 * a + b] = turned[b * chans : (b + 1) * chans, a * chans : (a + 1) * chans]
    half = 3 * chans // 2
    low = total[3 * chans :]
    both = jnp.concatenate([low, turn(low, -(TILE // 2))], axis=0)
    for a in range(3):
        at = slice((2 - a) * chans, (3 - a) * chans)
        second[3 * a + 2] = turn(total[at], -3 * chans)[:, 0:chans]
        second[3 * a + 1] = both[at, 0:chans]
        second[3 * a + 0] = turn(both[at], -chans)[:, 0:chans]


def call(kernel, outs, scratch, n_in, limit, flops=0, smem_first=False, **more):
    specs = [VMEM] * n_in
    if smem_first:
        specs[0] = SMEM
    more.setdefault("in_specs", specs)
    more.setdefault("out_specs", jax.tree.map(lambda _: VMEM, outs))
    return pl.pallas_call(
        kernel,
        out_shape=outs,
        scratch_shapes=scratch,
        compiler_params=pltpu.CompilerParams(vmem_limit_bytes=limit * MIB),
        cost_estimate=pl.CostEstimate(flops=flops, bytes_accessed=4 * MIB, transcendentals=0),
        **more,
    )


def predict(blended, bands, shape, parts, part, before):
    chans, height, span = shape
    rows = height // parts
    block = pl.BlockSpec((chans, rows, span), lambda i: (0, part, 0))
    whole = lambda a: pl.BlockSpec(a.shape, lambda i: (0,) * a.ndim)
    args = (blended, bands)
    specs = [whole(a) for a in args]
    more = {}
    if before is not None:
        args += (before,)
        specs.append(pl.BlockSpec(memory_space=pl.ANY))
        more["input_output_aliases"] = {2: 0}
    return call(
        functools.partial(predict_kernel, part),
        jax.ShapeDtypeStruct(shape, BF16),
        [
            pltpu.VMEM((chans * rows, span), BF16),
        ],
        len(args),
        12,
        flops=10**9,
        grid=(1,),
        in_specs=specs,
        out_specs=block,
        **more,
    )(*args)


def bf(*shape):
    return jax.ShapeDtypeStruct(shape, BF16)


def swapped(messages, axis):
    pairs = [p for p in swaps(lax.axis_size(axis)) if p]
    return [lax.ppermute(m, axis, p) for m, p in zip(messages, pairs)]


def pack_rows(index, skip, size, shifts, feat, counted=False):
    message = bf(size, feat.shape[2])
    if counted:
        message = (message, jax.ShapeDtypeStruct((8, TILE), jnp.int32))
    return call(
        functools.partial(feature_kernel, index, skip),
        message, [], 2, 16, smem_first=True,
    )(shifts, feat)


def main_pass(rest, lent, shifts, feat, sides, act_grad, views, bands):
    chans, height, span = feat.shape
    width = span + TILE
    full = height * chans
    groups = height // POOL
    band = 3 * (POOL + 2) * chans
    if rest:
        size = lent[0].shape[0]
        more = swapped([pack_rows(i, size, rest, shifts, feat) for i in (0, 1)], "rows")
        lent = [jnp.concatenate(pair, axis=0) for pair in zip(lent, more)]
    size = lent[0].shape[0]
    tall = pl.cdiv(height + 2 * EXT, 16) * 16
    grads, blended = call(
        main_kernel,
        (jax.ShapeDtypeStruct((9 * chans // 2, TILE), F32), bf((height + 2) * chans, width)),
        [
            pltpu.VMEM((2, size + 48, span), BF16),
            pltpu.VMEM((chans, tall, width), BF16),
        ]
        + [pltpu.VMEM((tall * chans, width), BF16)] * 3
        + [pltpu.VMEM(((height + 4 * POOL) * chans, width), BF16)]
        + [pltpu.VMEM(((groups + 4) * chans, width), BF16)] * 2
        + [pltpu.VMEM(((groups + 4) * chans, TILE), BF16)]
        + [
            pltpu.VMEM((full, span), BF16),
            pltpu.VMEM((band, POOL * chans), F32),
        ],
        11,
        20,
        flops=10**10,
        smem_first=True,
    )(
        shifts, feat, *lent, sides, act_grad, *views, *bands
    )

    return grads, blended


def shards(features, shifts, first_kernel, bottle_kernel, second_kernel, cotangent):
    imgs, chans, height, span = features.shape
    rows, cols, dp = (lax.axis_size(a) for a in ("rows", "cols", "dp"))
    full = height * chans

    width = span + TILE
    groups = height // POOL
    feat, cot, shifts = features[0], cotangent[0], shifts[0].T
    row_pairs = swaps(rows)

    usual = USUAL * chans
    message, total = pack_rows(0, 0, usual, shifts, feat, counted=True)
    message, total, cot = lax.optimization_barrier((message, total, cot))
    feat_a = lax.ppermute(message, "rows", row_pairs[0])
    bit = 1
    while bit < dp:
        total = jnp.maximum(total, lax.ppermute(total, "dp", [(i, i ^ bit) for i in range(dp)]))
        bit *= 2

    packed = chans * (height * SLOT // TILE)
    messages = call(
        column_kernel, (bf(packed, TILE),) * (1 if cols == 2 else 2), [], 2, 8, flops=2 * 10**10
    )(feat, cot)
    col_msgs = swapped(messages, "cols")
    ncols = len(col_msgs)
    message = pack_rows(1, 0, usual, shifts, feat)
    col_msgs, message, total = lax.optimization_barrier((col_msgs, message, total))
    feat_b = lax.ppermute(message, "rows", row_pairs[1])
    cot_rows = call(rows_kernel, bf(full, span), [], 1, 4)(cot)
    halo = bf(CHALO * chans + ncols * packed * TILE // span, span)
    messages = call(edge_kernel, (halo, halo), [], 1 + ncols, 8)(cot_rows, *col_msgs)
    row_msgs = swapped(messages, "rows")
    row_msgs[0], total = lax.optimization_barrier((row_msgs[0], total))
    fits = total[0, 0] <= usual
    row_msgs, feat_a, fits = lax.optimization_barrier((row_msgs, feat_a, fits))

    tall_c = (height + 2 * CHALO) * chans
    view = bf(tall_c, width)
    band = 3 * (POOL + 2) * chans
    act_grad, *rest = call(
        functools.partial(back_kernel, ncols),
        (
            jax.ShapeDtypeStruct((full, span), F32), view, view, view,
            bf(chans, 3 * height, TILE), bf(POOL * chans, band), bf(3 * chans, 3 * chans),
            bf(3 * POOL * chans, (POOL + 2) * chans),
        ),
        [pltpu.VMEM(((height + 2 * POOL) * chans, span), BF16)]
        + [pltpu.VMEM(((groups + 2) * chans, width), BF16)] * 2
        + [pltpu.VMEM(((groups + 2) * chans, TILE), BF16)]
        + [
            pltpu.VMEM((band, POOL * chans), F32),
            pltpu.VMEM((POOL * chans, band), BF16),
            pltpu.VMEM((9 * chans, TILE), F32),
            pltpu.VMEM((3 * chans, 3 * chans), BF16),
            pltpu.VMEM((chans, 9 * chans), F32),
        ],
        6 + ncols,
        16,
        flops=8 * 10**9,
    )(cot_rows, *row_msgs, *col_msgs, first_kernel, bottle_kernel, second_kernel)
    views, sides, weights = rest[:3], rest[3], rest[4:]

    grads, blended = lax.cond(
        fits,
        functools.partial(main_pass, 0),
        functools.partial(main_pass, LARGEST * chans - usual),
        (feat_a, feat_b), shifts, feat, sides, act_grad, tuple(views), tuple(weights[:2]),
    )

    steps = []
    for axis, size in (("dp", dp), ("cols", cols), ("rows", rows)):
        bit = 1
        while bit < size:
            steps.append((axis, [(i, i ^ bit) for i in range(size)]))
            bit *= 2
    parts, prediction = 2, None
    for step, (axis, pairs) in enumerate(steps):
        if step == len(steps) - 1:
            grads = lax.optimization_barrier(grads.astype(BF16))
        other = lax.ppermute(grads, axis, pairs)
        if 1 <= step <= parts:
            prediction = predict(
                blended, weights[2], (chans, height, span), parts, step - 1, prediction
            )
            other, prediction = lax.optimization_barrier((other, prediction))
        if step < len(steps) - 1:
            grads = grads + other
            if step < parts:
                grads, blended = lax.optimization_barrier((grads, blended))
    factor = 1.0 / math.sqrt(imgs * dp * height * rows * span * cols)
    shape = jax.ShapeDtypeStruct((9, chans, chans), F32)
    first_grad, second_grad = call(
        functools.partial(final_kernel, factor), (shape, shape), [], 2, 2
    )(grads, other)
    return (prediction[None], first_grad, second_grad)


def solution(mesh):
    placed = (
        P("dp", None, "rows", "cols"),
        P("dp", None, None),
        P(),
        P(),
        P(),
        P("dp", None, "rows", "cols"),
    )
    return jax.shard_map(
        shards,
        mesh=mesh,
        in_specs=placed,
        out_specs=(P("dp", None, "rows", "cols"), P(), P()),
        check_vma=False,
    )
```

```python
import functools
import math

import jax
import jax.numpy as jnp
from jax import lax
from jax.experimental import pallas as pl
from jax.experimental.pallas import tpu as pltpu
from jax.sharding import PartitionSpec as P


MAXSHIFT = 16
POOL = 4
TILE = 128
SLOT = 32
EXT = 9
FHALO = MAXSHIFT + EXT
USUAL = 14
LARGEST = FHALO + 1
CHALO = 5
F32 = jnp.float32
BF16 = jnp.bfloat16
VMEM = pl.BlockSpec(memory_space=pltpu.VMEM)
SMEM = pl.BlockSpec(memory_space=pltpu.SMEM)
MIB = 1024 * 1024


def lanes_of(shape):
    return lax.broadcasted_iota(jnp.int32, shape, len(shape) - 1)


def turn(values, shift):
    width = values.shape[-1]
    if isinstance(shift, int):
        shift = shift % width
        if shift == 0:
            return values
    return pltpu.roll(values, shift, values.ndim - 1)


def has_sides():
    row, col = lax.axis_index("rows"), lax.axis_index("cols")
    return (
        row > 0,
        row < lax.axis_size("rows") - 1,
        col > 0,
        col < lax.axis_size("cols") - 1,
    )


def as_bf(values):
    return values.astype(F32).astype(BF16)


def one_hot(mask):
    return jnp.where(mask, jnp.ones((), BF16), jnp.zeros((), BF16))


def rows_at(r, chans, count=1):
    if isinstance(r, int):
        return slice(r * chans, (r + count) * chans)
    return pl.ds(pl.multiple_of(r * chans, chans), count * chans)


def to_rows(block):
    chans, height, span = block.shape
    return jnp.transpose(block, (1, 0, 2)).reshape(height * chans, span)


def to_planes(block, chans):
    height = block.shape[0] // chans
    return jnp.transpose(block.reshape(height, chans, block.shape[1]), (1, 0, 2))


def tiles_of(span):
    return [slice(t, t + TILE) for t in range(0, span, TILE)]


def is_even(axis):
    return lax.rem(lax.axis_index(axis), 2) == 0


def swaps(size):
    first = [(i, i ^ 1) for i in range(size)]
    second = [(i, i + 1) for i in range(1, size - 1, 2)]
    return [first, second + [(j, i) for i, j in second]]


def needed(shift, below):
    return jnp.maximum(EXT + shift if below else EXT - shift, 0)


def feature_kernel(index, skip, shifts, feat, msg, *counts):
    chans, height, span = feat.shape
    full = chans * height
    size = msg.shape[0]
    chunk = size // 4
    source = feat[...].reshape(full, span)
    lane = lanes_of((8, full))
    chan, row = lane // height, lane % height
    to_below = is_even("rows") if index == 0 else jnp.logical_not(is_even("rows"))
    target = jnp.full((8, full), -1, jnp.int32)
    at, up, down = jnp.int32(-skip), jnp.int32(0), jnp.int32(0)
    for c in range(chans):
        shift = shifts[0, c]
        n_up, n_down = needed(shift, False), needed(shift, True)
        count = jnp.where(to_below, n_up, n_down)
        first = jnp.where(to_below, height - count, 0)
        mine = (chan == c) & (row >= first) & (row < first + count)
        target = jnp.where(mine, row + (at - first), target)
        at, up, down = at + count, up + n_up, down + n_down
    for out in counts:
        out[...] = jnp.full(out.shape, jnp.maximum(up, down), jnp.int32)
    place = as_bf(lax.broadcasted_iota(jnp.int32, (chunk, full), 0))
    for p in range(0, size, chunk):
        pick = one_hot(place == as_bf(target[0:1] - p))
        msg[p : p + chunk] = jnp.dot(pick, source, preferred_element_type=F32).astype(BF16)


def rows_kernel(source, out):
    for part in tiles_of(source.shape[2]):
        out[:, part] = to_rows(source[:, :, part])


def edge_lanes(shape, right, count):
    lane = lanes_of(shape)
    return jnp.where(jnp.where(right, TILE - 1 - lane, lane) < count, 1.0, 0.0).astype(BF16)


def slots(chans, height):
    half, block = chans // 2, height // 2
    for h in (0, 1):
        for m in (0, 1):
            yield 2 * h + m, slice(h * half, (h + 1) * half), slice(m * block, (m + 1) * block)


def column_kernel(feat, cot, *col_msgs):
    chans, height, span = feat.shape
    for index, msg in enumerate(col_msgs):
        right = is_even("cols") if index == 0 else jnp.logical_not(is_even("cols"))
        part = pl.ds(pl.multiple_of(jnp.where(right, span - TILE, 0), TILE), TILE)
        shape = (1, height // 2, TILE)
        inner = edge_lanes(shape, right, FHALO)
        outer = edge_lanes(shape, right, SLOT) - inner
        total = None
        for q, channels, rows in slots(chans, height):
            cots = turn(cot[channels, rows, part], jnp.where(right, TILE - FHALO, FHALO))
            piece = feat[channels, rows, part] * inner + cots * outer
            piece = turn(piece, jnp.where(right, (q + 1) * SLOT % TILE, q * SLOT))
            total = piece if total is None else total + piece
        msg[...] = total.reshape(msg.shape)


def edge_kernel(cot_rows, *rest):
    cols, (msg_a, msg_b) = rest[:-2], rest[-2:]
    span = cot_rows.shape[1]
    size = msg_a.shape[0] - sum(c.shape[0] * TILE // span for c in cols)
    edge = cot_rows.shape[0] - size
    chans = size // CHALO
    low = jnp.where(is_even("rows"), edge, 0)
    msg_a[0:size] = cot_rows[pl.ds(pl.multiple_of(low, chans), size), :]
    msg_b[0:size] = cot_rows[pl.ds(pl.multiple_of(edge - low, chans), size), :]
    at = size
    for col in cols:
        count = col.shape[0] * TILE // span
        for t, part in enumerate(tiles_of(span)):
            block = col[t * count : (t + 1) * count]
            msg_a[at : at + count, part] = block
            msg_b[at : at + count, part] = block
        at += count


def corner_views(msg, size, cols):
    span = msg.shape[1]
    views, at = [], size
    for col in cols:
        count = col.shape[0] * TILE // span
        views.append(
            jnp.concatenate([msg[at : at + count, part] for part in tiles_of(span)], axis=0)
        )
        at += count
    return views


def halo_block(sources, slot, rows, kind):
    total = None
    if kind == "features":
        count, shift_r, shift_l = FHALO, -slot * SLOT, TILE - (slot + 1) * SLOT
    else:
        count = CHALO
        shift_r, shift_l = -slot * SLOT - FHALO, TILE - (slot + 1) * SLOT + FHALO
    for index, source in enumerate(sources):
        from_right = is_even("cols") if index == 0 else jnp.logical_not(is_even("cols"))
        block = source.reshape(source.shape[0] // rows, rows, TILE)
        block = turn(block, jnp.where(from_right, shift_r % TILE, shift_l % TILE))
        block = block * edge_lanes((1, rows, TILE), jnp.logical_not(from_right), count)
        total = block if total is None else total + block
    return total


def halo_rows(sources, m, rows, kind):
    return to_rows(
        jnp.concatenate([halo_block(sources, 2 * h + m, rows, kind) for h in (0, 1)], axis=0)
    )


def columns_seen(shape, span):
    _, _, has_left, has_right = has_sides()
    lane = lanes_of(shape)
    middle = span + TILE // 2
    return (lane < span) | ((lane < middle) & has_right) | ((lane >= middle) & has_left)


def cell_matrix(width, by_cell):
    shape = (TILE, width) if by_cell else (width, TILE)
    lane = lax.broadcasted_iota(jnp.int32, shape, 1 if by_cell else 0)
    cell = lax.broadcasted_iota(jnp.int32, shape, 0 if by_cell else 1)
    place = lane // POOL + jnp.where(lane >= width - TILE // 2, TILE - width // POOL, 0)
    return jnp.where(place == cell, 1.0, 0.0).astype(BF16)


def cells_seen(shape, span):
    _, _, has_left, has_right = has_sides()
    lane = lanes_of(shape)
    count = span // POOL
    middle = (count + TILE) // 2
    return (lane < count) | ((lane < middle) & has_right) | ((lane >= middle) & has_left)


def store_split(high, low, at, total):
    top = total.astype(BF16)
    high[at, :] = top
    low[at, :] = (total - top.astype(F32)).astype(BF16)


def block_sums(high, low):
    matrix = cell_matrix(high.shape[1], False)
    return jnp.dot(high[...], matrix, preferred_element_type=F32) + jnp.dot(
        low[...], matrix, preferred_element_type=F32
    )


def spread(rows, width, count):
    values = jnp.concatenate(rows, axis=0)
    top = values.astype(BF16)
    rest = (values - top.astype(F32)).astype(BF16)
    matrix = cell_matrix(width, True)[:, 0:count]
    return jnp.dot(
        jnp.concatenate([top, rest], axis=1),
        jnp.concatenate([matrix, matrix], axis=0),
        preferred_element_type=F32,
    )


def fill_bands(out, kernel, count):
    chans = kernel.shape[1]
    out[...] = jnp.zeros(out.shape, out.dtype)
    for k in range(count):
        for b in range(3):
            for a in range(3):
                at = (b * (count + 2) + k + a) * chans
                out[k * chans : (k + 1) * chans, at : at + chans] = kernel[3 * a + b].astype(
                    out.dtype
                )


def fill_turned_bands(out, kernel, count):
    chans = kernel.shape[1]
    out[...] = jnp.zeros(out.shape, out.dtype)
    for k in range(count):
        for b in range(3):
            for a in range(3):
                at = (b * (count + 2) + k + a) * chans
                out[at : at + chans, k * chans : (k + 1) * chans] = kernel[8 - 3 * a - b].astype(
                    out.dtype
                )


def stacked(views, at):
    return jnp.concatenate([view[at, :] for view in views], axis=0)


def conv_sum(parts, chans, step):
    return (
        turn(parts[0:chans], step)
        + parts[chans : 2 * chans]
        + turn(parts[2 * chans : 3 * chans], -step)
    )


def back_kernel(
    ncols, cot, msg_a, msg_b, *rest,
):
    cols, (
        first, bottle, second,
        act_grad, cot_m, cot_0, cot_p, sides, first_bands, bottle_bands, second_bands,
        back, high, low, coarse, bands_f, bands, small_f, small, wide_f,
    ) = rest[:ncols], rest[ncols:]
    chans = second.shape[1]
    full, span = cot.shape
    height = full // chans
    width = span + TILE
    groups = height // POOL
    has_up, has_down, _, _ = has_sides()

    fill_turned_bands(bands_f, second, POOL)
    bands[...] = bands_f[...].T.astype(BF16)
    fill_turned_bands(small_f, bottle, 1)
    small_t = small_f[...].T
    for b in range(3):
        small[rows_at(b, chans)] = small_t[0:chans, 3 * b * chans : 3 * (b + 1) * chans].astype(BF16)
    fill_bands(first_bands, first, POOL)
    fill_bands(wide_f, bottle, 1)
    for b in range(3):
        bottle_bands[rows_at(b, chans)] = wide_f[
            0:chans, 3 * b * chans : 3 * (b + 1) * chans
        ].astype(BF16)
    second_bands[...] = jnp.zeros(second_bands.shape, BF16)
    for k in range(POOL):
        for b in range(3):
            for a in range(3):
                second_bands[
                    rows_at(3 * k + b, chans), (k + a) * chans : (k + a + 1) * chans
                ] = second[3 * a + b]

    size = CHALO * chans
    block = height // 2

    def halo_columns(sources, at):
        for q, channels, rows in slots(chans, height):
            sides[channels, at + rows.start : at + rows.stop, :] = halo_block(
                sources, q, block, "features"
            )

    own = [c[...] for c in cols]
    halo_columns(own, height)
    cot_0[rows_at(CHALO, chans, height), 0:span] = cot[...]
    for m in (0, 1):
        cot_0[rows_at(CHALO + m * block, chans, block), span:width] = halo_rows(
            own, m, block, "cotangent"
        )

    def vertical(up, down):
        cot_0[rows_at(0, chans, CHALO), 0:span] = up[0:size]
        cot_0[rows_at(CHALO + height, chans, CHALO), 0:span] = down[0:size]
        above, below = corner_views(up, size, cols), corner_views(down, size, cols)
        cot_0[rows_at(0, chans, CHALO), span:width] = halo_rows(above, 1, block, "cotangent")[
            (block - CHALO) * chans :
        ]
        cot_0[rows_at(CHALO + height, chans, CHALO), span:width] = halo_rows(
            below, 0, block, "cotangent"
        )[0:size]
        halo_columns(above, 0)
        halo_columns(below, 2 * height)

    pl.when(is_even("rows"))(lambda: vertical(msg_b, msg_a))
    pl.when(jnp.logical_not(is_even("rows")))(lambda: vertical(msg_a, msg_b))
    for j in range(height + 2 * CHALO):
        at = rows_at(j, chans)
        cot_m[at] = turn(cot_0[at], 1)
        cot_p[at] = turn(cot_0[at], -1)
    def group(g, _):
        at = rows_at(g * POOL, chans, POOL + 2)
        rows = jnp.dot(
            bands[...], stacked((cot_m, cot_0, cot_p), at), preferred_element_type=F32
        ).astype(BF16)
        back[rows_at(g * POOL, chans, POOL), :] = rows[:, 0:span]
        rows = rows.astype(F32)
        total = rows[0:chans]
        for k in range(1, POOL):
            total = total + rows[k * chans : (k + 1) * chans]
        store_split(high, low, rows_at(g, chans), total)
        return 0

    lax.fori_loop(0, groups + 2, group, 0, unroll=5)
    sums = block_sums(high, low)
    seen_cells = cells_seen((chans, TILE), span)
    for g in range(groups + 2):
        at = rows_at(g, chans)
        seen = seen_cells
        if g == 0:
            seen = seen & has_up
        elif g == groups + 1:
            seen = seen & has_down
        coarse[at] = jnp.where(seen, sums[at], 0.0).astype(BF16)
    means = []
    for g in range(groups):
        parts = jnp.dot(small[...], coarse[rows_at(g, chans, 3), :], preferred_element_type=F32)
        means.append(conv_sum(parts, chans, 1) * (1.0 / POOL**2))
    mean = spread(means, width, span)
    for r in range(height):
        act_grad[rows_at(r, chans), :] = (
            back[rows_at(r + POOL, chans), :].astype(F32) + mean[rows_at(r // POOL, chans)]
        )


def correlate(u, u0, views, v0, acc, height, chans, span):
    groups = range(0, height, POOL)
    left = jnp.concatenate(
        [
            jnp.concatenate(
                [view[rows_at(v0 + g, chans, POOL + 2), 0:span] for view in views], axis=0
            )
            for g in groups
        ],
        axis=1,
    )
    right = jnp.concatenate([u[rows_at(u0 + g, chans, POOL), 0:span] for g in groups], axis=1)
    acc[...] = lax.dot_general(
        left, right, (((1,), (1,)), ((), ())), preferred_element_type=F32
    )


def folded(acc, chans):
    lane = lanes_of((3 * chans, TILE))
    result = jnp.zeros((3 * chans, TILE), F32)
    for b in range(3):
        total = None
        for k in range(POOL):
            block = turn(
                acc[rows_at(b * (POOL + 2) + k, chans, 3), 0:TILE], (b - k) * chans
            )
            total = block if total is None else total + block
        result = jnp.where((lane >= b * chans) & (lane < (b + 1) * chans), total, result)
    return result


def main_kernel(
    shifts, feat, feat_a, feat_b, sides, act_grad, view_m, view_0, view_p, bands, small,
    grads, blended,
    lent, moved, warp_m, warp_0, warp_p, act, high, low, pooled, pre_grad, acc,
):
    chans, height, span = feat.shape
    tiles = span // TILE
    width = span + TILE
    groups = height // POOL
    has_up, has_down, has_left, has_right = has_sides()
    seen_cols = columns_seen((chans, width), span)

    size = feat_a.shape[0]
    window = lent.shape[1] - size
    lent[:, size:, :] = jnp.zeros((2, window, span), BF16)

    def borrow(up, down):
        lent[0, 0:size] = up[...]
        lent[1, 0:size] = down[...]

    pl.when(is_even("rows"))(lambda: borrow(feat_b, feat_a))
    pl.when(jnp.logical_not(is_even("rows")))(lambda: borrow(feat_a, feat_b))

    tall = moved.shape[1]
    lane = lanes_of((tall, TILE))
    seen_halo = one_hot(((lane < TILE // 2) & has_right) | ((lane >= TILE // 2) & has_left))
    lane, mirrored = as_bf(lane), as_bf(TILE - 1 - lane)
    step = as_bf(
        lanes_of((tall, 3 * height)) - lax.broadcasted_iota(jnp.int32, (tall, 3 * height), 0)
    )
    depth = 2 * window + height
    source = lanes_of((1, depth))
    apart = as_bf(lax.broadcasted_iota(jnp.int32, (tall, depth), 0) - lanes_of((tall, depth)))
    align = 16

    def warp(c, ats):
        at_up, at_down = ats
        shift, move = shifts[0, c], shifts[1, c]
        n_up, n_down = needed(shift, False), needed(shift, True)
        base_up, base_down = (
            pl.multiple_of(lax.div(at, align) * align, align) for at in (at_up, at_down)
        )
        skip_up, skip_down = at_up - base_up, at_down - base_down
        own = EXT - window - shift
        below = own - skip_down
        above = EXT - skip_up - n_up - shift
        in_up = (source >= skip_up) & (source < skip_up + n_up)
        first_down = window + height + skip_down
        in_down = (source >= first_down) & (source < first_down + n_down)
        none = 4 * depth
        offset = jnp.where(
            source < window,
            jnp.where(in_up, above, none),
            jnp.where(source < window + height, own, jnp.where(in_down, below, none)),
        )
        pick = one_hot(apart == as_bf(offset))
        rows = jnp.concatenate(
            [lent[0, pl.ds(base_up, window), :], feat[c], lent[1, pl.ds(base_down, window), :]], axis=0
        )
        plane = jnp.dot(pick, rows, preferred_element_type=F32).astype(BF16)
        pick = one_hot(step == as_bf(height - EXT + shift))
        plane = [plane[:, part] for part in tiles_of(span)]
        plane.append(jnp.dot(pick, sides[c], preferred_element_type=F32).astype(BF16))
        amount = jnp.where(move > 0, TILE - move, -move)
        parts = [turn(part, amount) for part in plane]
        inside = jnp.where(move > 0, lane, mirrored) < as_bf(TILE - jnp.abs(move))
        for t, part in enumerate(tiles_of(width)):
            after, before = parts[(t + 1) % (tiles + 1)], parts[t - 1]
            result = jnp.where(inside, parts[t], jnp.where(move > 0, after, before))
            moved[c, :, part] = result * seen_halo if t == tiles else result
        return at_up + n_up, at_down + n_down

    lax.fori_loop(0, chans, warp, (jnp.int32(0), jnp.int32(0)), unroll=8)
    chunk = 16
    for r in range(0, tall, chunk):
        for part in tiles_of(width):
            warp_0[rows_at(r, chans, chunk), part] = to_rows(moved[:, r : r + chunk, part])

    def clear(r, count):
        warp_0[rows_at(r, chans, count)] = jnp.zeros((count * chans, width), BF16)

    pl.when(jnp.logical_not(has_up))(lambda: clear(0, EXT))
    pl.when(jnp.logical_not(has_down))(lambda: clear(EXT + height, EXT))
    for j in range(height + 2 * EXT):
        at = rows_at(j, chans)
        warp_m[at] = turn(warp_0[at], 1)
        warp_p[at] = turn(warp_0[at], -1)

    def first_group(g, own):
        at = rows_at(g * POOL, chans, POOL + 2)
        pre = jnp.dot(
            bands[...], stacked((warp_m, warp_0, warp_p), at), preferred_element_type=F32
        )
        sigma = 0.5 * jnp.tanh(0.5 * pre) + 0.5
        rows = (pre * sigma).astype(BF16)
        act[rows_at(g * POOL, chans, POOL), :] = rows
        rows = rows.astype(F32)
        total = rows[0:chans]
        for k in range(1, POOL):
            total = total + rows[k * chans : (k + 1) * chans]
        store_split(high, low, rows_at(g, chans), total)
        if own:
            there = rows_at(g * POOL - 2 * POOL, chans, POOL)
            pre, sigma = pre[:, 0:span], sigma[:, 0:span]
            pre_grad[there, :] = (
                act_grad[there, :] * (sigma * (1.0 + pre * (1.0 - sigma)))
            ).astype(BF16)
        return 0

    for g in (0, 1, groups + 2, groups + 3):
        first_group(g, False)
    lax.fori_loop(2, groups + 2, lambda g, _: first_group(g, True), 0, unroll=4)
    sums = block_sums(high, low)
    seen_cells = cells_seen((chans, TILE), span)
    for g in range(groups + 4):
        at = rows_at(g, chans)
        seen = seen_cells
        if g < 2:
            seen = seen & has_up
        elif g >= groups + 2:
            seen = seen & has_down
        pooled[at] = jnp.where(seen, sums[at] * (1.0 / POOL**2), 0.0).astype(BF16)

    bottles = []
    for g in range(groups + 2):
        parts = jnp.dot(small[...], pooled[rows_at(g, chans, 3), :], preferred_element_type=F32)
        bottles.append(conv_sum(parts, chans, 1))
    bottle = spread(bottles, width, width)
    for g in range(groups + 2):
        rows, seen = range(POOL), seen_cols
        if g == 0:
            rows, seen = (POOL - 1,), seen & has_up
        elif g == groups + 1:
            rows, seen = (0,), seen & has_down
        for k in rows:
            row = act[rows_at((g + 1) * POOL + k, chans), :].astype(F32) + bottle[rows_at(g, chans)]
            blended[rows_at(g * POOL + k - POOL + 1, chans), :] = jnp.where(seen, row, 0.0).astype(
                BF16
            )

    correlate(pre_grad, 0, (warp_m, warp_0, warp_p), EXT - 1, acc, height, chans, span)
    first_part = folded(acc, chans)
    correlate(blended, 1, (view_m, view_0, view_p), CHALO - 1, acc, height, chans, span)
    second_part = folded(acc, chans)
    lane = lanes_of((3 * chans, TILE))
    grads[0 : 3 * chans] = jnp.where(lane < 3 * chans, first_part, turn(second_part, 3 * chans))
    half = 3 * chans // 2
    grads[3 * chans :] = jnp.where(
        lane[0:half] < TILE // 2,
        turn(second_part[0:half], -chans),
        turn(second_part[half:], TILE // 2 - chans),
    )


def predict_kernel(part, blended, bands, *rest):
    out, rows = rest[-2:]
    chans, height, span = out.shape

    def group(g, _):
        at = rows_at(part * height + g * POOL, chans, POOL + 2)
        parts = jnp.dot(bands[...], blended[at, :], preferred_element_type=F32)
        for k in range(POOL):
            row = conv_sum(parts[3 * k * chans : 3 * (k + 1) * chans], chans, 1)
            rows[rows_at(g * POOL + k, chans), :] = row[:, 0:span].astype(BF16)
        return 0

    lax.fori_loop(0, height // POOL, group, 0, unroll=2)
    for part in tiles_of(span):
        out[:, :, part] = to_planes(rows[:, part], chans)


def final_kernel(factor, mine, other, first, second):
    chans = first.shape[1]
    total = (mine[...].astype(F32) + other[...].astype(F32)) * factor
    turned = total[0 : 3 * chans].T
    for b in range(3):
        for a in range(3):
            first[3 * a + b] = turned[b * chans : (b + 1) * chans, a * chans : (a + 1) * chans]
    half = 3 * chans // 2
    low = total[3 * chans :]
    both = jnp.concatenate([low, turn(low, -(TILE // 2))], axis=0)
    for a in range(3):
        at = slice((2 - a) * chans, (3 - a) * chans)
        second[3 * a + 2] = turn(total[at], -3 * chans)[:, 0:chans]
        second[3 * a + 1] = both[at, 0:chans]
        second[3 * a + 0] = turn(both[at], -chans)[:, 0:chans]


def call(kernel, outs, scratch, n_in, limit, flops=0, smem_first=False, **more):
    specs = [VMEM] * n_in
    if smem_first:
        specs[0] = SMEM
    more.setdefault("in_specs", specs)
    more.setdefault("out_specs", jax.tree.map(lambda _: VMEM, outs))
    return pl.pallas_call(
        kernel,
        out_shape=outs,
        scratch_shapes=scratch,
        compiler_params=pltpu.CompilerParams(vmem_limit_bytes=limit * MIB),
        cost_estimate=pl.CostEstimate(flops=flops, bytes_accessed=4 * MIB, transcendentals=0),
        **more,
    )


def predict(blended, bands, shape, parts, part, before):
    chans, height, span = shape
    rows = height // parts
    block = pl.BlockSpec((chans, rows, span), lambda i: (0, part, 0))
    whole = lambda a: pl.BlockSpec(a.shape, lambda i: (0,) * a.ndim)
    args = (blended, bands)
    specs = [whole(a) for a in args]
    more = {}
    if before is not None:
        args += (before,)
        specs.append(pl.BlockSpec(memory_space=pl.ANY))
        more["input_output_aliases"] = {2: 0}
    return call(
        functools.partial(predict_kernel, part),
        jax.ShapeDtypeStruct(shape, BF16),
        [
            pltpu.VMEM((chans * rows, span), BF16),
        ],
        len(args),
        6,
        flops=10**9,
        grid=(1,),
        in_specs=specs,
        out_specs=block,
        **more,
    )(*args)


def bf(*shape):
    return jax.ShapeDtypeStruct(shape, BF16)


def swapped(messages, axis):
    pairs = [p for p in swaps(lax.axis_size(axis)) if p]
    return [lax.ppermute(m, axis, p) for m, p in zip(messages, pairs)]


def pack_rows(index, skip, size, shifts, feat, counted=False):
    message = bf(size, feat.shape[2])
    if counted:
        message = (message, jax.ShapeDtypeStruct((8, TILE), jnp.int32))
    return call(
        functools.partial(feature_kernel, index, skip),
        message, [], 2, 6, smem_first=True,
    )(shifts, feat)


def main_pass(rest, lent, shifts, feat, sides, act_grad, views, bands):
    chans, height, span = feat.shape
    width = span + TILE
    full = height * chans
    groups = height // POOL
    band = 3 * (POOL + 2) * chans
    if rest:
        size = lent[0].shape[0]
        more = swapped([pack_rows(i, size, rest, shifts, feat) for i in (0, 1)], "rows")
        lent = [jnp.concatenate(pair, axis=0) for pair in zip(lent, more)]
    size = lent[0].shape[0]
    tall = pl.cdiv(height + 2 * EXT, 16) * 16
    grads, blended = call(
        main_kernel,
        (jax.ShapeDtypeStruct((9 * chans // 2, TILE), F32), bf((height + 2) * chans, width)),
        [
            pltpu.VMEM((2, size + 48, span), BF16),
            pltpu.VMEM((chans, tall, width), BF16),
        ]
        + [pltpu.VMEM((tall * chans, width), BF16)] * 3
        + [pltpu.VMEM(((height + 4 * POOL) * chans, width), BF16)]
        + [pltpu.VMEM(((groups + 4) * chans, width), BF16)] * 2
        + [pltpu.VMEM(((groups + 4) * chans, TILE), BF16)]
        + [
            pltpu.VMEM((full, span), BF16),
            pltpu.VMEM((band, POOL * chans), F32),
        ],
        11,
        14,
        flops=10**10,
        smem_first=True,
    )(
        shifts, feat, *lent, sides, act_grad, *views, *bands
    )

    return grads, blended


def shards(features, shifts, first_kernel, bottle_kernel, second_kernel, cotangent):
    imgs, chans, height, span = features.shape
    rows, cols, dp = (lax.axis_size(a) for a in ("rows", "cols", "dp"))
    full = height * chans

    width = span + TILE
    groups = height // POOL
    feat, cot, shifts = features[0], cotangent[0], shifts[0].T
    row_pairs = swaps(rows)

    usual = USUAL * chans
    message, total = pack_rows(0, 0, usual, shifts, feat, counted=True)
    message, total, cot = lax.optimization_barrier((message, total, cot))
    feat_a = lax.ppermute(message, "rows", row_pairs[0])
    bit = 1
    while bit < dp:
        total = jnp.maximum(total, lax.ppermute(total, "dp", [(i, i ^ bit) for i in range(dp)]))
        bit *= 2

    packed = chans * (height * SLOT // TILE)
    messages = call(
        column_kernel, (bf(packed, TILE),) * (1 if cols == 2 else 2), [], 2, 4, flops=2 * 10**10
    )(feat, cot)
    col_msgs = swapped(messages, "cols")
    ncols = len(col_msgs)
    message = pack_rows(1, 0, usual, shifts, feat)
    col_msgs, message, total = lax.optimization_barrier((col_msgs, message, total))
    feat_b = lax.ppermute(message, "rows", row_pairs[1])
    cot_rows = call(rows_kernel, bf(full, span), [], 1, 4)(cot)
    halo = bf(CHALO * chans + ncols * packed * TILE // span, span)
    messages = call(edge_kernel, (halo, halo), [], 1 + ncols, 4)(cot_rows, *col_msgs)
    row_msgs = swapped(messages, "rows")
    row_msgs[0], total = lax.optimization_barrier((row_msgs[0], total))
    fits = total[0, 0] <= usual
    row_msgs, feat_a, fits = lax.optimization_barrier((row_msgs, feat_a, fits))

    tall_c = (height + 2 * CHALO) * chans
    view = bf(tall_c, width)
    band = 3 * (POOL + 2) * chans
    act_grad, *rest = call(
        functools.partial(back_kernel, ncols),
        (
            jax.ShapeDtypeStruct((full, span), F32), view, view, view,
            bf(chans, 3 * height, TILE), bf(POOL * chans, band), bf(3 * chans, 3 * chans),
            bf(3 * POOL * chans, (POOL + 2) * chans),
        ),
        [pltpu.VMEM(((height + 2 * POOL) * chans, span), BF16)]
        + [pltpu.VMEM(((groups + 2) * chans, width), BF16)] * 2
        + [pltpu.VMEM(((groups + 2) * chans, TILE), BF16)]
        + [
            pltpu.VMEM((band, POOL * chans), F32),
            pltpu.VMEM((POOL * chans, band), BF16),
            pltpu.VMEM((9 * chans, TILE), F32),
            pltpu.VMEM((3 * chans, 3 * chans), BF16),
            pltpu.VMEM((chans, 9 * chans), F32),
        ],
        6 + ncols,
        8,
        flops=8 * 10**9,
    )(cot_rows, *row_msgs, *col_msgs, first_kernel, bottle_kernel, second_kernel)
    views, sides, weights = rest[:3], rest[3], rest[4:]

    grads, blended = lax.cond(
        fits,
        functools.partial(main_pass, 0),
        functools.partial(main_pass, LARGEST * chans - usual),
        (feat_a, feat_b), shifts, feat, sides, act_grad, tuple(views), tuple(weights[:2]),
    )

    steps = []
    for axis, size in (("dp", dp), ("cols", cols), ("rows", rows)):
        bit = 1
        while bit < size:
            steps.append((axis, [(i, i ^ bit) for i in range(size)]))
            bit *= 2
    parts, prediction = 2, None
    for step, (axis, pairs) in enumerate(steps):
        if step == len(steps) - 1:
            grads = lax.optimization_barrier(grads.astype(BF16))
        other = lax.ppermute(grads, axis, pairs)
        if 1 <= step <= parts:
            prediction = predict(
                blended, weights[2], (chans, height, span), parts, step - 1, prediction
            )
            other, prediction = lax.optimization_barrier((other, prediction))
        if step < len(steps) - 1:
            grads = grads + other
            if step < parts:
                grads, blended = lax.optimization_barrier((grads, blended))
    factor = 1.0 / math.sqrt(imgs * dp * height * rows * span * cols)
    shape = jax.ShapeDtypeStruct((9, chans, chans), F32)
    first_grad, second_grad = call(
        functools.partial(final_kernel, factor), (shape, shape), [], 2, 2
    )(grads, other)
    return (prediction[None], first_grad, second_grad)


def solution(mesh):
    placed = (
        P("dp", None, "rows", "cols"),
        P("dp", None, None),
        P(),
        P(),
        P(),
        P("dp", None, "rows", "cols"),
    )
    return jax.shard_map(
        shards,
        mesh=mesh,
        in_specs=placed,
        out_specs=(P("dp", None, "rows", "cols"), P(), P()),
        check_vma=False,
    )
```

```python
import functools
import math

import jax
import jax.numpy as jnp
from jax import lax
from jax.experimental import pallas as pl
from jax.experimental.pallas import tpu as pltpu
from jax.sharding import PartitionSpec as P


MAXSHIFT = 16
POOL = 4
TILE = 128
SLOT = 32
EXT = 9
FHALO = MAXSHIFT + EXT
USUAL = 14
LARGEST = FHALO + 1
CHALO = 5
F32 = jnp.float32
BF16 = jnp.bfloat16
VMEM = pl.BlockSpec(memory_space=pltpu.VMEM)
SMEM = pl.BlockSpec(memory_space=pltpu.SMEM)
MIB = 1024 * 1024


def lanes_of(shape):
    return lax.broadcasted_iota(jnp.int32, shape, len(shape) - 1)


def turn(values, shift):
    width = values.shape[-1]
    if isinstance(shift, int):
        shift = shift % width
        if shift == 0:
            return values
    return pltpu.roll(values, shift, values.ndim - 1)


def has_sides():
    row, col = lax.axis_index("rows"), lax.axis_index("cols")
    return (
        row > 0,
        row < lax.axis_size("rows") - 1,
        col > 0,
        col < lax.axis_size("cols") - 1,
    )


def as_bf(values):
    return values.astype(F32).astype(BF16)


def one_hot(mask):
    return jnp.where(mask, jnp.ones((), BF16), jnp.zeros((), BF16))


def rows_at(r, chans, count=1):
    if isinstance(r, int):
        return slice(r * chans, (r + count) * chans)
    return pl.ds(pl.multiple_of(r * chans, chans), count * chans)


def to_rows(block):
    chans, height, span = block.shape
    return jnp.transpose(block, (1, 0, 2)).reshape(height * chans, span)


def to_planes(block, chans):
    height = block.shape[0] // chans
    return jnp.transpose(block.reshape(height, chans, block.shape[1]), (1, 0, 2))


def tiles_of(span):
    return [slice(t, t + TILE) for t in range(0, span, TILE)]


def is_even(axis):
    return lax.rem(lax.axis_index(axis), 2) == 0


def swaps(size):
    first = [(i, i ^ 1) for i in range(size)]
    second = [(i, i + 1) for i in range(1, size - 1, 2)]
    return [first, second + [(j, i) for i, j in second]]


def needed(shift, below):
    return jnp.maximum(EXT + shift if below else EXT - shift, 0)


def feature_kernel(index, skip, shifts, feat, msg, *counts):
    chans, height, span = feat.shape
    full = chans * height
    size = msg.shape[0]
    chunk = size // 4
    source = feat[...].reshape(full, span)
    lane = lanes_of((8, full))
    chan, row = lane // height, lane % height
    to_below = is_even("rows") if index == 0 else jnp.logical_not(is_even("rows"))
    target = jnp.full((8, full), -1, jnp.int32)
    at, up, down = jnp.int32(-skip), jnp.int32(0), jnp.int32(0)
    for c in range(chans):
        shift = shifts[0, c]
        n_up, n_down = needed(shift, False), needed(shift, True)
        count = jnp.where(to_below, n_up, n_down)
        first = jnp.where(to_below, height - count, 0)
        mine = (chan == c) & (row >= first) & (row < first + count)
        target = jnp.where(mine, row + (at - first), target)
        at, up, down = at + count, up + n_up, down + n_down
    for out in counts:
        out[...] = jnp.full(out.shape, jnp.maximum(up, down), jnp.int32)
    place = as_bf(lax.broadcasted_iota(jnp.int32, (chunk, full), 0))
    for p in range(0, size, chunk):
        pick = one_hot(place == as_bf(target[0:1] - p))
        msg[p : p + chunk] = jnp.dot(pick, source, preferred_element_type=F32).astype(BF16)


def rows_kernel(source, out):
    for part in tiles_of(source.shape[2]):
        out[:, part] = to_rows(source[:, :, part])


def edge_lanes(shape, right, count):
    lane = lanes_of(shape)
    return jnp.where(jnp.where(right, TILE - 1 - lane, lane) < count, 1.0, 0.0).astype(BF16)


def slots(chans, height):
    half, block = chans // 2, height // 2
    for h in (0, 1):
        for m in (0, 1):
            yield 2 * h + m, slice(h * half, (h + 1) * half), slice(m * block, (m + 1) * block)


def column_kernel(feat, cot, *col_msgs):
    chans, height, span = feat.shape
    for index, msg in enumerate(col_msgs):
        right = is_even("cols") if index == 0 else jnp.logical_not(is_even("cols"))
        part = pl.ds(pl.multiple_of(jnp.where(right, span - TILE, 0), TILE), TILE)
        shape = (1, height // 2, TILE)
        inner = edge_lanes(shape, right, FHALO)
        outer = edge_lanes(shape, right, SLOT) - inner
        total = None
        for q, channels, rows in slots(chans, height):
            cots = turn(cot[channels, rows, part], jnp.where(right, TILE - FHALO, FHALO))
            piece = feat[channels, rows, part] * inner + cots * outer
            piece = turn(piece, jnp.where(right, (q + 1) * SLOT % TILE, q * SLOT))
            total = piece if total is None else total + piece
        msg[...] = total.reshape(msg.shape)


def edge_kernel(cot_rows, *rest):
    cols, (msg_a, msg_b) = rest[:-2], rest[-2:]
    span = cot_rows.shape[1]
    size = msg_a.shape[0] - sum(c.shape[0] * TILE // span for c in cols)
    edge = cot_rows.shape[0] - size
    chans = size // CHALO
    low = jnp.where(is_even("rows"), edge, 0)
    msg_a[0:size] = cot_rows[pl.ds(pl.multiple_of(low, chans), size), :]
    msg_b[0:size] = cot_rows[pl.ds(pl.multiple_of(edge - low, chans), size), :]
    at = size
    for col in cols:
        count = col.shape[0] * TILE // span
        for t, part in enumerate(tiles_of(span)):
            block = col[t * count : (t + 1) * count]
            msg_a[at : at + count, part] = block
            msg_b[at : at + count, part] = block
        at += count


def corner_views(msg, size, cols):
    span = msg.shape[1]
    views, at = [], size
    for col in cols:
        count = col.shape[0] * TILE // span
        views.append(
            jnp.concatenate([msg[at : at + count, part] for part in tiles_of(span)], axis=0)
        )
        at += count
    return views


def halo_block(sources, slot, rows, kind):
    total = None
    if kind == "features":
        count, shift_r, shift_l = FHALO, -slot * SLOT, TILE - (slot + 1) * SLOT
    else:
        count = CHALO
        shift_r, shift_l = -slot * SLOT - FHALO, TILE - (slot + 1) * SLOT + FHALO
    for index, source in enumerate(sources):
        from_right = is_even("cols") if index == 0 else jnp.logical_not(is_even("cols"))
        block = source.reshape(source.shape[0] // rows, rows, TILE)
        block = turn(block, jnp.where(from_right, shift_r % TILE, shift_l % TILE))
        block = block * edge_lanes((1, rows, TILE), jnp.logical_not(from_right), count)
        total = block if total is None else total + block
    return total


def halo_rows(sources, m, rows, kind):
    return to_rows(
        jnp.concatenate([halo_block(sources, 2 * h + m, rows, kind) for h in (0, 1)], axis=0)
    )


def columns_seen(shape, span):
    _, _, has_left, has_right = has_sides()
    lane = lanes_of(shape)
    middle = span + TILE // 2
    return (lane < span) | ((lane < middle) & has_right) | ((lane >= middle) & has_left)


def cell_matrix(width, by_cell):
    shape = (TILE, width) if by_cell else (width, TILE)
    lane = lax.broadcasted_iota(jnp.int32, shape, 1 if by_cell else 0)
    cell = lax.broadcasted_iota(jnp.int32, shape, 0 if by_cell else 1)
    place = lane // POOL + jnp.where(lane >= width - TILE // 2, TILE - width // POOL, 0)
    return jnp.where(place == cell, 1.0, 0.0).astype(BF16)


def cells_seen(shape, span):
    _, _, has_left, has_right = has_sides()
    lane = lanes_of(shape)
    count = span // POOL
    middle = (count + TILE) // 2
    return (lane < count) | ((lane < middle) & has_right) | ((lane >= middle) & has_left)


def store_split(high, low, at, total):
    top = total.astype(BF16)
    high[at, :] = top
    low[at, :] = (total - top.astype(F32)).astype(BF16)


def block_sums(high, low):
    matrix = cell_matrix(high.shape[1], False)
    return jnp.dot(high[...], matrix, preferred_element_type=F32) + jnp.dot(
        low[...], matrix, preferred_element_type=F32
    )


def spread(rows, width, count):
    values = jnp.concatenate(rows, axis=0)
    top = values.astype(BF16)
    rest = (values - top.astype(F32)).astype(BF16)
    matrix = cell_matrix(width, True)[:, 0:count]
    return jnp.dot(
        jnp.concatenate([top, rest], axis=1),
        jnp.concatenate([matrix, matrix], axis=0),
        preferred_element_type=F32,
    )


def fill_bands(out, kernel, count):
    chans = kernel.shape[1]
    out[...] = jnp.zeros(out.shape, out.dtype)
    for k in range(count):
        for b in range(3):
            for a in range(3):
                at = (b * (count + 2) + k + a) * chans
                out[k * chans : (k + 1) * chans, at : at + chans] = kernel[3 * a + b].astype(
                    out.dtype
                )


def fill_turned_bands(out, kernel, count):
    chans = kernel.shape[1]
    out[...] = jnp.zeros(out.shape, out.dtype)
    for k in range(count):
        for b in range(3):
            for a in range(3):
                at = (b * (count + 2) + k + a) * chans
                out[at : at + chans, k * chans : (k + 1) * chans] = kernel[8 - 3 * a - b].astype(
                    out.dtype
                )


def stacked(views, at):
    return jnp.concatenate([view[at, :] for view in views], axis=0)


def conv_sum(parts, chans, step):
    return (
        turn(parts[0:chans], step)
        + parts[chans : 2 * chans]
        + turn(parts[2 * chans : 3 * chans], -step)
    )


def back_kernel(
    ncols, cot, msg_a, msg_b, *rest,
):
    cols, (
        first, bottle, second,
        act_grad, cot_m, cot_0, cot_p, sides, first_bands, bottle_bands, second_bands,
        back, high, low, coarse, bands_f, bands, small_f, small, wide_f,
    ) = rest[:ncols], rest[ncols:]
    chans = second.shape[1]
    full, span = cot.shape
    height = full // chans
    width = span + TILE
    groups = height // POOL
    has_up, has_down, _, _ = has_sides()

    fill_turned_bands(bands_f, second, POOL)
    bands[...] = bands_f[...].T.astype(BF16)
    fill_turned_bands(small_f, bottle, 1)
    small_t = small_f[...].T
    for b in range(3):
        small[rows_at(b, chans)] = small_t[0:chans, 3 * b * chans : 3 * (b + 1) * chans].astype(BF16)
    fill_bands(first_bands, first, POOL)
    fill_bands(wide_f, bottle, 1)
    for b in range(3):
        bottle_bands[rows_at(b, chans)] = wide_f[
            0:chans, 3 * b * chans : 3 * (b + 1) * chans
        ].astype(BF16)
    second_bands[...] = jnp.zeros(second_bands.shape, BF16)
    for k in range(POOL):
        for b in range(3):
            for a in range(3):
                second_bands[
                    rows_at(3 * k + b, chans), (k + a) * chans : (k + a + 1) * chans
                ] = second[3 * a + b]

    size = CHALO * chans
    block = height // 2

    def halo_columns(sources, at):
        for q, channels, rows in slots(chans, height):
            sides[channels, at + rows.start : at + rows.stop, :] = halo_block(
                sources, q, block, "features"
            )

    own = [c[...] for c in cols]
    halo_columns(own, height)
    cot_0[rows_at(CHALO, chans, height), 0:span] = cot[...]
    for m in (0, 1):
        cot_0[rows_at(CHALO + m * block, chans, block), span:width] = halo_rows(
            own, m, block, "cotangent"
        )

    def vertical(up, down):
        cot_0[rows_at(0, chans, CHALO), 0:span] = up[0:size]
        cot_0[rows_at(CHALO + height, chans, CHALO), 0:span] = down[0:size]
        above, below = corner_views(up, size, cols), corner_views(down, size, cols)
        cot_0[rows_at(0, chans, CHALO), span:width] = halo_rows(above, 1, block, "cotangent")[
            (block - CHALO) * chans :
        ]
        cot_0[rows_at(CHALO + height, chans, CHALO), span:width] = halo_rows(
            below, 0, block, "cotangent"
        )[0:size]
        halo_columns(above, 0)
        halo_columns(below, 2 * height)

    pl.when(is_even("rows"))(lambda: vertical(msg_b, msg_a))
    pl.when(jnp.logical_not(is_even("rows")))(lambda: vertical(msg_a, msg_b))
    for j in range(height + 2 * CHALO):
        at = rows_at(j, chans)
        cot_m[at] = turn(cot_0[at], 1)
        cot_p[at] = turn(cot_0[at], -1)
    def group(g, _):
        at = rows_at(g * POOL, chans, POOL + 2)
        rows = jnp.dot(
            bands[...], stacked((cot_m, cot_0, cot_p), at), preferred_element_type=F32
        ).astype(BF16)
        back[rows_at(g * POOL, chans, POOL), :] = rows[:, 0:span]
        rows = rows.astype(F32)
        total = rows[0:chans]
        for k in range(1, POOL):
            total = total + rows[k * chans : (k + 1) * chans]
        store_split(high, low, rows_at(g, chans), total)
        return 0

    lax.fori_loop(0, groups + 2, group, 0, unroll=5)
    sums = block_sums(high, low)
    seen_cells = cells_seen((chans, TILE), span)
    for g in range(groups + 2):
        at = rows_at(g, chans)
        seen = seen_cells
        if g == 0:
            seen = seen & has_up
        elif g == groups + 1:
            seen = seen & has_down
        coarse[at] = jnp.where(seen, sums[at], 0.0).astype(BF16)
    means = []
    for g in range(groups):
        parts = jnp.dot(small[...], coarse[rows_at(g, chans, 3), :], preferred_element_type=F32)
        means.append(conv_sum(parts, chans, 1) * (1.0 / POOL**2))
    mean = spread(means, width, span)
    for r in range(height):
        act_grad[rows_at(r, chans), :] = (
            back[rows_at(r + POOL, chans), :].astype(F32) + mean[rows_at(r // POOL, chans)]
        )


def correlate(u, u0, views, v0, acc, height, chans, span):
    groups = range(0, height, POOL)
    left = jnp.concatenate(
        [
            jnp.concatenate(
                [view[rows_at(v0 + g, chans, POOL + 2), 0:span] for view in views], axis=0
            )
            for g in groups
        ],
        axis=1,
    )
    right = jnp.concatenate([u[rows_at(u0 + g, chans, POOL), 0:span] for g in groups], axis=1)
    acc[...] = lax.dot_general(
        left, right, (((1,), (1,)), ((), ())), preferred_element_type=F32
    )


def folded(acc, chans):
    lane = lanes_of((3 * chans, TILE))
    result = jnp.zeros((3 * chans, TILE), F32)
    for b in range(3):
        total = None
        for k in range(POOL):
            block = turn(
                acc[rows_at(b * (POOL + 2) + k, chans, 3), 0:TILE], (b - k) * chans
            )
            total = block if total is None else total + block
        result = jnp.where((lane >= b * chans) & (lane < (b + 1) * chans), total, result)
    return result


def main_kernel(
    shifts, feat, feat_a, feat_b, sides, act_grad, view_m, view_0, view_p, bands, small,
    grads, blended,
    lent, moved, warp_m, warp_0, warp_p, act, high, low, pooled, pre_grad, acc,
):
    chans, height, span = feat.shape
    tiles = span // TILE
    width = span + TILE
    groups = height // POOL
    has_up, has_down, has_left, has_right = has_sides()
    seen_cols = columns_seen((chans, width), span)

    size = feat_a.shape[0]
    window = lent.shape[1] - size
    lent[:, size:, :] = jnp.zeros((2, window, span), BF16)

    def borrow(up, down):
        lent[0, 0:size] = up[...]
        lent[1, 0:size] = down[...]

    pl.when(is_even("rows"))(lambda: borrow(feat_b, feat_a))
    pl.when(jnp.logical_not(is_even("rows")))(lambda: borrow(feat_a, feat_b))

    tall = moved.shape[1]
    lane = lanes_of((tall, TILE))
    seen_halo = one_hot(((lane < TILE // 2) & has_right) | ((lane >= TILE // 2) & has_left))
    lane, mirrored = as_bf(lane), as_bf(TILE - 1 - lane)
    step = as_bf(
        lanes_of((tall, 3 * height)) - lax.broadcasted_iota(jnp.int32, (tall, 3 * height), 0)
    )
    depth = 2 * window + height
    source = lanes_of((1, depth))
    apart = as_bf(lax.broadcasted_iota(jnp.int32, (tall, depth), 0) - lanes_of((tall, depth)))
    align = 16

    def warp(c, ats):
        at_up, at_down = ats
        shift, move = shifts[0, c], shifts[1, c]
        n_up, n_down = needed(shift, False), needed(shift, True)
        base_up, base_down = (
            pl.multiple_of(lax.div(at, align) * align, align) for at in (at_up, at_down)
        )
        skip_up, skip_down = at_up - base_up, at_down - base_down
        own = EXT - window - shift
        below = own - skip_down
        above = EXT - skip_up - n_up - shift
        in_up = (source >= skip_up) & (source < skip_up + n_up)
        first_down = window + height + skip_down
        in_down = (source >= first_down) & (source < first_down + n_down)
        none = 4 * depth
        offset = jnp.where(
            source < window,
            jnp.where(in_up, above, none),
            jnp.where(source < window + height, own, jnp.where(in_down, below, none)),
        )
        pick = one_hot(apart == as_bf(offset))
        rows = jnp.concatenate(
            [lent[0, pl.ds(base_up, window), :], feat[c], lent[1, pl.ds(base_down, window), :]], axis=0
        )
        plane = jnp.dot(pick, rows, preferred_element_type=F32).astype(BF16)
        pick = one_hot(step == as_bf(height - EXT + shift))
        plane = [plane[:, part] for part in tiles_of(span)]
        plane.append(jnp.dot(pick, sides[c], preferred_element_type=F32).astype(BF16))
        amount = jnp.where(move > 0, TILE - move, -move)
        parts = [turn(part, amount) for part in plane]
        inside = jnp.where(move > 0, lane, mirrored) < as_bf(TILE - jnp.abs(move))
        for t, part in enumerate(tiles_of(width)):
            after, before = parts[(t + 1) % (tiles + 1)], parts[t - 1]
            result = jnp.where(inside, parts[t], jnp.where(move > 0, after, before))
            moved[c, :, part] = result * seen_halo if t == tiles else result
        return at_up + n_up, at_down + n_down

    lax.fori_loop(0, chans, warp, (jnp.int32(0), jnp.int32(0)), unroll=8)
    chunk = 16
    for r in range(0, tall, chunk):
        for part in tiles_of(width):
            warp_0[rows_at(r, chans, chunk), part] = to_rows(moved[:, r : r + chunk, part])

    def clear(r, count):
        warp_0[rows_at(r, chans, count)] = jnp.zeros((count * chans, width), BF16)

    pl.when(jnp.logical_not(has_up))(lambda: clear(0, EXT))
    pl.when(jnp.logical_not(has_down))(lambda: clear(EXT + height, EXT))
    for j in range(height + 2 * EXT):
        at = rows_at(j, chans)
        warp_m[at] = turn(warp_0[at], 1)
        warp_p[at] = turn(warp_0[at], -1)

    def first_group(g, own):
        at = rows_at(g * POOL, chans, POOL + 2)
        pre = jnp.dot(
            bands[...], stacked((warp_m, warp_0, warp_p), at), preferred_element_type=F32
        )
        sigma = 0.5 * jnp.tanh(0.5 * pre) + 0.5
        rows = (pre * sigma).astype(BF16)
        act[rows_at(g * POOL, chans, POOL), :] = rows
        rows = rows.astype(F32)
        total = rows[0:chans]
        for k in range(1, POOL):
            total = total + rows[k * chans : (k + 1) * chans]
        store_split(high, low, rows_at(g, chans), total)
        if own:
            there = rows_at(g * POOL - 2 * POOL, chans, POOL)
            pre, sigma = pre[:, 0:span], sigma[:, 0:span]
            pre_grad[there, :] = (
                act_grad[there, :] * (sigma * (1.0 + pre * (1.0 - sigma)))
            ).astype(BF16)
        return 0

    for g in (0, 1, groups + 2, groups + 3):
        first_group(g, False)
    lax.fori_loop(2, groups + 2, lambda g, _: first_group(g, True), 0, unroll=4)
    sums = block_sums(high, low)
    seen_cells = cells_seen((chans, TILE), span)
    for g in range(groups + 4):
        at = rows_at(g, chans)
        seen = seen_cells
        if g < 2:
            seen = seen & has_up
        elif g >= groups + 2:
            seen = seen & has_down
        pooled[at] = jnp.where(seen, sums[at] * (1.0 / POOL**2), 0.0).astype(BF16)

    bottles = []
    for g in range(groups + 2):
        parts = jnp.dot(small[...], pooled[rows_at(g, chans, 3), :], preferred_element_type=F32)
        bottles.append(conv_sum(parts, chans, 1))
    bottle = spread(bottles, width, width)
    for g in range(groups + 2):
        rows, seen = range(POOL), seen_cols
        if g == 0:
            rows, seen = (POOL - 1,), seen & has_up
        elif g == groups + 1:
            rows, seen = (0,), seen & has_down
        for k in rows:
            row = act[rows_at((g + 1) * POOL + k, chans), :].astype(F32) + bottle[rows_at(g, chans)]
            blended[rows_at(g * POOL + k - POOL + 1, chans), :] = jnp.where(seen, row, 0.0).astype(
                BF16
            )

    correlate(pre_grad, 0, (warp_m, warp_0, warp_p), EXT - 1, acc, height, chans, span)
    first_part = folded(acc, chans)
    correlate(blended, 1, (view_m, view_0, view_p), CHALO - 1, acc, height, chans, span)
    second_part = folded(acc, chans)
    lane = lanes_of((3 * chans, TILE))
    grads[0 : 3 * chans] = jnp.where(lane < 3 * chans, first_part, turn(second_part, 3 * chans))
    half = 3 * chans // 2
    grads[3 * chans :] = jnp.where(
        lane[0:half] < TILE // 2,
        turn(second_part[0:half], -chans),
        turn(second_part[half:], TILE // 2 - chans),
    )


def predict_kernel(part, blended, bands, *rest):
    out, rows = rest[-2:]
    chans, height, span = out.shape

    def group(g, _):
        at = rows_at(part * height + g * POOL, chans, POOL + 2)
        parts = jnp.dot(bands[...], blended[at, :], preferred_element_type=F32)
        for k in range(POOL):
            row = conv_sum(parts[3 * k * chans : 3 * (k + 1) * chans], chans, 1)
            rows[rows_at(g * POOL + k, chans), :] = row[:, 0:span].astype(BF16)
        return 0

    lax.fori_loop(0, height // POOL, group, 0, unroll=2)
    for part in tiles_of(span):
        out[:, :, part] = to_planes(rows[:, part], chans)


def final_kernel(factor, mine, other, first, second):
    chans = first.shape[1]
    total = (mine[...].astype(F32) + other[...].astype(F32)) * factor
    turned = total[0 : 3 * chans].T
    for b in range(3):
        for a in range(3):
            first[3 * a + b] = turned[b * chans : (b + 1) * chans, a * chans : (a + 1) * chans]
    half = 3 * chans // 2
    low = total[3 * chans :]
    both = jnp.concatenate([low, turn(low, -(TILE // 2))], axis=0)
    for a in range(3):
        at = slice((2 - a) * chans, (3 - a) * chans)
        second[3 * a + 2] = turn(total[at], -3 * chans)[:, 0:chans]
        second[3 * a + 1] = both[at, 0:chans]
        second[3 * a + 0] = turn(both[at], -chans)[:, 0:chans]


def call(kernel, outs, scratch, n_in, limit, flops=0, smem_first=False, **more):
    specs = [VMEM] * n_in
    if smem_first:
        specs[0] = SMEM
    more.setdefault("in_specs", specs)
    more.setdefault("out_specs", jax.tree.map(lambda _: VMEM, outs))
    return pl.pallas_call(
        kernel,
        out_shape=outs,
        scratch_shapes=scratch,
        compiler_params=pltpu.CompilerParams(vmem_limit_bytes=limit * MIB),
        cost_estimate=pl.CostEstimate(flops=flops, bytes_accessed=4 * MIB, transcendentals=0),
        **more,
    )


def predict(blended, bands, shape, parts, part, before):
    chans, height, span = shape
    rows = height // parts
    block = pl.BlockSpec((chans, rows, span), lambda i: (0, part, 0))
    whole = lambda a: pl.BlockSpec(a.shape, lambda i: (0,) * a.ndim)
    args = (blended, bands)
    specs = [whole(a) for a in args]
    more = {}
    if before is not None:
        args += (before,)
        specs.append(pl.BlockSpec(memory_space=pl.ANY))
        more["input_output_aliases"] = {2: 0}
    return call(
        functools.partial(predict_kernel, part),
        jax.ShapeDtypeStruct(shape, BF16),
        [
            pltpu.VMEM((chans * rows, span), BF16),
        ],
        len(args),
        12,
        flops=10**9,
        grid=(1,),
        in_specs=specs,
        out_specs=block,
        **more,
    )(*args)


def bf(*shape):
    return jax.ShapeDtypeStruct(shape, BF16)


def swapped(messages, axis):
    pairs = [p for p in swaps(lax.axis_size(axis)) if p]
    return [lax.ppermute(m, axis, p) for m, p in zip(messages, pairs)]


def pack_rows(index, skip, size, shifts, feat, counted=False):
    message = bf(size, feat.shape[2])
    if counted:
        message = (message, jax.ShapeDtypeStruct((8, TILE), jnp.int32))
    return call(
        functools.partial(feature_kernel, index, skip),
        message, [], 2, 16, smem_first=True,
    )(shifts, feat)


def main_pass(rest, lent, shifts, feat, sides, act_grad, views, bands):
    chans, height, span = feat.shape
    width = span + TILE
    full = height * chans
    groups = height // POOL
    band = 3 * (POOL + 2) * chans
    if rest:
        size = lent[0].shape[0]
        more = swapped([pack_rows(i, size, rest, shifts, feat) for i in (0, 1)], "rows")
        lent = [jnp.concatenate(pair, axis=0) for pair in zip(lent, more)]
    size = lent[0].shape[0]
    tall = pl.cdiv(height + 2 * EXT, 16) * 16
    grads, blended = call(
        main_kernel,
        (jax.ShapeDtypeStruct((9 * chans // 2, TILE), F32), bf((height + 2) * chans, width)),
        [
            pltpu.VMEM((2, size + 48, span), BF16),
            pltpu.VMEM((chans, tall, width), BF16),
        ]
        + [pltpu.VMEM((tall * chans, width), BF16)] * 3
        + [pltpu.VMEM(((height + 4 * POOL) * chans, width), BF16)]
        + [pltpu.VMEM(((groups + 4) * chans, width), BF16)] * 2
        + [pltpu.VMEM(((groups + 4) * chans, TILE), BF16)]
        + [
            pltpu.VMEM((full, span), BF16),
            pltpu.VMEM((band, POOL * chans), F32),
        ],
        11,
        20,
        flops=10**10,
        smem_first=True,
    )(
        shifts, feat, *lent, sides, act_grad, *views, *bands
    )

    return grads, blended


def shards(features, shifts, first_kernel, bottle_kernel, second_kernel, cotangent):
    imgs, chans, height, span = features.shape
    rows, cols, dp = (lax.axis_size(a) for a in ("rows", "cols", "dp"))
    full = height * chans

    width = span + TILE
    groups = height // POOL
    feat, cot, shifts = features[0], cotangent[0], shifts[0].T
    row_pairs = swaps(rows)

    usual = USUAL * chans
    message, total = pack_rows(0, 0, usual, shifts, feat, counted=True)
    message, total, cot = lax.optimization_barrier((message, total, cot))
    feat_a = lax.ppermute(message, "rows", row_pairs[0])
    bit = 1
    while bit < dp:
        total = jnp.maximum(total, lax.ppermute(total, "dp", [(i, i ^ bit) for i in range(dp)]))
        bit *= 2

    packed = chans * (height * SLOT // TILE)
    messages = call(
        column_kernel, (bf(packed, TILE),) * (1 if cols == 2 else 2), [], 2, 8, flops=2 * 10**10
    )(feat, cot)
    col_msgs = swapped(messages, "cols")
    ncols = len(col_msgs)
    message = pack_rows(1, 0, usual, shifts, feat)
    col_msgs, message, total = lax.optimization_barrier((col_msgs, message, total))
    feat_b = lax.ppermute(message, "rows", row_pairs[1])
    cot_rows = call(rows_kernel, bf(full, span), [], 1, 4)(cot)
    halo = bf(CHALO * chans + ncols * packed * TILE // span, span)
    messages = call(edge_kernel, (halo, halo), [], 1 + ncols, 8)(cot_rows, *col_msgs)
    row_msgs = swapped(messages, "rows")
    row_msgs[0], total = lax.optimization_barrier((row_msgs[0], total))
    row_msgs, feat_a = lax.optimization_barrier((row_msgs, feat_a))

    tall_c = (height + 2 * CHALO) * chans
    view = bf(tall_c, width)
    band = 3 * (POOL + 2) * chans
    act_grad, *rest = call(
        functools.partial(back_kernel, ncols),
        (
            jax.ShapeDtypeStruct((full, span), F32), view, view, view,
            bf(chans, 3 * height, TILE), bf(POOL * chans, band), bf(3 * chans, 3 * chans),
            bf(3 * POOL * chans, (POOL + 2) * chans),
        ),
        [pltpu.VMEM(((height + 2 * POOL) * chans, span), BF16)]
        + [pltpu.VMEM(((groups + 2) * chans, width), BF16)] * 2
        + [pltpu.VMEM(((groups + 2) * chans, TILE), BF16)]
        + [
            pltpu.VMEM((band, POOL * chans), F32),
            pltpu.VMEM((POOL * chans, band), BF16),
            pltpu.VMEM((9 * chans, TILE), F32),
            pltpu.VMEM((3 * chans, 3 * chans), BF16),
            pltpu.VMEM((chans, 9 * chans), F32),
        ],
        6 + ncols,
        16,
        flops=8 * 10**9,
    )(cot_rows, *row_msgs, *col_msgs, first_kernel, bottle_kernel, second_kernel)
    views, sides, weights = rest[:3], rest[3], rest[4:]

    grads, blended = lax.cond(
        total[0, 0] <= usual,
        functools.partial(main_pass, 0),
        functools.partial(main_pass, LARGEST * chans - usual),
        (feat_a, feat_b), shifts, feat, sides, act_grad, tuple(views), tuple(weights[:2]),
    )

    steps = []
    for axis, size in (("dp", dp), ("cols", cols), ("rows", rows)):
        bit = 1
        while bit < size:
            steps.append((axis, [(i, i ^ bit) for i in range(size)]))
            bit *= 2
    parts, prediction = 2, None
    for step, (axis, pairs) in enumerate(steps):
        if step >= len(steps) - 2:
            grads = lax.optimization_barrier(grads.astype(BF16))
        other = lax.ppermute(grads, axis, pairs)
        if 1 <= step <= parts:
            prediction = predict(
                blended, weights[2], (chans, height, span), parts, step - 1, prediction
            )
            other, prediction = lax.optimization_barrier((other, prediction))
        if step < len(steps) - 1:
            grads = grads.astype(F32) + other.astype(F32)
            if step < parts:
                grads, blended = lax.optimization_barrier((grads, blended))
    factor = 1.0 / math.sqrt(imgs * dp * height * rows * span * cols)
    shape = jax.ShapeDtypeStruct((9, chans, chans), F32)
    first_grad, second_grad = call(
        functools.partial(final_kernel, factor), (shape, shape), [], 2, 2
    )(grads, other)
    return (prediction[None], first_grad, second_grad)


def solution(mesh):
    placed = (
        P("dp", None, "rows", "cols"),
        P("dp", None, None),
        P(),
        P(),
        P(),
        P("dp", None, "rows", "cols"),
    )
    return jax.shard_map(
        shards,
        mesh=mesh,
        in_specs=placed,
        out_specs=(P("dp", None, "rows", "cols"), P(), P()),
        check_vma=False,
    )
```

```python
import functools
import math

import jax
import jax.numpy as jnp
from jax import lax
from jax.experimental import pallas as pl
from jax.experimental.pallas import tpu as pltpu
from jax.sharding import PartitionSpec as P


MAXSHIFT = 16
POOL = 4
BATCH = 8
TILE = 128
SLOT = 32
EXT = 9
FHALO = MAXSHIFT + EXT
USUAL = 14
LARGEST = FHALO + 1
CHALO = 5
F32 = jnp.float32
BF16 = jnp.bfloat16
VMEM = pl.BlockSpec(memory_space=pltpu.VMEM)
SMEM = pl.BlockSpec(memory_space=pltpu.SMEM)
MIB = 1024 * 1024


def lanes_of(shape):
    return lax.broadcasted_iota(jnp.int32, shape, len(shape) - 1)


def turn(values, shift):
    width = values.shape[-1]
    if isinstance(shift, int):
        shift = shift % width
        if shift == 0:
            return values
    return pltpu.roll(values, shift, values.ndim - 1)


def has_sides():
    row, col = lax.axis_index("rows"), lax.axis_index("cols")
    return (
        row > 0,
        row < lax.axis_size("rows") - 1,
        col > 0,
        col < lax.axis_size("cols") - 1,
    )


def as_bf(values):
    return values.astype(F32).astype(BF16)


def one_hot(mask):
    return jnp.where(mask, jnp.ones((), BF16), jnp.zeros((), BF16))


def rows_at(r, chans, count=1):
    if isinstance(r, int):
        return slice(r * chans, (r + count) * chans)
    return pl.ds(pl.multiple_of(r * chans, chans), count * chans)


def to_rows(block):
    chans, height, span = block.shape
    return jnp.transpose(block, (1, 0, 2)).reshape(height * chans, span)


def to_planes(block, chans):
    height = block.shape[0] // chans
    return jnp.transpose(block.reshape(height, chans, block.shape[1]), (1, 0, 2))


def tiles_of(span):
    return [slice(t, t + TILE) for t in range(0, span, TILE)]


def is_even(axis):
    return lax.rem(lax.axis_index(axis), 2) == 0


def swaps(size):
    first = [(i, i ^ 1) for i in range(size)]
    second = [(i, i + 1) for i in range(1, size - 1, 2)]
    return [first, second + [(j, i) for i, j in second]]


def needed(shift, below):
    return jnp.maximum(EXT + shift if below else EXT - shift, 0)


def feature_kernel(index, skip, shifts, feat, msg, *counts):
    chans, height, span = feat.shape
    full = chans * height
    size = msg.shape[0]
    chunk = size // 4
    source = feat[...].reshape(full, span)
    lane = lanes_of((8, full))
    chan, row = lane // height, lane % height
    to_below = is_even("rows") if index == 0 else jnp.logical_not(is_even("rows"))
    target = jnp.full((8, full), -1, jnp.int32)
    at, up, down = jnp.int32(-skip), jnp.int32(0), jnp.int32(0)
    for c in range(chans):
        shift = shifts[0, c]
        n_up, n_down = needed(shift, False), needed(shift, True)
        count = jnp.where(to_below, n_up, n_down)
        first = jnp.where(to_below, height - count, 0)
        mine = (chan == c) & (row >= first) & (row < first + count)
        target = jnp.where(mine, row + (at - first), target)
        at, up, down = at + count, up + n_up, down + n_down
    for out in counts:
        out[...] = jnp.full(out.shape, jnp.maximum(up, down), jnp.int32)
    place = as_bf(lax.broadcasted_iota(jnp.int32, (chunk, full), 0))
    for p in range(0, size, chunk):
        pick = one_hot(place == as_bf(target[0:1] - p))
        msg[p : p + chunk] = jnp.dot(pick, source, preferred_element_type=F32).astype(BF16)


def rows_kernel(source, out):
    for part in tiles_of(source.shape[2]):
        out[:, part] = to_rows(source[:, :, part])


def edge_lanes(shape, right, count):
    lane = lanes_of(shape)
    return jnp.where(jnp.where(right, TILE - 1 - lane, lane) < count, 1.0, 0.0).astype(BF16)


def slots(chans, height):
    half, block = chans // 2, height // 2
    for h in (0, 1):
        for m in (0, 1):
            yield 2 * h + m, slice(h * half, (h + 1) * half), slice(m * block, (m + 1) * block)


def column_kernel(feat, cot, *col_msgs):
    chans, height, span = feat.shape
    for index, msg in enumerate(col_msgs):
        right = is_even("cols") if index == 0 else jnp.logical_not(is_even("cols"))
        part = pl.ds(pl.multiple_of(jnp.where(right, span - TILE, 0), TILE), TILE)
        shape = (1, height // 2, TILE)
        inner = edge_lanes(shape, right, FHALO)
        outer = edge_lanes(shape, right, SLOT) - inner
        total = None
        for q, channels, rows in slots(chans, height):
            cots = turn(cot[channels, rows, part], jnp.where(right, TILE - FHALO, FHALO))
            piece = feat[channels, rows, part] * inner + cots * outer
            piece = turn(piece, jnp.where(right, (q + 1) * SLOT % TILE, q * SLOT))
            total = piece if total is None else total + piece
        msg[...] = total.reshape(msg.shape)


def edge_kernel(cot_rows, *rest):
    cols, (msg_a, msg_b) = rest[:-2], rest[-2:]
    span = cot_rows.shape[1]
    size = msg_a.shape[0] - sum(c.shape[0] * TILE // span for c in cols)
    edge = cot_rows.shape[0] - size
    chans = size // CHALO
    low = jnp.where(is_even("rows"), edge, 0)
    msg_a[0:size] = cot_rows[pl.ds(pl.multiple_of(low, chans), size), :]
    msg_b[0:size] = cot_rows[pl.ds(pl.multiple_of(edge - low, chans), size), :]
    at = size
    for col in cols:
        count = col.shape[0] * TILE // span
        for t, part in enumerate(tiles_of(span)):
            block = col[t * count : (t + 1) * count]
            msg_a[at : at + count, part] = block
            msg_b[at : at + count, part] = block
        at += count


def corner_views(msg, size, cols):
    span = msg.shape[1]
    views, at = [], size
    for col in cols:
        count = col.shape[0] * TILE // span
        views.append(
            jnp.concatenate([msg[at : at + count, part] for part in tiles_of(span)], axis=0)
        )
        at += count
    return views


def halo_block(sources, slot, rows, kind):
    total = None
    if kind == "features":
        count, shift_r, shift_l = FHALO, -slot * SLOT, TILE - (slot + 1) * SLOT
    else:
        count = CHALO
        shift_r, shift_l = -slot * SLOT - FHALO, TILE - (slot + 1) * SLOT + FHALO
    for index, source in enumerate(sources):
        from_right = is_even("cols") if index == 0 else jnp.logical_not(is_even("cols"))
        block = source.reshape(source.shape[0] // rows, rows, TILE)
        block = turn(block, jnp.where(from_right, shift_r % TILE, shift_l % TILE))
        block = block * edge_lanes((1, rows, TILE), jnp.logical_not(from_right), count)
        total = block if total is None else total + block
    return total


def halo_rows(sources, m, rows, kind):
    return to_rows(
        jnp.concatenate([halo_block(sources, 2 * h + m, rows, kind) for h in (0, 1)], axis=0)
    )


def columns_seen(shape, span):
    _, _, has_left, has_right = has_sides()
    lane = lanes_of(shape)
    middle = span + TILE // 2
    return (lane < span) | ((lane < middle) & has_right) | ((lane >= middle) & has_left)


def cell_matrix(width, by_cell):
    shape = (TILE, width) if by_cell else (width, TILE)
    lane = lax.broadcasted_iota(jnp.int32, shape, 1 if by_cell else 0)
    cell = lax.broadcasted_iota(jnp.int32, shape, 0 if by_cell else 1)
    place = lane // POOL + jnp.where(lane >= width - TILE // 2, TILE - width // POOL, 0)
    return jnp.where(place == cell, 1.0, 0.0).astype(BF16)


def cells_seen(shape, span):
    _, _, has_left, has_right = has_sides()
    lane = lanes_of(shape)
    count = span // POOL
    middle = (count + TILE) // 2
    return (lane < count) | ((lane < middle) & has_right) | ((lane >= middle) & has_left)


def store_split(high, low, at, total):
    top = total.astype(BF16)
    high[at, :] = top
    low[at, :] = (total - top.astype(F32)).astype(BF16)


def block_sums(high, low):
    matrix = cell_matrix(high.shape[1], False)
    return jnp.dot(high[...], matrix, preferred_element_type=F32) + jnp.dot(
        low[...], matrix, preferred_element_type=F32
    )


def spread(rows, width, count):
    values = jnp.concatenate(rows, axis=0)
    top = values.astype(BF16)
    rest = (values - top.astype(F32)).astype(BF16)
    matrix = cell_matrix(width, True)[:, 0:count]
    return jnp.dot(
        jnp.concatenate([top, rest], axis=1),
        jnp.concatenate([matrix, matrix], axis=0),
        preferred_element_type=F32,
    )


def fill_bands(out, kernel, count):
    chans = kernel.shape[1]
    out[...] = jnp.zeros(out.shape, out.dtype)
    for k in range(count):
        for b in range(3):
            for a in range(3):
                at = (b * (count + 2) + k + a) * chans
                out[k * chans : (k + 1) * chans, at : at + chans] = kernel[3 * a + b].astype(
                    out.dtype
                )


def fill_turned_bands(out, kernel, count):
    chans = kernel.shape[1]
    out[...] = jnp.zeros(out.shape, out.dtype)
    for k in range(count):
        for b in range(3):
            for a in range(3):
                at = (b * (count + 2) + k + a) * chans
                out[at : at + chans, k * chans : (k + 1) * chans] = kernel[8 - 3 * a - b].astype(
                    out.dtype
                )


def stacked(views, at):
    return jnp.concatenate([view[at, :] for view in views], axis=0)


def conv_sum(parts, chans, step):
    return (
        turn(parts[0:chans], step)
        + parts[chans : 2 * chans]
        + turn(parts[2 * chans : 3 * chans], -step)
    )


def back_kernel(
    ncols, cot, msg_a, msg_b, *rest,
):
    cols, (
        first, bottle, second,
        act_grad, cot_m, cot_0, cot_p, sides, first_bands, bottle_bands, second_bands,
        back, high, low, coarse, bands_f, bands, small_f, small, wide_f,
    ) = rest[:ncols], rest[ncols:]
    chans = second.shape[1]
    full, span = cot.shape
    height = full // chans
    width = span + TILE
    groups = height // POOL
    has_up, has_down, _, _ = has_sides()

    fill_turned_bands(bands_f, second, POOL)
    bands[...] = bands_f[...].T.astype(BF16)
    fill_turned_bands(small_f, bottle, 1)
    small_t = small_f[...].T
    for b in range(3):
        small[rows_at(b, chans)] = small_t[0:chans, 3 * b * chans : 3 * (b + 1) * chans].astype(BF16)
    fill_bands(first_bands, first, POOL)
    fill_bands(wide_f, bottle, 1)
    for b in range(3):
        bottle_bands[rows_at(b, chans)] = wide_f[
            0:chans, 3 * b * chans : 3 * (b + 1) * chans
        ].astype(BF16)
    second_bands[...] = jnp.zeros(second_bands.shape, BF16)
    for k in range(POOL):
        for b in range(3):
            for a in range(3):
                second_bands[
                    rows_at(3 * k + b, chans), (k + a) * chans : (k + a + 1) * chans
                ] = second[3 * a + b]

    size = CHALO * chans
    block = height // 2

    def halo_columns(sources, at):
        for q, channels, rows in slots(chans, height):
            sides[channels, at + rows.start : at + rows.stop, :] = halo_block(
                sources, q, block, "features"
            )

    own = [c[...] for c in cols]
    halo_columns(own, height)
    cot_0[rows_at(CHALO, chans, height), 0:span] = cot[...]
    for m in (0, 1):
        cot_0[rows_at(CHALO + m * block, chans, block), span:width] = halo_rows(
            own, m, block, "cotangent"
        )

    def vertical(up, down):
        cot_0[rows_at(0, chans, CHALO), 0:span] = up[0:size]
        cot_0[rows_at(CHALO + height, chans, CHALO), 0:span] = down[0:size]
        above, below = corner_views(up, size, cols), corner_views(down, size, cols)
        cot_0[rows_at(0, chans, CHALO), span:width] = halo_rows(above, 1, block, "cotangent")[
            (block - CHALO) * chans :
        ]
        cot_0[rows_at(CHALO + height, chans, CHALO), span:width] = halo_rows(
            below, 0, block, "cotangent"
        )[0:size]
        halo_columns(above, 0)
        halo_columns(below, 2 * height)

    pl.when(is_even("rows"))(lambda: vertical(msg_b, msg_a))
    pl.when(jnp.logical_not(is_even("rows")))(lambda: vertical(msg_a, msg_b))
    for j in range(height + 2 * CHALO):
        at = rows_at(j, chans)
        cot_m[at] = turn(cot_0[at], 1)
        cot_p[at] = turn(cot_0[at], -1)
    def group(g, _):
        at = rows_at(g * POOL, chans, POOL + 2)
        rows = jnp.dot(
            bands[...], stacked((cot_m, cot_0, cot_p), at), preferred_element_type=F32
        ).astype(BF16)
        back[rows_at(g * POOL, chans, POOL), :] = rows[:, 0:span]
        rows = rows.astype(F32)
        total = rows[0:chans]
        for k in range(1, POOL):
            total = total + rows[k * chans : (k + 1) * chans]
        store_split(high, low, rows_at(g, chans), total)
        return 0

    lax.fori_loop(0, groups + 2, group, 0, unroll=5)
    sums = block_sums(high, low)
    seen_cells = cells_seen((chans, TILE), span)
    for g in range(groups + 2):
        at = rows_at(g, chans)
        seen = seen_cells
        if g == 0:
            seen = seen & has_up
        elif g == groups + 1:
            seen = seen & has_down
        coarse[at] = jnp.where(seen, sums[at], 0.0).astype(BF16)
    means = []
    for g in range(groups):
        parts = jnp.dot(small[...], coarse[rows_at(g, chans, 3), :], preferred_element_type=F32)
        means.append(conv_sum(parts, chans, 1) * (1.0 / POOL**2))
    mean = spread(means, width, span)
    for r in range(height):
        act_grad[rows_at(r, chans), :] = (
            back[rows_at(r + POOL, chans), :].astype(F32) + mean[rows_at(r // POOL, chans)]
        )


def correlate(u, u0, views, v0, acc, height, chans, span):
    groups = range(0, height, BATCH)
    left = jnp.concatenate(
        [
            jnp.concatenate(
                [view[rows_at(v0 + g, chans, BATCH + 2), 0:span] for view in views], axis=0
            )
            for g in groups
        ],
        axis=1,
    )
    right = jnp.concatenate([u[rows_at(u0 + g, chans, BATCH), 0:span] for g in groups], axis=1)
    acc[...] = lax.dot_general(
        left, right, (((1,), (1,)), ((), ())), preferred_element_type=F32
    )


def folded(acc, chans):
    lane = lanes_of((3 * chans, TILE))
    result = jnp.zeros((3 * chans, TILE), F32)
    per_tile = TILE // chans
    for b in range(3):
        total = None
        for place in range(per_tile):
            column = None
            for k in range(place, BATCH, per_tile):
                part = slice(k // per_tile * TILE, (k // per_tile + 1) * TILE)
                block = acc[rows_at(b * (BATCH + 2) + k, chans, 3), part]
                column = block if column is None else column + block
            column = turn(column, (b - place) * chans)
            total = column if total is None else total + column
        result = jnp.where((lane >= b * chans) & (lane < (b + 1) * chans), total, result)
    return result


def main_kernel(
    shifts, feat, feat_a, feat_b, sides, act_grad, view_m, view_0, view_p, bands, small,
    grads, blended,
    lent, moved, warp_m, warp_0, warp_p, act, high, low, pooled, pre_grad, acc,
):
    chans, height, span = feat.shape
    tiles = span // TILE
    width = span + TILE
    groups = height // POOL
    has_up, has_down, has_left, has_right = has_sides()
    seen_cols = columns_seen((chans, width), span)

    size = feat_a.shape[0]
    window = lent.shape[1] - size
    lent[:, size:, :] = jnp.zeros((2, window, span), BF16)

    def borrow(up, down):
        lent[0, 0:size] = up[...]
        lent[1, 0:size] = down[...]

    pl.when(is_even("rows"))(lambda: borrow(feat_b, feat_a))
    pl.when(jnp.logical_not(is_even("rows")))(lambda: borrow(feat_a, feat_b))

    tall = moved.shape[1]
    lane = lanes_of((tall, TILE))
    seen_halo = one_hot(((lane < TILE // 2) & has_right) | ((lane >= TILE // 2) & has_left))
    lane, mirrored = as_bf(lane), as_bf(TILE - 1 - lane)
    step = as_bf(
        lanes_of((tall, 3 * height)) - lax.broadcasted_iota(jnp.int32, (tall, 3 * height), 0)
    )
    depth = 2 * window + height
    source = lanes_of((1, depth))
    apart = as_bf(lax.broadcasted_iota(jnp.int32, (tall, depth), 0) - lanes_of((tall, depth)))
    align = 16

    def warp(c, ats):
        at_up, at_down = ats
        shift, move = shifts[0, c], shifts[1, c]
        n_up, n_down = needed(shift, False), needed(shift, True)
        base_up, base_down = (
            pl.multiple_of(lax.div(at, align) * align, align) for at in (at_up, at_down)
        )
        skip_up, skip_down = at_up - base_up, at_down - base_down
        own = EXT - window - shift
        below = own - skip_down
        above = EXT - skip_up - n_up - shift
        in_up = (source >= skip_up) & (source < skip_up + n_up)
        first_down = window + height + skip_down
        in_down = (source >= first_down) & (source < first_down + n_down)
        none = 4 * depth
        offset = jnp.where(
            source < window,
            jnp.where(in_up, above, none),
            jnp.where(source < window + height, own, jnp.where(in_down, below, none)),
        )
        pick = one_hot(apart == as_bf(offset))
        rows = jnp.concatenate(
            [lent[0, pl.ds(base_up, window), :], feat[c], lent[1, pl.ds(base_down, window), :]], axis=0
        )
        plane = jnp.dot(pick, rows, preferred_element_type=F32).astype(BF16)
        pick = one_hot(step == as_bf(height - EXT + shift))
        plane = [plane[:, part] for part in tiles_of(span)]
        plane.append(jnp.dot(pick, sides[c], preferred_element_type=F32).astype(BF16))
        amount = jnp.where(move > 0, TILE - move, -move)
        parts = [turn(part, amount) for part in plane]
        inside = jnp.where(move > 0, lane, mirrored) < as_bf(TILE - jnp.abs(move))
        for t, part in enumerate(tiles_of(width)):
            after, before = parts[(t + 1) % (tiles + 1)], parts[t - 1]
            result = jnp.where(inside, parts[t], jnp.where(move > 0, after, before))
            moved[c, :, part] = result * seen_halo if t == tiles else result
        return at_up + n_up, at_down + n_down

    lax.fori_loop(0, chans, warp, (jnp.int32(0), jnp.int32(0)), unroll=8)
    chunk = 16
    for r in range(0, tall, chunk):
        for part in tiles_of(width):
            warp_0[rows_at(r, chans, chunk), part] = to_rows(moved[:, r : r + chunk, part])

    def clear(r, count):
        warp_0[rows_at(r, chans, count)] = jnp.zeros((count * chans, width), BF16)

    pl.when(jnp.logical_not(has_up))(lambda: clear(0, EXT))
    pl.when(jnp.logical_not(has_down))(lambda: clear(EXT + height, EXT))
    for j in range(height + 2 * EXT):
        at = rows_at(j, chans)
        warp_m[at] = turn(warp_0[at], 1)
        warp_p[at] = turn(warp_0[at], -1)

    def first_group(g, own):
        at = rows_at(g * POOL, chans, POOL + 2)
        pre = jnp.dot(
            bands[...], stacked((warp_m, warp_0, warp_p), at), preferred_element_type=F32
        )
        sigma = 0.5 * jnp.tanh(0.5 * pre) + 0.5
        rows = (pre * sigma).astype(BF16)
        act[rows_at(g * POOL, chans, POOL), :] = rows
        rows = rows.astype(F32)
        total = rows[0:chans]
        for k in range(1, POOL):
            total = total + rows[k * chans : (k + 1) * chans]
        store_split(high, low, rows_at(g, chans), total)
        if own:
            there = rows_at(g * POOL - 2 * POOL, chans, POOL)
            pre, sigma = pre[:, 0:span], sigma[:, 0:span]
            pre_grad[there, :] = (
                act_grad[there, :] * (sigma * (1.0 + pre * (1.0 - sigma)))
            ).astype(BF16)
        return 0

    for g in (0, 1, groups + 2, groups + 3):
        first_group(g, False)
    lax.fori_loop(2, groups + 2, lambda g, _: first_group(g, True), 0, unroll=8)
    sums = block_sums(high, low)
    seen_cells = cells_seen((chans, TILE), span)
    for g in range(groups + 4):
        at = rows_at(g, chans)
        seen = seen_cells
        if g < 2:
            seen = seen & has_up
        elif g >= groups + 2:
            seen = seen & has_down
        pooled[at] = jnp.where(seen, sums[at] * (1.0 / POOL**2), 0.0).astype(BF16)

    bottles = []
    for g in range(groups + 2):
        parts = jnp.dot(small[...], pooled[rows_at(g, chans, 3), :], preferred_element_type=F32)
        bottles.append(conv_sum(parts, chans, 1))
    bottle = spread(bottles, width, width)
    for g in range(groups + 2):
        rows, seen = range(POOL), seen_cols
        if g == 0:
            rows, seen = (POOL - 1,), seen & has_up
        elif g == groups + 1:
            rows, seen = (0,), seen & has_down
        for k in rows:
            row = act[rows_at((g + 1) * POOL + k, chans), :].astype(F32) + bottle[rows_at(g, chans)]
            blended[rows_at(g * POOL + k - POOL + 1, chans), :] = jnp.where(seen, row, 0.0).astype(
                BF16
            )

    correlate(pre_grad, 0, (warp_m, warp_0, warp_p), EXT - 1, acc, height, chans, span)
    first_part = folded(acc, chans)
    correlate(blended, 1, (view_m, view_0, view_p), CHALO - 1, acc, height, chans, span)
    second_part = folded(acc, chans)
    lane = lanes_of((3 * chans, TILE))
    grads[0 : 3 * chans] = jnp.where(lane < 3 * chans, first_part, turn(second_part, 3 * chans))
    half = 3 * chans // 2
    grads[3 * chans :] = jnp.where(
        lane[0:half] < TILE // 2,
        turn(second_part[0:half], -chans),
        turn(second_part[half:], TILE // 2 - chans),
    )


def predict_kernel(part, blended, bands, *rest):
    out, rows = rest[-2:]
    chans, height, span = out.shape

    def group(g, _):
        at = rows_at(part * height + g * POOL, chans, POOL + 2)
        parts = jnp.dot(bands[...], blended[at, :], preferred_element_type=F32)
        for k in range(POOL):
            row = conv_sum(parts[3 * k * chans : 3 * (k + 1) * chans], chans, 1)
            rows[rows_at(g * POOL + k, chans), :] = row[:, 0:span].astype(BF16)
        return 0

    lax.fori_loop(0, height // POOL, group, 0, unroll=2)
    for part in tiles_of(span):
        out[:, :, part] = to_planes(rows[:, part], chans)


def final_kernel(factor, mine, other, first, second):
    chans = first.shape[1]
    total = (mine[...].astype(F32) + other[...].astype(F32)) * factor
    turned = total[0 : 3 * chans].T
    for b in range(3):
        for a in range(3):
            first[3 * a + b] = turned[b * chans : (b + 1) * chans, a * chans : (a + 1) * chans]
    half = 3 * chans // 2
    low = total[3 * chans :]
    both = jnp.concatenate([low, turn(low, -(TILE // 2))], axis=0)
    for a in range(3):
        at = slice((2 - a) * chans, (3 - a) * chans)
        second[3 * a + 2] = turn(total[at], -3 * chans)[:, 0:chans]
        second[3 * a + 1] = both[at, 0:chans]
        second[3 * a + 0] = turn(both[at], -chans)[:, 0:chans]


def call(kernel, outs, scratch, n_in, limit, flops=0, smem_first=False, **more):
    specs = [VMEM] * n_in
    if smem_first:
        specs[0] = SMEM
    more.setdefault("in_specs", specs)
    more.setdefault("out_specs", jax.tree.map(lambda _: VMEM, outs))
    return pl.pallas_call(
        kernel,
        out_shape=outs,
        scratch_shapes=scratch,
        compiler_params=pltpu.CompilerParams(vmem_limit_bytes=limit * MIB),
        cost_estimate=pl.CostEstimate(flops=flops, bytes_accessed=4 * MIB, transcendentals=0),
        **more,
    )


def predict(blended, bands, shape, parts, part, before):
    chans, height, span = shape
    rows = height // parts
    block = pl.BlockSpec((chans, rows, span), lambda i: (0, part, 0))
    whole = lambda a: pl.BlockSpec(a.shape, lambda i: (0,) * a.ndim)
    args = (blended, bands)
    specs = [whole(a) for a in args]
    more = {}
    if before is not None:
        args += (before,)
        specs.append(pl.BlockSpec(memory_space=pl.ANY))
        more["input_output_aliases"] = {2: 0}
    return call(
        functools.partial(predict_kernel, part),
        jax.ShapeDtypeStruct(shape, BF16),
        [
            pltpu.VMEM((chans * rows, span), BF16),
        ],
        len(args),
        12,
        flops=10**9,
        grid=(1,),
        in_specs=specs,
        out_specs=block,
        **more,
    )(*args)


def bf(*shape):
    return jax.ShapeDtypeStruct(shape, BF16)


def swapped(messages, axis):
    pairs = [p for p in swaps(lax.axis_size(axis)) if p]
    return [lax.ppermute(m, axis, p) for m, p in zip(messages, pairs)]


def pack_rows(index, skip, size, shifts, feat, counted=False):
    message = bf(size, feat.shape[2])
    if counted:
        message = (message, jax.ShapeDtypeStruct((8, TILE), jnp.int32))
    return call(
        functools.partial(feature_kernel, index, skip),
        message, [], 2, 16, smem_first=True,
    )(shifts, feat)


def main_pass(rest, lent, shifts, feat, sides, act_grad, views, bands):
    chans, height, span = feat.shape
    width = span + TILE
    full = height * chans
    groups = height // POOL
    band = 3 * (POOL + 2) * chans
    if rest:
        size = lent[0].shape[0]
        more = swapped([pack_rows(i, size, rest, shifts, feat) for i in (0, 1)], "rows")
        lent = [jnp.concatenate(pair, axis=0) for pair in zip(lent, more)]
    size = lent[0].shape[0]
    tall = pl.cdiv(height + 2 * EXT, 16) * 16
    grads, blended = call(
        main_kernel,
        (jax.ShapeDtypeStruct((9 * chans // 2, TILE), F32), bf((height + 2) * chans, width)),
        [
            pltpu.VMEM((2, size + 48, span), BF16),
            pltpu.VMEM((chans, tall, width), BF16),
        ]
        + [pltpu.VMEM((tall * chans, width), BF16)] * 3
        + [pltpu.VMEM(((height + 4 * POOL) * chans, width), BF16)]
        + [pltpu.VMEM(((groups + 4) * chans, width), BF16)] * 2
        + [pltpu.VMEM(((groups + 4) * chans, TILE), BF16)]
        + [
            pltpu.VMEM((full, span), BF16),
            pltpu.VMEM((3 * (BATCH + 2) * chans, BATCH * chans), F32),
        ],
        11,
        20,
        flops=10**10,
        smem_first=True,
    )(
        shifts, feat, *lent, sides, act_grad, *views, *bands
    )

    return grads, blended


def shards(features, shifts, first_kernel, bottle_kernel, second_kernel, cotangent):
    imgs, chans, height, span = features.shape
    rows, cols, dp = (lax.axis_size(a) for a in ("rows", "cols", "dp"))
    full = height * chans

    width = span + TILE
    groups = height // POOL
    feat, cot, shifts = features[0], cotangent[0], shifts[0].T
    row_pairs = swaps(rows)

    usual = USUAL * chans
    message, total = pack_rows(0, 0, usual, shifts, feat, counted=True)
    message, total, cot = lax.optimization_barrier((message, total, cot))
    feat_a = lax.ppermute(message, "rows", row_pairs[0])
    bit = 1
    while bit < dp:
        total = jnp.maximum(total, lax.ppermute(total, "dp", [(i, i ^ bit) for i in range(dp)]))
        bit *= 2

    packed = chans * (height * SLOT // TILE)
    messages = call(
        column_kernel, (bf(packed, TILE),) * (1 if cols == 2 else 2), [], 2, 8, flops=2 * 10**10
    )(feat, cot)
    col_msgs = swapped(messages, "cols")
    ncols = len(col_msgs)
    message = pack_rows(1, 0, usual, shifts, feat)
    col_msgs, message, total = lax.optimization_barrier((col_msgs, message, total))
    feat_b = lax.ppermute(message, "rows", row_pairs[1])
    cot_rows = call(rows_kernel, bf(full, span), [], 1, 4)(cot)
    halo = bf(CHALO * chans + ncols * packed * TILE // span, span)
    messages = call(edge_kernel, (halo, halo), [], 1 + ncols, 8)(cot_rows, *col_msgs)
    row_msgs = swapped(messages, "rows")
    row_msgs[0], total = lax.optimization_barrier((row_msgs[0], total))
    row_msgs, feat_a = lax.optimization_barrier((row_msgs, feat_a))

    tall_c = (height + 2 * CHALO) * chans
    view = bf(tall_c, width)
    band = 3 * (POOL + 2) * chans
    act_grad, *rest = call(
        functools.partial(back_kernel, ncols),
        (
            jax.ShapeDtypeStruct((full, span), F32), view, view, view,
            bf(chans, 3 * height, TILE), bf(POOL * chans, band), bf(3 * chans, 3 * chans),
            bf(3 * POOL * chans, (POOL + 2) * chans),
        ),
        [pltpu.VMEM(((height + 2 * POOL) * chans, span), BF16)]
        + [pltpu.VMEM(((groups + 2) * chans, width), BF16)] * 2
        + [pltpu.VMEM(((groups + 2) * chans, TILE), BF16)]
        + [
            pltpu.VMEM((band, POOL * chans), F32),
            pltpu.VMEM((POOL * chans, band), BF16),
            pltpu.VMEM((9 * chans, TILE), F32),
            pltpu.VMEM((3 * chans, 3 * chans), BF16),
            pltpu.VMEM((chans, 9 * chans), F32),
        ],
        6 + ncols,
        16,
        flops=8 * 10**9,
    )(cot_rows, *row_msgs, *col_msgs, first_kernel, bottle_kernel, second_kernel)
    views, sides, weights = rest[:3], rest[3], rest[4:]

    grads, blended = lax.cond(
        total[0, 0] <= usual,
        functools.partial(main_pass, 0),
        functools.partial(main_pass, LARGEST * chans - usual),
        (feat_a, feat_b), shifts, feat, sides, act_grad, tuple(views), tuple(weights[:2]),
    )

    steps = []
    for axis, size in (("dp", dp), ("cols", cols), ("rows", rows)):
        bit = 1
        while bit < size:
            steps.append((axis, [(i, i ^ bit) for i in range(size)]))
            bit *= 2
    parts, prediction = 2, None
    for step, (axis, pairs) in enumerate(steps):
        if step >= len(steps) - 2:
            grads = lax.optimization_barrier(grads.astype(BF16))
        other = lax.ppermute(grads, axis, pairs)
        if 1 <= step <= parts:
            prediction = predict(
                blended, weights[2], (chans, height, span), parts, step - 1, prediction
            )
            other, prediction = lax.optimization_barrier((other, prediction))
        if step < len(steps) - 1:
            grads = grads.astype(F32) + other.astype(F32)
            if step < parts:
                grads, blended = lax.optimization_barrier((grads, blended))
    factor = 1.0 / math.sqrt(imgs * dp * height * rows * span * cols)
    shape = jax.ShapeDtypeStruct((9, chans, chans), F32)
    first_grad, second_grad = call(
        functools.partial(final_kernel, factor), (shape, shape), [], 2, 2
    )(grads, other)
    return (prediction[None], first_grad, second_grad)


def solution(mesh):
    placed = (
        P("dp", None, "rows", "cols"),
        P("dp", None, None),
        P(),
        P(),
        P(),
        P("dp", None, "rows", "cols"),
    )
    return jax.shard_map(
        shards,
        mesh=mesh,
        in_specs=placed,
        out_specs=(P("dp", None, "rows", "cols"), P(), P()),
        check_vma=False,
    )
```

```python
import functools
import math

import jax
import jax.numpy as jnp
from jax import lax
from jax.experimental import pallas as pl
from jax.experimental.pallas import tpu as pltpu
from jax.sharding import PartitionSpec as P


MAXSHIFT = 16
POOL = 4
BATCH = 8
TILE = 128
SLOT = 32
EXT = 9
FHALO = MAXSHIFT + EXT
USUAL = 14
LARGEST = FHALO + 1
CHALO = 5
F32 = jnp.float32
BF16 = jnp.bfloat16
VMEM = pl.BlockSpec(memory_space=pltpu.VMEM)
SMEM = pl.BlockSpec(memory_space=pltpu.SMEM)
MIB = 1024 * 1024


def lanes_of(shape):
    return lax.broadcasted_iota(jnp.int32, shape, len(shape) - 1)


def turn(values, shift):
    width = values.shape[-1]
    if isinstance(shift, int):
        shift = shift % width
        if shift == 0:
            return values
    return pltpu.roll(values, shift, values.ndim - 1)


def has_sides():
    row, col = lax.axis_index("rows"), lax.axis_index("cols")
    return (
        row > 0,
        row < lax.axis_size("rows") - 1,
        col > 0,
        col < lax.axis_size("cols") - 1,
    )


def as_bf(values):
    return values.astype(F32).astype(BF16)


def one_hot(mask):
    return jnp.where(mask, jnp.ones((), BF16), jnp.zeros((), BF16))


def rows_at(r, chans, count=1):
    if isinstance(r, int):
        return slice(r * chans, (r + count) * chans)
    return pl.ds(pl.multiple_of(r * chans, chans), count * chans)


def to_rows(block):
    chans, height, span = block.shape
    return jnp.transpose(block, (1, 0, 2)).reshape(height * chans, span)


def to_planes(block, chans):
    height = block.shape[0] // chans
    return jnp.transpose(block.reshape(height, chans, block.shape[1]), (1, 0, 2))


def tiles_of(span):
    return [slice(t, t + TILE) for t in range(0, span, TILE)]


def is_even(axis):
    return lax.rem(lax.axis_index(axis), 2) == 0


def swaps(size):
    first = [(i, i ^ 1) for i in range(size)]
    second = [(i, i + 1) for i in range(1, size - 1, 2)]
    return [first, second + [(j, i) for i, j in second]]


def needed(shift, below):
    return jnp.maximum(EXT + shift if below else EXT - shift, 0)


def feature_kernel(index, skip, shifts, feat, msg, *counts):
    chans, height, span = feat.shape
    full = chans * height
    size = msg.shape[0]
    chunk = size // 4
    source = feat[...].reshape(full, span)
    lane = lanes_of((8, full))
    chan, row = lane // height, lane % height
    to_below = is_even("rows") if index == 0 else jnp.logical_not(is_even("rows"))
    target = jnp.full((8, full), -1, jnp.int32)
    at, up, down = jnp.int32(-skip), jnp.int32(0), jnp.int32(0)
    for c in range(chans):
        shift = shifts[0, c]
        n_up, n_down = needed(shift, False), needed(shift, True)
        count = jnp.where(to_below, n_up, n_down)
        first = jnp.where(to_below, height - count, 0)
        mine = (chan == c) & (row >= first) & (row < first + count)
        target = jnp.where(mine, row + (at - first), target)
        at, up, down = at + count, up + n_up, down + n_down
    for out in counts:
        out[...] = jnp.full(out.shape, jnp.maximum(up, down), jnp.int32)
    place = as_bf(lax.broadcasted_iota(jnp.int32, (chunk, full), 0))
    for p in range(0, size, chunk):
        pick = one_hot(place == as_bf(target[0:1] - p))
        msg[p : p + chunk] = jnp.dot(pick, source, preferred_element_type=F32).astype(BF16)


def rows_kernel(source, out):
    for part in tiles_of(source.shape[2]):
        out[:, part] = to_rows(source[:, :, part])


def edge_lanes(shape, right, count):
    lane = lanes_of(shape)
    return jnp.where(jnp.where(right, TILE - 1 - lane, lane) < count, 1.0, 0.0).astype(BF16)


def slots(chans, height):
    half, block = chans // 2, height // 2
    for h in (0, 1):
        for m in (0, 1):
            yield 2 * h + m, slice(h * half, (h + 1) * half), slice(m * block, (m + 1) * block)


def column_kernel(feat, cot, *col_msgs):
    chans, height, span = feat.shape
    for index, msg in enumerate(col_msgs):
        right = is_even("cols") if index == 0 else jnp.logical_not(is_even("cols"))
        part = pl.ds(pl.multiple_of(jnp.where(right, span - TILE, 0), TILE), TILE)
        shape = (1, height // 2, TILE)
        inner = edge_lanes(shape, right, FHALO)
        outer = edge_lanes(shape, right, SLOT) - inner
        total = None
        for q, channels, rows in slots(chans, height):
            cots = turn(cot[channels, rows, part], jnp.where(right, TILE - FHALO, FHALO))
            piece = feat[channels, rows, part] * inner + cots * outer
            piece = turn(piece, jnp.where(right, (q + 1) * SLOT % TILE, q * SLOT))
            total = piece if total is None else total + piece
        msg[...] = total.reshape(msg.shape)


def edge_kernel(cot_rows, *rest):
    cols, (msg_a, msg_b) = rest[:-2], rest[-2:]
    span = cot_rows.shape[1]
    size = msg_a.shape[0] - sum(c.shape[0] * TILE // span for c in cols)
    edge = cot_rows.shape[0] - size
    chans = size // CHALO
    low = jnp.where(is_even("rows"), edge, 0)
    msg_a[0:size] = cot_rows[pl.ds(pl.multiple_of(low, chans), size), :]
    msg_b[0:size] = cot_rows[pl.ds(pl.multiple_of(edge - low, chans), size), :]
    at = size
    for col in cols:
        count = col.shape[0] * TILE // span
        for t, part in enumerate(tiles_of(span)):
            block = col[t * count : (t + 1) * count]
            msg_a[at : at + count, part] = block
            msg_b[at : at + count, part] = block
        at += count


def corner_views(msg, size, cols):
    span = msg.shape[1]
    views, at = [], size
    for col in cols:
        count = col.shape[0] * TILE // span
        views.append(
            jnp.concatenate([msg[at : at + count, part] for part in tiles_of(span)], axis=0)
        )
        at += count
    return views


def halo_block(sources, slot, rows, kind):
    total = None
    if kind == "features":
        count, shift_r, shift_l = FHALO, -slot * SLOT, TILE - (slot + 1) * SLOT
    else:
        count = CHALO
        shift_r, shift_l = -slot * SLOT - FHALO, TILE - (slot + 1) * SLOT + FHALO
    for index, source in enumerate(sources):
        from_right = is_even("cols") if index == 0 else jnp.logical_not(is_even("cols"))
        block = source.reshape(source.shape[0] // rows, rows, TILE)
        block = turn(block, jnp.where(from_right, shift_r % TILE, shift_l % TILE))
        block = block * edge_lanes((1, rows, TILE), jnp.logical_not(from_right), count)
        total = block if total is None else total + block
    return total


def halo_rows(sources, m, rows, kind):
    return to_rows(
        jnp.concatenate([halo_block(sources, 2 * h + m, rows, kind) for h in (0, 1)], axis=0)
    )


def columns_seen(shape, span):
    _, _, has_left, has_right = has_sides()
    lane = lanes_of(shape)
    middle = span + TILE // 2
    return (lane < span) | ((lane < middle) & has_right) | ((lane >= middle) & has_left)


def cell_matrix(width, by_cell):
    shape = (TILE, width) if by_cell else (width, TILE)
    lane = lax.broadcasted_iota(jnp.int32, shape, 1 if by_cell else 0)
    cell = lax.broadcasted_iota(jnp.int32, shape, 0 if by_cell else 1)
    place = lane // POOL + jnp.where(lane >= width - TILE // 2, TILE - width // POOL, 0)
    return jnp.where(place == cell, 1.0, 0.0).astype(BF16)


def cells_seen(shape, span):
    _, _, has_left, has_right = has_sides()
    lane = lanes_of(shape)
    count = span // POOL
    middle = (count + TILE) // 2
    return (lane < count) | ((lane < middle) & has_right) | ((lane >= middle) & has_left)


def store_split(high, low, at, total):
    top = total.astype(BF16)
    high[at, :] = top
    low[at, :] = (total - top.astype(F32)).astype(BF16)


def block_sums(high, low):
    matrix = cell_matrix(high.shape[1], False)
    return jnp.dot(
        jnp.concatenate([high[...], low[...]], axis=1),
        jnp.concatenate([matrix, matrix], axis=0),
        preferred_element_type=F32,
    )


def spread(rows, width, count):
    values = jnp.concatenate(rows, axis=0)
    top = values.astype(BF16)
    rest = (values - top.astype(F32)).astype(BF16)
    matrix = cell_matrix(width, True)[:, 0:count]
    return jnp.dot(
        jnp.concatenate([top, rest], axis=1),
        jnp.concatenate([matrix, matrix], axis=0),
        preferred_element_type=F32,
    )


def fill_bands(out, kernel, count):
    chans = kernel.shape[1]
    out[...] = jnp.zeros(out.shape, out.dtype)
    for k in range(count):
        for b in range(3):
            for a in range(3):
                at = (b * (count + 2) + k + a) * chans
                out[k * chans : (k + 1) * chans, at : at + chans] = kernel[3 * a + b].astype(
                    out.dtype
                )


def fill_turned_bands(out, kernel, count):
    chans = kernel.shape[1]
    out[...] = jnp.zeros(out.shape, out.dtype)
    for k in range(count):
        for b in range(3):
            for a in range(3):
                at = (b * (count + 2) + k + a) * chans
                out[at : at + chans, k * chans : (k + 1) * chans] = kernel[8 - 3 * a - b].astype(
                    out.dtype
                )


def stacked(views, at):
    return jnp.concatenate([view[at, :] for view in views], axis=0)


def paired(bands, views, g, chans):
    width = views[0].shape[1]
    sides = [
        stacked(views, rows_at((g + i) * POOL, chans, POOL + 2)) for i in (0, 1)
    ]
    parts = jnp.dot(
        bands[...], jnp.concatenate(sides, axis=1), preferred_element_type=F32
    )
    return parts[:, 0:width], parts[:, width:]


def conv_sum(parts, chans, step):
    return (
        turn(parts[0:chans], step)
        + parts[chans : 2 * chans]
        + turn(parts[2 * chans : 3 * chans], -step)
    )


def back_kernel(
    ncols, cot, msg_a, msg_b, *rest,
):
    cols, (
        first, bottle, second,
        act_grad, cot_m, cot_0, cot_p, sides, first_bands, bottle_bands, second_bands,
        back, high, low, coarse, bands_f, bands, small_f, small, wide_f,
    ) = rest[:ncols], rest[ncols:]
    chans = second.shape[1]
    full, span = cot.shape
    height = full // chans
    width = span + TILE
    groups = height // POOL
    has_up, has_down, _, _ = has_sides()

    fill_turned_bands(bands_f, second, POOL)
    bands[...] = bands_f[...].T.astype(BF16)
    fill_turned_bands(small_f, bottle, 1)
    small_t = small_f[...].T
    for b in range(3):
        small[rows_at(b, chans)] = small_t[0:chans, 3 * b * chans : 3 * (b + 1) * chans].astype(BF16)
    fill_bands(first_bands, first, POOL)
    fill_bands(wide_f, bottle, 1)
    for b in range(3):
        bottle_bands[rows_at(b, chans)] = wide_f[
            0:chans, 3 * b * chans : 3 * (b + 1) * chans
        ].astype(BF16)
    second_bands[...] = jnp.zeros(second_bands.shape, BF16)
    for k in range(POOL):
        for b in range(3):
            for a in range(3):
                second_bands[
                    rows_at(3 * k + b, chans), (k + a) * chans : (k + a + 1) * chans
                ] = second[3 * a + b]

    size = CHALO * chans
    block = height // 2

    def halo_columns(sources, at):
        for q, channels, rows in slots(chans, height):
            sides[channels, at + rows.start : at + rows.stop, :] = halo_block(
                sources, q, block, "features"
            )

    own = [c[...] for c in cols]
    halo_columns(own, height)
    cot_0[rows_at(CHALO, chans, height), 0:span] = cot[...]
    for m in (0, 1):
        cot_0[rows_at(CHALO + m * block, chans, block), span:width] = halo_rows(
            own, m, block, "cotangent"
        )

    def vertical(up, down):
        cot_0[rows_at(0, chans, CHALO), 0:span] = up[0:size]
        cot_0[rows_at(CHALO + height, chans, CHALO), 0:span] = down[0:size]
        above, below = corner_views(up, size, cols), corner_views(down, size, cols)
        cot_0[rows_at(0, chans, CHALO), span:width] = halo_rows(above, 1, block, "cotangent")[
            (block - CHALO) * chans :
        ]
        cot_0[rows_at(CHALO + height, chans, CHALO), span:width] = halo_rows(
            below, 0, block, "cotangent"
        )[0:size]
        halo_columns(above, 0)
        halo_columns(below, 2 * height)

    pl.when(is_even("rows"))(lambda: vertical(msg_b, msg_a))
    pl.when(jnp.logical_not(is_even("rows")))(lambda: vertical(msg_a, msg_b))
    for j in range(height + 2 * CHALO):
        at = rows_at(j, chans)
        cot_m[at] = turn(cot_0[at], 1)
        cot_p[at] = turn(cot_0[at], -1)
    def pair(p, _):
        both = paired(bands, (cot_m, cot_0, cot_p), 2 * p, chans)
        for g, rows in zip((2 * p, 2 * p + 1), both):
            rows = rows.astype(BF16)
            back[rows_at(g * POOL, chans, POOL), :] = rows[:, 0:span]
            rows = rows.astype(F32)
            total = rows[0:chans]
            for k in range(1, POOL):
                total = total + rows[k * chans : (k + 1) * chans]
            store_split(high, low, rows_at(g, chans), total)
        return 0

    lax.fori_loop(0, (groups + 2) // 2, pair, 0, unroll=5)
    sums = block_sums(high, low)
    seen_cells = cells_seen((chans, TILE), span)
    for g in range(groups + 2):
        at = rows_at(g, chans)
        seen = seen_cells
        if g == 0:
            seen = seen & has_up
        elif g == groups + 1:
            seen = seen & has_down
        coarse[at] = jnp.where(seen, sums[at], 0.0).astype(BF16)
    means = []
    for g in range(groups):
        parts = jnp.dot(small[...], coarse[rows_at(g, chans, 3), :], preferred_element_type=F32)
        means.append(conv_sum(parts, chans, 1) * (1.0 / POOL**2))
    mean = spread(means, width, span)
    for r in range(height):
        act_grad[rows_at(r, chans), :] = (
            back[rows_at(r + POOL, chans), :].astype(F32) + mean[rows_at(r // POOL, chans)]
        )


def correlate(u, u0, views, v0, acc, height, chans, span):
    groups = range(0, height, BATCH)
    left = jnp.concatenate(
        [
            jnp.concatenate(
                [view[rows_at(v0 + g, chans, BATCH + 2), 0:span] for view in views], axis=0
            )
            for g in groups
        ],
        axis=1,
    )
    right = jnp.concatenate([u[rows_at(u0 + g, chans, BATCH), 0:span] for g in groups], axis=1)
    acc[...] = lax.dot_general(
        left, right, (((1,), (1,)), ((), ())), preferred_element_type=F32
    )


def folded(acc, chans):
    lane = lanes_of((3 * chans, TILE))
    result = jnp.zeros((3 * chans, TILE), F32)
    per_tile = TILE // chans
    for b in range(3):
        total = None
        for place in range(per_tile):
            column = None
            for k in range(place, BATCH, per_tile):
                part = slice(k // per_tile * TILE, (k // per_tile + 1) * TILE)
                block = acc[rows_at(b * (BATCH + 2) + k, chans, 3), part]
                column = block if column is None else column + block
            column = turn(column, (b - place) * chans)
            total = column if total is None else total + column
        result = jnp.where((lane >= b * chans) & (lane < (b + 1) * chans), total, result)
    return result


def main_kernel(
    shifts, feat, feat_a, feat_b, sides, act_grad, view_m, view_0, view_p, bands, small,
    grads, blended,
    lent, moved, warp_m, warp_0, warp_p, act, high, low, pooled, pre_grad, acc,
):
    chans, height, span = feat.shape
    tiles = span // TILE
    width = span + TILE
    groups = height // POOL
    has_up, has_down, has_left, has_right = has_sides()
    seen_cols = columns_seen((chans, width), span)

    size = feat_a.shape[0]
    window = lent.shape[1] - size
    lent[:, size:, :] = jnp.zeros((2, window, span), BF16)

    def borrow(up, down):
        lent[0, 0:size] = up[...]
        lent[1, 0:size] = down[...]

    pl.when(is_even("rows"))(lambda: borrow(feat_b, feat_a))
    pl.when(jnp.logical_not(is_even("rows")))(lambda: borrow(feat_a, feat_b))

    tall = moved.shape[1]
    lane = lanes_of((tall, TILE))
    seen_halo = one_hot(((lane < TILE // 2) & has_right) | ((lane >= TILE // 2) & has_left))
    lane, mirrored = as_bf(lane), as_bf(TILE - 1 - lane)
    step = as_bf(
        lanes_of((tall, 3 * height)) - lax.broadcasted_iota(jnp.int32, (tall, 3 * height), 0)
    )
    depth = 2 * window + height
    source = lanes_of((1, depth))
    apart = as_bf(lax.broadcasted_iota(jnp.int32, (tall, depth), 0) - lanes_of((tall, depth)))
    align = 16

    def warp(c, ats):
        at_up, at_down = ats
        shift, move = shifts[0, c], shifts[1, c]
        n_up, n_down = needed(shift, False), needed(shift, True)
        base_up, base_down = (
            pl.multiple_of(lax.div(at, align) * align, align) for at in (at_up, at_down)
        )
        skip_up, skip_down = at_up - base_up, at_down - base_down
        own = EXT - window - shift
        below = own - skip_down
        above = EXT - skip_up - n_up - shift
        in_up = (source >= skip_up) & (source < skip_up + n_up)
        first_down = window + height + skip_down
        in_down = (source >= first_down) & (source < first_down + n_down)
        none = 4 * depth
        offset = jnp.where(
            source < window,
            jnp.where(in_up, above, none),
            jnp.where(source < window + height, own, jnp.where(in_down, below, none)),
        )
        pick = one_hot(apart == as_bf(offset))
        rows = jnp.concatenate(
            [lent[0, pl.ds(base_up, window), :], feat[c], lent[1, pl.ds(base_down, window), :]], axis=0
        )
        plane = jnp.dot(pick, rows, preferred_element_type=F32).astype(BF16)
        pick = one_hot(step == as_bf(height - EXT + shift))
        plane = [plane[:, part] for part in tiles_of(span)]
        plane.append(jnp.dot(pick, sides[c], preferred_element_type=F32).astype(BF16))
        amount = jnp.where(move > 0, TILE - move, -move)
        parts = [turn(part, amount) for part in plane]
        inside = jnp.where(move > 0, lane, mirrored) < as_bf(TILE - jnp.abs(move))
        for t, part in enumerate(tiles_of(width)):
            after, before = parts[(t + 1) % (tiles + 1)], parts[t - 1]
            result = jnp.where(inside, parts[t], jnp.where(move > 0, after, before))
            moved[c, :, part] = result * seen_halo if t == tiles else result
        return at_up + n_up, at_down + n_down

    lax.fori_loop(0, chans, warp, (jnp.int32(0), jnp.int32(0)), unroll=8)
    chunk = 16
    for r in range(0, tall, chunk):
        for part in tiles_of(width):
            warp_0[rows_at(r, chans, chunk), part] = to_rows(moved[:, r : r + chunk, part])

    def clear(r, count):
        warp_0[rows_at(r, chans, count)] = jnp.zeros((count * chans, width), BF16)

    pl.when(jnp.logical_not(has_up))(lambda: clear(0, EXT))
    pl.when(jnp.logical_not(has_down))(lambda: clear(EXT + height, EXT))
    for j in range(height + 2 * EXT):
        at = rows_at(j, chans)
        warp_m[at] = turn(warp_0[at], 1)
        warp_p[at] = turn(warp_0[at], -1)

    for g in range(0, groups + 4, 2):
        both = paired(bands, (warp_m, warp_0, warp_p), g, chans)
        for g, pre in zip((g, g + 1), both):
            sigma = 0.5 * jnp.tanh(0.5 * pre) + 0.5
            rows = (pre * sigma).astype(BF16)
            act[rows_at(g * POOL, chans, POOL), :] = rows
            rows = rows.astype(F32)
            total = rows[0:chans]
            for k in range(1, POOL):
                total = total + rows[k * chans : (k + 1) * chans]
            store_split(high, low, rows_at(g, chans), total)
            if 2 <= g < groups + 2:
                there = rows_at(g * POOL - 2 * POOL, chans, POOL)
                pre, sigma = pre[:, 0:span], sigma[:, 0:span]
                pre_grad[there, :] = (
                    act_grad[there, :] * (sigma * (1.0 + pre * (1.0 - sigma)))
                ).astype(BF16)
    sums = block_sums(high, low)
    seen_cells = cells_seen((chans, TILE), span)
    for g in range(groups + 4):
        at = rows_at(g, chans)
        seen = seen_cells
        if g < 2:
            seen = seen & has_up
        elif g >= groups + 2:
            seen = seen & has_down
        pooled[at] = jnp.where(seen, sums[at] * (1.0 / POOL**2), 0.0).astype(BF16)

    bottles = []
    for g in range(groups + 2):
        parts = jnp.dot(small[...], pooled[rows_at(g, chans, 3), :], preferred_element_type=F32)
        bottles.append(conv_sum(parts, chans, 1))
    bottle = spread(bottles, width, width)
    for g in range(groups + 2):
        rows, seen = range(POOL), seen_cols
        if g == 0:
            rows, seen = (POOL - 1,), seen & has_up
        elif g == groups + 1:
            rows, seen = (0,), seen & has_down
        for k in rows:
            row = act[rows_at((g + 1) * POOL + k, chans), :].astype(F32) + bottle[rows_at(g, chans)]
            blended[rows_at(g * POOL + k - POOL + 1, chans), :] = jnp.where(seen, row, 0.0).astype(
                BF16
            )

    correlate(pre_grad, 0, (warp_m, warp_0, warp_p), EXT - 1, acc, height, chans, span)
    first_part = folded(acc, chans)
    correlate(blended, 1, (view_m, view_0, view_p), CHALO - 1, acc, height, chans, span)
    second_part = folded(acc, chans)
    lane = lanes_of((3 * chans, TILE))
    grads[0 : 3 * chans] = jnp.where(lane < 3 * chans, first_part, turn(second_part, 3 * chans))
    half = 3 * chans // 2
    grads[3 * chans :] = jnp.where(
        lane[0:half] < TILE // 2,
        turn(second_part[0:half], -chans),
        turn(second_part[half:], TILE // 2 - chans),
    )


def predict_kernel(part, blended, bands, *rest):
    out, rows = rest[-2:]
    chans, height, span = out.shape

    def group(g, _):
        at = rows_at(part * height + g * POOL, chans, POOL + 2)
        parts = jnp.dot(bands[...], blended[at, :], preferred_element_type=F32)
        for k in range(POOL):
            row = conv_sum(parts[3 * k * chans : 3 * (k + 1) * chans], chans, 1)
            rows[rows_at(g * POOL + k, chans), :] = row[:, 0:span].astype(BF16)
        return 0

    lax.fori_loop(0, height // POOL, group, 0, unroll=2)
    for part in tiles_of(span):
        out[:, :, part] = to_planes(rows[:, part], chans)


def final_kernel(factor, mine, other, first, second):
    chans = first.shape[1]
    total = (mine[...].astype(F32) + other[...].astype(F32)) * factor
    turned = total[0 : 3 * chans].T
    for b in range(3):
        for a in range(3):
            first[3 * a + b] = turned[b * chans : (b + 1) * chans, a * chans : (a + 1) * chans]
    half = 3 * chans // 2
    low = total[3 * chans :]
    both = jnp.concatenate([low, turn(low, -(TILE // 2))], axis=0)
    for a in range(3):
        at = slice((2 - a) * chans, (3 - a) * chans)
        second[3 * a + 2] = turn(total[at], -3 * chans)[:, 0:chans]
        second[3 * a + 1] = both[at, 0:chans]
        second[3 * a + 0] = turn(both[at], -chans)[:, 0:chans]


def call(kernel, outs, scratch, n_in, limit, flops=0, smem_first=False, **more):
    specs = [VMEM] * n_in
    if smem_first:
        specs[0] = SMEM
    more.setdefault("in_specs", specs)
    more.setdefault("out_specs", jax.tree.map(lambda _: VMEM, outs))
    return pl.pallas_call(
        kernel,
        out_shape=outs,
        scratch_shapes=scratch,
        compiler_params=pltpu.CompilerParams(vmem_limit_bytes=limit * MIB),
        cost_estimate=pl.CostEstimate(flops=flops, bytes_accessed=4 * MIB, transcendentals=0),
        **more,
    )


def predict(blended, bands, shape, parts, part, before):
    chans, height, span = shape
    rows = height // parts
    block = pl.BlockSpec((chans, rows, span), lambda i: (0, part, 0))
    whole = lambda a: pl.BlockSpec(a.shape, lambda i: (0,) * a.ndim)
    args = (blended, bands)
    specs = [whole(a) for a in args]
    more = {}
    if before is not None:
        args += (before,)
        specs.append(pl.BlockSpec(memory_space=pl.ANY))
        more["input_output_aliases"] = {2: 0}
    return call(
        functools.partial(predict_kernel, part),
        jax.ShapeDtypeStruct(shape, BF16),
        [
            pltpu.VMEM((chans * rows, span), BF16),
        ],
        len(args),
        12,
        flops=10**9,
        grid=(1,),
        in_specs=specs,
        out_specs=block,
        **more,
    )(*args)


def bf(*shape):
    return jax.ShapeDtypeStruct(shape, BF16)


def swapped(messages, axis):
    pairs = [p for p in swaps(lax.axis_size(axis)) if p]
    return [lax.ppermute(m, axis, p) for m, p in zip(messages, pairs)]


def pack_rows(index, skip, size, shifts, feat, counted=False):
    message = bf(size, feat.shape[2])
    if counted:
        message = (message, jax.ShapeDtypeStruct((8, TILE), jnp.int32))
    return call(
        functools.partial(feature_kernel, index, skip),
        message, [], 2, 16, smem_first=True,
    )(shifts, feat)


def main_pass(rest, lent, shifts, feat, sides, act_grad, views, bands):
    chans, height, span = feat.shape
    width = span + TILE
    full = height * chans
    groups = height // POOL
    band = 3 * (POOL + 2) * chans
    if rest:
        size = lent[0].shape[0]
        more = swapped([pack_rows(i, size, rest, shifts, feat) for i in (0, 1)], "rows")
        lent = [jnp.concatenate(pair, axis=0) for pair in zip(lent, more)]
    size = lent[0].shape[0]
    tall = pl.cdiv(height + 2 * EXT, 16) * 16
    grads, blended = call(
        main_kernel,
        (jax.ShapeDtypeStruct((9 * chans // 2, TILE), F32), bf((height + 2) * chans, width)),
        [
            pltpu.VMEM((2, size + 48, span), BF16),
            pltpu.VMEM((chans, tall, width), BF16),
        ]
        + [pltpu.VMEM((tall * chans, width), BF16)] * 3
        + [pltpu.VMEM(((height + 4 * POOL) * chans, width), BF16)]
        + [pltpu.VMEM(((groups + 4) * chans, width), BF16)] * 2
        + [pltpu.VMEM(((groups + 4) * chans, TILE), BF16)]
        + [
            pltpu.VMEM((full, span), BF16),
            pltpu.VMEM((3 * (BATCH + 2) * chans, BATCH * chans), F32),
        ],
        11,
        20,
        flops=10**10,
        smem_first=True,
    )(
        shifts, feat, *lent, sides, act_grad, *views, *bands
    )

    return grads, blended


def shards(features, shifts, first_kernel, bottle_kernel, second_kernel, cotangent):
    imgs, chans, height, span = features.shape
    rows, cols, dp = (lax.axis_size(a) for a in ("rows", "cols", "dp"))
    full = height * chans

    width = span + TILE
    groups = height // POOL
    feat, cot, shifts = features[0], cotangent[0], shifts[0].T
    row_pairs = swaps(rows)

    usual = USUAL * chans
    message, total = pack_rows(0, 0, usual, shifts, feat, counted=True)
    message, total, cot = lax.optimization_barrier((message, total, cot))
    feat_a = lax.ppermute(message, "rows", row_pairs[0])
    bit = 1
    while bit < dp:
        total = jnp.maximum(total, lax.ppermute(total, "dp", [(i, i ^ bit) for i in range(dp)]))
        bit *= 2

    packed = chans * (height * SLOT // TILE)
    messages = call(
        column_kernel, (bf(packed, TILE),) * (1 if cols == 2 else 2), [], 2, 8, flops=2 * 10**10
    )(feat, cot)
    col_msgs = swapped(messages, "cols")
    ncols = len(col_msgs)
    message = pack_rows(1, 0, usual, shifts, feat)
    col_msgs, message, total = lax.optimization_barrier((col_msgs, message, total))
    feat_b = lax.ppermute(message, "rows", row_pairs[1])
    cot_rows = call(rows_kernel, bf(full, span), [], 1, 4)(cot)
    halo = bf(CHALO * chans + ncols * packed * TILE // span, span)
    messages = call(edge_kernel, (halo, halo), [], 1 + ncols, 8)(cot_rows, *col_msgs)
    row_msgs = swapped(messages, "rows")
    row_msgs[0], total = lax.optimization_barrier((row_msgs[0], total))
    row_msgs, feat_a = lax.optimization_barrier((row_msgs, feat_a))

    tall_c = (height + 2 * CHALO) * chans
    view = bf(tall_c, width)
    band = 3 * (POOL + 2) * chans
    act_grad, *rest = call(
        functools.partial(back_kernel, ncols),
        (
            jax.ShapeDtypeStruct((full, span), F32), view, view, view,
            bf(chans, 3 * height, TILE), bf(POOL * chans, band), bf(3 * chans, 3 * chans),
            bf(3 * POOL * chans, (POOL + 2) * chans),
        ),
        [pltpu.VMEM(((height + 2 * POOL) * chans, span), BF16)]
        + [pltpu.VMEM(((groups + 2) * chans, width), BF16)] * 2
        + [pltpu.VMEM(((groups + 2) * chans, TILE), BF16)]
        + [
            pltpu.VMEM((band, POOL * chans), F32),
            pltpu.VMEM((POOL * chans, band), BF16),
            pltpu.VMEM((9 * chans, TILE), F32),
            pltpu.VMEM((3 * chans, 3 * chans), BF16),
            pltpu.VMEM((chans, 9 * chans), F32),
        ],
        6 + ncols,
        16,
        flops=8 * 10**9,
    )(cot_rows, *row_msgs, *col_msgs, first_kernel, bottle_kernel, second_kernel)
    views, sides, weights = rest[:3], rest[3], rest[4:]

    grads, blended = lax.cond(
        total[0, 0] <= usual,
        functools.partial(main_pass, 0),
        functools.partial(main_pass, LARGEST * chans - usual),
        (feat_a, feat_b), shifts, feat, sides, act_grad, tuple(views), tuple(weights[:2]),
    )

    steps = []
    for axis, size in (("dp", dp), ("cols", cols), ("rows", rows)):
        bit = 1
        while bit < size:
            steps.append((axis, [(i, i ^ bit) for i in range(size)]))
            bit *= 2
    parts, prediction = 2, None
    for step, (axis, pairs) in enumerate(steps):
        if step >= len(steps) - 2:
            grads = lax.optimization_barrier(grads.astype(BF16))
        other = lax.ppermute(grads, axis, pairs)
        if 1 <= step <= parts:
            prediction = predict(
                blended, weights[2], (chans, height, span), parts, step - 1, prediction
            )
            other, prediction = lax.optimization_barrier((other, prediction))
        if step < len(steps) - 1:
            grads = grads.astype(F32) + other.astype(F32)
            if step < parts:
                grads, blended = lax.optimization_barrier((grads, blended))
    factor = 1.0 / math.sqrt(imgs * dp * height * rows * span * cols)
    shape = jax.ShapeDtypeStruct((9, chans, chans), F32)
    first_grad, second_grad = call(
        functools.partial(final_kernel, factor), (shape, shape), [], 2, 2
    )(grads, other)
    return (prediction[None], first_grad, second_grad)


def solution(mesh):
    placed = (
        P("dp", None, "rows", "cols"),
        P("dp", None, None),
        P(),
        P(),
        P(),
        P("dp", None, "rows", "cols"),
    )
    return jax.shard_map(
        shards,
        mesh=mesh,
        in_specs=placed,
        out_specs=(P("dp", None, "rows", "cols"), P(), P()),
        check_vma=False,
    )
```

```python
import functools
import math

import jax
import jax.numpy as jnp
from jax import lax
from jax.experimental import pallas as pl
from jax.experimental.pallas import tpu as pltpu
from jax.sharding import PartitionSpec as P


MAXSHIFT = 16
POOL = 4
BATCH = 8
TILE = 128
SLOT = 32
EXT = 9
FHALO = MAXSHIFT + EXT
USUAL = 14
LARGEST = FHALO + 1
CHALO = 5
F32 = jnp.float32
BF16 = jnp.bfloat16
VMEM = pl.BlockSpec(memory_space=pltpu.VMEM)
SMEM = pl.BlockSpec(memory_space=pltpu.SMEM)
MIB = 1024 * 1024


def lanes_of(shape):
    return lax.broadcasted_iota(jnp.int32, shape, len(shape) - 1)


def turn(values, shift):
    width = values.shape[-1]
    if isinstance(shift, int):
        shift = shift % width
        if shift == 0:
            return values
    return pltpu.roll(values, shift, values.ndim - 1)


def has_sides():
    row, col = lax.axis_index("rows"), lax.axis_index("cols")
    return (
        row > 0,
        row < lax.axis_size("rows") - 1,
        col > 0,
        col < lax.axis_size("cols") - 1,
    )


def as_bf(values):
    return values.astype(F32).astype(BF16)


def one_hot(mask):
    return jnp.where(mask, jnp.ones((), BF16), jnp.zeros((), BF16))


def rows_at(r, chans, count=1):
    if isinstance(r, int):
        return slice(r * chans, (r + count) * chans)
    return pl.ds(pl.multiple_of(r * chans, chans), count * chans)


def to_rows(block):
    chans, height, span = block.shape
    return jnp.transpose(block, (1, 0, 2)).reshape(height * chans, span)


def to_planes(block, chans):
    height = block.shape[0] // chans
    return jnp.transpose(block.reshape(height, chans, block.shape[1]), (1, 0, 2))


def tiles_of(span):
    return [slice(t, t + TILE) for t in range(0, span, TILE)]


def is_even(axis):
    return lax.rem(lax.axis_index(axis), 2) == 0


def swaps(size):
    first = [(i, i ^ 1) for i in range(size)]
    second = [(i, i + 1) for i in range(1, size - 1, 2)]
    return [first, second + [(j, i) for i, j in second]]


def needed(shift, below):
    return jnp.maximum(EXT + shift if below else EXT - shift, 0)


def feature_kernel(index, skip, shifts, feat, msg, *counts):
    chans, height, span = feat.shape
    full = chans * height
    size = msg.shape[0]
    chunk = size // 4
    source = feat[...].reshape(full, span)
    lane = lanes_of((8, full))
    chan, row = lane // height, lane % height
    to_below = is_even("rows") if index == 0 else jnp.logical_not(is_even("rows"))
    target = jnp.full((8, full), -1, jnp.int32)
    at, up, down = jnp.int32(-skip), jnp.int32(0), jnp.int32(0)
    for c in range(chans):
        shift = shifts[0, c]
        n_up, n_down = needed(shift, False), needed(shift, True)
        count = jnp.where(to_below, n_up, n_down)
        first = jnp.where(to_below, height - count, 0)
        mine = (chan == c) & (row >= first) & (row < first + count)
        target = jnp.where(mine, row + (at - first), target)
        at, up, down = at + count, up + n_up, down + n_down
    for out in counts:
        out[...] = jnp.full(out.shape, jnp.maximum(up, down), jnp.int32)
    place = as_bf(lax.broadcasted_iota(jnp.int32, (chunk, full), 0))
    for p in range(0, size, chunk):
        late = (p + skip) // FHALO * height // TILE * TILE
        pick = one_hot(place[:, late:] == as_bf(target[0:1, late:] - p))
        msg[p : p + chunk] = jnp.dot(
            pick, source[late:], preferred_element_type=F32
        ).astype(BF16)


def rows_kernel(source, out):
    for part in tiles_of(source.shape[2]):
        out[:, part] = to_rows(source[:, :, part])


def edge_lanes(shape, right, count):
    lane = lanes_of(shape)
    return jnp.where(jnp.where(right, TILE - 1 - lane, lane) < count, 1.0, 0.0).astype(BF16)


def slots(chans, height):
    half, block = chans // 2, height // 2
    for h in (0, 1):
        for m in (0, 1):
            yield 2 * h + m, slice(h * half, (h + 1) * half), slice(m * block, (m + 1) * block)


def column_kernel(feat, cot, *rest):
    col_msgs, (feat_edge, cot_edge, sems) = rest[:-3], rest[-3:]
    chans, height, span = feat.shape
    for index, msg in enumerate(col_msgs):
        right = is_even("cols") if index == 0 else jnp.logical_not(is_even("cols"))
        part = pl.ds(pl.multiple_of(jnp.where(right, span - TILE, 0), TILE), TILE)
        copies = [
            pltpu.make_async_copy(ref.at[:, :, part], edge, sems.at[i])
            for i, (ref, edge) in enumerate(((feat, feat_edge), (cot, cot_edge)))
        ]
        for copy in copies:
            copy.start()
        for copy in copies:
            copy.wait()
        shape = (1, height // 2, TILE)
        inner = edge_lanes(shape, right, FHALO)
        outer = edge_lanes(shape, right, SLOT) - inner
        total = None
        for q, channels, rows in slots(chans, height):
            cots = turn(cot_edge[channels, rows, :], jnp.where(right, TILE - FHALO, FHALO))
            piece = feat_edge[channels, rows, :] * inner + cots * outer
            piece = turn(piece, jnp.where(right, (q + 1) * SLOT % TILE, q * SLOT))
            total = piece if total is None else total + piece
        msg[...] = total.reshape(msg.shape)


def edge_kernel(cot_rows, *rest):
    cols, (msg_a, msg_b) = rest[:-2], rest[-2:]
    span = cot_rows.shape[1]
    size = msg_a.shape[0] - sum(c.shape[0] * TILE // span for c in cols)
    edge = cot_rows.shape[0] - size
    chans = size // CHALO
    low = jnp.where(is_even("rows"), edge, 0)
    msg_a[0:size] = cot_rows[pl.ds(pl.multiple_of(low, chans), size), :]
    msg_b[0:size] = cot_rows[pl.ds(pl.multiple_of(edge - low, chans), size), :]
    at = size
    for col in cols:
        count = col.shape[0] * TILE // span
        for t, part in enumerate(tiles_of(span)):
            block = col[t * count : (t + 1) * count]
            msg_a[at : at + count, part] = block
            msg_b[at : at + count, part] = block
        at += count


def corner_views(msg, size, cols):
    span = msg.shape[1]
    views, at = [], size
    for col in cols:
        count = col.shape[0] * TILE // span
        views.append(
            jnp.concatenate([msg[at : at + count, part] for part in tiles_of(span)], axis=0)
        )
        at += count
    return views


def halo_block(sources, slot, rows, kind):
    total = None
    if kind == "features":
        count, shift_r, shift_l = FHALO, -slot * SLOT, TILE - (slot + 1) * SLOT
    else:
        count = CHALO
        shift_r, shift_l = -slot * SLOT - FHALO, TILE - (slot + 1) * SLOT + FHALO
    for index, source in enumerate(sources):
        from_right = is_even("cols") if index == 0 else jnp.logical_not(is_even("cols"))
        block = source.reshape(source.shape[0] // rows, rows, TILE)
        block = turn(block, jnp.where(from_right, shift_r % TILE, shift_l % TILE))
        block = block * edge_lanes((1, rows, TILE), jnp.logical_not(from_right), count)
        total = block if total is None else total + block
    return total


def halo_rows(sources, m, rows, kind):
    return to_rows(
        jnp.concatenate([halo_block(sources, 2 * h + m, rows, kind) for h in (0, 1)], axis=0)
    )


def columns_seen(shape, span):
    _, _, has_left, has_right = has_sides()
    lane = lanes_of(shape)
    middle = span + TILE // 2
    return (lane < span) | ((lane < middle) & has_right) | ((lane >= middle) & has_left)


def cell_matrix(width, by_cell):
    shape = (TILE, width) if by_cell else (width, TILE)
    lane = lax.broadcasted_iota(jnp.int32, shape, 1 if by_cell else 0)
    cell = lax.broadcasted_iota(jnp.int32, shape, 0 if by_cell else 1)
    place = lane // POOL + jnp.where(lane >= width - TILE // 2, TILE - width // POOL, 0)
    return jnp.where(place == cell, 1.0, 0.0).astype(BF16)


def cells_seen(shape, span):
    _, _, has_left, has_right = has_sides()
    lane = lanes_of(shape)
    count = span // POOL
    middle = (count + TILE) // 2
    return (lane < count) | ((lane < middle) & has_right) | ((lane >= middle) & has_left)


def store_split(high, low, at, total):
    top = total.astype(BF16)
    high[at, :] = top
    low[at, :] = (total - top.astype(F32)).astype(BF16)


def block_sums(high, low):
    matrix = cell_matrix(high.shape[1], False)
    return jnp.dot(
        jnp.concatenate([high[...], low[...]], axis=1),
        jnp.concatenate([matrix, matrix], axis=0),
        preferred_element_type=F32,
    )


def spread(rows, width, count):
    values = jnp.concatenate(rows, axis=0)
    top = values.astype(BF16)
    rest = (values - top.astype(F32)).astype(BF16)
    matrix = cell_matrix(width, True)[:, 0:count]
    return jnp.dot(
        jnp.concatenate([top, rest], axis=1),
        jnp.concatenate([matrix, matrix], axis=0),
        preferred_element_type=F32,
    )


def fill_bands(out, kernel, count):
    chans = kernel.shape[1]
    out[...] = jnp.zeros(out.shape, out.dtype)
    for k in range(count):
        for b in range(3):
            for a in range(3):
                at = (b * (count + 2) + k + a) * chans
                out[k * chans : (k + 1) * chans, at : at + chans] = kernel[3 * a + b].astype(
                    out.dtype
                )


def fill_turned_bands(out, kernel, count):
    chans = kernel.shape[1]
    out[...] = jnp.zeros(out.shape, out.dtype)
    for k in range(count):
        for b in range(3):
            for a in range(3):
                at = (b * (count + 2) + k + a) * chans
                out[at : at + chans, k * chans : (k + 1) * chans] = kernel[8 - 3 * a - b].astype(
                    out.dtype
                )


def stacked(views, at):
    return jnp.concatenate([view[at, :] for view in views], axis=0)


def paired(bands, views, g, chans):
    width = views[0].shape[1]
    sides = [
        stacked(views, rows_at((g + i) * POOL, chans, POOL + 2)) for i in (0, 1)
    ]
    parts = jnp.dot(
        bands[...], jnp.concatenate(sides, axis=1), preferred_element_type=F32
    )
    return parts[:, 0:width], parts[:, width:]


def conv_sum(parts, chans, step):
    return (
        turn(parts[0:chans], step)
        + parts[chans : 2 * chans]
        + turn(parts[2 * chans : 3 * chans], -step)
    )


def back_kernel(
    ncols, cot, msg_a, msg_b, *rest,
):
    cols, (
        first, bottle, second,
        act_grad, cot_m, cot_0, cot_p, sides, first_bands, bottle_bands, second_bands,
        back, high, low, coarse, bands_f, bands, small_f, small, wide_f,
    ) = rest[:ncols], rest[ncols:]
    chans = second.shape[1]
    full, span = cot.shape
    height = full // chans
    width = span + TILE
    groups = height // POOL
    has_up, has_down, _, _ = has_sides()

    fill_turned_bands(bands_f, second, POOL)
    bands[...] = bands_f[...].T.astype(BF16)
    fill_turned_bands(small_f, bottle, 1)
    small_t = small_f[...].T
    for b in range(3):
        small[rows_at(b, chans)] = small_t[0:chans, 3 * b * chans : 3 * (b + 1) * chans].astype(BF16)
    fill_bands(first_bands, first, POOL)
    fill_bands(wide_f, bottle, 1)
    for b in range(3):
        bottle_bands[rows_at(b, chans)] = wide_f[
            0:chans, 3 * b * chans : 3 * (b + 1) * chans
        ].astype(BF16)
    second_bands[...] = jnp.zeros(second_bands.shape, BF16)
    for k in range(POOL):
        for b in range(3):
            for a in range(3):
                second_bands[
                    rows_at(3 * k + b, chans), (k + a) * chans : (k + a + 1) * chans
                ] = second[3 * a + b]

    size = CHALO * chans
    block = height // 2

    def halo_columns(sources, at):
        for q, channels, rows in slots(chans, height):
            sides[channels, at + rows.start : at + rows.stop, :] = halo_block(
                sources, q, block, "features"
            )

    own = [c[...] for c in cols]
    halo_columns(own, height)
    cot_0[rows_at(CHALO, chans, height), 0:span] = cot[...]
    for m in (0, 1):
        cot_0[rows_at(CHALO + m * block, chans, block), span:width] = halo_rows(
            own, m, block, "cotangent"
        )

    def vertical(up, down):
        cot_0[rows_at(0, chans, CHALO), 0:span] = up[0:size]
        cot_0[rows_at(CHALO + height, chans, CHALO), 0:span] = down[0:size]
        above, below = corner_views(up, size, cols), corner_views(down, size, cols)
        cot_0[rows_at(0, chans, CHALO), span:width] = halo_rows(above, 1, block, "cotangent")[
            (block - CHALO) * chans :
        ]
        cot_0[rows_at(CHALO + height, chans, CHALO), span:width] = halo_rows(
            below, 0, block, "cotangent"
        )[0:size]
        halo_columns(above, 0)
        halo_columns(below, 2 * height)

    pl.when(is_even("rows"))(lambda: vertical(msg_b, msg_a))
    pl.when(jnp.logical_not(is_even("rows")))(lambda: vertical(msg_a, msg_b))
    for j in range(height + 2 * CHALO):
        at = rows_at(j, chans)
        cot_m[at] = turn(cot_0[at], 1)
        cot_p[at] = turn(cot_0[at], -1)
    def pair(p, _):
        both = paired(bands, (cot_m, cot_0, cot_p), 2 * p, chans)
        for g, rows in zip((2 * p, 2 * p + 1), both):
            rows = rows.astype(BF16)
            back[rows_at(g * POOL, chans, POOL), :] = rows[:, 0:span]
            rows = rows.astype(F32)
            total = rows[0:chans]
            for k in range(1, POOL):
                total = total + rows[k * chans : (k + 1) * chans]
            store_split(high, low, rows_at(g, chans), total)
        return 0

    lax.fori_loop(0, (groups + 2) // 2, pair, 0, unroll=5)
    sums = block_sums(high, low)
    seen_cells = cells_seen((chans, TILE), span)
    for g in range(groups + 2):
        at = rows_at(g, chans)
        seen = seen_cells
        if g == 0:
            seen = seen & has_up
        elif g == groups + 1:
            seen = seen & has_down
        coarse[at] = jnp.where(seen, sums[at], 0.0).astype(BF16)
    means = []
    for g in range(groups):
        parts = jnp.dot(small[...], coarse[rows_at(g, chans, 3), :], preferred_element_type=F32)
        means.append(conv_sum(parts, chans, 1) * (1.0 / POOL**2))
    mean = spread(means, width, span)
    for r in range(height):
        act_grad[rows_at(r, chans), :] = (
            back[rows_at(r + POOL, chans), :].astype(F32) + mean[rows_at(r // POOL, chans)]
        )


def correlate(u, u0, views, v0, acc, height, chans, span):
    groups = range(0, height, BATCH)
    left = jnp.concatenate(
        [
            jnp.concatenate(
                [view[rows_at(v0 + g, chans, BATCH + 2), 0:span] for view in views], axis=0
            )
            for g in groups
        ],
        axis=1,
    )
    right = jnp.concatenate([u[rows_at(u0 + g, chans, BATCH), 0:span] for g in groups], axis=1)
    acc[...] = lax.dot_general(
        left, right, (((1,), (1,)), ((), ())), preferred_element_type=F32
    )


def folded(acc, chans):
    lane = lanes_of((3 * chans, TILE))
    result = jnp.zeros((3 * chans, TILE), F32)
    per_tile = TILE // chans
    for b in range(3):
        total = None
        for place in range(per_tile):
            column = None
            for k in range(place, BATCH, per_tile):
                part = slice(k // per_tile * TILE, (k // per_tile + 1) * TILE)
                block = acc[rows_at(b * (BATCH + 2) + k, chans, 3), part]
                column = block if column is None else column + block
            column = turn(column, (b - place) * chans)
            total = column if total is None else total + column
        result = jnp.where((lane >= b * chans) & (lane < (b + 1) * chans), total, result)
    return result


def main_kernel(
    shifts, feat, feat_a, feat_b, sides, act_grad, view_m, view_0, view_p, bands, small,
    grads, blended,
    lent, moved, warp_m, warp_0, warp_p, act, high, low, pooled, pre_grad, acc,
):
    chans, height, span = feat.shape
    tiles = span // TILE
    width = span + TILE
    groups = height // POOL
    has_up, has_down, has_left, has_right = has_sides()
    seen_cols = columns_seen((chans, width), span)

    size = feat_a.shape[0]
    window = lent.shape[1] - size
    lent[:, size:, :] = jnp.zeros((2, window, span), BF16)

    def borrow(up, down):
        lent[0, 0:size] = up[...]
        lent[1, 0:size] = down[...]

    pl.when(is_even("rows"))(lambda: borrow(feat_b, feat_a))
    pl.when(jnp.logical_not(is_even("rows")))(lambda: borrow(feat_a, feat_b))

    tall = moved.shape[1]
    lane = lanes_of((tall, TILE))
    seen_halo = one_hot(((lane < TILE // 2) & has_right) | ((lane >= TILE // 2) & has_left))
    lane, mirrored = as_bf(lane), as_bf(TILE - 1 - lane)
    step = as_bf(
        lanes_of((tall, 3 * height)) - lax.broadcasted_iota(jnp.int32, (tall, 3 * height), 0)
    )
    depth = 2 * window + height
    source = lanes_of((1, depth))
    apart = as_bf(lax.broadcasted_iota(jnp.int32, (tall, depth), 0) - lanes_of((tall, depth)))
    align = 16

    def warp(c, ats):
        at_up, at_down = ats
        shift, move = shifts[0, c], shifts[1, c]
        n_up, n_down = needed(shift, False), needed(shift, True)
        base_up, base_down = (
            pl.multiple_of(lax.div(at, align) * align, align) for at in (at_up, at_down)
        )
        skip_up, skip_down = at_up - base_up, at_down - base_down
        own = EXT - window - shift
        below = own - skip_down
        above = EXT - skip_up - n_up - shift
        in_up = (source >= skip_up) & (source < skip_up + n_up)
        first_down = window + height + skip_down
        in_down = (source >= first_down) & (source < first_down + n_down)
        none = 4 * depth
        offset = jnp.where(
            source < window,
            jnp.where(in_up, above, none),
            jnp.where(source < window + height, own, jnp.where(in_down, below, none)),
        )
        pick = one_hot(apart == as_bf(offset))
        rows = jnp.concatenate(
            [lent[0, pl.ds(base_up, window), :], feat[c], lent[1, pl.ds(base_down, window), :]], axis=0
        )
        plane = jnp.dot(pick, rows, preferred_element_type=F32).astype(BF16)
        pick = one_hot(step == as_bf(height - EXT + shift))
        plane = [plane[:, part] for part in tiles_of(span)]
        plane.append(jnp.dot(pick, sides[c], preferred_element_type=F32).astype(BF16))
        amount = jnp.where(move > 0, TILE - move, -move)
        parts = [turn(part, amount) for part in plane]
        inside = jnp.where(move > 0, lane, mirrored) < as_bf(TILE - jnp.abs(move))
        for t, part in enumerate(tiles_of(width)):
            after, before = parts[(t + 1) % (tiles + 1)], parts[t - 1]
            result = jnp.where(inside, parts[t], jnp.where(move > 0, after, before))
            moved[c, :, part] = result * seen_halo if t == tiles else result
        return at_up + n_up, at_down + n_down

    lax.fori_loop(0, chans, warp, (jnp.int32(0), jnp.int32(0)), unroll=8)
    chunk = 16
    for r in range(0, tall, chunk):
        for part in tiles_of(width):
            warp_0[rows_at(r, chans, chunk), part] = to_rows(moved[:, r : r + chunk, part])

    def clear(r, count):
        warp_0[rows_at(r, chans, count)] = jnp.zeros((count * chans, width), BF16)

    pl.when(jnp.logical_not(has_up))(lambda: clear(0, EXT))
    pl.when(jnp.logical_not(has_down))(lambda: clear(EXT + height, EXT))
    for j in range(height + 2 * EXT):
        at = rows_at(j, chans)
        warp_m[at] = turn(warp_0[at], 1)
        warp_p[at] = turn(warp_0[at], -1)

    for g in range(0, groups + 4, 2):
        both = paired(bands, (warp_m, warp_0, warp_p), g, chans)
        for g, pre in zip((g, g + 1), both):
            sigma = 0.5 * jnp.tanh(0.5 * pre) + 0.5
            rows = (pre * sigma).astype(BF16)
            act[rows_at(g * POOL, chans, POOL), :] = rows
            rows = rows.astype(F32)
            total = rows[0:chans]
            for k in range(1, POOL):
                total = total + rows[k * chans : (k + 1) * chans]
            store_split(high, low, rows_at(g, chans), total)
            if 2 <= g < groups + 2:
                there = rows_at(g * POOL - 2 * POOL, chans, POOL)
                pre, sigma = pre[:, 0:span], sigma[:, 0:span]
                pre_grad[there, :] = (
                    act_grad[there, :] * (sigma * (1.0 + pre * (1.0 - sigma)))
                ).astype(BF16)
    sums = block_sums(high, low)
    seen_cells = cells_seen((chans, TILE), span)
    for g in range(groups + 4):
        at = rows_at(g, chans)
        seen = seen_cells
        if g < 2:
            seen = seen & has_up
        elif g >= groups + 2:
            seen = seen & has_down
        pooled[at] = jnp.where(seen, sums[at] * (1.0 / POOL**2), 0.0).astype(BF16)

    bottles = []
    for g in range(groups + 2):
        parts = jnp.dot(small[...], pooled[rows_at(g, chans, 3), :], preferred_element_type=F32)
        bottles.append(conv_sum(parts, chans, 1))
    bottle = spread(bottles, width, width)
    for g in range(groups + 2):
        rows, seen = range(POOL), seen_cols
        if g == 0:
            rows, seen = (POOL - 1,), seen & has_up
        elif g == groups + 1:
            rows, seen = (0,), seen & has_down
        for k in rows:
            row = act[rows_at((g + 1) * POOL + k, chans), :].astype(F32) + bottle[rows_at(g, chans)]
            blended[rows_at(g * POOL + k - POOL + 1, chans), :] = jnp.where(seen, row, 0.0).astype(
                BF16
            )

    correlate(pre_grad, 0, (warp_m, warp_0, warp_p), EXT - 1, acc, height, chans, span)
    first_part = folded(acc, chans)
    correlate(blended, 1, (view_m, view_0, view_p), CHALO - 1, acc, height, chans, span)
    second_part = folded(acc, chans)
    lane = lanes_of((3 * chans, TILE))
    grads[0 : 3 * chans] = jnp.where(lane < 3 * chans, first_part, turn(second_part, 3 * chans))
    half = 3 * chans // 2
    grads[3 * chans :] = jnp.where(
        lane[0:half] < TILE // 2,
        turn(second_part[0:half], -chans),
        turn(second_part[half:], TILE // 2 - chans),
    )


def predict_kernel(part, blended, bands, *rest):
    out, rows = rest[-2:]
    chans, height, span = out.shape

    def group(g, _):
        at = rows_at(part * height + g * POOL, chans, POOL + 2)
        parts = jnp.dot(bands[...], blended[at, :], preferred_element_type=F32)
        for k in range(POOL):
            row = conv_sum(parts[3 * k * chans : 3 * (k + 1) * chans], chans, 1)
            rows[rows_at(g * POOL + k, chans), :] = row[:, 0:span].astype(BF16)
        return 0

    lax.fori_loop(0, height // POOL, group, 0, unroll=2)
    for part in tiles_of(span):
        out[:, :, part] = to_planes(rows[:, part], chans)


def final_kernel(factor, mine, other, first, second):
    chans = first.shape[1]
    total = (mine[...].astype(F32) + other[...].astype(F32)) * factor
    turned = total[0 : 3 * chans].T
    for b in range(3):
        for a in range(3):
            first[3 * a + b] = turned[b * chans : (b + 1) * chans, a * chans : (a + 1) * chans]
    half = 3 * chans // 2
    low = total[3 * chans :]
    both = jnp.concatenate([low, turn(low, -(TILE // 2))], axis=0)
    for a in range(3):
        at = slice((2 - a) * chans, (3 - a) * chans)
        second[3 * a + 2] = turn(total[at], -3 * chans)[:, 0:chans]
        second[3 * a + 1] = both[at, 0:chans]
        second[3 * a + 0] = turn(both[at], -chans)[:, 0:chans]


def call(kernel, outs, scratch, n_in, limit, flops=0, smem_first=False, **more):
    specs = [VMEM] * n_in
    if smem_first:
        specs[0] = SMEM
    more.setdefault("in_specs", specs)
    more.setdefault("out_specs", jax.tree.map(lambda _: VMEM, outs))
    return pl.pallas_call(
        kernel,
        out_shape=outs,
        scratch_shapes=scratch,
        compiler_params=pltpu.CompilerParams(vmem_limit_bytes=limit * MIB),
        cost_estimate=pl.CostEstimate(flops=flops, bytes_accessed=4 * MIB, transcendentals=0),
        **more,
    )


def predict(blended, bands, shape, parts, part, before):
    chans, height, span = shape
    rows = height // parts
    block = pl.BlockSpec((chans, rows, span), lambda i: (0, part, 0))
    whole = lambda a: pl.BlockSpec(a.shape, lambda i: (0,) * a.ndim)
    args = (blended, bands)
    specs = [whole(a) for a in args]
    more = {}
    if before is not None:
        args += (before,)
        specs.append(pl.BlockSpec(memory_space=pl.ANY))
        more["input_output_aliases"] = {2: 0}
    return call(
        functools.partial(predict_kernel, part),
        jax.ShapeDtypeStruct(shape, BF16),
        [
            pltpu.VMEM((chans * rows, span), BF16),
        ],
        len(args),
        12,
        flops=10**9,
        grid=(1,),
        in_specs=specs,
        out_specs=block,
        **more,
    )(*args)


def bf(*shape):
    return jax.ShapeDtypeStruct(shape, BF16)


def swapped(messages, axis):
    pairs = [p for p in swaps(lax.axis_size(axis)) if p]
    return [lax.ppermute(m, axis, p) for m, p in zip(messages, pairs)]


def pack_rows(index, skip, size, shifts, feat, counted=False):
    message = bf(size, feat.shape[2])
    if counted:
        message = (message, jax.ShapeDtypeStruct((8, TILE), jnp.int32))
    return call(
        functools.partial(feature_kernel, index, skip),
        message, [], 2, 16, smem_first=True,
    )(shifts, feat)


def main_pass(rest, lent, shifts, feat, sides, act_grad, views, bands):
    chans, height, span = feat.shape
    width = span + TILE
    full = height * chans
    groups = height // POOL
    band = 3 * (POOL + 2) * chans
    if rest:
        size = lent[0].shape[0]
        more = swapped([pack_rows(i, size, rest, shifts, feat) for i in (0, 1)], "rows")
        lent = [jnp.concatenate(pair, axis=0) for pair in zip(lent, more)]
    size = lent[0].shape[0]
    tall = pl.cdiv(height + 2 * EXT, 16) * 16
    grads, blended = call(
        main_kernel,
        (jax.ShapeDtypeStruct((9 * chans // 2, TILE), F32), bf((height + 2) * chans, width)),
        [
            pltpu.VMEM((2, size + 48, span), BF16),
            pltpu.VMEM((chans, tall, width), BF16),
        ]
        + [pltpu.VMEM((tall * chans, width), BF16)] * 3
        + [pltpu.VMEM(((height + 4 * POOL) * chans, width), BF16)]
        + [pltpu.VMEM(((groups + 4) * chans, width), BF16)] * 2
        + [pltpu.VMEM(((groups + 4) * chans, TILE), BF16)]
        + [
            pltpu.VMEM((full, span), BF16),
            pltpu.VMEM((3 * (BATCH + 2) * chans, BATCH * chans), F32),
        ],
        11,
        20,
        flops=10**10,
        smem_first=True,
    )(
        shifts, feat, *lent, sides, act_grad, *views, *bands
    )

    return grads, blended


def shards(features, shifts, first_kernel, bottle_kernel, second_kernel, cotangent):
    imgs, chans, height, span = features.shape
    rows, cols, dp = (lax.axis_size(a) for a in ("rows", "cols", "dp"))
    full = height * chans

    width = span + TILE
    groups = height // POOL
    feat, cot, shifts = features[0], cotangent[0], shifts[0].T
    row_pairs = swaps(rows)

    usual = USUAL * chans
    message, total = pack_rows(0, 0, usual, shifts, feat, counted=True)
    message, total, cot = lax.optimization_barrier((message, total, cot))
    feat_a = lax.ppermute(message, "rows", row_pairs[0])
    bit = 1
    while bit < dp:
        total = jnp.maximum(total, lax.ppermute(total, "dp", [(i, i ^ bit) for i in range(dp)]))
        bit *= 2

    packed = chans * (height * SLOT // TILE)
    anywhere = pl.BlockSpec(memory_space=pl.ANY)
    messages = call(
        column_kernel,
        (bf(packed, TILE),) * (1 if cols == 2 else 2),
        [pltpu.VMEM((chans, height, TILE), BF16)] * 2 + [pltpu.SemaphoreType.DMA((2,))],
        2,
        8,
        flops=2 * 10**10,
        in_specs=[anywhere, anywhere],
    )(feat, cot)
    col_msgs = swapped(messages, "cols")
    ncols = len(col_msgs)
    message = pack_rows(1, 0, usual, shifts, feat)
    col_msgs, message, total = lax.optimization_barrier((col_msgs, message, total))
    feat_b = lax.ppermute(message, "rows", row_pairs[1])
    cot_rows = call(rows_kernel, bf(full, span), [], 1, 4)(cot)
    halo = bf(CHALO * chans + ncols * packed * TILE // span, span)
    messages = call(edge_kernel, (halo, halo), [], 1 + ncols, 8)(cot_rows, *col_msgs)
    row_msgs = swapped(messages, "rows")
    row_msgs[0], total = lax.optimization_barrier((row_msgs[0], total))
    row_msgs, feat_a = lax.optimization_barrier((row_msgs, feat_a))

    tall_c = (height + 2 * CHALO) * chans
    view = bf(tall_c, width)
    band = 3 * (POOL + 2) * chans
    act_grad, *rest = call(
        functools.partial(back_kernel, ncols),
        (
            jax.ShapeDtypeStruct((full, span), F32), view, view, view,
            bf(chans, 3 * height, TILE), bf(POOL * chans, band), bf(3 * chans, 3 * chans),
            bf(3 * POOL * chans, (POOL + 2) * chans),
        ),
        [pltpu.VMEM(((height + 2 * POOL) * chans, span), BF16)]
        + [pltpu.VMEM(((groups + 2) * chans, width), BF16)] * 2
        + [pltpu.VMEM(((groups + 2) * chans, TILE), BF16)]
        + [
            pltpu.VMEM((band, POOL * chans), F32),
            pltpu.VMEM((POOL * chans, band), BF16),
            pltpu.VMEM((9 * chans, TILE), F32),
            pltpu.VMEM((3 * chans, 3 * chans), BF16),
            pltpu.VMEM((chans, 9 * chans), F32),
        ],
        6 + ncols,
        16,
        flops=8 * 10**9,
    )(cot_rows, *row_msgs, *col_msgs, first_kernel, bottle_kernel, second_kernel)
    views, sides, weights = rest[:3], rest[3], rest[4:]

    grads, blended = lax.cond(
        total[0, 0] <= usual,
        functools.partial(main_pass, 0),
        functools.partial(main_pass, LARGEST * chans - usual),
        (feat_a, feat_b), shifts, feat, sides, act_grad, tuple(views), tuple(weights[:2]),
    )

    steps = []
    for axis, size in (("dp", dp), ("cols", cols), ("rows", rows)):
        bit = 1
        while bit < size:
            steps.append((axis, [(i, i ^ bit) for i in range(size)]))
            bit *= 2
    parts, prediction = 2, None
    for step, (axis, pairs) in enumerate(steps):
        if step >= len(steps) - 2:
            grads = lax.optimization_barrier(grads.astype(BF16))
        other = lax.ppermute(grads, axis, pairs)
        if 1 <= step <= parts:
            prediction = predict(
                blended, weights[2], (chans, height, span), parts, step - 1, prediction
            )
            other, prediction = lax.optimization_barrier((other, prediction))
        if step < len(steps) - 1:
            grads = grads.astype(F32) + other.astype(F32)
            if step < parts:
                grads, blended = lax.optimization_barrier((grads, blended))
    factor = 1.0 / math.sqrt(imgs * dp * height * rows * span * cols)
    shape = jax.ShapeDtypeStruct((9, chans, chans), F32)
    first_grad, second_grad = call(
        functools.partial(final_kernel, factor), (shape, shape), [], 2, 2
    )(grads, other)
    return (prediction[None], first_grad, second_grad)


def solution(mesh):
    placed = (
        P("dp", None, "rows", "cols"),
        P("dp", None, None),
        P(),
        P(),
        P(),
        P("dp", None, "rows", "cols"),
    )
    return jax.shard_map(
        shards,
        mesh=mesh,
        in_specs=placed,
        out_specs=(P("dp", None, "rows", "cols"), P(), P()),
        check_vma=False,
    )
```

```python
import functools
import math

import jax
import jax.numpy as jnp
from jax import lax
from jax.experimental import pallas as pl
from jax.experimental.pallas import tpu as pltpu
from jax.sharding import PartitionSpec as P


MAXSHIFT = 16
POOL = 4
BATCH = 8
TILE = 128
SLOT = 32
EXT = 9
FHALO = MAXSHIFT + EXT
USUAL = 14
LARGEST = FHALO + 1
CHALO = 5
F32 = jnp.float32
BF16 = jnp.bfloat16
VMEM = pl.BlockSpec(memory_space=pltpu.VMEM)
SMEM = pl.BlockSpec(memory_space=pltpu.SMEM)
MIB = 1024 * 1024


def lanes_of(shape):
    return lax.broadcasted_iota(jnp.int32, shape, len(shape) - 1)


def turn(values, shift):
    width = values.shape[-1]
    if isinstance(shift, int):
        shift = shift % width
        if shift == 0:
            return values
    return pltpu.roll(values, shift, values.ndim - 1)


def has_sides():
    row, col = lax.axis_index("rows"), lax.axis_index("cols")
    return (
        row > 0,
        row < lax.axis_size("rows") - 1,
        col > 0,
        col < lax.axis_size("cols") - 1,
    )


def as_bf(values):
    return values.astype(F32).astype(BF16)


def one_hot(mask):
    return jnp.where(mask, jnp.ones((), BF16), jnp.zeros((), BF16))


def rows_at(r, chans, count=1):
    if isinstance(r, int):
        return slice(r * chans, (r + count) * chans)
    return pl.ds(pl.multiple_of(r * chans, chans), count * chans)


def to_rows(block):
    chans, height, span = block.shape
    return jnp.transpose(block, (1, 0, 2)).reshape(height * chans, span)


def to_planes(block, chans):
    height = block.shape[0] // chans
    return jnp.transpose(block.reshape(height, chans, block.shape[1]), (1, 0, 2))


def tiles_of(span):
    return [slice(t, t + TILE) for t in range(0, span, TILE)]


def is_even(axis):
    return lax.rem(lax.axis_index(axis), 2) == 0


def swaps(size):
    first = [(i, i ^ 1) for i in range(size)]
    second = [(i, i + 1) for i in range(1, size - 1, 2)]
    return [first, second + [(j, i) for i, j in second]]


def needed(shift, below):
    return jnp.maximum(EXT + shift if below else EXT - shift, 0)


def feature_kernel(index, skip, shifts, feat, msg, *counts):
    chans, height, span = feat.shape
    full = chans * height
    size = msg.shape[0]
    chunk = size // 4
    source = feat[...].reshape(full, span)
    lane = lanes_of((8, full))
    chan, row = lane // height, lane % height
    to_below = is_even("rows") if index == 0 else jnp.logical_not(is_even("rows"))
    target = jnp.full((8, full), -1, jnp.int32)
    at, up, down = jnp.int32(-skip), jnp.int32(0), jnp.int32(0)
    for c in range(chans):
        shift = shifts[0, c]
        n_up, n_down = needed(shift, False), needed(shift, True)
        count = jnp.where(to_below, n_up, n_down)
        first = jnp.where(to_below, height - count, 0)
        mine = (chan == c) & (row >= first) & (row < first + count)
        target = jnp.where(mine, row + (at - first), target)
        at, up, down = at + count, up + n_up, down + n_down
    for out in counts:
        out[...] = jnp.full(out.shape, jnp.maximum(up, down), jnp.int32)
    place = as_bf(lax.broadcasted_iota(jnp.int32, (chunk, full), 0))
    for p in range(0, size, chunk):
        late = (p + skip) // FHALO * height // TILE * TILE
        pick = one_hot(place[:, late:] == as_bf(target[0:1, late:] - p))
        msg[p : p + chunk] = jnp.dot(
            pick, source[late:], preferred_element_type=F32
        ).astype(BF16)


def rows_kernel(source, out):
    for part in tiles_of(source.shape[2]):
        out[:, part] = to_rows(source[:, :, part])


def edge_lanes(shape, right, count):
    lane = lanes_of(shape)
    return jnp.where(jnp.where(right, TILE - 1 - lane, lane) < count, 1.0, 0.0).astype(BF16)


def slots(chans, height):
    half, block = chans // 2, height // 2
    for h in (0, 1):
        for m in (0, 1):
            yield 2 * h + m, slice(h * half, (h + 1) * half), slice(m * block, (m + 1) * block)


def column_kernel(feat, cot, *rest):
    col_msgs, (feat_edge, cot_edge, sems) = rest[:-3], rest[-3:]
    chans, height, span = feat.shape
    for index, msg in enumerate(col_msgs):
        right = is_even("cols") if index == 0 else jnp.logical_not(is_even("cols"))
        part = pl.ds(pl.multiple_of(jnp.where(right, span - TILE, 0), TILE), TILE)
        copies = [
            pltpu.make_async_copy(ref.at[:, :, part], edge, sems.at[i])
            for i, (ref, edge) in enumerate(((feat, feat_edge), (cot, cot_edge)))
        ]
        for copy in copies:
            copy.start()
        for copy in copies:
            copy.wait()
        shape = (1, height // 2, TILE)
        inner = edge_lanes(shape, right, FHALO)
        outer = edge_lanes(shape, right, SLOT) - inner
        total = None
        for q, channels, rows in slots(chans, height):
            cots = turn(cot_edge[channels, rows, :], jnp.where(right, TILE - FHALO, FHALO))
            piece = feat_edge[channels, rows, :] * inner + cots * outer
            piece = turn(piece, jnp.where(right, (q + 1) * SLOT % TILE, q * SLOT))
            total = piece if total is None else total + piece
        msg[...] = total.reshape(msg.shape)


def edge_kernel(cot_rows, *rest):
    cols, (msg_a, msg_b) = rest[:-2], rest[-2:]
    span = cot_rows.shape[1]
    size = msg_a.shape[0] - sum(c.shape[0] * TILE // span for c in cols)
    edge = cot_rows.shape[0] - size
    chans = size // CHALO
    low = jnp.where(is_even("rows"), edge, 0)
    msg_a[0:size] = cot_rows[pl.ds(pl.multiple_of(low, chans), size), :]
    msg_b[0:size] = cot_rows[pl.ds(pl.multiple_of(edge - low, chans), size), :]
    at = size
    for col in cols:
        count = col.shape[0] * TILE // span
        for t, part in enumerate(tiles_of(span)):
            block = col[t * count : (t + 1) * count]
            msg_a[at : at + count, part] = block
            msg_b[at : at + count, part] = block
        at += count


def corner_views(msg, size, cols):
    span = msg.shape[1]
    views, at = [], size
    for col in cols:
        count = col.shape[0] * TILE // span
        views.append(
            jnp.concatenate([msg[at : at + count, part] for part in tiles_of(span)], axis=0)
        )
        at += count
    return views


def halo_block(sources, slot, rows, kind):
    total = None
    if kind == "features":
        count, shift_r, shift_l = FHALO, -slot * SLOT, TILE - (slot + 1) * SLOT
    else:
        count = CHALO
        shift_r, shift_l = -slot * SLOT - FHALO, TILE - (slot + 1) * SLOT + FHALO
    for index, source in enumerate(sources):
        from_right = is_even("cols") if index == 0 else jnp.logical_not(is_even("cols"))
        block = source.reshape(source.shape[0] // rows, rows, TILE)
        block = turn(block, jnp.where(from_right, shift_r % TILE, shift_l % TILE))
        block = block * edge_lanes((1, rows, TILE), jnp.logical_not(from_right), count)
        total = block if total is None else total + block
    return total


def halo_rows(sources, m, rows, kind):
    return to_rows(
        jnp.concatenate([halo_block(sources, 2 * h + m, rows, kind) for h in (0, 1)], axis=0)
    )


def columns_seen(shape, span):
    _, _, has_left, has_right = has_sides()
    lane = lanes_of(shape)
    middle = span + TILE // 2
    return (lane < span) | ((lane < middle) & has_right) | ((lane >= middle) & has_left)


def cell_matrix(width, by_cell):
    shape = (TILE, width) if by_cell else (width, TILE)
    lane = lax.broadcasted_iota(jnp.int32, shape, 1 if by_cell else 0)
    cell = lax.broadcasted_iota(jnp.int32, shape, 0 if by_cell else 1)
    place = lane // POOL + jnp.where(lane >= width - TILE // 2, TILE - width // POOL, 0)
    return jnp.where(place == cell, 1.0, 0.0).astype(BF16)


def cells_seen(shape, span):
    _, _, has_left, has_right = has_sides()
    lane = lanes_of(shape)
    count = span // POOL
    middle = (count + TILE) // 2
    return (lane < count) | ((lane < middle) & has_right) | ((lane >= middle) & has_left)


def store_split(high, low, at, total):
    top = total.astype(BF16)
    high[at, :] = top
    low[at, :] = (total - top.astype(F32)).astype(BF16)


def block_sums(high, low):
    matrix = cell_matrix(high.shape[1], False)
    return jnp.dot(
        jnp.concatenate([high[...], low[...]], axis=1),
        jnp.concatenate([matrix, matrix], axis=0),
        preferred_element_type=F32,
    )


def spread(rows, width, count):
    values = jnp.concatenate(rows, axis=0)
    top = values.astype(BF16)
    rest = (values - top.astype(F32)).astype(BF16)
    matrix = cell_matrix(width, True)[:, 0:count]
    return jnp.dot(
        jnp.concatenate([top, rest], axis=1),
        jnp.concatenate([matrix, matrix], axis=0),
        preferred_element_type=F32,
    )


def fill_bands(out, kernel, count):
    chans = kernel.shape[1]
    out[...] = jnp.zeros(out.shape, out.dtype)
    for k in range(count):
        for b in range(3):
            for a in range(3):
                at = (b * (count + 2) + k + a) * chans
                out[k * chans : (k + 1) * chans, at : at + chans] = kernel[3 * a + b].astype(
                    out.dtype
                )


def fill_turned_bands(out, kernel, count):
    chans = kernel.shape[1]
    out[...] = jnp.zeros(out.shape, out.dtype)
    for k in range(count):
        for b in range(3):
            for a in range(3):
                at = (b * (count + 2) + k + a) * chans
                out[at : at + chans, k * chans : (k + 1) * chans] = kernel[8 - 3 * a - b].astype(
                    out.dtype
                )


def stacked(views, at):
    return jnp.concatenate([view[at, :] for view in views], axis=0)


def paired(bands, views, g, chans):
    width = views[0].shape[1]
    sides = [
        stacked(views, rows_at((g + i) * POOL, chans, POOL + 2)) for i in (0, 1)
    ]
    parts = jnp.dot(
        bands[...], jnp.concatenate(sides, axis=1), preferred_element_type=F32
    )
    return parts[:, 0:width], parts[:, width:]


def conv_sum(parts, chans, step):
    return (
        turn(parts[0:chans], step)
        + parts[chans : 2 * chans]
        + turn(parts[2 * chans : 3 * chans], -step)
    )


def back_kernel(
    ncols, cot, msg_a, msg_b, *rest,
):
    cols, (
        first, bottle, second,
        act_grad, cot_m, cot_0, cot_p, sides, first_bands, bottle_bands, second_bands,
        back, high, low, coarse, bands_f, bands, small_f, small, wide_f,
    ) = rest[:ncols], rest[ncols:]
    chans = second.shape[1]
    full, span = cot.shape
    height = full // chans
    width = span + TILE
    groups = height // POOL
    has_up, has_down, _, _ = has_sides()

    fill_turned_bands(bands_f, second, POOL)
    bands[...] = bands_f[...].T.astype(BF16)
    fill_turned_bands(small_f, bottle, 1)
    small_t = small_f[...].T
    for b in range(3):
        small[rows_at(b, chans)] = small_t[0:chans, 3 * b * chans : 3 * (b + 1) * chans].astype(BF16)
    fill_bands(first_bands, first, POOL)
    fill_bands(wide_f, bottle, 1)
    for b in range(3):
        bottle_bands[rows_at(b, chans)] = wide_f[
            0:chans, 3 * b * chans : 3 * (b + 1) * chans
        ].astype(BF16)
    second_bands[...] = jnp.zeros(second_bands.shape, BF16)
    for k in range(POOL):
        for b in range(3):
            for a in range(3):
                second_bands[
                    rows_at(3 * k + b, chans), (k + a) * chans : (k + a + 1) * chans
                ] = second[3 * a + b]

    size = CHALO * chans
    block = height // 2

    def halo_columns(sources, at):
        for q, channels, rows in slots(chans, height):
            sides[channels, at + rows.start : at + rows.stop, :] = halo_block(
                sources, q, block, "features"
            )

    own = [c[...] for c in cols]
    halo_columns(own, height)
    cot_0[rows_at(CHALO, chans, height), 0:span] = cot[...]
    for m in (0, 1):
        cot_0[rows_at(CHALO + m * block, chans, block), span:width] = halo_rows(
            own, m, block, "cotangent"
        )

    def vertical(up, down):
        cot_0[rows_at(0, chans, CHALO), 0:span] = up[0:size]
        cot_0[rows_at(CHALO + height, chans, CHALO), 0:span] = down[0:size]
        above, below = corner_views(up, size, cols), corner_views(down, size, cols)
        cot_0[rows_at(0, chans, CHALO), span:width] = halo_rows(above, 1, block, "cotangent")[
            (block - CHALO) * chans :
        ]
        cot_0[rows_at(CHALO + height, chans, CHALO), span:width] = halo_rows(
            below, 0, block, "cotangent"
        )[0:size]
        halo_columns(above, 0)
        halo_columns(below, 2 * height)

    pl.when(is_even("rows"))(lambda: vertical(msg_b, msg_a))
    pl.when(jnp.logical_not(is_even("rows")))(lambda: vertical(msg_a, msg_b))
    for j in range(height + 2 * CHALO):
        at = rows_at(j, chans)
        cot_m[at] = turn(cot_0[at], 1)
        cot_p[at] = turn(cot_0[at], -1)
    def pair(p, _):
        both = paired(bands, (cot_m, cot_0, cot_p), 2 * p, chans)
        for g, rows in zip((2 * p, 2 * p + 1), both):
            rows = rows.astype(BF16)
            back[rows_at(g * POOL, chans, POOL), :] = rows[:, 0:span]
            rows = rows.astype(F32)
            total = rows[0:chans]
            for k in range(1, POOL):
                total = total + rows[k * chans : (k + 1) * chans]
            store_split(high, low, rows_at(g, chans), total)
        return 0

    lax.fori_loop(0, (groups + 2) // 2, pair, 0, unroll=5)
    sums = block_sums(high, low)
    seen_cells = cells_seen((chans, TILE), span)
    for g in range(groups + 2):
        at = rows_at(g, chans)
        seen = seen_cells
        if g == 0:
            seen = seen & has_up
        elif g == groups + 1:
            seen = seen & has_down
        coarse[at] = jnp.where(seen, sums[at], 0.0).astype(BF16)
    means = []
    for g in range(groups):
        parts = jnp.dot(small[...], coarse[rows_at(g, chans, 3), :], preferred_element_type=F32)
        means.append(conv_sum(parts, chans, 1) * (1.0 / POOL**2))
    mean = spread(means, width, span)
    for r in range(height):
        act_grad[rows_at(r, chans), :] = (
            back[rows_at(r + POOL, chans), :].astype(F32) + mean[rows_at(r // POOL, chans)]
        )


def correlate(u, u0, views, v0, acc, height, chans, span):
    groups = range(0, height, BATCH)
    left = jnp.concatenate(
        [
            jnp.concatenate(
                [view[rows_at(v0 + g, chans, BATCH + 2), 0:span] for view in views], axis=0
            )
            for g in groups
        ],
        axis=1,
    )
    right = jnp.concatenate([u[rows_at(u0 + g, chans, BATCH), 0:span] for g in groups], axis=1)
    acc[...] = lax.dot_general(
        left, right, (((1,), (1,)), ((), ())), preferred_element_type=F32
    )


def folded(acc, chans):
    lane = lanes_of((3 * chans, TILE))
    result = jnp.zeros((3 * chans, TILE), F32)
    per_tile = TILE // chans
    for b in range(3):
        total = None
        for place in range(per_tile):
            column = None
            for k in range(place, BATCH, per_tile):
                part = slice(k // per_tile * TILE, (k // per_tile + 1) * TILE)
                block = acc[rows_at(b * (BATCH + 2) + k, chans, 3), part]
                column = block if column is None else column + block
            column = turn(column, (b - place) * chans)
            total = column if total is None else total + column
        result = jnp.where((lane >= b * chans) & (lane < (b + 1) * chans), total, result)
    return result


def main_kernel(
    shifts, feat, feat_a, feat_b, sides, act_grad, view_m, view_0, view_p, bands, small,
    grads, blended,
    lent, moved, warp_m, warp_0, warp_p, act, high, low, pooled, pre_grad, acc,
):
    chans, height, span = feat.shape
    tiles = span // TILE
    width = span + TILE
    groups = height // POOL
    has_up, has_down, has_left, has_right = has_sides()
    seen_cols = columns_seen((chans, width), span)

    size = feat_a.shape[0]
    window = lent.shape[1] - size
    lent[:, size:, :] = jnp.zeros((2, window, span), BF16)

    def borrow(up, down):
        lent[0, 0:size] = up[...]
        lent[1, 0:size] = down[...]

    pl.when(is_even("rows"))(lambda: borrow(feat_b, feat_a))
    pl.when(jnp.logical_not(is_even("rows")))(lambda: borrow(feat_a, feat_b))

    tall = moved.shape[1]
    lane = lanes_of((tall, TILE))
    seen_halo = one_hot(((lane < TILE // 2) & has_right) | ((lane >= TILE // 2) & has_left))
    lane, mirrored = as_bf(lane), as_bf(TILE - 1 - lane)
    step = as_bf(
        lanes_of((tall, 3 * height)) - lax.broadcasted_iota(jnp.int32, (tall, 3 * height), 0)
    )
    depth = 2 * window + height
    source = lanes_of((1, depth))
    apart = as_bf(lax.broadcasted_iota(jnp.int32, (tall, depth), 0) - lanes_of((tall, depth)))
    align = 16

    def warp(c, ats):
        at_up, at_down = ats
        shift, move = shifts[0, c], shifts[1, c]
        n_up, n_down = needed(shift, False), needed(shift, True)
        base_up, base_down = (
            pl.multiple_of(lax.div(at, align) * align, align) for at in (at_up, at_down)
        )
        skip_up, skip_down = at_up - base_up, at_down - base_down
        own = EXT - window - shift
        below = own - skip_down
        above = EXT - skip_up - n_up - shift
        in_up = (source >= skip_up) & (source < skip_up + n_up)
        first_down = window + height + skip_down
        in_down = (source >= first_down) & (source < first_down + n_down)
        none = 4 * depth
        offset = jnp.where(
            source < window,
            jnp.where(in_up, above, none),
            jnp.where(source < window + height, own, jnp.where(in_down, below, none)),
        )
        pick = one_hot(apart == as_bf(offset))
        rows = jnp.concatenate(
            [lent[0, pl.ds(base_up, window), :], feat[c], lent[1, pl.ds(base_down, window), :]], axis=0
        )
        plane = jnp.dot(pick, rows, preferred_element_type=F32).astype(BF16)
        pick = one_hot(step == as_bf(height - EXT + shift))
        plane = [plane[:, part] for part in tiles_of(span)]
        plane.append(jnp.dot(pick, sides[c], preferred_element_type=F32).astype(BF16))
        amount = jnp.where(move > 0, TILE - move, -move)
        parts = [turn(part, amount) for part in plane]
        inside = jnp.where(move > 0, lane, mirrored) < as_bf(TILE - jnp.abs(move))
        for t, part in enumerate(tiles_of(width)):
            after, before = parts[(t + 1) % (tiles + 1)], parts[t - 1]
            result = jnp.where(inside, parts[t], jnp.where(move > 0, after, before))
            moved[c, :, part] = result * seen_halo if t == tiles else result
        return at_up + n_up, at_down + n_down

    lax.fori_loop(0, chans, warp, (jnp.int32(0), jnp.int32(0)), unroll=16)
    chunk = 16
    for r in range(0, tall, chunk):
        for part in tiles_of(width):
            warp_0[rows_at(r, chans, chunk), part] = to_rows(moved[:, r : r + chunk, part])

    def clear(r, count):
        warp_0[rows_at(r, chans, count)] = jnp.zeros((count * chans, width), BF16)

    pl.when(jnp.logical_not(has_up))(lambda: clear(0, EXT))
    pl.when(jnp.logical_not(has_down))(lambda: clear(EXT + height, EXT))
    for j in range(height + 2 * EXT):
        at = rows_at(j, chans)
        warp_m[at] = turn(warp_0[at], 1)
        warp_p[at] = turn(warp_0[at], -1)

    for g in range(0, groups + 4, 2):
        both = paired(bands, (warp_m, warp_0, warp_p), g, chans)
        for g, pre in zip((g, g + 1), both):
            sigma = 0.5 * jnp.tanh(0.5 * pre) + 0.5
            rows = (pre * sigma).astype(BF16)
            act[rows_at(g * POOL, chans, POOL), :] = rows
            rows = rows.astype(F32)
            total = rows[0:chans]
            for k in range(1, POOL):
                total = total + rows[k * chans : (k + 1) * chans]
            store_split(high, low, rows_at(g, chans), total)
            if 2 <= g < groups + 2:
                there = rows_at(g * POOL - 2 * POOL, chans, POOL)
                pre, sigma = pre[:, 0:span], sigma[:, 0:span]
                pre_grad[there, :] = (
                    act_grad[there, :] * (sigma * (1.0 + pre * (1.0 - sigma)))
                ).astype(BF16)
    sums = block_sums(high, low)
    seen_cells = cells_seen((chans, TILE), span)
    for g in range(groups + 4):
        at = rows_at(g, chans)
        seen = seen_cells
        if g < 2:
            seen = seen & has_up
        elif g >= groups + 2:
            seen = seen & has_down
        pooled[at] = jnp.where(seen, sums[at] * (1.0 / POOL**2), 0.0).astype(BF16)

    bottles = []
    for g in range(groups + 2):
        parts = jnp.dot(small[...], pooled[rows_at(g, chans, 3), :], preferred_element_type=F32)
        bottles.append(conv_sum(parts, chans, 1))
    bottle = spread(bottles, width, width)
    for g in range(groups + 2):
        rows, seen = range(POOL), seen_cols
        if g == 0:
            rows, seen = (POOL - 1,), seen & has_up
        elif g == groups + 1:
            rows, seen = (0,), seen & has_down
        for k in rows:
            row = act[rows_at((g + 1) * POOL + k, chans), :].astype(F32) + bottle[rows_at(g, chans)]
            blended[rows_at(g * POOL + k - POOL + 1, chans), :] = jnp.where(seen, row, 0.0).astype(
                BF16
            )

    correlate(pre_grad, 0, (warp_m, warp_0, warp_p), EXT - 1, acc, height, chans, span)
    first_part = folded(acc, chans)
    correlate(blended, 1, (view_m, view_0, view_p), CHALO - 1, acc, height, chans, span)
    second_part = folded(acc, chans)
    lane = lanes_of((3 * chans, TILE))
    grads[0 : 3 * chans] = jnp.where(lane < 3 * chans, first_part, turn(second_part, 3 * chans))
    half = 3 * chans // 2
    grads[3 * chans :] = jnp.where(
        lane[0:half] < TILE // 2,
        turn(second_part[0:half], -chans),
        turn(second_part[half:], TILE // 2 - chans),
    )


def predict_kernel(part, blended, bands, *rest):
    out, rows = rest[-2:]
    chans, height, span = out.shape

    def group(g, _):
        at = rows_at(part * height + g * POOL, chans, POOL + 2)
        parts = jnp.dot(bands[...], blended[at, :], preferred_element_type=F32)
        for k in range(POOL):
            row = conv_sum(parts[3 * k * chans : 3 * (k + 1) * chans], chans, 1)
            rows[rows_at(g * POOL + k, chans), :] = row[:, 0:span].astype(BF16)
        return 0

    lax.fori_loop(0, height // POOL, group, 0, unroll=4)
    for part in tiles_of(span):
        out[:, :, part] = to_planes(rows[:, part], chans)


def final_kernel(factor, mine, other, first, second):
    chans = first.shape[1]
    total = (mine[...].astype(F32) + other[...].astype(F32)) * factor
    turned = total[0 : 3 * chans].T
    for b in range(3):
        for a in range(3):
            first[3 * a + b] = turned[b * chans : (b + 1) * chans, a * chans : (a + 1) * chans]
    half = 3 * chans // 2
    low = total[3 * chans :]
    both = jnp.concatenate([low, turn(low, -(TILE // 2))], axis=0)
    for a in range(3):
        at = slice((2 - a) * chans, (3 - a) * chans)
        second[3 * a + 2] = turn(total[at], -3 * chans)[:, 0:chans]
        second[3 * a + 1] = both[at, 0:chans]
        second[3 * a + 0] = turn(both[at], -chans)[:, 0:chans]


def call(kernel, outs, scratch, n_in, limit, flops=0, smem_first=False, **more):
    specs = [VMEM] * n_in
    if smem_first:
        specs[0] = SMEM
    more.setdefault("in_specs", specs)
    more.setdefault("out_specs", jax.tree.map(lambda _: VMEM, outs))
    return pl.pallas_call(
        kernel,
        out_shape=outs,
        scratch_shapes=scratch,
        compiler_params=pltpu.CompilerParams(vmem_limit_bytes=limit * MIB),
        cost_estimate=pl.CostEstimate(flops=flops, bytes_accessed=4 * MIB, transcendentals=0),
        **more,
    )


def predict(blended, bands, shape, parts, part, before):
    chans, height, span = shape
    rows = height // parts
    block = pl.BlockSpec((chans, rows, span), lambda i: (0, part, 0))
    whole = lambda a: pl.BlockSpec(a.shape, lambda i: (0,) * a.ndim)
    args = (blended, bands)
    specs = [whole(a) for a in args]
    more = {}
    if before is not None:
        args += (before,)
        specs.append(pl.BlockSpec(memory_space=pl.ANY))
        more["input_output_aliases"] = {2: 0}
    return call(
        functools.partial(predict_kernel, part),
        jax.ShapeDtypeStruct(shape, BF16),
        [
            pltpu.VMEM((chans * rows, span), BF16),
        ],
        len(args),
        12,
        flops=10**9,
        grid=(1,),
        in_specs=specs,
        out_specs=block,
        **more,
    )(*args)


def bf(*shape):
    return jax.ShapeDtypeStruct(shape, BF16)


def swapped(messages, axis):
    pairs = [p for p in swaps(lax.axis_size(axis)) if p]
    return [lax.ppermute(m, axis, p) for m, p in zip(messages, pairs)]


def pack_rows(index, skip, size, shifts, feat, counted=False):
    message = bf(size, feat.shape[2])
    if counted:
        message = (message, jax.ShapeDtypeStruct((8, TILE), jnp.int32))
    return call(
        functools.partial(feature_kernel, index, skip),
        message, [], 2, 16, smem_first=True,
    )(shifts, feat)


def main_pass(rest, lent, shifts, feat, sides, act_grad, views, bands):
    chans, height, span = feat.shape
    width = span + TILE
    full = height * chans
    groups = height // POOL
    band = 3 * (POOL + 2) * chans
    if rest:
        size = lent[0].shape[0]
        more = swapped([pack_rows(i, size, rest, shifts, feat) for i in (0, 1)], "rows")
        lent = [jnp.concatenate(pair, axis=0) for pair in zip(lent, more)]
    size = lent[0].shape[0]
    tall = pl.cdiv(height + 2 * EXT, 16) * 16
    grads, blended = call(
        main_kernel,
        (jax.ShapeDtypeStruct((9 * chans // 2, TILE), F32), bf((height + 2) * chans, width)),
        [
            pltpu.VMEM((2, size + 48, span), BF16),
            pltpu.VMEM((chans, tall, width), BF16),
        ]
        + [pltpu.VMEM((tall * chans, width), BF16)] * 3
        + [pltpu.VMEM(((height + 4 * POOL) * chans, width), BF16)]
        + [pltpu.VMEM(((groups + 4) * chans, width), BF16)] * 2
        + [pltpu.VMEM(((groups + 4) * chans, TILE), BF16)]
        + [
            pltpu.VMEM((full, span), BF16),
            pltpu.VMEM((3 * (BATCH + 2) * chans, BATCH * chans), F32),
        ],
        11,
        20,
        flops=10**10,
        smem_first=True,
    )(
        shifts, feat, *lent, sides, act_grad, *views, *bands
    )

    return grads, blended


def shards(features, shifts, first_kernel, bottle_kernel, second_kernel, cotangent):
    imgs, chans, height, span = features.shape
    rows, cols, dp = (lax.axis_size(a) for a in ("rows", "cols", "dp"))
    full = height * chans

    width = span + TILE
    groups = height // POOL
    feat, cot, shifts = features[0], cotangent[0], shifts[0].T
    row_pairs = swaps(rows)

    usual = USUAL * chans
    message, total = pack_rows(0, 0, usual, shifts, feat, counted=True)
    message, total, cot = lax.optimization_barrier((message, total, cot))
    feat_a = lax.ppermute(message, "rows", row_pairs[0])
    bit = 1
    while bit < dp:
        total = jnp.maximum(total, lax.ppermute(total, "dp", [(i, i ^ bit) for i in range(dp)]))
        bit *= 2

    packed = chans * (height * SLOT // TILE)
    anywhere = pl.BlockSpec(memory_space=pl.ANY)
    messages = call(
        column_kernel,
        (bf(packed, TILE),) * (1 if cols == 2 else 2),
        [pltpu.VMEM((chans, height, TILE), BF16)] * 2 + [pltpu.SemaphoreType.DMA((2,))],
        2,
        8,
        flops=2 * 10**10,
        in_specs=[anywhere, anywhere],
    )(feat, cot)
    col_msgs = swapped(messages, "cols")
    ncols = len(col_msgs)
    message = pack_rows(1, 0, usual, shifts, feat)
    col_msgs, message, total = lax.optimization_barrier((col_msgs, message, total))
    feat_b = lax.ppermute(message, "rows", row_pairs[1])
    cot_rows = call(rows_kernel, bf(full, span), [], 1, 4)(cot)
    halo = bf(CHALO * chans + ncols * packed * TILE // span, span)
    messages = call(edge_kernel, (halo, halo), [], 1 + ncols, 8)(cot_rows, *col_msgs)
    row_msgs = swapped(messages, "rows")
    row_msgs[0], total = lax.optimization_barrier((row_msgs[0], total))
    row_msgs, feat_a = lax.optimization_barrier((row_msgs, feat_a))

    tall_c = (height + 2 * CHALO) * chans
    view = bf(tall_c, width)
    band = 3 * (POOL + 2) * chans
    act_grad, *rest = call(
        functools.partial(back_kernel, ncols),
        (
            jax.ShapeDtypeStruct((full, span), F32), view, view, view,
            bf(chans, 3 * height, TILE), bf(POOL * chans, band), bf(3 * chans, 3 * chans),
            bf(3 * POOL * chans, (POOL + 2) * chans),
        ),
        [pltpu.VMEM(((height + 2 * POOL) * chans, span), BF16)]
        + [pltpu.VMEM(((groups + 2) * chans, width), BF16)] * 2
        + [pltpu.VMEM(((groups + 2) * chans, TILE), BF16)]
        + [
            pltpu.VMEM((band, POOL * chans), F32),
            pltpu.VMEM((POOL * chans, band), BF16),
            pltpu.VMEM((9 * chans, TILE), F32),
            pltpu.VMEM((3 * chans, 3 * chans), BF16),
            pltpu.VMEM((chans, 9 * chans), F32),
        ],
        6 + ncols,
        16,
        flops=8 * 10**9,
    )(cot_rows, *row_msgs, *col_msgs, first_kernel, bottle_kernel, second_kernel)
    views, sides, weights = rest[:3], rest[3], rest[4:]

    grads, blended = lax.cond(
        total[0, 0] <= usual,
        functools.partial(main_pass, 0),
        functools.partial(main_pass, LARGEST * chans - usual),
        (feat_a, feat_b), shifts, feat, sides, act_grad, tuple(views), tuple(weights[:2]),
    )

    steps = []
    for axis, size in (("dp", dp), ("cols", cols), ("rows", rows)):
        bit = 1
        while bit < size:
            steps.append((axis, [(i, i ^ bit) for i in range(size)]))
            bit *= 2
    parts, prediction = 2, None
    for step, (axis, pairs) in enumerate(steps):
        if step >= len(steps) - 2:
            grads = lax.optimization_barrier(grads.astype(BF16))
        other = lax.ppermute(grads, axis, pairs)
        if 1 <= step <= parts:
            prediction = predict(
                blended, weights[2], (chans, height, span), parts, step - 1, prediction
            )
            other, prediction = lax.optimization_barrier((other, prediction))
        if step < len(steps) - 1:
            grads = grads.astype(F32) + other.astype(F32)
            if step < parts:
                grads, blended = lax.optimization_barrier((grads, blended))
    factor = 1.0 / math.sqrt(imgs * dp * height * rows * span * cols)
    shape = jax.ShapeDtypeStruct((9, chans, chans), F32)
    first_grad, second_grad = call(
        functools.partial(final_kernel, factor), (shape, shape), [], 2, 2
    )(grads, other)
    return (prediction[None], first_grad, second_grad)


def solution(mesh):
    placed = (
        P("dp", None, "rows", "cols"),
        P("dp", None, None),
        P(),
        P(),
        P(),
        P("dp", None, "rows", "cols"),
    )
    return jax.shard_map(
        shards,
        mesh=mesh,
        in_specs=placed,
        out_specs=(P("dp", None, "rows", "cols"), P(), P()),
        check_vma=False,
    )
```
